32 devices in a mesh: section: 2 (over core), dp: 4 (over y, x), mp: 4 (over z).
Axes of the slice: x: 2, y: 2, z: 4, core: 2. Of those that a mesh axis runs over, the one named last changes fastest.
Arguments:
- layer_input: bfloat16 [2, 4, 1024, 1024], P(None, 'dp', 'mp'), may hold values from -6 to 6
- cotangent: bfloat16 [2, 4, 1024, 1024], P(None, 'dp', 'mp'), may hold values from -6 to 6
- example_lengths: int32 [2, 4, 4], P(None, 'dp'), may hold values from 1 to 976, as said below
- attn_gain: bfloat16 [2, 1024], P('section'), may hold values from 0.5 to 1.5
- attn_shift: bfloat16 [2, 1024], P('section'), may hold values from -1.75 to 1.75
- query_key_value_weight: bfloat16 [2, 1024, 3072], P('section', None, 'mp'), may hold values from -0.1875 to 0.1875
- qkv_bias: bfloat16 [2, 3072], P('section', 'mp'), may hold values from -1.75 to 1.75
- attention_output_weight: bfloat16 [2, 1024, 1024], P('section', 'mp'), may hold values from -0.75 to 0.75
- out_bias: bfloat16 [2, 1024], P('section'), may hold values from -1.75 to 1.75
- ffn_gain: bfloat16 [2, 1024], P('section'), may hold values from 0.5 to 1.5
- ffn_shift: bfloat16 [2, 1024], P('section'), may hold values from -1.75 to 1.75
- up_projection_weight: bfloat16 [2, 1024, 4096], P('section', None, 'mp'), may hold values from -0.1875 to 0.1875
- up_projection_bias: bfloat16 [2, 4096], P('section', 'mp'), may hold values from -1.75 to 1.75
- down_projection_weight: bfloat16 [2, 4096, 1024], P('section', 'mp'), may hold values from -0.09375 to 0.09375
- down_bias: bfloat16 [2, 1024], P('section'), may hold values from -1.75 to 1.75
- prefix_table: bfloat16 [10, 1024], replicated, may hold values from -6 to 6
- mid_weight: bfloat16 [1024, 512], replicated, may hold values from -0.1875 to 0.1875
- mid_bias: bfloat16 [512], replicated, may hold values from -1.75 to 1.75
- prefix_weight: bfloat16 [512, 4096], P(None, ('section', 'mp')), may hold values from -0.25 to 0.25
- prefix_bias: bfloat16 [4096], P(('section', 'mp')), may hold values from -1.75 to 1.75
Outputs:
- activations: bfloat16 [2, 2, 4, 1024, 1024], P('section', None, 'dp', 'mp')
- input_grads: bfloat16 [2, 2, 4, 1024, 1024], P('section', None, 'dp', 'mp')
- table_grad: float32 [10, 1024], replicated
- mid_weight_grad: float32 [1024, 512], replicated
- mid_bias_grad: float32 [512], replicated
- prefix_weight_grad: float32 [512, 4096], P(None, ('section', 'mp'))
- prefix_bias_grad: float32 [4096], P(('section', 'mp'))
The draws below stay inside these ranges and needn't reach their ends.
Inputs may be any that keep to these rules, and one draw needn't show every extreme that they name: `example_lengths`: the 4 examples of a sequence are consecutive runs of rows that together fill its 1024 rows.
All inputs are finite; a program needn't handle non-finite values.
Results may differ from the reference program's by a relative error of at most 0.02.
Values may be sent and summed in bfloat16 or wider, within the bound.
A program may use at most 256 MiB of HBM per device.

```python
import jax
import jax.numpy as jnp
from jax import lax

D = 1024
HEADS = 16
HEAD_DIM = 64
FF = 4096
MID = 512
PREFIX = 10
EX = 4
SEQ_LEN = 1024
MB = 2
SEQ_MB = 1
LAYERS = 2
SEQS = 4


def draw_example_lengths(key, part):
    key = jax.random.fold_in(key, 11)
    weight_key, pick_key = jax.random.split(key)
    shares = jax.random.randint(weight_key, (MB, SEQS, EX), 1, 9).astype(jnp.int32)
    share_total = jnp.sum(shares, axis=-1, keepdims=True)
    lengths = shares * SEQ_LEN // share_total
    missing = SEQ_LEN - jnp.sum(lengths, axis=-1)
    lengths = lengths.at[:, :, EX - 1].add(missing)
    groups = SEQS // SEQ_MB
    chosen_slot = jax.random.randint(pick_key, (groups,), 0, MB * SEQ_MB).astype(jnp.int32)
    batch_ids = jnp.arange(MB, dtype=jnp.int32)[:, None]
    seq_ids = jnp.arange(SEQS, dtype=jnp.int32)[None, :]
    slot_ids = batch_ids * SEQ_MB + seq_ids % SEQ_MB
    chosen = slot_ids == chosen_slot[seq_ids // SEQ_MB]
    short_run = SEQ_LEN // 64
    spanning = jnp.full((EX,), short_run, jnp.int32).at[1].set(SEQ_LEN - (EX - 1) * short_run)
    return jnp.where(chosen[:, :, None], spanning[None, None, :], lengths).astype(jnp.int32)


def level_of(stream_key, shape, cuts, least, high):
    def one(axis_at, blocks):
        steps = jax.random.uniform(jax.random.fold_in(jax.random.fold_in(stream_key, 6), axis_at), (blocks,), jnp.float32, least / len(cuts), high / len(cuts))
        return jnp.repeat(jnp.exp(steps), shape[axis_at] // blocks).reshape((-1,) + (1,) * (len(shape) - axis_at - 1))

    loudness = one(*cuts[0])
    for cut in cuts[1:]:
        loudness = loudness * one(*cut)
    return loudness


def scatter_about(stream_key, shape, deviation, bound, pieces=(), held_as=jnp.bfloat16):
    result = deviation * jax.random.normal(stream_key, shape, jnp.float32)
    if pieces:
        result = result * level_of(stream_key, shape, pieces, -0.22, 0.18)
    return jnp.clip(result, -bound, bound).astype(held_as)


def setup_inputs(seed: int = 0) -> dict:
    key_list = jax.random.split(jax.random.key(seed), 21)
    layer_input = scatter_about(key_list[0], (MB, SEQS, SEQ_LEN, D), 1.0, 6.0, ((1, 4), (2, 4)))
    cotangent = scatter_about(key_list[1], (MB, SEQS, SEQ_LEN, D), 1.0, 6.0, ((1, 4), (2, 4)))
    example_lengths = draw_example_lengths(jax.random.fold_in(key_list[20], 71), 0)
    attn_gain = jnp.clip(1.0 + 0.1 * jax.random.normal(key_list[3], (LAYERS, D), jnp.float32), 0.5, 1.5).astype(jnp.bfloat16)
    attn_shift = scatter_about(key_list[4], (LAYERS, D), 0.3, 1.75, ((0, 2),))
    query_key_value_weight = scatter_about(key_list[5], (LAYERS, D, 3 * D), D ** -0.5, 0.1875, ((0, 2), (2, 4)))
    qkv_bias = scatter_about(key_list[6], (LAYERS, 3 * D), 0.3, 1.75, ((0, 2), (1, 4)))
    attention_output_weight = scatter_about(key_list[7], (LAYERS, D, D), (D // 16) ** -0.5, 0.75, ((0, 2), (1, 4)))
    out_bias = scatter_about(key_list[8], (LAYERS, D), 0.3, 1.75, ((0, 2),))
    ffn_gain = jnp.clip(1.0 + 0.1 * jax.random.normal(key_list[9], (LAYERS, D), jnp.float32), 0.5, 1.5).astype(jnp.bfloat16)
    ffn_shift = scatter_about(key_list[10], (LAYERS, D), 0.3, 1.75, ((0, 2),))
    up_projection_weight = scatter_about(key_list[11], (LAYERS, D, FF), D ** -0.5, 0.1875, ((0, 2), (2, 4)))
    up_projection_bias = scatter_about(key_list[12], (LAYERS, FF), 0.3, 1.75, ((0, 2), (1, 4)))
    down_projection_weight = scatter_about(key_list[13], (LAYERS, FF, D), FF ** -0.5, 0.09375, ((0, 2), (1, 4)))
    down_bias = scatter_about(key_list[14], (LAYERS, D), 0.3, 1.75, ((0, 2),))
    prefix_table = scatter_about(key_list[15], (PREFIX, D), 1.0, 6.0)
    mid_weight = scatter_about(key_list[16], (D, MID), D ** -0.5, 0.1875)
    mid_bias = scatter_about(key_list[17], (MID,), 0.3, 1.75)
    prefix_weight = scatter_about(key_list[18], (MID, 2 * LAYERS * D), MID ** -0.5, 0.25, ((1, 8),))
    prefix_bias = scatter_about(key_list[19], (2 * LAYERS * D,), 0.3, 1.75, ((0, 8),))
    return dict(layer_input=layer_input, cotangent=cotangent, example_lengths=example_lengths, attn_gain=attn_gain, attn_shift=attn_shift, query_key_value_weight=query_key_value_weight, qkv_bias=qkv_bias, attention_output_weight=attention_output_weight, out_bias=out_bias, ffn_gain=ffn_gain, ffn_shift=ffn_shift, up_projection_weight=up_projection_weight, up_projection_bias=up_projection_bias, down_projection_weight=down_projection_weight, down_bias=down_bias, prefix_table=prefix_table, mid_weight=mid_weight, mid_bias=mid_bias, prefix_weight=prefix_weight, prefix_bias=prefix_bias)


@jax.custom_vjp
def low(v):
    return lax.optimization_barrier(v.astype(jnp.bfloat16)).astype(jnp.float32)

@jax.custom_vjp
def low_back(v):
    return v

def low_keep(v):
    return (low(v), None)

def low_pass(kept, grad):
    return (grad,)

def back_keep(v):
    return (v, None)

def back_low(kept, grad):
    return (low(grad),)
low.defvjp(low_keep, low_pass)
low_back.defvjp(back_keep, back_low)
EPSILON = 1e-05
HIGHEST = lax.Precision.HIGHEST

def product(left, right):
    return jnp.dot(left, right, precision=HIGHEST)

def norm_rows(values, gain, shift):
    average = lax.optimization_barrier(jnp.mean(values, axis=-1, keepdims=True))
    centred = values - average
    spread = lax.optimization_barrier(jnp.mean(centred * centred, axis=-1, keepdims=True))
    return centred * lax.rsqrt(spread + EPSILON) * gain + shift

def visible_of(lengths):
    run_ends = jnp.cumsum(lengths).astype(jnp.int32)
    positions = jnp.arange(SEQ_LEN, dtype=jnp.int32)
    segment_ids = lax.optimization_barrier(jnp.sum((positions[:, None] >= run_ends[None, :]).astype(jnp.int32), axis=1))
    inside = (segment_ids[:, None] == segment_ids[None, :]) & (positions[:, None] >= positions[None, :])
    return jnp.concatenate([jnp.ones((SEQ_LEN, PREFIX), dtype=bool), inside], axis=1)

def layer_apply(hidden, params, prefix_pair, visible):
    attn_gain, attn_shift, query_key_value_weight, qkv_bias, attention_output_weight, out_bias, ffn_gain, ffn_shift, up_projection_weight, up_projection_bias, down_projection_weight, down_bias = params
    normed = low(norm_rows(hidden, attn_gain, attn_shift))
    triple = low(low_back(product(normed, query_key_value_weight) + qkv_bias)).reshape(SEQ_LEN, HEADS, 3, HEAD_DIM)
    key_rows = jnp.concatenate([prefix_pair[:, :, 0], triple[:, :, 1]], axis=0)
    value_rows = jnp.concatenate([prefix_pair[:, :, 1], triple[:, :, 2]], axis=0)
    scores = low_back(jnp.einsum('qhd,khd->hqk', triple[:, :, 0], key_rows, precision=HIGHEST) * HEAD_DIM ** (-0.5))
    scores = jnp.where(visible[None], scores, -1e+30)
    highest = lax.optimization_barrier(jnp.max(scores, axis=-1, keepdims=True))
    raised = jnp.exp(scores - highest)
    probs_low = low(raised / lax.optimization_barrier(jnp.sum(raised, axis=-1, keepdims=True)))
    head_mixed_rows = low(low_back(jnp.einsum('hqk,khd->qhd', probs_low, value_rows, precision=HIGHEST))).reshape(SEQ_LEN, D)
    after_attn = low_back(hidden + product(head_mixed_rows, attention_output_weight) + out_bias)
    normed_two = low(norm_rows(after_attn, ffn_gain, ffn_shift))
    up_pre = low_back(product(normed_two, up_projection_weight) + up_projection_bias)
    gelu_output_rows = low(jax.nn.gelu(up_pre, approximate=True))
    return after_attn + product(gelu_output_rows, down_projection_weight) + down_bias

def two_layers(params, prefix_kv, added_taps, entering, lengths):
    visible = visible_of(lengths)
    hidden = low_back(entering + added_taps[0])
    outputs = []
    for layer_index in range(LAYERS):
        own_params = tuple((piece[layer_index] for piece in params))
        hidden = layer_apply(hidden, own_params, prefix_kv[:, layer_index], visible)
        outputs.append(low(hidden))
        if layer_index + 1 < LAYERS:
            hidden = low_back(low(hidden) + added_taps[layer_index + 1])
    return (hidden, jnp.stack(outputs))

def reference(layer_input, cotangent, example_lengths, attn_gain, attn_shift, query_key_value_weight, qkv_bias, attention_output_weight, out_bias, ffn_gain, ffn_shift, up_projection_weight, up_projection_bias, down_projection_weight, down_bias, prefix_table, mid_weight, mid_bias, prefix_weight, prefix_bias):
    params = tuple((piece.astype(jnp.float32) for piece in (attn_gain, attn_shift, query_key_value_weight, qkv_bias, attention_output_weight, out_bias, ffn_gain, ffn_shift, up_projection_weight, up_projection_bias, down_projection_weight, down_bias)))
    reparam = tuple((piece.astype(jnp.float32) for piece in (prefix_table, mid_weight, mid_bias, prefix_weight, prefix_bias)))

    def prefix_fn(table, mid_w, mid_b, pre_w, pre_b):
        hidden_act = low(jnp.tanh(low_back(product(table, mid_w) + mid_b)))
        pairs = low(low_back(product(hidden_act, pre_w) + pre_b))
        return pairs.reshape(PREFIX, LAYERS, HEADS, 2, HEAD_DIM)
    prefix_kv, prefix_back = jax.vjp(prefix_fn, *reparam)
    flat_input = layer_input.reshape(MB * SEQS, SEQ_LEN, D).astype(jnp.float32)
    flat_cot = cotangent.reshape(MB * SEQS, SEQ_LEN, D).astype(jnp.float32)
    flat_lengths = example_lengths.reshape(MB * SEQS, EX)
    zero_taps = jnp.zeros((LAYERS, SEQ_LEN, D), jnp.float32)

    def one_sequence(total_kv, sequence_items):
        entering, grad_out, lengths = sequence_items

        def sequence_block(kv_in, taps_in):
            return two_layers(params, kv_in, taps_in, entering, lengths)
        block_out, back_fn, outputs = jax.vjp(sequence_block, prefix_kv, zero_taps, has_aux=True)
        grads_kv, grads_taps = back_fn(grad_out)
        return (total_kv + grads_kv, (outputs.astype(jnp.bfloat16), grads_taps.astype(jnp.bfloat16)))
    start_total = jnp.zeros_like(prefix_kv)
    total_kv, (outputs_all, tap_grads) = lax.scan(one_sequence, start_total, (flat_input, flat_cot, flat_lengths))
    table_grad, mid_weight_grad, mid_bias_grad, prefix_weight_grad, prefix_bias_grad = prefix_back(total_kv)
    activations = outputs_all.reshape(MB, SEQS, LAYERS, SEQ_LEN, D).transpose(2, 0, 1, 3, 4)
    input_grads = tap_grads.reshape(MB, SEQS, LAYERS, SEQ_LEN, D).transpose(2, 0, 1, 3, 4)
    return (activations, input_grads, table_grad, mid_weight_grad, mid_bias_grad, prefix_weight_grad, prefix_bias_grad)
```

```python
import jax
import jax.numpy as jnp
from jax import lax
from jax.sharding import PartitionSpec as P

HEAD_DIM = 64
PREFIX = 10
SEQ_LEN = 1024


EPSILON = 1e-05
NEG_LARGE = -1e30


def norm_rows(values, gain, shift):
    average = jnp.mean(values, axis=-1, keepdims=True)
    centred = values - average
    spread = jnp.mean(centred * centred, axis=-1, keepdims=True)
    return centred * lax.rsqrt(spread + EPSILON) * gain + shift


def norm_input_grad(values, gain, shift, incoming):

    def apply_norm(inputs):
        return norm_rows(inputs, gain, shift)

    norm_value, norm_back = jax.vjp(apply_norm, values)
    return norm_back(incoming)[0]


def gelu_tanh(values):
    return jax.nn.gelu(values, approximate=True)


def visible_of(lengths, first_row, count):
    run_ends = jnp.cumsum(lengths, axis=-1)
    keys_at = jnp.arange(SEQ_LEN, dtype=jnp.int32)
    query_at = first_row + jnp.arange(count, dtype=jnp.int32)
    key_seg = jnp.sum((keys_at[None, :, None] >= run_ends[:, None, :]).astype(jnp.int32), axis=-1)
    query_seg = jnp.sum(
        (query_at[None, :, None] >= run_ends[:, None, :]).astype(jnp.int32), axis=-1
    )
    causal = (query_at[:, None] >= keys_at[None, :])[None]
    inside = (query_seg[:, :, None] == key_seg[:, None, :]) & causal
    leading = jnp.ones((lengths.shape[0], count, PREFIX), dtype=bool)
    return jnp.concatenate([leading, inside], axis=2)


def gather_rows(piece):
    return lax.all_gather(piece, "mp", axis=1, tiled=True)


def reduce_rows(partial_sum):
    return lax.psum_scatter(
        partial_sum.astype(jnp.bfloat16), "mp", scatter_dimension=1, tiled=True
    ).astype(jnp.float32)


def with_prefix(prefix_kv, pair_keys, pair_values, heads_count):
    prefix_pair = prefix_kv.reshape(PREFIX, heads_count, 2, HEAD_DIM)
    key_rows = jnp.concatenate([prefix_pair[None, :, :, 0], pair_keys], axis=1)
    value_rows = jnp.concatenate([prefix_pair[None, :, :, 1], pair_values], axis=1)
    return (key_rows, value_rows)


def attend(query_rows, key_rows, value_rows, visible):
    score_scale = HEAD_DIM ** (-0.5)
    scores = (
        jnp.einsum("sqhd,skhd->shqk", query_rows, key_rows, preferred_element_type=jnp.float32)
        * score_scale
    )
    scores = jnp.where(visible[:, None], scores, NEG_LARGE)
    highest = jnp.max(scores, axis=-1, keepdims=True)
    raised = jnp.exp(scores - highest)
    softmax_probs = raised / jnp.sum(raised, axis=-1, keepdims=True)
    probs_low = softmax_probs.astype(jnp.bfloat16)
    head_mixed_rows = jnp.einsum(
        "shqk,skhd->sqhd", probs_low, value_rows, preferred_element_type=jnp.float32
    )
    batch_size, query_count, heads_count, head_size = head_mixed_rows.shape
    head_mixed_rows = head_mixed_rows.astype(jnp.bfloat16).reshape(
        batch_size, query_count, heads_count * head_size
    )
    return (softmax_probs, probs_low, head_mixed_rows)


def attend_back(grad_mix, query_rows, key_rows, value_rows, softmax_probs, probs_low):
    grad_heads = grad_mix.reshape(query_rows.shape)
    grad_probs = jnp.einsum(
        "sqhd,skhd->shqk", grad_heads, value_rows, preferred_element_type=jnp.float32
    )
    value_grad = jnp.einsum(
        "shqk,sqhd->skhd", probs_low, grad_heads, preferred_element_type=jnp.float32
    )
    row_term = jnp.sum(grad_probs * softmax_probs, axis=-1, keepdims=True)
    grad_scores = (softmax_probs * (grad_probs - row_term)).astype(jnp.bfloat16)
    score_scale = HEAD_DIM ** (-0.5)
    query_grad = (
        jnp.einsum("shqk,skhd->sqhd", grad_scores, key_rows, preferred_element_type=jnp.float32)
        * score_scale
    )
    key_grad = (
        jnp.einsum("shqk,sqhd->skhd", grad_scores, query_rows, preferred_element_type=jnp.float32)
        * score_scale
    )
    return (query_grad, key_grad, value_grad)


def prefix_part(key_grad, value_grad):
    pair_sum = jnp.stack(
        [jnp.sum(key_grad[:, :PREFIX], axis=0), jnp.sum(value_grad[:, :PREFIX], axis=0)], axis=2
    )
    return pair_sum.reshape(PREFIX, -1)


def tensor_forward(own_rows, weights, prefix_kv, visible):
    (
        attn_gain,
        attn_shift,
        query_key_value_weight,
        qkv_bias,
        attention_output_weight,
        out_bias,
        ffn_gain,
        ffn_shift,
        up_projection_weight,
        up_projection_bias,
        down_projection_weight,
        down_bias,
        out_full,
    ) = weights
    normed = norm_rows(own_rows, attn_gain, attn_shift).astype(jnp.bfloat16)
    normalized_input_rows = gather_rows(normed)
    batch_size, seq_len, model_width = normalized_input_rows.shape
    heads_here = query_key_value_weight.shape[1] // (3 * HEAD_DIM)
    projected = (
        jnp.einsum(
            "naj,jk->nak",
            normalized_input_rows,
            query_key_value_weight,
            preferred_element_type=jnp.float32,
        )
        + qkv_bias
    )
    triple = projected.astype(jnp.bfloat16).reshape(batch_size, seq_len, heads_here, 3, HEAD_DIM)
    query_rows = triple[:, :, :, 0]
    key_rows, value_rows = with_prefix(
        prefix_kv, triple[:, :, :, 1], triple[:, :, :, 2], heads_here
    )
    softmax_probs, probs_low, head_mixed_rows = attend(query_rows, key_rows, value_rows, visible)
    attn_part = reduce_rows(
        jnp.einsum(
            "hgm,mt->hgt",
            head_mixed_rows,
            attention_output_weight,
            preferred_element_type=jnp.float32,
        )
    )
    after_attn = own_rows + attn_part + out_bias
    normed_two = norm_rows(after_attn, ffn_gain, ffn_shift).astype(jnp.bfloat16)
    second_norm_rows = gather_rows(normed_two)
    up_pre = (
        jnp.einsum(
            "rmy,yq->rmq",
            second_norm_rows,
            up_projection_weight,
            preferred_element_type=jnp.float32,
        )
        + up_projection_bias
    )
    gelu_output_rows = gelu_tanh(up_pre).astype(jnp.bfloat16)
    mlp_part = reduce_rows(
        jnp.einsum(
            "epj,jq->epq",
            gelu_output_rows,
            down_projection_weight,
            preferred_element_type=jnp.float32,
        )
    )
    result = after_attn + mlp_part + down_bias
    kept_values = (query_rows, key_rows, value_rows, softmax_probs, probs_low, after_attn, up_pre)
    return (result, kept_values)


def tensor_backward(own_rows, arriving, weights, kept_values):
    (
        attn_gain,
        attn_shift,
        query_key_value_weight,
        qkv_bias,
        attention_output_weight,
        out_bias,
        ffn_gain,
        ffn_shift,
        up_projection_weight,
        up_projection_bias,
        down_projection_weight,
        down_bias,
        out_full,
    ) = weights
    query_rows, key_rows, value_rows, softmax_probs, probs_low, after_attn, up_pre = kept_values
    gradient_gathered = gather_rows(arriving)
    gradient_activation = jnp.einsum(
        "bhi,vi->bhv", gradient_gathered, down_projection_weight, preferred_element_type=jnp.float32
    )
    gelu_value, gelu_back = jax.vjp(gelu_tanh, up_pre)
    gradient_up_projection = gelu_back(gradient_activation)[0].astype(jnp.bfloat16)
    grad_two = reduce_rows(
        jnp.einsum(
            "yca,ja->ycj",
            gradient_up_projection,
            up_projection_weight,
            preferred_element_type=jnp.float32,
        )
    )
    grad_after = norm_input_grad(after_attn, ffn_gain, ffn_shift, grad_two)
    grad_mid = (grad_after + arriving.astype(jnp.float32)).astype(jnp.bfloat16)
    middle_gathered = gather_rows(grad_mid)
    grad_mix = jnp.einsum(
        "taq,kq->tak", middle_gathered, attention_output_weight, preferred_element_type=jnp.float32
    ).astype(jnp.bfloat16)
    query_grad, key_grad, value_grad = attend_back(
        grad_mix, query_rows, key_rows, value_rows, softmax_probs, probs_low
    )
    prefix_g = prefix_part(key_grad, value_grad)
    batch_size, seq_len = (query_grad.shape[0], query_grad.shape[1])
    gradient_query_key_value = jnp.stack(
        [query_grad, key_grad[:, PREFIX:], value_grad[:, PREFIX:]], axis=3
    )
    gradient_query_key_value = gradient_query_key_value.astype(jnp.bfloat16).reshape(
        batch_size, seq_len, -1
    )
    grad_one = reduce_rows(
        jnp.einsum(
            "tvq,xq->tvx",
            gradient_query_key_value,
            query_key_value_weight,
            preferred_element_type=jnp.float32,
        )
    )
    grad_input = norm_input_grad(own_rows, attn_gain, attn_shift, grad_one)
    grad_input = (grad_input + grad_mid.astype(jnp.float32)).astype(jnp.bfloat16)
    return (grad_input, prefix_g)


def both_layers(piece):
    return lax.all_gather(piece[0], "section", axis=0, tiled=False)


def body(
    layer_input,
    cotangent,
    example_lengths,
    attn_gain,
    attn_shift,
    query_key_value_weight,
    qkv_bias,
    attention_output_weight,
    out_bias,
    ffn_gain,
    ffn_shift,
    up_projection_weight,
    up_projection_bias,
    down_projection_weight,
    down_bias,
    prefix_table,
    mid_weight,
    mid_bias,
    prefix_weight,
    prefix_bias,
):
    layers = lax.axis_size("section")
    section_index = lax.axis_index("section")
    hidden_pre = jnp.dot(
        prefix_table, mid_weight, preferred_element_type=jnp.float32
    ) + mid_bias.astype(jnp.float32)
    hidden_act = jnp.tanh(hidden_pre)
    hidden_low = hidden_act.astype(jnp.bfloat16)
    prefix_kv = (
        jnp.dot(hidden_low, prefix_weight, preferred_element_type=jnp.float32)
        + prefix_bias.astype(jnp.float32)
    ).astype(jnp.bfloat16)
    prefix_all = lax.all_gather(prefix_kv, "section", axis=0, tiled=False)
    floats = [
        both_layers(piece).astype(jnp.float32)
        for piece in (attn_gain, attn_shift, qkv_bias, out_bias, ffn_gain, ffn_shift,
                      up_projection_bias, down_bias)
    ]
    matrices = [
        both_layers(piece)
        for piece in (query_key_value_weight, attention_output_weight,
                      up_projection_weight, down_projection_weight)
    ]

    def weights_of(layer):
        g1, s1, bq, bo, g2, s2, bu, bd = [piece[layer] for piece in floats]
        wq, wo, wu, wd = [piece[layer] for piece in matrices]
        return (g1, s1, wq, bq, wo, bo, g2, s2, wu, bu, wd, bd, wo)

    batch_count = layer_input.shape[0]
    own_input = lax.dynamic_index_in_dim(layer_input, section_index, 0, keepdims=False)
    own_cotangent = lax.dynamic_index_in_dim(cotangent, section_index, 0, keepdims=False)
    lengths = lax.dynamic_index_in_dim(example_lengths, section_index, 0, keepdims=False)
    visible = visible_of(lengths, 0, SEQ_LEN)
    entering = own_input
    entered, produced, kept = [], [], []
    for layer in range(layers):
        entered.append(entering.astype(jnp.float32))
        result, kept_values = tensor_forward(
            entered[layer], weights_of(layer), prefix_all[layer], visible
        )
        entering = result.astype(jnp.bfloat16)
        produced.append(entering)
        kept.append(kept_values)
    gradient = own_cotangent
    sent_grads = [None] * layers
    prefix_parts = [None] * layers
    for layer in reversed(range(layers)):
        gradient, prefix_parts[layer] = tensor_backward(
            entered[layer], gradient, weights_of(layer), kept[layer]
        )
        sent_grads[layer] = gradient
    activations = lax.all_to_all(jnp.stack(produced), "section", 0, 0, tiled=False)
    input_grads = lax.all_to_all(jnp.stack(sent_grads), "section", 0, 0, tiled=False)
    prefix_sum = lax.psum(jnp.stack(prefix_parts), ("dp", "section"))
    prefix_sum = lax.dynamic_index_in_dim(prefix_sum, section_index, 0, keepdims=False)
    prefix_low = prefix_sum.astype(jnp.bfloat16)
    prefix_bias_grad = jnp.sum(prefix_low.astype(jnp.float32), axis=0)
    prefix_weight_grad = jnp.dot(hidden_low.T, prefix_low, preferred_element_type=jnp.float32)
    hidden_part = jnp.dot(prefix_low, prefix_weight.T, preferred_element_type=jnp.float32)
    hidden_grad = lax.psum(hidden_part, ("section", "mp"))
    pre_grad = (hidden_grad * (1.0 - hidden_act * hidden_act)).astype(jnp.bfloat16)
    mid_bias_grad = jnp.sum(pre_grad.astype(jnp.float32), axis=0)
    mid_weight_grad = jnp.dot(prefix_table.T, pre_grad, preferred_element_type=jnp.float32)
    table_grad = jnp.dot(pre_grad, mid_weight.T, preferred_element_type=jnp.float32)
    return (
        activations[None],
        input_grads[None],
        table_grad,
        mid_weight_grad,
        mid_bias_grad,
        prefix_weight_grad,
        prefix_bias_grad,
    )


def solution(mesh):
    placed = (
        P(None, "dp", "mp", None),
        P(None, "dp", "mp", None),
        P(None, "dp", None),
        P("section", None),
        P("section", None),
        P("section", None, "mp"),
        P("section", "mp"),
        P("section", "mp", None),
        P("section", None),
        P("section", None),
        P("section", None),
        P("section", None, "mp"),
        P("section", "mp"),
        P("section", "mp", None),
        P("section", None),
        P(),
        P(),
        P(),
        P(None, ("section", "mp")),
        P(("section", "mp")),
    )
    return jax.shard_map(
        body,
        mesh=mesh,
        in_specs=placed,
        out_specs=(
            P("section", None, "dp", "mp", None),
            P("section", None, "dp", "mp", None),
            P(),
            P(),
            P(),
            P(None, ("section", "mp")),
            P(("section", "mp")),
        ),
        check_vma=False,
    )
```

```python
import jax
import jax.numpy as jnp
from jax import lax
from jax.experimental import pallas as pl
from jax.experimental.pallas import tpu as pltpu
from jax.sharding import PartitionSpec as P

HEAD_DIM = 64
PREFIX = 10
SEQ_LEN = 1024


EPSILON = 1e-05
NEG_LARGE = -1e30
GELU_A = 0.7978845608028654
GELU_B = 0.044715


def norm_rows(values, gain, shift):
    average = jnp.mean(values, axis=-1, keepdims=True)
    centred = values - average
    spread = jnp.mean(centred * centred, axis=-1, keepdims=True)
    return centred * lax.rsqrt(spread + EPSILON) * gain + shift


def norm_input_grad(values, gain, shift, incoming):

    def apply_norm(inputs):
        return norm_rows(inputs, gain, shift)

    norm_value, norm_back = jax.vjp(apply_norm, values)
    return norm_back(incoming)[0]


def gelu_tanh(values):
    return jax.nn.gelu(values, approximate=True)


def visible_of(lengths, first_row, count):
    run_ends = jnp.cumsum(lengths, axis=-1)
    keys_at = jnp.arange(SEQ_LEN, dtype=jnp.int32)
    query_at = first_row + jnp.arange(count, dtype=jnp.int32)
    key_seg = jnp.sum((keys_at[None, :, None] >= run_ends[:, None, :]).astype(jnp.int32), axis=-1)
    query_seg = jnp.sum(
        (query_at[None, :, None] >= run_ends[:, None, :]).astype(jnp.int32), axis=-1
    )
    causal = (query_at[:, None] >= keys_at[None, :])[None]
    inside = (query_seg[:, :, None] == key_seg[:, None, :]) & causal
    leading = jnp.ones((lengths.shape[0], count, PREFIX), dtype=bool)
    return jnp.concatenate([leading, inside], axis=2)


def gather_rows(piece):
    return lax.all_gather(piece, "mp", axis=1, tiled=True)


def reduce_rows(partial_sum):
    return lax.psum_scatter(
        partial_sum.astype(jnp.bfloat16), "mp", scatter_dimension=1, tiled=True
    ).astype(jnp.float32)


def with_prefix(prefix_kv, pair_keys, pair_values, heads_count):
    prefix_pair = prefix_kv.reshape(PREFIX, heads_count, 2, HEAD_DIM)
    key_rows = jnp.concatenate([prefix_pair[None, :, :, 0], pair_keys], axis=1)
    value_rows = jnp.concatenate([prefix_pair[None, :, :, 1], pair_values], axis=1)
    return (key_rows, value_rows)


def attend(query_rows, key_rows, value_rows, visible):
    score_scale = HEAD_DIM ** (-0.5)
    scores = (
        jnp.einsum("sqhd,skhd->shqk", query_rows, key_rows, preferred_element_type=jnp.float32)
        * score_scale
    )
    scores = jnp.where(visible[:, None], scores, NEG_LARGE)
    highest = jnp.max(scores, axis=-1, keepdims=True)
    raised = jnp.exp(scores - highest)
    softmax_probs = raised / jnp.sum(raised, axis=-1, keepdims=True)
    probs_low = softmax_probs.astype(jnp.bfloat16)
    head_mixed_rows = jnp.einsum(
        "shqk,skhd->sqhd", probs_low, value_rows, preferred_element_type=jnp.float32
    )
    batch_size, query_count, heads_count, head_size = head_mixed_rows.shape
    head_mixed_rows = head_mixed_rows.astype(jnp.bfloat16).reshape(
        batch_size, query_count, heads_count * head_size
    )
    return (softmax_probs, probs_low, head_mixed_rows)


def attend_back(grad_mix, query_rows, key_rows, value_rows, softmax_probs, probs_low):
    grad_heads = grad_mix.reshape(query_rows.shape)
    grad_probs = jnp.einsum(
        "sqhd,skhd->shqk", grad_heads, value_rows, preferred_element_type=jnp.float32
    )
    value_grad = jnp.einsum(
        "shqk,sqhd->skhd", probs_low, grad_heads, preferred_element_type=jnp.float32
    )
    row_term = jnp.sum(grad_probs * softmax_probs, axis=-1, keepdims=True)
    grad_scores = (softmax_probs * (grad_probs - row_term)).astype(jnp.bfloat16)
    score_scale = HEAD_DIM ** (-0.5)
    query_grad = (
        jnp.einsum("shqk,skhd->sqhd", grad_scores, key_rows, preferred_element_type=jnp.float32)
        * score_scale
    )
    key_grad = (
        jnp.einsum("shqk,sqhd->skhd", grad_scores, query_rows, preferred_element_type=jnp.float32)
        * score_scale
    )
    return (query_grad, key_grad, value_grad)


def prefix_part(key_grad, value_grad):
    pair_sum = jnp.stack(
        [jnp.sum(key_grad[:, :PREFIX], axis=0), jnp.sum(value_grad[:, :PREFIX], axis=0)], axis=2
    )
    return pair_sum.reshape(PREFIX, -1)


def tensor_forward(own_rows, weights, prefix_kv, visible):
    (
        attn_gain,
        attn_shift,
        query_key_value_weight,
        qkv_bias,
        attention_output_weight,
        out_bias,
        ffn_gain,
        ffn_shift,
        up_projection_weight,
        up_projection_bias,
        down_projection_weight,
        down_bias,
        out_full,
    ) = weights
    normed = norm_rows(own_rows, attn_gain, attn_shift).astype(jnp.bfloat16)
    normalized_input_rows = gather_rows(normed)
    batch_size, seq_len, model_width = normalized_input_rows.shape
    heads_here = query_key_value_weight.shape[1] // (3 * HEAD_DIM)
    projected = (
        jnp.einsum(
            "naj,jk->nak",
            normalized_input_rows,
            query_key_value_weight,
            preferred_element_type=jnp.float32,
        )
        + qkv_bias
    )
    triple = projected.astype(jnp.bfloat16).reshape(batch_size, seq_len, heads_here, 3, HEAD_DIM)
    query_rows = triple[:, :, :, 0]
    key_rows, value_rows = with_prefix(
        prefix_kv, triple[:, :, :, 1], triple[:, :, :, 2], heads_here
    )
    softmax_probs, probs_low, head_mixed_rows = attend(query_rows, key_rows, value_rows, visible)
    attn_part = reduce_rows(
        jnp.einsum(
            "hgm,mt->hgt",
            head_mixed_rows,
            attention_output_weight,
            preferred_element_type=jnp.float32,
        )
    )
    after_attn = own_rows + attn_part + out_bias
    normed_two = norm_rows(after_attn, ffn_gain, ffn_shift).astype(jnp.bfloat16)
    second_norm_rows = gather_rows(normed_two)
    up_pre = (
        jnp.einsum(
            "rmy,yq->rmq",
            second_norm_rows,
            up_projection_weight,
            preferred_element_type=jnp.float32,
        )
        + up_projection_bias
    )
    gelu_output_rows = gelu_tanh(up_pre).astype(jnp.bfloat16)
    mlp_part = reduce_rows(
        jnp.einsum(
            "epj,jq->epq",
            gelu_output_rows,
            down_projection_weight,
            preferred_element_type=jnp.float32,
        )
    )
    result = after_attn + mlp_part + down_bias
    kept_values = (query_rows, key_rows, value_rows, softmax_probs, probs_low, after_attn, up_pre)
    return (result, kept_values)


def tensor_backward(own_rows, arriving, weights, kept_values):
    (
        attn_gain,
        attn_shift,
        query_key_value_weight,
        qkv_bias,
        attention_output_weight,
        out_bias,
        ffn_gain,
        ffn_shift,
        up_projection_weight,
        up_projection_bias,
        down_projection_weight,
        down_bias,
        out_full,
    ) = weights
    query_rows, key_rows, value_rows, softmax_probs, probs_low, after_attn, up_pre = kept_values
    gradient_gathered = gather_rows(arriving)
    gradient_activation = jnp.einsum(
        "bhi,vi->bhv", gradient_gathered, down_projection_weight, preferred_element_type=jnp.float32
    )
    gelu_value, gelu_back = jax.vjp(gelu_tanh, up_pre)
    gradient_up_projection = gelu_back(gradient_activation)[0].astype(jnp.bfloat16)
    grad_two = reduce_rows(
        jnp.einsum(
            "yca,ja->ycj",
            gradient_up_projection,
            up_projection_weight,
            preferred_element_type=jnp.float32,
        )
    )
    grad_after = norm_input_grad(after_attn, ffn_gain, ffn_shift, grad_two)
    grad_mid = (grad_after + arriving.astype(jnp.float32)).astype(jnp.bfloat16)
    middle_gathered = gather_rows(grad_mid)
    grad_mix = jnp.einsum(
        "taq,kq->tak", middle_gathered, attention_output_weight, preferred_element_type=jnp.float32
    ).astype(jnp.bfloat16)
    query_grad, key_grad, value_grad = attend_back(
        grad_mix, query_rows, key_rows, value_rows, softmax_probs, probs_low
    )
    prefix_g = prefix_part(key_grad, value_grad)
    batch_size, seq_len = (query_grad.shape[0], query_grad.shape[1])
    gradient_query_key_value = jnp.stack(
        [query_grad, key_grad[:, PREFIX:], value_grad[:, PREFIX:]], axis=3
    )
    gradient_query_key_value = gradient_query_key_value.astype(jnp.bfloat16).reshape(
        batch_size, seq_len, -1
    )
    grad_one = reduce_rows(
        jnp.einsum(
            "tvq,xq->tvx",
            gradient_query_key_value,
            query_key_value_weight,
            preferred_element_type=jnp.float32,
        )
    )
    grad_input = norm_input_grad(own_rows, attn_gain, attn_shift, grad_one)
    grad_input = (grad_input + grad_mid.astype(jnp.float32)).astype(jnp.bfloat16)
    return (grad_input, prefix_g)


def prefix_back(prefix_sum, hidden_act, hidden_low, prefix_table, mid_weight, prefix_weight):
    prefix_low = prefix_sum.astype(jnp.bfloat16)
    prefix_bias_grad = jnp.sum(prefix_low.astype(jnp.float32), axis=0)
    prefix_weight_grad = jnp.dot(hidden_low.T, prefix_low, preferred_element_type=jnp.float32)
    hidden_part = jnp.dot(prefix_low, prefix_weight.T, preferred_element_type=jnp.float32)
    hidden_grad = lax.psum(hidden_part, ("section", "mp"))
    pre_grad = (hidden_grad * (1.0 - hidden_act * hidden_act)).astype(jnp.bfloat16)
    mid_bias_grad = jnp.sum(pre_grad.astype(jnp.float32), axis=0)
    mid_weight_grad = jnp.dot(prefix_table.T, pre_grad, preferred_element_type=jnp.float32)
    table_grad = jnp.dot(pre_grad, mid_weight.T, preferred_element_type=jnp.float32)
    return (table_grad, mid_weight_grad, mid_bias_grad, prefix_weight_grad, prefix_bias_grad)


def both_layers(piece):
    return lax.all_gather(piece[0], "section", axis=0, tiled=False)


def body(
    layer_input,
    cotangent,
    example_lengths,
    attn_gain,
    attn_shift,
    query_key_value_weight,
    qkv_bias,
    attention_output_weight,
    out_bias,
    ffn_gain,
    ffn_shift,
    up_projection_weight,
    up_projection_bias,
    down_projection_weight,
    down_bias,
    prefix_table,
    mid_weight,
    mid_bias,
    prefix_weight,
    prefix_bias,
):
    layers = lax.axis_size("section")
    section_index = lax.axis_index("section")
    hidden_pre = jnp.dot(
        prefix_table, mid_weight, preferred_element_type=jnp.float32
    ) + mid_bias.astype(jnp.float32)
    hidden_act = jnp.tanh(hidden_pre)
    hidden_low = hidden_act.astype(jnp.bfloat16)
    prefix_kv = (
        jnp.dot(hidden_low, prefix_weight, preferred_element_type=jnp.float32)
        + prefix_bias.astype(jnp.float32)
    ).astype(jnp.bfloat16)
    prefix_all = lax.all_gather(prefix_kv, "section", axis=0, tiled=False)
    floats = [
        both_layers(piece).astype(jnp.float32)
        for piece in (attn_gain, attn_shift, qkv_bias, out_bias, ffn_gain, ffn_shift,
                      up_projection_bias, down_bias)
    ]
    matrices = [
        both_layers(piece)
        for piece in (query_key_value_weight, attention_output_weight,
                      up_projection_weight, down_projection_weight)
    ]

    def weights_of(layer):
        g1, s1, bq, bo, g2, s2, bu, bd = [piece[layer] for piece in floats]
        wq, wo, wu, wd = [piece[layer] for piece in matrices]
        return (g1, s1, wq, bq, wo, bo, g2, s2, wu, bu, wd, bd, wo)

    batch_count = layer_input.shape[0]
    own_input = lax.dynamic_index_in_dim(layer_input, section_index, 0, keepdims=False)
    own_cotangent = lax.dynamic_index_in_dim(cotangent, section_index, 0, keepdims=False)
    lengths = lax.dynamic_index_in_dim(example_lengths, section_index, 0, keepdims=False)
    visible = visible_of(lengths, 0, SEQ_LEN)
    entering = own_input
    entered, produced, kept = [], [], []
    for layer in range(layers):
        entered.append(entering.astype(jnp.float32))
        result, kept_values = tensor_forward(
            entered[layer], weights_of(layer), prefix_all[layer], visible
        )
        entering = result.astype(jnp.bfloat16)
        produced.append(entering)
        kept.append(kept_values)
    gradient = own_cotangent
    sent_grads = [None] * layers
    prefix_parts = [None] * layers
    for layer in reversed(range(layers)):
        gradient, prefix_parts[layer] = tensor_backward(
            entered[layer], gradient, weights_of(layer), kept[layer]
        )
        sent_grads[layer] = gradient
    activations = lax.all_to_all(jnp.stack(produced), "section", 0, 0, tiled=False)
    input_grads = lax.all_to_all(jnp.stack(sent_grads), "section", 0, 0, tiled=False)
    prefix_sum = lax.psum(jnp.stack(prefix_parts), ("dp", "section"))
    prefix_sum = lax.dynamic_index_in_dim(prefix_sum, section_index, 0, keepdims=False)
    return (activations[None], input_grads[None]) + prefix_back(
        prefix_sum, hidden_act, hidden_low, prefix_table, mid_weight, prefix_weight
    )


MESH = pl.DeviceIdType.MESH
BLOCK = 256
LOG2E = 1.4426950408889634
CHUNK = 32


def role_of(z):
    return (((z + 1) // 2) + 1) % 2


def block_of(s, j):
    return j * 3 + s * (1 - 2 * j)


def core_of(block):
    return ((block + 1) // 2) % 2


def guarded(when, action):
    if when is None:
        action()
    else:
        pl.when(when)(action)


def dot_nn(a, b):
    return lax.dot_general(a, b, (((1,), (0,)), ((), ())), preferred_element_type=jnp.float32)


def dot_nt(a, b):
    return lax.dot_general(a, b, (((1,), (1,)), ((), ())), preferred_element_type=jnp.float32)


def dot_tn(a, b):
    return lax.dot_general(a, b, (((0,), (0,)), ((), ())), preferred_element_type=jnp.float32)


class Sends:
    def __init__(self, sems):
        self.sems, self.used, self.pending = sems, 0, []

    def start(self, src, dst, recv_sem, target, when=None):
        copy = pltpu.make_async_remote_copy(
            src_ref=src, dst_ref=dst, send_sem=self.sems.at[self.used], recv_sem=recv_sem,
            device_id=target, device_id_type=MESH,
        )
        self.used += 1
        guarded(when, copy.start)
        self.pending.append((when, copy))

    def start_or_keep(self, src, dst, recv_sem, target, is_here):
        @pl.when(is_here)
        def _():
            pltpu.make_async_copy(src, dst, recv_sem).start()

        self.start(src, dst, recv_sem, target, when=jnp.logical_not(is_here))

    def finish(self):
        for when, copy in self.pending:
            guarded(when, copy.wait_send)
        self.pending = []


def layer_kernel(
    x_hbm, cot_hbm, wq_hbm, wo_hbm, wu_hbm, wd_hbm, vec_hbm, pre_hbm, ends,
    act_out, ig_out, pg_out,
    wq, wo, wu, wd, vec, pre,
    x_in, g_in, y_out, normed, kv, q_own, o_own, lse, bias, after, acc, slope, wide,
    ts, m_acc, l_acc, o_acc, dk_acc, dv_acc, dkv_own, dkv_send, dkv_recv, kp, vp, pk_acc, pv_acc, gt,
    ssem, vec_sem, pre_sem, x_sem, g_sem, act_sem, ig_sem, own_sem, z_sem, a_sem, b_sem, c_sem,
    kv_ssem, kv_rsem, dkv_ssem, dkv_rsem,
):
    s, d, z = lax.axis_index("section"), lax.axis_index("dp"), lax.axis_index("mp")
    role, micro = role_of(z), z // 2
    other = 1 - s
    partner = z + 1 - 2 * (z % 2)
    x_near, y_near = d + 1 - 2 * (d % 2), (d + 2) % 4
    near1 = jnp.where(s == 0, x_near, y_near)
    near2 = jnp.where(s == 0, y_near, x_near)
    sends = Sends(ssem)

    barrier = pltpu.get_barrier_semaphore()
    for ds in range(2):
        for dz in range(4):
            if ds or dz:
                pl.semaphore_signal(barrier, inc=1, device_id=((s + ds) % 2, d, (z + dz) % 4), device_id_type=MESH)
    for near in (x_near, y_near):
        pl.semaphore_signal(barrier, inc=1, device_id=(s, near, z), device_id_type=MESH)
    pl.semaphore_wait(barrier, 9)

    def arrived(dst, sem):
        pltpu.make_async_remote_copy(
            src_ref=dst, dst_ref=dst, send_sem=ssem.at[0], recv_sem=sem,
            device_id=(other, d, z), device_id_type=MESH,
        ).wait_recv()

    low_plane, high_plane = jnp.where(s == 0, 1, 0), jnp.where(s == 0, 2, 3)
    planes = (low_plane, high_plane)
    owner = core_of(z)
    mine = s == owner
    for k, chip in ((0, 1), (1, 2)):
        slot = pl.ds(pl.multiple_of((z // 2) * BLOCK, BLOCK), BLOCK)
        target = (s, d, chip)
        is_here = z == chip

        @pl.when(jnp.logical_and(mine, is_here))
        def _():
            pltpu.make_async_copy(x_hbm.at[k], x_in.at[slot], x_sem.at[z // 2]).start()

        sends.start(x_hbm.at[k], x_in.at[slot], x_sem.at[z // 2], target,
                    when=jnp.logical_and(mine, jnp.logical_not(is_here)))
    for t in planes:
        for h in range(2):
            is_here = jnp.logical_and(z == t, s == h)
            sends.start_or_keep(vec_hbm, vec.at[z], vec_sem.at[z], (h, d, t), is_here)
            sends.start_or_keep(pre_hbm, pre.at[z], pre_sem.at[z], (h, d, t), is_here)
    matrices = ((wq_hbm, wq), (wo_hbm, wo), (wu_hbm, wu), (wd_hbm, wd))
    swapped = (d % 2) * 2 + d // 2

    def part(w, h):
        rows = matrices[w][1].shape[1] // 8
        place = swapped if h else d
        return pl.ds(pl.multiple_of((place + 4 * h) * rows, rows), rows)

    for w, (held, full) in enumerate(matrices):
        for t in planes:
            for h in range(2):
                sends.start(held.at[part(w, h)], full.at[z, part(w, h)], z_sem.at[w, z], (h, d, t), when=z != t)

        @pl.when(role == s)
        def _():
            pltpu.make_async_copy(held, full.at[z], own_sem.at[w]).start()

        sends.start(held, full.at[z], own_sem.at[w], (other, d, z), when=role == s)
    for k, chip in ((0, 0), (1, 3)):
        slot = pl.ds(pl.multiple_of((z // 2) * BLOCK, BLOCK), BLOCK)
        is_here = z == chip

        @pl.when(jnp.logical_and(mine, is_here))
        def _():
            pltpu.make_async_copy(cot_hbm.at[k], g_in.at[slot], g_sem.at[z // 2]).start()

        sends.start(cot_hbm.at[k], g_in.at[slot], g_sem.at[z // 2], (s, d, chip),
                    when=jnp.logical_and(mine, jnp.logical_not(is_here)))

    place = jnp.where(s == 0, d, swapped)

    def mine_part(w, start, count):
        rows = matrices[w][1].shape[1] // 8
        return pl.ds(pl.multiple_of((start + 4 * s) * rows, rows), rows * count)

    units = [(w, i) for w in (0, 1) for i in range(1, 4)] + [(w, i) for i in range(1, 4) for w in (2, 3)]

    def piece(w, i, start, count):
        return matrices[w][1].at[(z + i) % 4, mine_part(w, start, count)]

    pair_start = (place // 2) * 2
    far_start = 2 - pair_start

    def relay(step):
        stages = [units[step - k] if 0 <= step - k < len(units) else None for k in range(4)]
        if stages[0]:
            w, i = stages[0]
            q = (z + i) % 4
            arrived(piece(w, i, place, 1), z_sem.at[w, q])
            sends.start(piece(w, i, place, 1), piece(w, i, place, 1), a_sem.at[w, q], (s, near1, z))
        if stages[1]:
            w, i = stages[1]
            q = (z + i) % 4
            arrived(piece(w, i, pair_start + 1 - place % 2, 1), a_sem.at[w, q])
            sends.start(piece(w, i, pair_start, 2), piece(w, i, pair_start, 2), b_sem.at[w, q], (s, near2, z))
        if stages[2]:
            w, i = stages[2]
            q = (z + i) % 4
            arrived(piece(w, i, far_start, 2), b_sem.at[w, q])
            sends.start(piece(w, i, 0, 4), piece(w, i, 0, 4), c_sem.at[w, q], (other, d, z))
        if stages[3]:
            w, i = stages[3]
            q = (z + i) % 4
            rows = matrices[w][1].shape[1] // 2
            half = pl.ds(pl.multiple_of(other * rows, rows), rows)
            arrived(matrices[w][1].at[q, half], c_sem.at[w, q])

    for step in range(len(units) + 3):
        relay(step)
    for w, (held, full) in enumerate(matrices):
        arrived(full.at[z], own_sem.at[w])
    for q in range(4):
        arrived(vec.at[q], vec_sem.at[q])
        arrived(pre.at[q], pre_sem.at[q])

    first16 = lax.broadcasted_iota(jnp.int32, (16, 128), 1) < HEAD_DIM
    first = lax.broadcasted_iota(jnp.int32, (BLOCK, 128), 1) < HEAD_DIM
    lane = lax.broadcasted_iota(jnp.int32, (1, 128), 1)
    half0 = jnp.where(lane < HEAD_DIM, 1.0, 0.0).astype(jnp.bfloat16)
    half1 = jnp.where(lane < HEAD_DIM, 0.0, 1.0).astype(jnp.bfloat16)
    pre_mask = jnp.where(lane % HEAD_DIM < PREFIX, 0.0, NEG_LARGE)
    kp[...] = jnp.zeros(kp.shape, kp.dtype)
    vp[...] = jnp.zeros(vp.shape, vp.dtype)
    for q in range(4):
        for p in range(2):
            t0 = pre[q, :, p * 256 : p * 256 + 128].astype(jnp.float32)
            t1 = pre[q, :, p * 256 + 128 : p * 256 + 256].astype(jnp.float32)
            kp[2 * q + p, 0:16, :] = jnp.where(first16, t0, 0.0).astype(jnp.bfloat16)
            kp[2 * q + p, 64:80, :] = jnp.where(first16, 0.0, pltpu.roll(t1, 64, 1)).astype(jnp.bfloat16)
            vp[2 * q + p, 0:16, :] = jnp.where(first16, pltpu.roll(t0, 64, 1), 0.0).astype(jnp.bfloat16)
            vp[2 * q + p, 64:80, :] = jnp.where(first16, 0.0, t1).astype(jnp.bfloat16)

    for j in range(2):
        row0 = block_of(s, j) * BLOCK
        row_at = row0 + lax.broadcasted_iota(jnp.int32, (BLOCK, 1), 0)
        begin = jnp.zeros((BLOCK, 1), jnp.int32)
        for e in range(ends.shape[1]):
            begin = jnp.where(row_at >= ends[micro, e], ends[micro, e], begin)

        def mask_block(kb, carry):
            key_at = kb * BLOCK + lax.broadcasted_iota(jnp.int32, (BLOCK, BLOCK), 1)
            keep = jnp.logical_and(key_at <= row_at, key_at >= begin)
            bias[j, kb] = jnp.where(keep, 0.0, NEG_LARGE)
            return carry

        lax.fori_loop(0, 4, mask_block, 0)

    def vector(k, q=0, width=1024):
        return vec[q, k : k + 1, 0:width]

    rows_total = 2 * BLOCK
    chunks = rows_total // CHUNK

    def over_rows(action, start=0, stop=chunks):
        def one(c, carry):
            action(pl.ds(pl.multiple_of(c * CHUNK, CHUNK), CHUNK))
            return carry

        lax.fori_loop(start, stop, one, 0)

    def standardize(v):
        average = jnp.mean(v, axis=-1, keepdims=True)
        centred = v - average
        spread = jnp.mean(centred * centred, axis=-1, keepdims=True)
        return centred, lax.rsqrt(spread + EPSILON)

    def norm_back(v, gain, incoming):
        centred, inverse = standardize(v)
        xhat = centred * inverse
        e = incoming * gain
        return (e - jnp.mean(e, axis=-1, keepdims=True) - xhat * jnp.mean(e * xhat, axis=-1, keepdims=True)) * inverse

    def columns(n, width=256):
        return pl.ds(pl.multiple_of(n * width, width), width)

    for j in range(2):
        arrived(x_in.at[j * BLOCK : (j + 1) * BLOCK], x_sem.at[j])

    def norm_one(rows):
        centred, inverse = standardize(x_in[rows, :].astype(jnp.float32))
        normed[rows, :] = (centred * inverse * vector(0) + vector(1)).astype(jnp.bfloat16)

    over_rows(norm_one)
    first_all = lax.broadcasted_iota(jnp.int32, (rows_total, 128), 1) < HEAD_DIM

    def project(q, carry):
        triple = dot_nn(normed[...], wq[q]) + vec[q, 7:8, 0:768]
        for p in range(2):
            t0, t1, t2 = (triple[:, p * 384 + n * 128 : p * 384 + n * 128 + 128] for n in range(3))
            q_own[2 * q + p] = jnp.where(first_all, t0, t1).astype(jnp.bfloat16)
            kv[s, 2 * q + p, 0] = pltpu.roll(jnp.where(first_all, t2, t0), 64, 1).astype(jnp.bfloat16)
            kv[s, 2 * q + p, 1] = jnp.where(first_all, t1, t2).astype(jnp.bfloat16)
        pltpu.make_async_remote_copy(
            src_ref=kv.at[s, pl.ds(2 * q, 2)], dst_ref=kv.at[s, pl.ds(2 * q, 2)],
            send_sem=kv_ssem.at[q], recv_sem=kv_rsem.at[q], device_id=(other, d, z), device_id_type=MESH,
        ).start()
        return carry

    lax.fori_loop(0, 4, project, 0)

    def kv_wait(q, carry):
        pltpu.make_async_remote_copy(
            src_ref=kv.at[s, pl.ds(2 * q, 2)], dst_ref=kv.at[other, pl.ds(2 * q, 2)],
            send_sem=kv_ssem.at[q], recv_sem=kv_rsem.at[q], device_id=(other, d, z), device_id_type=MESH,
        ).wait()
        return carry

    lax.fori_loop(0, 4, kv_wait, 0)

    scale = LOG2E * HEAD_DIM ** (-0.5)

    def key_rows(kb):
        return pl.ds(pl.multiple_of((kb // 2) * BLOCK, BLOCK), BLOCK)

    def attend_pair(pair, carry):
        cols = columns(pair, 128)

        def attend_block(j, carry):
            rows = pl.ds(pl.multiple_of(j * BLOCK, BLOCK), BLOCK)
            blocks = block_of(s, j) + 1
            q_pair = q_own[pair, rows, :]
            q_half = (q_pair * half0, q_pair * half1)
            t_pre = dot_nt(q_pair, kp[pair]) * scale + pre_mask
            m_acc[0] = jnp.where(first, t_pre, NEG_LARGE)
            m_acc[1] = jnp.where(first, NEG_LARGE, t_pre)

            def scores(kb, carry):
                keys = kv[core_of(kb), pair, 0, key_rows(kb), :]
                for h in range(2):
                    t = dot_nt(q_half[h], keys) * scale + bias[j, kb]
                    ts[h, kb] = t
                    m_acc[h] = jnp.maximum(m_acc[h], jnp.maximum(t[:, :128], t[:, 128:]))
                return carry

            lax.fori_loop(0, blocks, scores, 0)
            highest = [jnp.max(m_acc[h], axis=1, keepdims=True) for h in range(2)]
            e_pre = jnp.exp2(t_pre - jnp.where(first, highest[0], highest[1]))
            l_acc[0] = jnp.where(first, e_pre, 0.0)
            l_acc[1] = jnp.where(first, 0.0, e_pre)
            o_acc[...] = jnp.zeros(o_acc.shape, jnp.float32)

            def mix(kb, carry):
                values = kv[core_of(kb), pair, 1, key_rows(kb), :]
                for h in range(2):
                    e = jnp.exp2(ts[h, kb] - highest[h])
                    l_acc[h] += e[:, :128] + e[:, 128:]
                    o_acc[h] += dot_nn(e.astype(jnp.bfloat16), values)
                return carry

            lax.fori_loop(0, blocks, mix, 0)
            total = [jnp.sum(l_acc[h], axis=1, keepdims=True) for h in range(2)]
            share = [1.0 / total[h] for h in range(2)]
            p_pre = (e_pre * jnp.where(first, share[0], share[1])).astype(jnp.bfloat16)
            mixed = jnp.where(first, o_acc[0] * share[0], o_acc[1] * share[1]) + dot_nn(p_pre, vp[pair])
            o_own[rows, cols] = mixed.astype(jnp.bfloat16)
            logs = [highest[h] + jnp.log(total[h]) * LOG2E for h in range(2)]
            lse[pair, rows, :] = jnp.where(first, logs[0], logs[1])
            return carry

        return lax.fori_loop(0, 2, attend_block, carry)

    lax.fori_loop(0, 8, attend_pair, 0)

    def out_project(n, carry):
        cols = columns(n)
        part_sum = jnp.zeros((rows_total, 256), jnp.float32)
        for q in range(4):
            part_sum += dot_nn(o_own[:, q * 256 : q * 256 + 256], wo[q, :, cols])
        after[:, cols] = x_in[:, cols].astype(jnp.float32) + part_sum + vec[0, 2:3, cols]
        return carry

    lax.fori_loop(0, 4, out_project, 0)

    def norm_two(rows):
        centred, inverse = standardize(after[rows, :])
        normed[rows, :] = (centred * inverse * vector(3) + vector(4)).astype(jnp.bfloat16)
        acc[rows, :] = after[rows, :] + vector(5)

    over_rows(norm_two)

    def feed_quarter(q, carry):
        def up(n, carry):
            cols = columns(n)
            for half in range(2):
                rows = slice(half * BLOCK, half * BLOCK + BLOCK)
                u = dot_nn(normed[rows, :], wu[q, :, cols]) + vec[q, 6:7, cols]
                u2 = u * u
                t = jnp.tanh(u * (GELU_A + (GELU_A * GELU_B) * u2))
                half_t = 0.5 + 0.5 * t
                wide[rows, cols] = (u * half_t).astype(jnp.bfloat16)
                inner = u * (GELU_A + (3.0 * GELU_A * GELU_B) * u2)
                slope[q, rows, cols] = (half_t + 0.5 * inner * (1.0 - t * t)).astype(jnp.bfloat16)
            return carry

        lax.fori_loop(0, 4, up, 0)

        def down(n, carry):
            cols = columns(n)
            acc[:, cols] += dot_nn(wide[...], wd[q, :, cols])
            return carry

        lax.fori_loop(0, 4, down, 0)
        return carry

    lax.fori_loop(0, 4, feed_quarter, 0)

    def give_out(rows):
        y_out[rows, :] = acc[rows, :].astype(jnp.bfloat16)

    def send_rows(j, out, sem):
        block = block_of(s, j)
        rows = slice(j * BLOCK, j * BLOCK + BLOCK)
        sends.start_or_keep(
            y_out.at[rows], out.at[micro], sem.at[micro], (role, d, block),
            jnp.logical_and(role == s, z == block),
        )

    for j in range(2):
        over_rows(give_out, j * chunks // 2, (j + 1) * chunks // 2)
        rows = slice(j * BLOCK, j * BLOCK + BLOCK)
        sends.start(y_out.at[rows], x_in.at[rows], x_sem.at[j], (s, d, partner), when=role == 0)
    for j in range(2):
        send_rows(j, act_out, act_sem)

    for j in range(2):
        arrived(g_in.at[j * BLOCK : (j + 1) * BLOCK], g_sem.at[j])

    def clear(rows):
        acc[rows, :] = jnp.zeros((CHUNK, 1024), jnp.float32)

    over_rows(clear)

    def feed_back(q, carry):
        def down(n, carry):
            cols = columns(n)
            for half in range(2):
                rows = slice(half * BLOCK, half * BLOCK + BLOCK)
                grad_act = dot_nt(g_in[rows, :], wd[q, cols, :])
                wide[rows, cols] = (grad_act * slope[q, rows, cols].astype(jnp.float32)).astype(jnp.bfloat16)
            return carry

        lax.fori_loop(0, 4, down, 0)

        def up(n, carry):
            cols = columns(n)
            acc[:, cols] += dot_nt(wide[...], wu[q, cols, :])
            return carry

        lax.fori_loop(0, 4, up, 0)
        return carry

    lax.fori_loop(0, 4, feed_back, 0)

    def middle(rows):
        dv = norm_back(after[rows, :], vector(3), acc[rows, :])
        normed[rows, :] = (g_in[rows, :].astype(jnp.float32) + dv).astype(jnp.bfloat16)

    over_rows(middle)

    def mix_back(q, carry):
        wide[:, columns(q)] = dot_nt(normed[...], wo[q]).astype(jnp.bfloat16)
        return carry

    lax.fori_loop(0, 4, mix_back, 0)

    def back_pair(pair, carry):
        cols = columns(pair, 128)
        dk_acc[...] = jnp.zeros(dk_acc.shape, jnp.float32)
        dv_acc[...] = jnp.zeros(dv_acc.shape, jnp.float32)
        pk_acc[...] = jnp.zeros(pk_acc.shape, jnp.float32)
        pv_acc[...] = jnp.zeros(pv_acc.shape, jnp.float32)

        def back_block(j, carry):
            rows = pl.ds(pl.multiple_of(j * BLOCK, BLOCK), BLOCK)
            blocks = block_of(s, j) + 1
            q_pair = q_own[pair, rows, :]
            q_half = (q_pair * half0, q_pair * half1)
            g_pair = wide[rows, cols]
            g_half = (g_pair * half0, g_pair * half1)
            product = g_pair.astype(jnp.float32) * o_own[rows, cols].astype(jnp.float32)
            row_term = [
                jnp.sum(jnp.where(first, product, 0.0), axis=1, keepdims=True),
                jnp.sum(jnp.where(first, 0.0, product), axis=1, keepdims=True),
            ]
            logs = lse[pair, rows, :]
            log_half = (logs[:, 0:1], logs[:, 64:65])
            p_pre = jnp.exp2(dot_nt(q_pair, kp[pair]) * scale + pre_mask - logs)
            dp_pre = dot_nt(g_pair, vp[pair])
            ds_pre = (p_pre * (dp_pre - jnp.where(first, row_term[0], row_term[1]))).astype(jnp.bfloat16)
            pv_acc[...] += dot_tn(p_pre.astype(jnp.bfloat16), g_pair)
            pk_acc[...] += dot_tn(ds_pre, q_pair)
            dq_pre = dot_nn(ds_pre, kp[pair])
            o_acc[...] = jnp.zeros(o_acc.shape, jnp.float32)

            def back_keys(kb, carry):
                keys = kv[core_of(kb), pair, 0, key_rows(kb), :]
                values = kv[core_of(kb), pair, 1, key_rows(kb), :]
                at = pl.ds(pl.multiple_of(kb * BLOCK, BLOCK), BLOCK)
                for h in range(2):
                    probs = jnp.exp2(dot_nt(q_half[h], keys) * scale + bias[j, kb] - log_half[h])
                    grad_probs = dot_nt(g_half[h], values)
                    grad_scores = (probs * (grad_probs - row_term[h])).astype(jnp.bfloat16)
                    dv_acc[at, :] += dot_tn(probs.astype(jnp.bfloat16), g_half[h])
                    dk_acc[at, :] += dot_tn(grad_scores, q_half[h])
                    o_acc[h] += dot_nn(grad_scores, keys)
                return carry

            lax.fori_loop(0, blocks, back_keys, 0)
            dq = (jnp.where(first, o_acc[0], o_acc[1]) + dq_pre) * HEAD_DIM ** (-0.5)
            q_own[pair, rows, :] = dq.astype(jnp.bfloat16)
            return carry

        lax.fori_loop(0, 2, back_block, 0)
        for j in range(2):
            rows = slice(j * BLOCK, j * BLOCK + BLOCK)
            for owner_core, held in ((s, dkv_own), (other, dkv_send)):
                at = pl.ds(pl.multiple_of(block_of(owner_core, j) * BLOCK, BLOCK), BLOCK)
                held[pair, 0, rows, :] = dk_acc[at, :].astype(jnp.bfloat16)
                held[pair, 1, rows, :] = dv_acc[at, :].astype(jnp.bfloat16)
        pltpu.make_async_remote_copy(
            src_ref=dkv_send.at[pair], dst_ref=dkv_recv.at[pair], send_sem=dkv_ssem.at[pair],
            recv_sem=dkv_rsem.at[pair], device_id=(other, d, z), device_id_type=MESH,
        ).start()
        pg_out[pair, 0] = jnp.where(first16, pk_acc[0:16, :], pk_acc[64:80, :]) * HEAD_DIM ** (-0.5)
        pg_out[pair, 1] = jnp.where(first16, pv_acc[0:16, :], pv_acc[64:80, :])
        return carry

    lax.fori_loop(0, 8, back_pair, 0)
    over_rows(clear)

    def project_back(q, carry):
        for p in range(2):
            pair = 2 * q + p
            pltpu.make_async_remote_copy(
                src_ref=dkv_send.at[pair], dst_ref=dkv_recv.at[pair], send_sem=dkv_ssem.at[pair],
                recv_sem=dkv_rsem.at[pair], device_id=(other, d, z), device_id_type=MESH,
            ).wait()
            dq = q_own[pair].astype(jnp.float32)
            dk = (dkv_own[pair, 0].astype(jnp.float32) + dkv_recv[pair, 0].astype(jnp.float32)) * HEAD_DIM ** (-0.5)
            dv = dkv_own[pair, 1].astype(jnp.float32) + dkv_recv[pair, 1].astype(jnp.float32)
            dk = pltpu.roll(dk, 64, 1)
            gt[:, p * 384 : p * 384 + 128] = jnp.where(first_all, dq, dk).astype(jnp.bfloat16)
            gt[:, p * 384 + 128 : p * 384 + 256] = jnp.where(first_all, dv, dq).astype(jnp.bfloat16)
            gt[:, p * 384 + 256 : p * 384 + 384] = jnp.where(first_all, dk, dv).astype(jnp.bfloat16)

        def columns_back(n, carry):
            cols = columns(n)
            acc[:, cols] += dot_nt(gt[...], wq[q, cols, :])
            return carry

        lax.fori_loop(0, 4, columns_back, 0)
        return carry

    lax.fori_loop(0, 4, project_back, 0)
    sends.finish()

    def give_back(rows):
        dv = norm_back(x_in[rows, :].astype(jnp.float32), vector(0), acc[rows, :])
        y_out[rows, :] = (normed[rows, :].astype(jnp.float32) + dv).astype(jnp.bfloat16)

    for j in range(2):
        over_rows(give_back, j * chunks // 2, (j + 1) * chunks // 2)
        rows = slice(j * BLOCK, j * BLOCK + BLOCK)
        sends.start(y_out.at[rows], g_in.at[rows], g_sem.at[j], (s, d, partner), when=role == 1)
    for j in range(2):
        send_rows(j, ig_out, ig_sem)
    for k in range(2):
        arrived(act_out.at[k], act_sem.at[k])
        arrived(ig_out.at[k], ig_sem.at[k])
    sends.finish()


def run_layers(x, cot, wq, wo, wu, wd, vec, pre, ends):
    bf, f32 = jnp.bfloat16, jnp.float32
    vm, dma = pltpu.VMEM, pltpu.SemaphoreType.DMA
    rows = 2 * BLOCK
    width = x.shape[-1]
    pairs = width // 128
    scratch = [
        vm((4,) + wq.shape, bf), vm((4,) + wo.shape, bf), vm((4,) + wu.shape, bf), vm((4,) + wd.shape, bf),
        vm((4,) + vec.shape, f32), vm((4,) + pre.shape, bf),
        vm((rows, width), bf), vm((rows, width), bf), vm((rows, width), bf), vm((rows, width), bf),
        vm((2, pairs, 2, rows, 128), bf), vm((pairs, rows, 128), bf), vm((rows, width), bf),
        vm((pairs, rows, 128), f32), vm((2, 4, BLOCK, BLOCK), f32), vm((rows, width), f32), vm((rows, width), f32),
        vm((4, rows, wu.shape[1]), bf), vm((rows, wu.shape[1]), bf),
        vm((2, 4, BLOCK, BLOCK), f32), vm((2, BLOCK, 128), f32), vm((2, BLOCK, 128), f32), vm((2, BLOCK, 128), f32),
        vm((4 * BLOCK, 128), f32), vm((4 * BLOCK, 128), f32),
        vm((pairs, 2, rows, 128), bf), vm((pairs, 2, rows, 128), bf), vm((pairs, 2, rows, 128), bf),
        vm((pairs, 128, 128), bf), vm((pairs, 128, 128), bf), vm((128, 128), f32), vm((128, 128), f32),
        vm((rows, wq.shape[1]), bf),
        dma((96,)), dma((4,)), dma((4,)), dma((2,)), dma((2,)), dma((2,)), dma((2,)), dma((4,)),
        dma((4, 4)), dma((4, 4)), dma((4, 4)), dma((4, 4)),
        dma((4,)), dma((4,)), dma((pairs,)), dma((pairs,)),
    ]
    anywhere = pl.BlockSpec(memory_space=pl.ANY)
    return pl.pallas_call(
        layer_kernel,
        out_shape=(
            jax.ShapeDtypeStruct(x.shape, bf), jax.ShapeDtypeStruct(x.shape, bf),
            jax.ShapeDtypeStruct((pairs, 2, 16, 128), f32),
        ),
        in_specs=[anywhere] * 8 + [pl.BlockSpec(memory_space=pltpu.SMEM)],
        out_specs=(anywhere, anywhere, pl.BlockSpec(memory_space=pltpu.VMEM)),
        scratch_shapes=scratch,
        name="two_layers",
        compiler_params=pltpu.CompilerParams(
            collective_id=0, has_side_effects=True, vmem_limit_bytes=63 * 2**20
        ),
    )(x, cot, wq, wo, wu, wd, vec, pre, ends)


def pair_body(
    layer_input, cotangent, example_lengths, attn_gain, attn_shift, query_key_value_weight, qkv_bias,
    attention_output_weight, out_bias, ffn_gain, ffn_shift, up_projection_weight, up_projection_bias,
    down_projection_weight, down_bias, prefix_table, mid_weight, mid_bias, prefix_weight, prefix_bias,
):
    section_index, z = lax.axis_index("section"), lax.axis_index("mp")
    hidden_pre = jnp.dot(
        prefix_table, mid_weight, preferred_element_type=jnp.float32
    ) + mid_bias.astype(jnp.float32)
    hidden_act = jnp.tanh(hidden_pre)
    hidden_low = hidden_act.astype(jnp.bfloat16)
    prefix_kv = (
        jnp.dot(hidden_low, prefix_weight, preferred_element_type=jnp.float32)
        + prefix_bias.astype(jnp.float32)
    ).astype(jnp.bfloat16)
    pre = jnp.pad(prefix_kv, ((0, 6), (0, 0)))
    pieces = [attn_gain, attn_shift, out_bias, ffn_gain, ffn_shift, down_bias, up_projection_bias, qkv_bias]
    width = layer_input.shape[-1]
    vec = jnp.concatenate(
        [jnp.pad(p.astype(jnp.float32), ((0, 0), (0, width - p.shape[1]))) for p in pieces], axis=0
    )
    ends = jnp.cumsum(example_lengths[:, 0], axis=-1).astype(jnp.int32)
    activations, input_grads, prefix_part = run_layers(
        layer_input[:, 0], cotangent[:, 0], query_key_value_weight[0], attention_output_weight[0],
        up_projection_weight[0], down_projection_weight[0], vec, pre, ends,
    )
    pairs = prefix_part.shape[0]
    part = prefix_part.reshape(pairs, 2, 16, 2, HEAD_DIM)[:, :, :PREFIX]
    part = part.transpose(2, 0, 3, 1, 4).reshape(PREFIX, -1)
    role = role_of(z)
    both = jnp.stack([jnp.where(role == layer, part, 0.0) for layer in range(2)])
    prefix_sum = lax.psum(both, ("section", "dp", "mp"))
    own = prefix_bias.shape[0]
    prefix_sum = lax.dynamic_slice(prefix_sum, (section_index, 0, z * own), (1, PREFIX, own))[0]
    return (activations[None, :, None], input_grads[None, :, None]) + prefix_back(
        prefix_sum, hidden_act, hidden_low, prefix_table, mid_weight, prefix_weight
    )


def solution(mesh):
    placed = (
        P(None, "dp", "mp", None),
        P(None, "dp", "mp", None),
        P(None, "dp", None),
        P("section", None),
        P("section", None),
        P("section", None, "mp"),
        P("section", "mp"),
        P("section", "mp", None),
        P("section", None),
        P("section", None),
        P("section", None),
        P("section", None, "mp"),
        P("section", "mp"),
        P("section", "mp", None),
        P("section", None),
        P(),
        P(),
        P(),
        P(None, ("section", "mp")),
        P(("section", "mp")),
    )
    paired = mesh.shape["mp"] == 4 and mesh.shape["dp"] == 4
    return jax.shard_map(
        pair_body if paired else body,
        mesh=mesh,
        in_specs=placed,
        out_specs=(
            P("section", None, "dp", "mp", None),
            P("section", None, "dp", "mp", None),
            P(),
            P(),
            P(),
            P(None, ("section", "mp")),
            P(("section", "mp")),
        ),
        check_vma=False,
    )
```

```python
import jax
import jax.numpy as jnp
from jax import lax
from jax.experimental import pallas as pl
from jax.experimental.pallas import tpu as pltpu
from jax.sharding import PartitionSpec as P

HEAD_DIM = 64
PREFIX = 10
SEQ_LEN = 1024


EPSILON = 1e-05
NEG_LARGE = -1e30
GELU_A = 0.7978845608028654
GELU_B = 0.044715


def norm_rows(values, gain, shift):
    average = jnp.mean(values, axis=-1, keepdims=True)
    centred = values - average
    spread = jnp.mean(centred * centred, axis=-1, keepdims=True)
    return centred * lax.rsqrt(spread + EPSILON) * gain + shift


def norm_input_grad(values, gain, shift, incoming):

    def apply_norm(inputs):
        return norm_rows(inputs, gain, shift)

    norm_value, norm_back = jax.vjp(apply_norm, values)
    return norm_back(incoming)[0]


def gelu_tanh(values):
    return jax.nn.gelu(values, approximate=True)


def visible_of(lengths, first_row, count):
    run_ends = jnp.cumsum(lengths, axis=-1)
    keys_at = jnp.arange(SEQ_LEN, dtype=jnp.int32)
    query_at = first_row + jnp.arange(count, dtype=jnp.int32)
    key_seg = jnp.sum((keys_at[None, :, None] >= run_ends[:, None, :]).astype(jnp.int32), axis=-1)
    query_seg = jnp.sum(
        (query_at[None, :, None] >= run_ends[:, None, :]).astype(jnp.int32), axis=-1
    )
    causal = (query_at[:, None] >= keys_at[None, :])[None]
    inside = (query_seg[:, :, None] == key_seg[:, None, :]) & causal
    leading = jnp.ones((lengths.shape[0], count, PREFIX), dtype=bool)
    return jnp.concatenate([leading, inside], axis=2)


def gather_rows(piece):
    return lax.all_gather(piece, "mp", axis=1, tiled=True)


def reduce_rows(partial_sum):
    return lax.psum_scatter(
        partial_sum.astype(jnp.bfloat16), "mp", scatter_dimension=1, tiled=True
    ).astype(jnp.float32)


def with_prefix(prefix_kv, pair_keys, pair_values, heads_count):
    prefix_pair = prefix_kv.reshape(PREFIX, heads_count, 2, HEAD_DIM)
    key_rows = jnp.concatenate([prefix_pair[None, :, :, 0], pair_keys], axis=1)
    value_rows = jnp.concatenate([prefix_pair[None, :, :, 1], pair_values], axis=1)
    return (key_rows, value_rows)


def attend(query_rows, key_rows, value_rows, visible):
    score_scale = HEAD_DIM ** (-0.5)
    scores = (
        jnp.einsum("sqhd,skhd->shqk", query_rows, key_rows, preferred_element_type=jnp.float32)
        * score_scale
    )
    scores = jnp.where(visible[:, None], scores, NEG_LARGE)
    highest = jnp.max(scores, axis=-1, keepdims=True)
    raised = jnp.exp(scores - highest)
    softmax_probs = raised / jnp.sum(raised, axis=-1, keepdims=True)
    probs_low = softmax_probs.astype(jnp.bfloat16)
    head_mixed_rows = jnp.einsum(
        "shqk,skhd->sqhd", probs_low, value_rows, preferred_element_type=jnp.float32
    )
    batch_size, query_count, heads_count, head_size = head_mixed_rows.shape
    head_mixed_rows = head_mixed_rows.astype(jnp.bfloat16).reshape(
        batch_size, query_count, heads_count * head_size
    )
    return (softmax_probs, probs_low, head_mixed_rows)


def attend_back(grad_mix, query_rows, key_rows, value_rows, softmax_probs, probs_low):
    grad_heads = grad_mix.reshape(query_rows.shape)
    grad_probs = jnp.einsum(
        "sqhd,skhd->shqk", grad_heads, value_rows, preferred_element_type=jnp.float32
    )
    value_grad = jnp.einsum(
        "shqk,sqhd->skhd", probs_low, grad_heads, preferred_element_type=jnp.float32
    )
    row_term = jnp.sum(grad_probs * softmax_probs, axis=-1, keepdims=True)
    grad_scores = (softmax_probs * (grad_probs - row_term)).astype(jnp.bfloat16)
    score_scale = HEAD_DIM ** (-0.5)
    query_grad = (
        jnp.einsum("shqk,skhd->sqhd", grad_scores, key_rows, preferred_element_type=jnp.float32)
        * score_scale
    )
    key_grad = (
        jnp.einsum("shqk,sqhd->skhd", grad_scores, query_rows, preferred_element_type=jnp.float32)
        * score_scale
    )
    return (query_grad, key_grad, value_grad)


def prefix_part(key_grad, value_grad):
    pair_sum = jnp.stack(
        [jnp.sum(key_grad[:, :PREFIX], axis=0), jnp.sum(value_grad[:, :PREFIX], axis=0)], axis=2
    )
    return pair_sum.reshape(PREFIX, -1)


def tensor_forward(own_rows, weights, prefix_kv, visible):
    (
        attn_gain,
        attn_shift,
        query_key_value_weight,
        qkv_bias,
        attention_output_weight,
        out_bias,
        ffn_gain,
        ffn_shift,
        up_projection_weight,
        up_projection_bias,
        down_projection_weight,
        down_bias,
        out_full,
    ) = weights
    normed = norm_rows(own_rows, attn_gain, attn_shift).astype(jnp.bfloat16)
    normalized_input_rows = gather_rows(normed)
    batch_size, seq_len, model_width = normalized_input_rows.shape
    heads_here = query_key_value_weight.shape[1] // (3 * HEAD_DIM)
    projected = (
        jnp.einsum(
            "naj,jk->nak",
            normalized_input_rows,
            query_key_value_weight,
            preferred_element_type=jnp.float32,
        )
        + qkv_bias
    )
    triple = projected.astype(jnp.bfloat16).reshape(batch_size, seq_len, heads_here, 3, HEAD_DIM)
    query_rows = triple[:, :, :, 0]
    key_rows, value_rows = with_prefix(
        prefix_kv, triple[:, :, :, 1], triple[:, :, :, 2], heads_here
    )
    softmax_probs, probs_low, head_mixed_rows = attend(query_rows, key_rows, value_rows, visible)
    attn_part = reduce_rows(
        jnp.einsum(
            "hgm,mt->hgt",
            head_mixed_rows,
            attention_output_weight,
            preferred_element_type=jnp.float32,
        )
    )
    after_attn = own_rows + attn_part + out_bias
    normed_two = norm_rows(after_attn, ffn_gain, ffn_shift).astype(jnp.bfloat16)
    second_norm_rows = gather_rows(normed_two)
    up_pre = (
        jnp.einsum(
            "rmy,yq->rmq",
            second_norm_rows,
            up_projection_weight,
            preferred_element_type=jnp.float32,
        )
        + up_projection_bias
    )
    gelu_output_rows = gelu_tanh(up_pre).astype(jnp.bfloat16)
    mlp_part = reduce_rows(
        jnp.einsum(
            "epj,jq->epq",
            gelu_output_rows,
            down_projection_weight,
            preferred_element_type=jnp.float32,
        )
    )
    result = after_attn + mlp_part + down_bias
    kept_values = (query_rows, key_rows, value_rows, softmax_probs, probs_low, after_attn, up_pre)
    return (result, kept_values)


def tensor_backward(own_rows, arriving, weights, kept_values):
    (
        attn_gain,
        attn_shift,
        query_key_value_weight,
        qkv_bias,
        attention_output_weight,
        out_bias,
        ffn_gain,
        ffn_shift,
        up_projection_weight,
        up_projection_bias,
        down_projection_weight,
        down_bias,
        out_full,
    ) = weights
    query_rows, key_rows, value_rows, softmax_probs, probs_low, after_attn, up_pre = kept_values
    gradient_gathered = gather_rows(arriving)
    gradient_activation = jnp.einsum(
        "bhi,vi->bhv", gradient_gathered, down_projection_weight, preferred_element_type=jnp.float32
    )
    gelu_value, gelu_back = jax.vjp(gelu_tanh, up_pre)
    gradient_up_projection = gelu_back(gradient_activation)[0].astype(jnp.bfloat16)
    grad_two = reduce_rows(
        jnp.einsum(
            "yca,ja->ycj",
            gradient_up_projection,
            up_projection_weight,
            preferred_element_type=jnp.float32,
        )
    )
    grad_after = norm_input_grad(after_attn, ffn_gain, ffn_shift, grad_two)
    grad_mid = (grad_after + arriving.astype(jnp.float32)).astype(jnp.bfloat16)
    middle_gathered = gather_rows(grad_mid)
    grad_mix = jnp.einsum(
        "taq,kq->tak", middle_gathered, attention_output_weight, preferred_element_type=jnp.float32
    ).astype(jnp.bfloat16)
    query_grad, key_grad, value_grad = attend_back(
        grad_mix, query_rows, key_rows, value_rows, softmax_probs, probs_low
    )
    prefix_g = prefix_part(key_grad, value_grad)
    batch_size, seq_len = (query_grad.shape[0], query_grad.shape[1])
    gradient_query_key_value = jnp.stack(
        [query_grad, key_grad[:, PREFIX:], value_grad[:, PREFIX:]], axis=3
    )
    gradient_query_key_value = gradient_query_key_value.astype(jnp.bfloat16).reshape(
        batch_size, seq_len, -1
    )
    grad_one = reduce_rows(
        jnp.einsum(
            "tvq,xq->tvx",
            gradient_query_key_value,
            query_key_value_weight,
            preferred_element_type=jnp.float32,
        )
    )
    grad_input = norm_input_grad(own_rows, attn_gain, attn_shift, grad_one)
    grad_input = (grad_input + grad_mid.astype(jnp.float32)).astype(jnp.bfloat16)
    return (grad_input, prefix_g)


def prefix_back(prefix_sum, hidden_grad, hidden_act, hidden_low, prefix_table, mid_weight):
    prefix_low = prefix_sum.astype(jnp.bfloat16)
    prefix_bias_grad = jnp.sum(prefix_low.astype(jnp.float32), axis=0)
    prefix_weight_grad = jnp.dot(hidden_low.T, prefix_low, preferred_element_type=jnp.float32)
    pre_grad = (hidden_grad * (1.0 - hidden_act * hidden_act)).astype(jnp.bfloat16)
    mid_bias_grad = jnp.sum(pre_grad.astype(jnp.float32), axis=0)
    mid_weight_grad = jnp.dot(prefix_table.T, pre_grad, preferred_element_type=jnp.float32)
    table_grad = jnp.dot(pre_grad, mid_weight.T, preferred_element_type=jnp.float32)
    return (table_grad, mid_weight_grad, mid_bias_grad, prefix_weight_grad, prefix_bias_grad)


def both_layers(piece):
    return lax.all_gather(piece[0], "section", axis=0, tiled=False)


def body(
    layer_input,
    cotangent,
    example_lengths,
    attn_gain,
    attn_shift,
    query_key_value_weight,
    qkv_bias,
    attention_output_weight,
    out_bias,
    ffn_gain,
    ffn_shift,
    up_projection_weight,
    up_projection_bias,
    down_projection_weight,
    down_bias,
    prefix_table,
    mid_weight,
    mid_bias,
    prefix_weight,
    prefix_bias,
):
    layers = lax.axis_size("section")
    section_index = lax.axis_index("section")
    hidden_pre = jnp.dot(
        prefix_table, mid_weight, preferred_element_type=jnp.float32
    ) + mid_bias.astype(jnp.float32)
    hidden_act = jnp.tanh(hidden_pre)
    hidden_low = hidden_act.astype(jnp.bfloat16)
    prefix_kv = (
        jnp.dot(hidden_low, prefix_weight, preferred_element_type=jnp.float32)
        + prefix_bias.astype(jnp.float32)
    ).astype(jnp.bfloat16)
    prefix_all = lax.all_gather(prefix_kv, "section", axis=0, tiled=False)
    floats = [
        both_layers(piece).astype(jnp.float32)
        for piece in (attn_gain, attn_shift, qkv_bias, out_bias, ffn_gain, ffn_shift,
                      up_projection_bias, down_bias)
    ]
    matrices = [
        both_layers(piece)
        for piece in (query_key_value_weight, attention_output_weight,
                      up_projection_weight, down_projection_weight)
    ]

    def weights_of(layer):
        g1, s1, bq, bo, g2, s2, bu, bd = [piece[layer] for piece in floats]
        wq, wo, wu, wd = [piece[layer] for piece in matrices]
        return (g1, s1, wq, bq, wo, bo, g2, s2, wu, bu, wd, bd, wo)

    batch_count = layer_input.shape[0]
    own_input = lax.dynamic_index_in_dim(layer_input, section_index, 0, keepdims=False)
    own_cotangent = lax.dynamic_index_in_dim(cotangent, section_index, 0, keepdims=False)
    lengths = lax.dynamic_index_in_dim(example_lengths, section_index, 0, keepdims=False)
    visible = visible_of(lengths, 0, SEQ_LEN)
    entering = own_input
    entered, produced, kept = [], [], []
    for layer in range(layers):
        entered.append(entering.astype(jnp.float32))
        result, kept_values = tensor_forward(
            entered[layer], weights_of(layer), prefix_all[layer], visible
        )
        entering = result.astype(jnp.bfloat16)
        produced.append(entering)
        kept.append(kept_values)
    gradient = own_cotangent
    sent_grads = [None] * layers
    prefix_parts = [None] * layers
    for layer in reversed(range(layers)):
        gradient, prefix_parts[layer] = tensor_backward(
            entered[layer], gradient, weights_of(layer), kept[layer]
        )
        sent_grads[layer] = gradient
    activations = lax.all_to_all(jnp.stack(produced), "section", 0, 0, tiled=False)
    input_grads = lax.all_to_all(jnp.stack(sent_grads), "section", 0, 0, tiled=False)
    prefix_sum = lax.psum(jnp.stack(prefix_parts), ("dp", "section"))
    prefix_sum = lax.dynamic_index_in_dim(prefix_sum, section_index, 0, keepdims=False)
    hidden_part = jnp.dot(
        prefix_sum.astype(jnp.bfloat16), prefix_weight.T, preferred_element_type=jnp.float32
    )
    hidden_grad = lax.psum(hidden_part, ("section", "mp"))
    return (activations[None], input_grads[None]) + prefix_back(
        prefix_sum, hidden_grad, hidden_act, hidden_low, prefix_table, mid_weight
    )


MESH = pl.DeviceIdType.MESH
BLOCK = 256
LOG2E = 1.4426950408889634
CHUNK = 32
UNITS = 12
UNIT_ROWS = 512
PART_ROWS = UNIT_ROWS // 8


def role_of(z):
    return (((z + 1) // 2) + 1) % 2


def block_of(s, j):
    return j * 3 + s * (1 - 2 * j)


def core_of(block):
    return ((block + 1) // 2) % 2


def guarded(when, action):
    if when is None:
        action()
    else:
        pl.when(when)(action)


def dot_nn(a, b):
    return lax.dot_general(a, b, (((1,), (0,)), ((), ())), preferred_element_type=jnp.float32)


def dot_nt(a, b):
    return lax.dot_general(a, b, (((1,), (1,)), ((), ())), preferred_element_type=jnp.float32)


def dot_tn(a, b):
    return lax.dot_general(a, b, (((0,), (0,)), ((), ())), preferred_element_type=jnp.float32)


class Sends:
    def __init__(self, sems):
        self.sems, self.used, self.pending = sems, 0, []

    def start(self, src, dst, recv_sem, target, when=None):
        copy = pltpu.make_async_remote_copy(
            src_ref=src, dst_ref=dst, send_sem=self.sems.at[self.used], recv_sem=recv_sem,
            device_id=target, device_id_type=MESH,
        )
        self.used += 1
        guarded(when, copy.start)
        self.pending.append((when, copy))

    def start_or_keep(self, src, dst, recv_sem, target, is_here):
        @pl.when(is_here)
        def _():
            pltpu.make_async_copy(src, dst, recv_sem).start()

        self.start(src, dst, recv_sem, target, when=jnp.logical_not(is_here))

    def finish(self, early=None):
        left = []
        for when, copy in self.pending:
            if early is None:
                guarded(when, copy.wait_send)
            else:
                guarded(early if when is None else jnp.logical_and(when, early), copy.wait_send)
                late = jnp.logical_not(early)
                left.append((late if when is None else jnp.logical_and(when, late), copy))
        self.pending = left


def layer_kernel(
    x_hbm, cot_hbm, wq_hbm, wo_hbm, wu_hbm, wd_hbm, vec_hbm, pre_hbm, pw, ends,
    act_out, ig_out, sum_out, hidden_out,
    wq, wo, wud, vec, pre,
    x_in, g_in, y_out, normed, kv, q_own, o_own, lse, bias, after, acc, slope, wide,
    pg, pg_near, pg_far, hidden_all, ts, dk_acc, dv_acc, dkv_own, dkv_send, dkv_recv, kp, vp, pk_acc, pv_acc, gt,
    ssem, vec_sem, pre_sem, x_sem, g_sem, act_sem, ig_sem, own_sem, z_sem, a_sem, b_sem, c_sem,
    zr_sem, ar_sem, br_sem, cr_sem, zs_sem, as_sem, bs_sem, cs_sem, go_sem,
    kv_ssem, kv_rsem, dkv_ssem, dkv_rsem, pg_sem, far_sem, hidden_sem,
):
    s, d, z = lax.axis_index("section"), lax.axis_index("dp"), lax.axis_index("mp")
    role, micro = role_of(z), z // 2
    other = 1 - s
    partner = z + 1 - 2 * (z % 2)
    x_near, y_near = d + 1 - 2 * (d % 2), (d + 2) % 4
    near1 = jnp.where(s == 0, x_near, y_near)
    near2 = jnp.where(s == 0, y_near, x_near)
    sends = Sends(ssem)

    barrier = pltpu.get_barrier_semaphore()
    for ds in range(2):
        for dz in range(4):
            if ds or dz:
                pl.semaphore_signal(barrier, inc=1, device_id=((s + ds) % 2, d, (z + dz) % 4), device_id_type=MESH)
    for near in (x_near, y_near, 3 - d):
        pl.semaphore_signal(barrier, inc=1, device_id=(s, near, z), device_id_type=MESH)
    pl.semaphore_wait(barrier, 10)

    def arrived(dst, sem):
        pltpu.make_async_remote_copy(
            src_ref=dst, dst_ref=dst, send_sem=ssem.at[0], recv_sem=sem,
            device_id=(other, d, z), device_id_type=MESH,
        ).wait_recv()

    low_plane, high_plane = jnp.where(s == 0, 1, 0), jnp.where(s == 0, 2, 3)
    planes = (low_plane, high_plane)
    mine = s == core_of(z)
    row_slot = pl.ds(pl.multiple_of((z // 2) * BLOCK, BLOCK), BLOCK)

    def send_block(source, landing, sem, k, chip, when):
        when = jnp.logical_and(mine, when)

        @pl.when(jnp.logical_and(when, z == chip))
        def _():
            pltpu.make_async_copy(source.at[k], landing.at[row_slot], sem.at[z // 2]).start()

        sends.start(source.at[k], landing.at[row_slot], sem.at[z // 2], (s, d, chip),
                    when=jnp.logical_and(when, z != chip))

    for t in planes:
        for h in range(2):
            is_here = jnp.logical_and(z == t, s == h)
            sends.start_or_keep(vec_hbm, vec.at[z], vec_sem.at[z], (h, d, t), is_here)
            sends.start_or_keep(pre_hbm, pre.at[z], pre_sem.at[z], (h, d, t), is_here)
    swapped = (d % 2) * 2 + d // 2
    place = jnp.where(s == 0, d, swapped)
    pair_start = (place // 2) * 2
    far_start = 2 - pair_start
    firsts = ((wq_hbm, wq), (wo_hbm, wo))

    def eighths(rows, start, count, h):
        return pl.ds(pl.multiple_of((start + 4 * h) * rows, rows), rows * count)

    def supply_firsts(when):
        for w, (held, full) in enumerate(firsts):
            rows = held.shape[0] // 8
            for t in planes:
                for h in range(2):
                    at = eighths(rows, swapped if h else d, 1, h)
                    sends.start(held.at[at], full.at[z, at], z_sem.at[w, z], (h, d, t),
                                when=jnp.logical_and(when, z != t))

    def supply_copies(i, c, then):
        t = (z + 3 - i) % 4
        held, base = ((wu_hbm, 0), (wd_hbm, 1024))[c // 2]

        @pl.when(role_of(t) == s)
        def _():
            for h in range(2):
                at = eighths(PART_ROWS, swapped if h else d, 1, h)
                start = (c % 2) * UNIT_ROWS + at.start
                then(pltpu.make_async_remote_copy(
                    src_ref=held.at[pl.ds(pl.multiple_of(start, PART_ROWS), PART_ROWS)],
                    dst_ref=wud.at[z, pl.ds(pl.multiple_of(base + start, PART_ROWS), PART_ROWS)],
                    send_sem=zs_sem.at[4 * i + c, h], recv_sem=zr_sem.at[4 * i + c],
                    device_id=(h, d, t), device_id_type=MESH,
                ))

    def supply_all(i, carry):
        for c in range(4):
            supply_copies(i, c, lambda copy: copy.start())
        return carry

    def supply_done(i, carry):
        for c in range(4):
            supply_copies(i, c, lambda copy: copy.wait_send())
        return carry

    def supply_paced(i, carry):
        for c in range(4):
            supply_copies(i, c, lambda copy: copy.start())
            if c:
                supply_copies(i, c - 1, lambda copy: copy.wait_send())
        supply_copies(i, 3, lambda copy: copy.wait_send())
        return carry

    supply_firsts(s == 0)
    for k, chip in ((0, 1), (1, 2)):
        send_block(x_hbm, x_in, x_sem, k, chip, True)
    owned = ((wq_hbm, wq.at[z]), (wo_hbm, wo.at[z]), (wu_hbm, wud.at[z, 0:1024]), (wd_hbm, wud.at[z, 1024:2048]))
    for w, (held, full) in enumerate(owned):
        @pl.when(role == s)
        def _():
            pltpu.make_async_copy(held, full, own_sem.at[w]).start()

        sends.start(held, full, own_sem.at[w], (other, d, z), when=role == s)

    feeds_zero = jnp.logical_and(role == 1, s == 0)

    sends.finish(feeds_zero)

    @pl.when(feeds_zero)
    def _():
        lax.fori_loop(0, 3, supply_paced, 0)

    @pl.when(jnp.logical_and(role == 1, s == 1))
    def _():
        pl.semaphore_wait(go_sem, 1)

    supply_first_one = jnp.logical_and(role == 1, s == 1)
    supply_firsts(supply_first_one)

    @pl.when(supply_first_one)
    def _():
        lax.fori_loop(0, 3, supply_all, 0)

    first_units = [(w, i) for w in (0, 1) for i in range(1, 4)]

    def first_piece(w, i, start, count):
        full = firsts[w][1]
        return full.at[(z + i) % 4, eighths(full.shape[1] // 8, start, count, s)]

    def relay_first(step):
        stages = [first_units[step - k] if 0 <= step - k < len(first_units) else None for k in range(4)]
        if stages[0]:
            w, i = stages[0]
            q = (z + i) % 4
            arrived(first_piece(w, i, place, 1), z_sem.at[w, q])
            sends.start(first_piece(w, i, place, 1), first_piece(w, i, place, 1), a_sem.at[w, q], (s, near1, z))
        if stages[1]:
            w, i = stages[1]
            q = (z + i) % 4
            arrived(first_piece(w, i, pair_start + 1 - place % 2, 1), a_sem.at[w, q])
            sends.start(first_piece(w, i, pair_start, 2), first_piece(w, i, pair_start, 2), b_sem.at[w, q], (s, near2, z))
        if stages[2]:
            w, i = stages[2]
            q = (z + i) % 4
            arrived(first_piece(w, i, far_start, 2), b_sem.at[w, q])
            sends.start(first_piece(w, i, 0, 4), first_piece(w, i, 0, 4), c_sem.at[w, q], (other, d, z))
        if stages[3]:
            w, i = stages[3]
            full = firsts[w][1]
            arrived(full.at[(z + i) % 4, eighths(full.shape[1] // 8, 0, 4, other)], c_sem.at[w, (z + i) % 4])

    for step in range(len(first_units) + 3):
        relay_first(step)

    feeds_one = jnp.logical_and(role == 0, s == 1)

    @pl.when(feeds_one)
    def _():
        pl.semaphore_signal(go_sem, inc=1, device_id=(1, d, partner), device_id_type=MESH)

    supply_firsts(feeds_one)
    feeds_zero_late = jnp.logical_and(role == 0, s == 0)

    @pl.when(feeds_zero_late)
    def _():
        lax.fori_loop(0, 3, supply_all, 0)

    def unit_piece(m, start, count, h):
        q = (z + 1 + m // 4) % 4
        first_row = (m % 4) * UNIT_ROWS + (start + 4 * h) * PART_ROWS
        return wud.at[q, pl.ds(pl.multiple_of(first_row, PART_ROWS), PART_ROWS * count)]

    def relay_copy(m, stage):
        start, count = ((place, 1), (pair_start, 2), (0, 4))[stage]
        at = unit_piece(m, start, count, s)
        return pltpu.make_async_remote_copy(
            src_ref=at, dst_ref=at, send_sem=(as_sem, bs_sem, cs_sem)[stage].at[m],
            recv_sem=(ar_sem, br_sem, cr_sem)[stage].at[m],
            device_id=((s, near1, z), (s, near2, z), (other, d, z))[stage], device_id_type=MESH,
        )

    def relay(n):
        for c in range(4):

            @pl.when(jnp.logical_and(feeds_one, jnp.logical_and(n < UNITS, n % 4 == c)))
            def _():
                supply_copies(n // 4, c, lambda copy: copy.start())

        for k in range(4):
            m = n - k

            @pl.when(jnp.logical_and(m >= 0, m < UNITS))
            def _():
                if k == 0:
                    arrived(unit_piece(m, place, 1, s), zr_sem.at[m])
                if k == 1:
                    arrived(unit_piece(m, pair_start + 1 - place % 2, 1, s), ar_sem.at[m])
                if k == 2:
                    arrived(unit_piece(m, far_start, 2, s), br_sem.at[m])
                if k == 3:
                    arrived(unit_piece(m, 0, 4, other), cr_sem.at[m])
                if k < 3:
                    relay_copy(m, k).start()

    def relay_while(start, stop, when):
        def one(n, carry):
            relay(n)
            return carry

        lax.fori_loop(start, jnp.where(when, stop, start), one, 0)

    early = role == 0
    relay_while(0, UNITS + 3, role == 1)
    for k, chip in ((0, 0), (1, 3)):
        send_block(cot_hbm, g_in, g_sem, k, chip, role == 1)
    arrived(wq.at[z], own_sem.at[0])
    arrived(wo.at[z], own_sem.at[1])
    arrived(wud.at[z, 0:1024], own_sem.at[2])
    arrived(wud.at[z, 1024:2048], own_sem.at[3])
    for q in range(4):
        arrived(vec.at[q], vec_sem.at[q])
        arrived(pre.at[q], pre_sem.at[q])

    first16 = lax.broadcasted_iota(jnp.int32, (16, 128), 1) < HEAD_DIM
    first = lax.broadcasted_iota(jnp.int32, (BLOCK, 128), 1) < HEAD_DIM
    lane = lax.broadcasted_iota(jnp.int32, (1, 128), 1)
    half0 = jnp.where(lane < HEAD_DIM, 1.0, 0.0).astype(jnp.bfloat16)
    half1 = jnp.where(lane < HEAD_DIM, 0.0, 1.0).astype(jnp.bfloat16)
    pre_mask = jnp.where(lane % HEAD_DIM < PREFIX, 0.0, NEG_LARGE)
    kp[...] = jnp.zeros(kp.shape, kp.dtype)
    vp[...] = jnp.zeros(vp.shape, vp.dtype)
    for q in range(4):
        for p in range(2):
            t0 = pre[q, :, p * 256 : p * 256 + 128].astype(jnp.float32)
            t1 = pre[q, :, p * 256 + 128 : p * 256 + 256].astype(jnp.float32)
            kp[2 * q + p, 0:16, :] = jnp.where(first16, t0, 0.0).astype(jnp.bfloat16)
            kp[2 * q + p, 64:80, :] = jnp.where(first16, 0.0, pltpu.roll(t1, 64, 1)).astype(jnp.bfloat16)
            vp[2 * q + p, 0:16, :] = jnp.where(first16, pltpu.roll(t0, 64, 1), 0.0).astype(jnp.bfloat16)
            vp[2 * q + p, 64:80, :] = jnp.where(first16, 0.0, t1).astype(jnp.bfloat16)

    for j in range(2):
        row0 = block_of(s, j) * BLOCK
        row_at = row0 + lax.broadcasted_iota(jnp.int32, (BLOCK, 1), 0)
        begin = jnp.zeros((BLOCK, 1), jnp.int32)
        for e in range(ends.shape[1]):
            begin = jnp.where(row_at >= ends[micro, e], ends[micro, e], begin)

        def mask_block(kb, carry):
            key_at = kb * BLOCK + lax.broadcasted_iota(jnp.int32, (BLOCK, BLOCK), 1)
            keep = jnp.logical_and(key_at <= row_at, key_at >= begin)
            bias[j, kb] = jnp.where(keep, 0.0, NEG_LARGE)
            return carry

        lax.fori_loop(0, 4, mask_block, 0)

    def vector(k, q=0, width=1024):
        return vec[q, k : k + 1, 0:width]

    rows_total = 2 * BLOCK
    chunks = rows_total // CHUNK

    def over_rows(action, start=0, stop=chunks):
        def one(c, carry):
            action(pl.ds(pl.multiple_of(c * CHUNK, CHUNK), CHUNK))
            return carry

        lax.fori_loop(start, stop, one, 0)

    def standardize(v):
        average = jnp.mean(v, axis=-1, keepdims=True)
        centred = v - average
        spread = jnp.mean(centred * centred, axis=-1, keepdims=True)
        return centred, lax.rsqrt(spread + EPSILON)

    def norm_back(v, gain, incoming):
        centred, inverse = standardize(v)
        xhat = centred * inverse
        e = incoming * gain
        return (e - jnp.mean(e, axis=-1, keepdims=True) - xhat * jnp.mean(e * xhat, axis=-1, keepdims=True)) * inverse

    def columns(n, width=256):
        return pl.ds(pl.multiple_of(n * width, width), width)

    for j in range(2):
        arrived(x_in.at[j * BLOCK : (j + 1) * BLOCK], x_sem.at[j])

    def norm_one(rows):
        centred, inverse = standardize(x_in[rows, :].astype(jnp.float32))
        normed[rows, :] = (centred * inverse * vector(0) + vector(1)).astype(jnp.bfloat16)

    over_rows(norm_one)
    first_all = lax.broadcasted_iota(jnp.int32, (rows_total, 128), 1) < HEAD_DIM

    def project(q, carry):
        triple = dot_nn(normed[...], wq[q]) + vec[q, 7:8, 0:768]
        for p in range(2):
            t0, t1, t2 = (triple[:, p * 384 + n * 128 : p * 384 + n * 128 + 128] for n in range(3))
            q_own[2 * q + p] = jnp.where(first_all, t0, t1).astype(jnp.bfloat16)
            kv[s, 2 * q + p, 0] = pltpu.roll(jnp.where(first_all, t2, t0), 64, 1).astype(jnp.bfloat16)
            kv[s, 2 * q + p, 1] = jnp.where(first_all, t1, t2).astype(jnp.bfloat16)
        pltpu.make_async_remote_copy(
            src_ref=kv.at[s, pl.ds(2 * q, 2)], dst_ref=kv.at[s, pl.ds(2 * q, 2)],
            send_sem=kv_ssem.at[q], recv_sem=kv_rsem.at[q], device_id=(other, d, z), device_id_type=MESH,
        ).start()
        return carry

    lax.fori_loop(0, 4, project, 0)

    def kv_wait(q, carry):
        pltpu.make_async_remote_copy(
            src_ref=kv.at[s, pl.ds(2 * q, 2)], dst_ref=kv.at[other, pl.ds(2 * q, 2)],
            send_sem=kv_ssem.at[q], recv_sem=kv_rsem.at[q], device_id=(other, d, z), device_id_type=MESH,
        ).wait()
        return carry

    lax.fori_loop(0, 4, kv_wait, 0)

    scale = LOG2E * HEAD_DIM ** (-0.5)

    def key_rows(kb):
        return pl.ds(pl.multiple_of((kb // 2) * BLOCK, BLOCK), BLOCK)

    def attend_rows(pair, j, blocks):
        cols = columns(pair, 128)
        rows = slice(j * BLOCK, j * BLOCK + BLOCK)
        q_pair = q_own[pair, rows, :]
        q_half = (q_pair * half0, q_pair * half1)
        t_pre = dot_nt(q_pair, kp[pair]) * scale + pre_mask
        tops = [jnp.where(first, t_pre, NEG_LARGE), jnp.where(first, NEG_LARGE, t_pre)]
        for kb in range(blocks):
            keys = kv[core_of(kb), pair, 0, (kb // 2) * BLOCK : (kb // 2 + 1) * BLOCK, :]
            for h in range(2):
                t = dot_nt(q_half[h], keys) * scale + bias[j, kb]
                ts[h, kb] = t
                tops[h] = jnp.maximum(tops[h], jnp.maximum(t[:, :128], t[:, 128:]))
        highest = [jnp.max(tops[h], axis=1, keepdims=True) for h in range(2)]
        e_pre = jnp.exp2(t_pre - jnp.where(first, highest[0], highest[1]))
        sums = [jnp.where(first, e_pre, 0.0), jnp.where(first, 0.0, e_pre)]
        mixed = [jnp.zeros((BLOCK, 128), jnp.float32) for _ in range(2)]
        for kb in range(blocks):
            values = kv[core_of(kb), pair, 1, (kb // 2) * BLOCK : (kb // 2 + 1) * BLOCK, :]
            for h in range(2):
                e = jnp.exp2(ts[h, kb] - highest[h])
                sums[h] += e[:, :128] + e[:, 128:]
                mixed[h] += dot_nn(e.astype(jnp.bfloat16), values)
        total = [jnp.sum(sums[h], axis=1, keepdims=True) for h in range(2)]
        share = [1.0 / total[h] for h in range(2)]
        p_pre = (e_pre * jnp.where(first, share[0], share[1])).astype(jnp.bfloat16)
        result = jnp.where(first, mixed[0] * share[0], mixed[1] * share[1]) + dot_nn(p_pre, vp[pair])
        o_own[rows, cols] = result.astype(jnp.bfloat16)
        logs = [highest[h] + jnp.log(total[h]) * LOG2E for h in range(2)]
        lse[pair, rows, :] = jnp.where(first, logs[0], logs[1])

    def attend_all():
        for core in range(2):

            @pl.when(s == core)
            def _():
                def attend_pair(pair, carry):
                    relay_while(pair // 2, pair // 2 + pair % 2, early)
                    for j in range(2):
                        attend_rows(pair, j, block_of(core, j) + 1)
                    return carry

                lax.fori_loop(0, 8, attend_pair, 0)

    attend_all()

    def out_project(n, carry):
        cols = columns(n)
        part_sum = jnp.zeros((rows_total, 256), jnp.float32)
        for q in range(4):
            part_sum += dot_nn(o_own[:, q * 256 : q * 256 + 256], wo[q, :, cols])
        after[:, cols] = x_in[:, cols].astype(jnp.float32) + part_sum + vec[0, 2:3, cols]
        return carry

    lax.fori_loop(0, 4, out_project, 0)
    relay_while(4, 5, early)


    def norm_two(rows):
        centred, inverse = standardize(after[rows, :])
        normed[rows, :] = (centred * inverse * vector(3) + vector(4)).astype(jnp.bfloat16)
        acc[rows, :] = after[rows, :] + vector(5)

    over_rows(norm_two)

    def feed_quarter(i, carry):
        q = (z + i) % 4
        relay_while(jnp.where(i == 1, 6, 4 * i + 1), 4 * i + 3, jnp.logical_and(early, i > 0))

        def up(n, carry):
            cols = columns(n)
            inside = jnp.logical_and(n % 2 == 1, jnp.logical_and(i < 3, jnp.logical_or(i > 0, n == 1)))
            step = jnp.where(i == 0, 5, 4 * i + 3 + n // 2)
            relay_while(step, step + 1, jnp.logical_and(early, inside))
            for half in range(2):
                rows = slice(half * BLOCK, half * BLOCK + BLOCK)
                u = dot_nn(normed[rows, :], wud[q, 0:1024, cols]) + vec[q, 6:7, cols]
                u2 = u * u
                t = jnp.tanh(u * (GELU_A + (GELU_A * GELU_B) * u2))
                half_t = 0.5 + 0.5 * t
                wide[rows, cols] = (u * half_t).astype(jnp.bfloat16)
                inner = u * (GELU_A + (3.0 * GELU_A * GELU_B) * u2)
                slope[q, rows, cols] = (half_t + 0.5 * inner * (1.0 - t * t)).astype(jnp.bfloat16)
            return carry

        lax.fori_loop(0, 4, up, 0)

        def down(n, carry):
            cols = columns(n)
            acc[:, cols] += dot_nn(wide[...], wud[q, 1024:2048, cols])
            return carry

        lax.fori_loop(0, 4, down, 0)
        return carry

    lax.fori_loop(0, 4, feed_quarter, 0)
    for k, chip in ((0, 0), (1, 3)):
        send_block(cot_hbm, g_in, g_sem, k, chip, role == 0)

    def give_out(rows):
        y_out[rows, :] = acc[rows, :].astype(jnp.bfloat16)

    def send_rows(j, out, sem):
        block = block_of(s, j)
        rows = slice(j * BLOCK, j * BLOCK + BLOCK)
        sends.start_or_keep(
            y_out.at[rows], out.at[micro], sem.at[micro], (role, d, block),
            jnp.logical_and(role == s, z == block),
        )

    for j in range(2):
        over_rows(give_out, j * chunks // 2, (j + 1) * chunks // 2)
        rows = slice(j * BLOCK, j * BLOCK + BLOCK)
        sends.start(y_out.at[rows], x_in.at[rows], x_sem.at[j], (s, d, partner), when=role == 0)
    for j in range(2):
        send_rows(j, act_out, act_sem)

    for j in range(2):
        arrived(g_in.at[j * BLOCK : (j + 1) * BLOCK], g_sem.at[j])

    def clear(rows):
        acc[rows, :] = jnp.zeros((CHUNK, 1024), jnp.float32)

    over_rows(clear)

    def feed_back(q, carry):
        def down(n, carry):
            cols = columns(n)
            for half in range(2):
                rows = slice(half * BLOCK, half * BLOCK + BLOCK)
                grad_act = dot_nt(g_in[rows, :], wud[q, pl.ds(pl.multiple_of(1024 + n * 256, 256), 256), :])
                wide[rows, cols] = (grad_act * slope[q, rows, cols].astype(jnp.float32)).astype(jnp.bfloat16)
            return carry

        lax.fori_loop(0, 4, down, 0)

        def up(n, carry):
            cols = columns(n)
            acc[:, cols] += dot_nt(wide[...], wud[q, cols, :])
            return carry

        lax.fori_loop(0, 4, up, 0)
        return carry

    lax.fori_loop(0, 4, feed_back, 0)

    def middle(rows):
        dv = norm_back(after[rows, :], vector(3), acc[rows, :])
        normed[rows, :] = (g_in[rows, :].astype(jnp.float32) + dv).astype(jnp.bfloat16)

    over_rows(middle)

    def mix_back(q, carry):
        wide[:, columns(q)] = dot_nt(normed[...], wo[q]).astype(jnp.bfloat16)
        return carry

    lax.fori_loop(0, 4, mix_back, 0)

    def back_pair(pair, carry):
        cols = columns(pair, 128)
        dk_acc[...] = jnp.zeros(dk_acc.shape, jnp.float32)
        dv_acc[...] = jnp.zeros(dv_acc.shape, jnp.float32)
        pk_acc[...] = jnp.zeros(pk_acc.shape, jnp.float32)
        pv_acc[...] = jnp.zeros(pv_acc.shape, jnp.float32)

        def back_rows(j, blocks):
            rows = slice(j * BLOCK, j * BLOCK + BLOCK)
            q_pair = q_own[pair, rows, :]
            q_half = (q_pair * half0, q_pair * half1)
            g_pair = wide[rows, cols]
            g_half = (g_pair * half0, g_pair * half1)
            product = g_pair.astype(jnp.float32) * o_own[rows, cols].astype(jnp.float32)
            row_term = [
                jnp.sum(jnp.where(first, product, 0.0), axis=1, keepdims=True),
                jnp.sum(jnp.where(first, 0.0, product), axis=1, keepdims=True),
            ]
            logs = lse[pair, rows, :]
            log_half = (logs[:, 0:1], logs[:, 64:65])
            p_pre = jnp.exp2(dot_nt(q_pair, kp[pair]) * scale + pre_mask - logs)
            dp_pre = dot_nt(g_pair, vp[pair])
            ds_pre = (p_pre * (dp_pre - jnp.where(first, row_term[0], row_term[1]))).astype(jnp.bfloat16)
            pv_acc[...] += dot_tn(p_pre.astype(jnp.bfloat16), g_pair)
            pk_acc[...] += dot_tn(ds_pre, q_pair)
            dq_pre = dot_nn(ds_pre, kp[pair])
            dqs = [jnp.zeros((BLOCK, 128), jnp.float32) for _ in range(2)]
            for kb in range(blocks):
                keys = kv[core_of(kb), pair, 0, (kb // 2) * BLOCK : (kb // 2 + 1) * BLOCK, :]
                values = kv[core_of(kb), pair, 1, (kb // 2) * BLOCK : (kb // 2 + 1) * BLOCK, :]
                at = slice(kb * BLOCK, kb * BLOCK + BLOCK)
                dv, dk = 0.0, 0.0
                for h in range(2):
                    probs = jnp.exp2(dot_nt(q_half[h], keys) * scale + bias[j, kb] - log_half[h])
                    grad_probs = dot_nt(g_half[h], values)
                    grad_scores = (probs * (grad_probs - row_term[h])).astype(jnp.bfloat16)
                    dv += dot_tn(probs.astype(jnp.bfloat16), g_half[h])
                    dk += dot_tn(grad_scores, q_half[h])
                    dqs[h] += dot_nn(grad_scores, keys)
                dv_acc[at, :] += dv
                dk_acc[at, :] += dk
            dq = (jnp.where(first, dqs[0], dqs[1]) + dq_pre) * HEAD_DIM ** (-0.5)
            q_own[pair, rows, :] = dq.astype(jnp.bfloat16)

        for core in range(2):

            @pl.when(s == core)
            def _():
                for j in range(2):
                    back_rows(j, block_of(core, j) + 1)

        for j in range(2):
            rows = slice(j * BLOCK, j * BLOCK + BLOCK)
            for owner_core, held in ((s, dkv_own), (other, dkv_send)):
                at = pl.ds(pl.multiple_of(block_of(owner_core, j) * BLOCK, BLOCK), BLOCK)
                held[pair, 0, rows, :] = dk_acc[at, :].astype(jnp.bfloat16)
                held[pair, 1, rows, :] = dv_acc[at, :].astype(jnp.bfloat16)
        pltpu.make_async_remote_copy(
            src_ref=dkv_send.at[pair], dst_ref=dkv_recv.at[pair], send_sem=dkv_ssem.at[pair],
            recv_sem=dkv_rsem.at[pair], device_id=(other, d, z), device_id_type=MESH,
        ).start()
        pg[pair, 0] = jnp.where(first16, pk_acc[0:16, :], pk_acc[64:80, :]) * HEAD_DIM ** (-0.5)
        pg[pair, 1] = jnp.where(first16, pv_acc[0:16, :], pv_acc[64:80, :])
        return carry

    lax.fori_loop(0, 8, back_pair, 0)
    contribution = micro * 2 + s
    for q in range(4):
        sends.start_or_keep(
            pg.at[2 * q : 2 * q + 2], pg_near.at[contribution], pg_sem.at[contribution], (role, d, q),
            jnp.logical_and(role == s, z == q),
        )
    over_rows(clear)

    def project_back(q, carry):
        for p in range(2):
            pair = 2 * q + p
            pltpu.make_async_remote_copy(
                src_ref=dkv_send.at[pair], dst_ref=dkv_recv.at[pair], send_sem=dkv_ssem.at[pair],
                recv_sem=dkv_rsem.at[pair], device_id=(other, d, z), device_id_type=MESH,
            ).wait()
            dq = q_own[pair].astype(jnp.float32)
            dk = (dkv_own[pair, 0].astype(jnp.float32) + dkv_recv[pair, 0].astype(jnp.float32)) * HEAD_DIM ** (-0.5)
            dv = dkv_own[pair, 1].astype(jnp.float32) + dkv_recv[pair, 1].astype(jnp.float32)
            dk = pltpu.roll(dk, 64, 1)
            gt[:, p * 384 : p * 384 + 128] = jnp.where(first_all, dq, dk).astype(jnp.bfloat16)
            gt[:, p * 384 + 128 : p * 384 + 256] = jnp.where(first_all, dv, dq).astype(jnp.bfloat16)
            gt[:, p * 384 + 256 : p * 384 + 384] = jnp.where(first_all, dk, dv).astype(jnp.bfloat16)

        def columns_back(n, carry):
            cols = columns(n)
            acc[:, cols] += dot_nt(gt[...], wq[q, cols, :])
            return carry

        lax.fori_loop(0, 4, columns_back, 0)
        return carry

    lax.fori_loop(0, 4, project_back, 0)
    sends.finish()

    def give_back(rows):
        dv = norm_back(x_in[rows, :].astype(jnp.float32), vector(0), acc[rows, :])
        y_out[rows, :] = (normed[rows, :].astype(jnp.float32) + dv).astype(jnp.bfloat16)

    for j in range(2):
        over_rows(give_back, j * chunks // 2, (j + 1) * chunks // 2)
        rows = slice(j * BLOCK, j * BLOCK + BLOCK)
        sends.start(y_out.at[rows], g_in.at[rows], g_sem.at[j], (s, d, partner), when=role == 1)
    for j in range(2):
        send_rows(j, ig_out, ig_sem)
    for k in range(4):
        arrived(pg_near.at[k], pg_sem.at[k])
    pg_far[d] = (pg_near[0] + pg_near[1]) + (pg_near[2] + pg_near[3])
    for k in range(1, 4):
        sends.start(pg_far.at[d], pg_far.at[d], far_sem.at[d], (s, (d + k) % 4, z))
    for k in range(1, 4):
        arrived(pg_far.at[(d + k) % 4], far_sem.at[(d + k) % 4])
    total_pg = (pg_far[0] + pg_far[1]) + (pg_far[2] + pg_far[3])
    for p in range(2):
        keys, values = total_pg[p, 0], total_pg[p, 1]
        sum_out[:, p * 256 : p * 256 + 128] = jnp.where(first16, keys, pltpu.roll(values, 64, 1))
        sum_out[:, p * 256 + 128 : p * 256 + 256] = jnp.where(first16, pltpu.roll(keys, 64, 1), values)
    here = s * 4 + z
    hidden_all[here] = dot_nt(sum_out[...].astype(jnp.bfloat16), pw[...])
    for ds in range(2):
        for dz in range(4):
            if ds or dz:
                sends.start(hidden_all.at[here], hidden_all.at[here], hidden_sem.at[here],
                            ((s + ds) % 2, d, (z + dz) % 4))
    for ds in range(2):
        for dz in range(4):
            if ds or dz:
                there = ((s + ds) % 2) * 4 + (z + dz) % 4
                arrived(hidden_all.at[there], hidden_sem.at[there])
    hidden_sum = hidden_all[0]
    for k in range(1, 8):
        hidden_sum += hidden_all[k]
    hidden_out[...] = hidden_sum

    @pl.when(jnp.logical_not(feeds_zero))
    def _():
        lax.fori_loop(0, 3, supply_done, 0)

    def relays_done(m, carry):
        for stage in range(3):
            relay_copy(m, stage).wait_send()
        return carry

    lax.fori_loop(0, UNITS, relays_done, 0)
    for k in range(2):
        arrived(act_out.at[k], act_sem.at[k])
        arrived(ig_out.at[k], ig_sem.at[k])
    sends.finish()


def run_layers(x, cot, wq, wo, wu, wd, vec, pre, pw, ends):
    bf, f32 = jnp.bfloat16, jnp.float32
    vm, dma = pltpu.VMEM, pltpu.SemaphoreType.DMA
    rows = 2 * BLOCK
    width = x.shape[-1]
    pairs = width // 128
    scratch = [
        vm((4,) + wq.shape, bf), vm((4,) + wo.shape, bf), vm((4, 2 * wu.shape[0], width), bf),
        vm((4,) + vec.shape, f32), vm((4,) + pre.shape, bf),
        vm((rows, width), bf), vm((rows, width), bf), vm((rows, width), bf), vm((rows, width), bf),
        vm((2, pairs, 2, rows, 128), bf), vm((pairs, rows, 128), bf), vm((rows, width), bf),
        vm((pairs, rows, 128), f32), vm((2, 4, BLOCK, BLOCK), f32), vm((rows, width), f32), vm((rows, width), f32),
        vm((4, rows, wu.shape[1]), bf), vm((rows, wu.shape[1]), bf),
        vm((pairs, 2, 16, 128), f32), vm((4, 2, 2, 16, 128), f32), vm((4, 2, 2, 16, 128), f32), vm((8, 16, pw.shape[0]), f32),
        vm((2, 4, BLOCK, BLOCK), f32),
        vm((4 * BLOCK, 128), f32), vm((4 * BLOCK, 128), f32),
        vm((pairs, 2, rows, 128), bf), vm((pairs, 2, rows, 128), bf), vm((pairs, 2, rows, 128), bf),
        vm((pairs, 128, 128), bf), vm((pairs, 128, 128), bf), vm((128, 128), f32), vm((128, 128), f32),
        vm((rows, wq.shape[1]), bf),
        dma((96,)), dma((4,)), dma((4,)), dma((2,)), dma((2,)), dma((2,)), dma((2,)), dma((4,)),
        dma((2, 4)), dma((2, 4)), dma((2, 4)), dma((2, 4)),
        dma((UNITS,)), dma((UNITS,)), dma((UNITS,)), dma((UNITS,)), dma((UNITS, 2)), dma((UNITS,)), dma((UNITS,)), dma((UNITS,)),
        pltpu.SemaphoreType.REGULAR,
        dma((4,)), dma((4,)), dma((pairs,)), dma((pairs,)), dma((4,)), dma((4,)), dma((8,)),
    ]
    anywhere = pl.BlockSpec(memory_space=pl.ANY)
    return pl.pallas_call(
        layer_kernel,
        out_shape=(
            jax.ShapeDtypeStruct(x.shape, bf), jax.ShapeDtypeStruct(x.shape, bf),
            jax.ShapeDtypeStruct((16, pw.shape[1]), f32), jax.ShapeDtypeStruct((16, pw.shape[0]), f32),
        ),
        in_specs=[anywhere] * 8 + [pl.BlockSpec(memory_space=pltpu.VMEM), pl.BlockSpec(memory_space=pltpu.SMEM)],
        out_specs=(anywhere, anywhere, pl.BlockSpec(memory_space=pltpu.VMEM), pl.BlockSpec(memory_space=pltpu.VMEM)),
        scratch_shapes=scratch,
        name="two_layers",
        compiler_params=pltpu.CompilerParams(
            collective_id=0, has_side_effects=True, vmem_limit_bytes=63 * 2**20
        ),
    )(x, cot, wq, wo, wu, wd, vec, pre, pw, ends)


def pair_body(
    layer_input, cotangent, example_lengths, attn_gain, attn_shift, query_key_value_weight, qkv_bias,
    attention_output_weight, out_bias, ffn_gain, ffn_shift, up_projection_weight, up_projection_bias,
    down_projection_weight, down_bias, prefix_table, mid_weight, mid_bias, prefix_weight, prefix_bias,
):
    hidden_pre = jnp.dot(
        prefix_table, mid_weight, preferred_element_type=jnp.float32
    ) + mid_bias.astype(jnp.float32)
    hidden_act = jnp.tanh(hidden_pre)
    hidden_low = hidden_act.astype(jnp.bfloat16)
    prefix_kv = (
        jnp.dot(hidden_low, prefix_weight, preferred_element_type=jnp.float32)
        + prefix_bias.astype(jnp.float32)
    ).astype(jnp.bfloat16)
    pre = jnp.pad(prefix_kv, ((0, 6), (0, 0)))
    pieces = [attn_gain, attn_shift, out_bias, ffn_gain, ffn_shift, down_bias, up_projection_bias, qkv_bias]
    width = layer_input.shape[-1]
    vec = jnp.concatenate(
        [jnp.pad(p.astype(jnp.float32), ((0, 0), (0, width - p.shape[1]))) for p in pieces], axis=0
    )
    ends = jnp.cumsum(example_lengths[:, 0], axis=-1).astype(jnp.int32)
    activations, input_grads, prefix_sum, hidden_grad = run_layers(
        layer_input[:, 0], cotangent[:, 0], query_key_value_weight[0], attention_output_weight[0],
        up_projection_weight[0], down_projection_weight[0], vec, pre, prefix_weight, ends,
    )
    return (activations[None, :, None], input_grads[None, :, None]) + prefix_back(
        prefix_sum[:PREFIX], hidden_grad[:PREFIX], hidden_act, hidden_low, prefix_table, mid_weight
    )


def solution(mesh):
    placed = (
        P(None, "dp", "mp", None),
        P(None, "dp", "mp", None),
        P(None, "dp", None),
        P("section", None),
        P("section", None),
        P("section", None, "mp"),
        P("section", "mp"),
        P("section", "mp", None),
        P("section", None),
        P("section", None),
        P("section", None),
        P("section", None, "mp"),
        P("section", "mp"),
        P("section", "mp", None),
        P("section", None),
        P(),
        P(),
        P(),
        P(None, ("section", "mp")),
        P(("section", "mp")),
    )
    paired = mesh.shape["mp"] == 4 and mesh.shape["dp"] == 4
    return jax.shard_map(
        pair_body if paired else body,
        mesh=mesh,
        in_specs=placed,
        out_specs=(
            P("section", None, "dp", "mp", None),
            P("section", None, "dp", "mp", None),
            P(),
            P(),
            P(),
            P(None, ("section", "mp")),
            P(("section", "mp")),
        ),
        check_vma=False,
    )
```

```python
import jax
import jax.numpy as jnp
from jax import lax
from jax.experimental import pallas as pl
from jax.experimental.pallas import tpu as pltpu
from jax.sharding import PartitionSpec as P

HEAD_DIM = 64
PREFIX = 10
SEQ_LEN = 1024


EPSILON = 1e-05
NEG_LARGE = -1e30
GELU_A = 0.7978845608028654
GELU_B = 0.044715


def norm_rows(values, gain, shift):
    average = jnp.mean(values, axis=-1, keepdims=True)
    centred = values - average
    spread = jnp.mean(centred * centred, axis=-1, keepdims=True)
    return centred * lax.rsqrt(spread + EPSILON) * gain + shift


def norm_input_grad(values, gain, shift, incoming):

    def apply_norm(inputs):
        return norm_rows(inputs, gain, shift)

    norm_value, norm_back = jax.vjp(apply_norm, values)
    return norm_back(incoming)[0]


def gelu_tanh(values):
    return jax.nn.gelu(values, approximate=True)


def visible_of(lengths, first_row, count):
    run_ends = jnp.cumsum(lengths, axis=-1)
    keys_at = jnp.arange(SEQ_LEN, dtype=jnp.int32)
    query_at = first_row + jnp.arange(count, dtype=jnp.int32)
    key_seg = jnp.sum((keys_at[None, :, None] >= run_ends[:, None, :]).astype(jnp.int32), axis=-1)
    query_seg = jnp.sum(
        (query_at[None, :, None] >= run_ends[:, None, :]).astype(jnp.int32), axis=-1
    )
    causal = (query_at[:, None] >= keys_at[None, :])[None]
    inside = (query_seg[:, :, None] == key_seg[:, None, :]) & causal
    leading = jnp.ones((lengths.shape[0], count, PREFIX), dtype=bool)
    return jnp.concatenate([leading, inside], axis=2)


def gather_rows(piece):
    return lax.all_gather(piece, "mp", axis=1, tiled=True)


def reduce_rows(partial_sum):
    return lax.psum_scatter(
        partial_sum.astype(jnp.bfloat16), "mp", scatter_dimension=1, tiled=True
    ).astype(jnp.float32)


def with_prefix(prefix_kv, pair_keys, pair_values, heads_count):
    prefix_pair = prefix_kv.reshape(PREFIX, heads_count, 2, HEAD_DIM)
    key_rows = jnp.concatenate([prefix_pair[None, :, :, 0], pair_keys], axis=1)
    value_rows = jnp.concatenate([prefix_pair[None, :, :, 1], pair_values], axis=1)
    return (key_rows, value_rows)


def attend(query_rows, key_rows, value_rows, visible):
    score_scale = HEAD_DIM ** (-0.5)
    scores = (
        jnp.einsum("sqhd,skhd->shqk", query_rows, key_rows, preferred_element_type=jnp.float32)
        * score_scale
    )
    scores = jnp.where(visible[:, None], scores, NEG_LARGE)
    highest = jnp.max(scores, axis=-1, keepdims=True)
    raised = jnp.exp(scores - highest)
    softmax_probs = raised / jnp.sum(raised, axis=-1, keepdims=True)
    probs_low = softmax_probs.astype(jnp.bfloat16)
    head_mixed_rows = jnp.einsum(
        "shqk,skhd->sqhd", probs_low, value_rows, preferred_element_type=jnp.float32
    )
    batch_size, query_count, heads_count, head_size = head_mixed_rows.shape
    head_mixed_rows = head_mixed_rows.astype(jnp.bfloat16).reshape(
        batch_size, query_count, heads_count * head_size
    )
    return (softmax_probs, probs_low, head_mixed_rows)


def attend_back(grad_mix, query_rows, key_rows, value_rows, softmax_probs, probs_low):
    grad_heads = grad_mix.reshape(query_rows.shape)
    grad_probs = jnp.einsum(
        "sqhd,skhd->shqk", grad_heads, value_rows, preferred_element_type=jnp.float32
    )
    value_grad = jnp.einsum(
        "shqk,sqhd->skhd", probs_low, grad_heads, preferred_element_type=jnp.float32
    )
    row_term = jnp.sum(grad_probs * softmax_probs, axis=-1, keepdims=True)
    grad_scores = (softmax_probs * (grad_probs - row_term)).astype(jnp.bfloat16)
    score_scale = HEAD_DIM ** (-0.5)
    query_grad = (
        jnp.einsum("shqk,skhd->sqhd", grad_scores, key_rows, preferred_element_type=jnp.float32)
        * score_scale
    )
    key_grad = (
        jnp.einsum("shqk,sqhd->skhd", grad_scores, query_rows, preferred_element_type=jnp.float32)
        * score_scale
    )
    return (query_grad, key_grad, value_grad)


def prefix_part(key_grad, value_grad):
    pair_sum = jnp.stack(
        [jnp.sum(key_grad[:, :PREFIX], axis=0), jnp.sum(value_grad[:, :PREFIX], axis=0)], axis=2
    )
    return pair_sum.reshape(PREFIX, -1)


def tensor_forward(own_rows, weights, prefix_kv, visible):
    (
        attn_gain,
        attn_shift,
        query_key_value_weight,
        qkv_bias,
        attention_output_weight,
        out_bias,
        ffn_gain,
        ffn_shift,
        up_projection_weight,
        up_projection_bias,
        down_projection_weight,
        down_bias,
        out_full,
    ) = weights
    normed = norm_rows(own_rows, attn_gain, attn_shift).astype(jnp.bfloat16)
    normalized_input_rows = gather_rows(normed)
    batch_size, seq_len, model_width = normalized_input_rows.shape
    heads_here = query_key_value_weight.shape[1] // (3 * HEAD_DIM)
    projected = (
        jnp.einsum(
            "naj,jk->nak",
            normalized_input_rows,
            query_key_value_weight,
            preferred_element_type=jnp.float32,
        )
        + qkv_bias
    )
    triple = projected.astype(jnp.bfloat16).reshape(batch_size, seq_len, heads_here, 3, HEAD_DIM)
    query_rows = triple[:, :, :, 0]
    key_rows, value_rows = with_prefix(
        prefix_kv, triple[:, :, :, 1], triple[:, :, :, 2], heads_here
    )
    softmax_probs, probs_low, head_mixed_rows = attend(query_rows, key_rows, value_rows, visible)
    attn_part = reduce_rows(
        jnp.einsum(
            "hgm,mt->hgt",
            head_mixed_rows,
            attention_output_weight,
            preferred_element_type=jnp.float32,
        )
    )
    after_attn = own_rows + attn_part + out_bias
    normed_two = norm_rows(after_attn, ffn_gain, ffn_shift).astype(jnp.bfloat16)
    second_norm_rows = gather_rows(normed_two)
    up_pre = (
        jnp.einsum(
            "rmy,yq->rmq",
            second_norm_rows,
            up_projection_weight,
            preferred_element_type=jnp.float32,
        )
        + up_projection_bias
    )
    gelu_output_rows = gelu_tanh(up_pre).astype(jnp.bfloat16)
    mlp_part = reduce_rows(
        jnp.einsum(
            "epj,jq->epq",
            gelu_output_rows,
            down_projection_weight,
            preferred_element_type=jnp.float32,
        )
    )
    result = after_attn + mlp_part + down_bias
    kept_values = (query_rows, key_rows, value_rows, softmax_probs, probs_low, after_attn, up_pre)
    return (result, kept_values)


def tensor_backward(own_rows, arriving, weights, kept_values):
    (
        attn_gain,
        attn_shift,
        query_key_value_weight,
        qkv_bias,
        attention_output_weight,
        out_bias,
        ffn_gain,
        ffn_shift,
        up_projection_weight,
        up_projection_bias,
        down_projection_weight,
        down_bias,
        out_full,
    ) = weights
    query_rows, key_rows, value_rows, softmax_probs, probs_low, after_attn, up_pre = kept_values
    gradient_gathered = gather_rows(arriving)
    gradient_activation = jnp.einsum(
        "bhi,vi->bhv", gradient_gathered, down_projection_weight, preferred_element_type=jnp.float32
    )
    gelu_value, gelu_back = jax.vjp(gelu_tanh, up_pre)
    gradient_up_projection = gelu_back(gradient_activation)[0].astype(jnp.bfloat16)
    grad_two = reduce_rows(
        jnp.einsum(
            "yca,ja->ycj",
            gradient_up_projection,
            up_projection_weight,
            preferred_element_type=jnp.float32,
        )
    )
    grad_after = norm_input_grad(after_attn, ffn_gain, ffn_shift, grad_two)
    grad_mid = (grad_after + arriving.astype(jnp.float32)).astype(jnp.bfloat16)
    middle_gathered = gather_rows(grad_mid)
    grad_mix = jnp.einsum(
        "taq,kq->tak", middle_gathered, attention_output_weight, preferred_element_type=jnp.float32
    ).astype(jnp.bfloat16)
    query_grad, key_grad, value_grad = attend_back(
        grad_mix, query_rows, key_rows, value_rows, softmax_probs, probs_low
    )
    prefix_g = prefix_part(key_grad, value_grad)
    batch_size, seq_len = (query_grad.shape[0], query_grad.shape[1])
    gradient_query_key_value = jnp.stack(
        [query_grad, key_grad[:, PREFIX:], value_grad[:, PREFIX:]], axis=3
    )
    gradient_query_key_value = gradient_query_key_value.astype(jnp.bfloat16).reshape(
        batch_size, seq_len, -1
    )
    grad_one = reduce_rows(
        jnp.einsum(
            "tvq,xq->tvx",
            gradient_query_key_value,
            query_key_value_weight,
            preferred_element_type=jnp.float32,
        )
    )
    grad_input = norm_input_grad(own_rows, attn_gain, attn_shift, grad_one)
    grad_input = (grad_input + grad_mid.astype(jnp.float32)).astype(jnp.bfloat16)
    return (grad_input, prefix_g)


def prefix_back(prefix_sum, hidden_grad, hidden_act, hidden_low, prefix_table, mid_weight):
    prefix_low = prefix_sum.astype(jnp.bfloat16)
    prefix_bias_grad = jnp.sum(prefix_low.astype(jnp.float32), axis=0)
    prefix_weight_grad = jnp.dot(hidden_low.T, prefix_low, preferred_element_type=jnp.float32)
    pre_grad = (hidden_grad * (1.0 - hidden_act * hidden_act)).astype(jnp.bfloat16)
    mid_bias_grad = jnp.sum(pre_grad.astype(jnp.float32), axis=0)
    mid_weight_grad = jnp.dot(prefix_table.T, pre_grad, preferred_element_type=jnp.float32)
    table_grad = jnp.dot(pre_grad, mid_weight.T, preferred_element_type=jnp.float32)
    return (table_grad, mid_weight_grad, mid_bias_grad, prefix_weight_grad, prefix_bias_grad)


def both_layers(piece):
    return lax.all_gather(piece[0], "section", axis=0, tiled=False)


def body(
    layer_input,
    cotangent,
    example_lengths,
    attn_gain,
    attn_shift,
    query_key_value_weight,
    qkv_bias,
    attention_output_weight,
    out_bias,
    ffn_gain,
    ffn_shift,
    up_projection_weight,
    up_projection_bias,
    down_projection_weight,
    down_bias,
    prefix_table,
    mid_weight,
    mid_bias,
    prefix_weight,
    prefix_bias,
):
    layers = lax.axis_size("section")
    section_index = lax.axis_index("section")
    hidden_pre = jnp.dot(
        prefix_table, mid_weight, preferred_element_type=jnp.float32
    ) + mid_bias.astype(jnp.float32)
    hidden_act = jnp.tanh(hidden_pre)
    hidden_low = hidden_act.astype(jnp.bfloat16)
    prefix_kv = (
        jnp.dot(hidden_low, prefix_weight, preferred_element_type=jnp.float32)
        + prefix_bias.astype(jnp.float32)
    ).astype(jnp.bfloat16)
    prefix_all = lax.all_gather(prefix_kv, "section", axis=0, tiled=False)
    floats = [
        both_layers(piece).astype(jnp.float32)
        for piece in (attn_gain, attn_shift, qkv_bias, out_bias, ffn_gain, ffn_shift,
                      up_projection_bias, down_bias)
    ]
    matrices = [
        both_layers(piece)
        for piece in (query_key_value_weight, attention_output_weight,
                      up_projection_weight, down_projection_weight)
    ]

    def weights_of(layer):
        g1, s1, bq, bo, g2, s2, bu, bd = [piece[layer] for piece in floats]
        wq, wo, wu, wd = [piece[layer] for piece in matrices]
        return (g1, s1, wq, bq, wo, bo, g2, s2, wu, bu, wd, bd, wo)

    batch_count = layer_input.shape[0]
    own_input = lax.dynamic_index_in_dim(layer_input, section_index, 0, keepdims=False)
    own_cotangent = lax.dynamic_index_in_dim(cotangent, section_index, 0, keepdims=False)
    lengths = lax.dynamic_index_in_dim(example_lengths, section_index, 0, keepdims=False)
    visible = visible_of(lengths, 0, SEQ_LEN)
    entering = own_input
    entered, produced, kept = [], [], []
    for layer in range(layers):
        entered.append(entering.astype(jnp.float32))
        result, kept_values = tensor_forward(
            entered[layer], weights_of(layer), prefix_all[layer], visible
        )
        entering = result.astype(jnp.bfloat16)
        produced.append(entering)
        kept.append(kept_values)
    gradient = own_cotangent
    sent_grads = [None] * layers
    prefix_parts = [None] * layers
    for layer in reversed(range(layers)):
        gradient, prefix_parts[layer] = tensor_backward(
            entered[layer], gradient, weights_of(layer), kept[layer]
        )
        sent_grads[layer] = gradient
    activations = lax.all_to_all(jnp.stack(produced), "section", 0, 0, tiled=False)
    input_grads = lax.all_to_all(jnp.stack(sent_grads), "section", 0, 0, tiled=False)
    prefix_sum = lax.psum(jnp.stack(prefix_parts), ("dp", "section"))
    prefix_sum = lax.dynamic_index_in_dim(prefix_sum, section_index, 0, keepdims=False)
    hidden_part = jnp.dot(
        prefix_sum.astype(jnp.bfloat16), prefix_weight.T, preferred_element_type=jnp.float32
    )
    hidden_grad = lax.psum(hidden_part, ("section", "mp"))
    return (activations[None], input_grads[None]) + prefix_back(
        prefix_sum, hidden_grad, hidden_act, hidden_low, prefix_table, mid_weight
    )


MESH = pl.DeviceIdType.MESH
BLOCK = 256
LOG2E = 1.4426950408889634
CHUNK = 32
UNITS = 12
AHEAD = 8
UNIT_ROWS = 512
PART_ROWS = UNIT_ROWS // 8


def role_of(z):
    return (((z + 1) // 2) + 1) % 2


def block_of(s, j):
    return j * 3 + s * (1 - 2 * j)


def core_of(block):
    return ((block + 1) // 2) % 2


def guarded(when, action):
    if when is None:
        action()
    else:
        pl.when(when)(action)


def dot_nn(a, b):
    return lax.dot_general(a, b, (((1,), (0,)), ((), ())), preferred_element_type=jnp.float32)


def dot_nt(a, b):
    return lax.dot_general(a, b, (((1,), (1,)), ((), ())), preferred_element_type=jnp.float32)


def dot_tn(a, b):
    return lax.dot_general(a, b, (((0,), (0,)), ((), ())), preferred_element_type=jnp.float32)


class Sends:
    def __init__(self, sems):
        self.sems, self.used, self.pending = sems, 0, []

    def start(self, src, dst, recv_sem, target, when=None):
        copy = pltpu.make_async_remote_copy(
            src_ref=src, dst_ref=dst, send_sem=self.sems.at[self.used], recv_sem=recv_sem,
            device_id=target, device_id_type=MESH,
        )
        self.used += 1
        guarded(when, copy.start)
        self.pending.append((when, copy))

    def start_or_keep(self, src, dst, recv_sem, target, is_here, when=True):
        @pl.when(jnp.logical_and(when, is_here))
        def _():
            pltpu.make_async_copy(src, dst, recv_sem).start()

        self.start(src, dst, recv_sem, target, when=jnp.logical_and(when, jnp.logical_not(is_here)))

    def finish(self):
        for when, copy in self.pending:
            guarded(when, copy.wait_send)
        self.pending = []


def layer_kernel(
    x_hbm, cot_hbm, wq_hbm, wo_hbm, wu_hbm, wd_hbm, vec_hbm, pre_hbm, pw, ends,
    act_out, ig_out, sum_out, hidden_out,
    wq, wo, wud, vec, pre,
    x_in, g_in, y_out, normed, kv, q_own, o_own, lse, bias, after, acc, slope, wide,
    pg, pg_near, pg_far, hidden_all, ts, dkv_own, dkv_send, dkv_recv, kp, vp, gt,
    ssem, vec_sem, pre_sem, x_sem, g_sem, act_sem, ig_sem, own_sem, z_sem, a_sem, b_sem, c_sem,
    zr_sem, ar_sem, br_sem, cr_sem, fs_sem, zs_sem, as_sem, bs_sem, cs_sem, go_sem,
    kv_ssem, kv_rsem, dkv_ssem, dkv_rsem, pg_sem, far_sem, hidden_sem,
    hand_sem, cot_sem,
):
    s, d, z = lax.axis_index("section"), lax.axis_index("dp"), lax.axis_index("mp")
    role, micro = role_of(z), z // 2
    other = 1 - s
    partner = z + 1 - 2 * (z % 2)
    x_near, y_near = d + 1 - 2 * (d % 2), (d + 2) % 4
    near1 = jnp.where(s == 0, x_near, y_near)
    near2 = jnp.where(s == 0, y_near, x_near)
    sends = Sends(ssem)

    barrier = pltpu.get_barrier_semaphore()
    for ds in range(2):
        for dz in range(4):
            if ds or dz:
                pl.semaphore_signal(barrier, inc=1, device_id=((s + ds) % 2, d, (z + dz) % 4), device_id_type=MESH)
    for near in (x_near, y_near, 3 - d):
        pl.semaphore_signal(barrier, inc=1, device_id=(s, near, z), device_id_type=MESH)
    pl.semaphore_wait(barrier, 10)

    def arrived(dst, sem):
        pltpu.make_async_remote_copy(
            src_ref=dst, dst_ref=dst, send_sem=ssem.at[0], recv_sem=sem,
            device_id=(other, d, z), device_id_type=MESH,
        ).wait_recv()

    low_plane, high_plane = jnp.where(s == 0, 1, 0), jnp.where(s == 0, 2, 3)
    planes = (low_plane, high_plane)
    mine = s == core_of(z)
    row_slot = pl.ds(pl.multiple_of((z // 2) * BLOCK, BLOCK), BLOCK)

    def send_block(source, landing, sem, k, chip, when):
        when = jnp.logical_and(mine, when)

        @pl.when(jnp.logical_and(when, z == chip))
        def _():
            pltpu.make_async_copy(source.at[k], landing.at[row_slot], sem.at[z // 2]).start()

        sends.start(source.at[k], landing.at[row_slot], sem.at[z // 2], (s, d, chip),
                    when=jnp.logical_and(when, z != chip))

    def send_small(when):
        for t in planes:
            for h in range(2):
                is_here = jnp.logical_and(z == t, s == h)
                sends.start_or_keep(vec_hbm, vec.at[z], vec_sem.at[z], (h, d, t), is_here, when)
                sends.start_or_keep(pre_hbm, pre.at[z], pre_sem.at[z], (h, d, t), is_here, when)

    def send_x(when):
        for k, chip in ((0, 1), (1, 2)):
            send_block(x_hbm, x_in, x_sem, k, chip, when)

    toward = jnp.where(z < 2, 1, -1)

    def quarter(i):
        return (z + 4 + toward * i) % 4

    def taker(i):
        low, high = (z + 3 - i) % 4, (z + 1 + i) % 4
        return jnp.where(low == low_plane, low, high), jnp.logical_or(low == low_plane, high == high_plane)

    swapped = (d % 2) * 2 + d // 2
    place = jnp.where(s == 0, d, swapped)
    pair_start = (place // 2) * 2
    far_start = 2 - pair_start
    firsts = ((wq_hbm, wq), (wo_hbm, wo))

    def eighths(rows, start, count, h):
        return pl.ds(pl.multiple_of((start + 4 * h) * rows, rows), rows * count)

    def supply_first(w, i, then):
        t, taken = taker(i)
        held, full = firsts[w]

        @pl.when(taken)
        def _():
            for h in range(2):
                at = eighths(held.shape[0] // 8, swapped if h else d, 1, h)
                then(pltpu.make_async_remote_copy(
                    src_ref=held.at[at], dst_ref=full.at[z, at], send_sem=fs_sem.at[3 * w + i, h],
                    recv_sem=z_sem.at[w, z], device_id=(h, d, t), device_id_type=MESH,
                ))

    def supply_firsts(when, w):
        @pl.when(when)
        def _():
            def one(i, carry):
                supply_first(w, i, lambda copy: copy.start())
                return carry

            lax.fori_loop(0, 3, one, 0)

    def supply_firsts_paced(when, w):
        @pl.when(when)
        def _():
            def one(i, carry):
                supply_first(w, i, lambda copy: copy.start())
                supply_first(w, i, lambda copy: copy.wait_send())
                return carry

            lax.fori_loop(0, 3, one, 0)

    def supply_copies(i, c, then):
        t, taken = taker(i)
        held, base = ((wu_hbm, 0), (wd_hbm, 1024))[c // 2]

        @pl.when(taken)
        def _():
            for h in range(2):
                at = eighths(PART_ROWS, swapped if h else d, 1, h)
                start = (c % 2) * UNIT_ROWS + at.start
                then(pltpu.make_async_remote_copy(
                    src_ref=held.at[pl.ds(pl.multiple_of(start, PART_ROWS), PART_ROWS)],
                    dst_ref=wud.at[z, pl.ds(pl.multiple_of(base + start, PART_ROWS), PART_ROWS)],
                    send_sem=zs_sem.at[4 * i + c, h], recv_sem=zr_sem.at[4 * i + c],
                    device_id=(h, d, t), device_id_type=MESH,
                ))

    def supply_all(i, carry):
        for c in range(4):
            supply_copies(i, c, lambda copy: copy.start())
        return carry

    def supply_done(i, carry):
        for c in range(4):
            supply_copies(i, c, lambda copy: copy.wait_send())
        return carry

    def supply_paced(i, carry):
        for c in range(4):
            supply_copies(i, c, lambda copy: copy.start())
            if c:
                supply_copies(i, c - 1, lambda copy: copy.wait_send())
        supply_copies(i, 3, lambda copy: copy.wait_send())
        return carry

    feeds_zero = jnp.logical_and(role == 1, s == 0)
    feeds_zero_late = jnp.logical_and(role == 0, s == 0)
    feeds_one = jnp.logical_and(role == 0, s == 1)
    feeds_one_late = jnp.logical_and(role == 1, s == 1)
    supply_firsts(feeds_zero_late, 0)
    supply_firsts_paced(feeds_zero, 0)
    send_x(feeds_zero)
    send_small(feeds_zero)
    supply_firsts_paced(feeds_zero, 1)
    owned = ((wq_hbm, wq.at[z]), (wo_hbm, wo.at[z]), (wu_hbm, wud.at[z, 0:1024]), (wd_hbm, wud.at[z, 1024:2048]))
    for w, (held, full) in enumerate(owned):
        @pl.when(role == s)
        def _():
            pltpu.make_async_copy(held, full, own_sem.at[w]).start()

        sends.start(held, full, own_sem.at[w], (other, d, z), when=role == s)

    @pl.when(feeds_zero)
    def _():
        lax.fori_loop(0, 3, supply_paced, 0)

    @pl.when(feeds_one_late)
    def _():
        pl.semaphore_wait(go_sem, 1)

    send_small(feeds_one_late)
    supply_firsts(feeds_one_late, 0)
    supply_firsts(feeds_one_late, 1)

    first_units = [(w, i) for w in (0, 1) for i in range(1, 4)]

    def first_piece(w, i, start, count):
        full = firsts[w][1]
        return full.at[quarter(i), eighths(full.shape[1] // 8, start, count, s)]

    def relay_first(step):
        stages = [first_units[step - k] if 0 <= step - k < len(first_units) else None for k in range(4)]
        if stages[0]:
            w, i = stages[0]
            q = quarter(i)
            arrived(first_piece(w, i, place, 1), z_sem.at[w, q])
            sends.start(first_piece(w, i, place, 1), first_piece(w, i, place, 1), a_sem.at[w, q], (s, near1, z))
        if stages[1]:
            w, i = stages[1]
            q = quarter(i)
            arrived(first_piece(w, i, pair_start + 1 - place % 2, 1), a_sem.at[w, q])
            sends.start(first_piece(w, i, pair_start, 2), first_piece(w, i, pair_start, 2), b_sem.at[w, q], (s, near2, z))
        if stages[2]:
            w, i = stages[2]
            q = quarter(i)
            arrived(first_piece(w, i, far_start, 2), b_sem.at[w, q])
            sends.start(first_piece(w, i, 0, 4), first_piece(w, i, 0, 4), c_sem.at[w, q], (other, d, z))
        if stages[3]:
            w, i = stages[3]
            full = firsts[w][1]
            arrived(full.at[quarter(i), eighths(full.shape[1] // 8, 0, 4, other)], c_sem.at[w, quarter(i)])

    for step in range(len(first_units) + 3):
        relay_first(step)
        if step == 0:
            send_x(role == 0)
            send_small(feeds_zero_late)
            supply_firsts(feeds_zero_late, 1)
        if step == 3:
            @pl.when(feeds_one)
            def _():
                pl.semaphore_signal(go_sem, inc=1, device_id=(1, d, partner), device_id_type=MESH)

            supply_firsts(feeds_one, 0)
        if step == 6:
            send_small(feeds_one)
            supply_firsts(feeds_one, 1)

        @pl.when(feeds_zero_late)
        def _():
            if 1 <= step < 5:
                supply_copies(0, step - 1, lambda copy: copy.start())

    @pl.when(feeds_one_late)
    def _():
        lax.fori_loop(0, 3, supply_all, 0)

    def unit_piece(m, start, count, h):
        q = quarter(1 + m // 4)
        first_row = (m % 4) * UNIT_ROWS + (start + 4 * h) * PART_ROWS
        return wud.at[q, pl.ds(pl.multiple_of(first_row, PART_ROWS), PART_ROWS * count)]

    def relay_copy(m, stage):
        start, count = ((place, 1), (pair_start, 2), (0, 4))[stage]
        at = unit_piece(m, start, count, s)
        return pltpu.make_async_remote_copy(
            src_ref=at, dst_ref=at, send_sem=(as_sem, bs_sem, cs_sem)[stage].at[m],
            recv_sem=(ar_sem, br_sem, cr_sem)[stage].at[m],
            device_id=((s, near1, z), (s, near2, z), (other, d, z))[stage], device_id_type=MESH,
        )

    def relay(n):
        for c in range(4):

            @pl.when(jnp.logical_and(feeds_one, jnp.logical_and(n < UNITS, n % 4 == c)))
            def _():
                supply_copies(n // 4, c, lambda copy: copy.start())

        for k in range(4):
            m = n - k

            @pl.when(jnp.logical_and(m >= 0, m < UNITS))
            def _():
                if k == 0:
                    arrived(unit_piece(m, place, 1, s), zr_sem.at[m])
                if k == 1:
                    arrived(unit_piece(m, pair_start + 1 - place % 2, 1, s), ar_sem.at[m])
                if k == 2:
                    arrived(unit_piece(m, far_start, 2, s), br_sem.at[m])
                if k == 3:
                    arrived(unit_piece(m, 0, 4, other), cr_sem.at[m])
                if k < 3:
                    relay_copy(m, k).start()

    def cot_copies(then):
        for k, chip in ((0, 0), (1, 3)):

            @pl.when(jnp.logical_and(mine, z != chip))
            def _():
                then(pltpu.make_async_remote_copy(
                    src_ref=cot_hbm.at[k], dst_ref=g_in.at[row_slot], send_sem=cot_sem.at[k],
                    recv_sem=g_sem.at[z // 2], device_id=(s, d, chip), device_id_type=MESH,
                ))

    for k, chip in ((0, 0), (1, 3)):

        @pl.when(jnp.logical_and(mine, z == chip))
        def _():
            pltpu.make_async_copy(cot_hbm.at[k], g_in.at[row_slot], g_sem.at[z // 2]).start()

    @pl.when(role == 1)
    def _():
        cot_copies(lambda copy: copy.start())
    def relay_steps(start, stop):
        def one(n, carry):
            relay(n)
            return carry

        lax.fori_loop(start, stop, one, 0)

    relay_steps(0, jnp.where(role == 1, AHEAD, 0))
    arrived(wq.at[z], own_sem.at[0])
    arrived(wo.at[z], own_sem.at[1])
    arrived(wud.at[z, 0:1024], own_sem.at[2])
    arrived(wud.at[z, 1024:2048], own_sem.at[3])
    for q in range(4):
        arrived(vec.at[q], vec_sem.at[q])
        arrived(pre.at[q], pre_sem.at[q])

    first16 = lax.broadcasted_iota(jnp.int32, (16, 128), 1) < HEAD_DIM
    first = lax.broadcasted_iota(jnp.int32, (BLOCK, 128), 1) < HEAD_DIM
    lane = lax.broadcasted_iota(jnp.int32, (1, 128), 1)
    half0 = jnp.where(lane < HEAD_DIM, 1.0, 0.0).astype(jnp.bfloat16)
    half1 = jnp.where(lane < HEAD_DIM, 0.0, 1.0).astype(jnp.bfloat16)
    pre_mask = jnp.where(lane % HEAD_DIM < PREFIX, 0.0, NEG_LARGE)
    kp[...] = jnp.zeros(kp.shape, kp.dtype)
    vp[...] = jnp.zeros(vp.shape, vp.dtype)
    for q in range(4):
        for p in range(2):
            t0 = pre[q, :, p * 256 : p * 256 + 128].astype(jnp.float32)
            t1 = pre[q, :, p * 256 + 128 : p * 256 + 256].astype(jnp.float32)
            kp[2 * q + p, 0:16, :] = jnp.where(first16, t0, 0.0).astype(jnp.bfloat16)
            kp[2 * q + p, 64:80, :] = jnp.where(first16, 0.0, pltpu.roll(t1, 64, 1)).astype(jnp.bfloat16)
            vp[2 * q + p, 0:16, :] = jnp.where(first16, pltpu.roll(t0, 64, 1), 0.0).astype(jnp.bfloat16)
            vp[2 * q + p, 64:80, :] = jnp.where(first16, 0.0, t1).astype(jnp.bfloat16)

    for j in range(2):
        row0 = block_of(s, j) * BLOCK
        row_at = row0 + lax.broadcasted_iota(jnp.int32, (BLOCK, 1), 0)
        begin = jnp.zeros((BLOCK, 1), jnp.int32)
        for e in range(ends.shape[1]):
            begin = jnp.where(row_at >= ends[micro, e], ends[micro, e], begin)

        def mask_block(kb, carry):
            key_at = kb * BLOCK + lax.broadcasted_iota(jnp.int32, (BLOCK, BLOCK), 1)
            keep = jnp.logical_and(key_at <= row_at, key_at >= begin)
            bias[j, kb] = jnp.where(keep, 0.0, NEG_LARGE)
            return carry

        lax.fori_loop(0, 4, mask_block, 0)

    def vector(k, q=0, width=1024):
        return vec[q, k : k + 1, 0:width]

    def columns(n, width):
        return pl.ds(pl.multiple_of(n * width, width), width)

    def block_rows(j):
        return pl.ds(pl.multiple_of(j * BLOCK, BLOCK), BLOCK)

    def over_rows(j, action):
        def one(c, carry):
            action(pl.ds(pl.multiple_of(j * BLOCK + c * CHUNK, CHUNK), CHUNK))
            return carry

        lax.fori_loop(0, BLOCK // CHUNK, one, 0)

    def standardize(v):
        average = jnp.mean(v, axis=-1, keepdims=True)
        centred = v - average
        spread = jnp.mean(centred * centred, axis=-1, keepdims=True)
        return centred, lax.rsqrt(spread + EPSILON)

    def norm_back(v, gain, incoming):
        centred, inverse = standardize(v)
        xhat = centred * inverse
        e = incoming * gain
        return (e - jnp.mean(e, axis=-1, keepdims=True) - xhat * jnp.mean(e * xhat, axis=-1, keepdims=True)) * inverse

    def to_core(ref, send_sem, recv_sem):
        return pltpu.make_async_remote_copy(
            src_ref=ref, dst_ref=ref, send_sem=send_sem, recv_sem=recv_sem,
            device_id=(other, d, z), device_id_type=MESH,
        )

    scale = LOG2E * HEAD_DIM ** (-0.5)

    def enter(j):
        rows = block_rows(j)
        arrived(x_in.at[rows], x_sem.at[j])

        def norm_one(rows):
            centred, inverse = standardize(x_in[rows, :].astype(jnp.float32))
            normed[rows, :] = (centred * inverse * vector(0) + vector(1)).astype(jnp.bfloat16)

        over_rows(j, norm_one)

        def project(q, carry):
            triple = dot_nn(normed[rows, :], wq[q]) + vec[q, 7:8, 0:768]
            for p in range(2):
                t0, t1, t2 = (triple[:, p * 384 + n * 128 : p * 384 + n * 128 + 128] for n in range(3))
                q_own[2 * q + p, rows, :] = jnp.where(first, t0, t1).astype(jnp.bfloat16)
                kv[s, 2 * q + p, 0, rows, :] = pltpu.roll(jnp.where(first, t2, t0), 64, 1).astype(jnp.bfloat16)
                kv[s, 2 * q + p, 1, rows, :] = jnp.where(first, t1, t2).astype(jnp.bfloat16)
            to_core(kv.at[s, pl.ds(2 * q, 2), :, rows], kv_ssem.at[j, q], kv_rsem.at[j, q]).start()
            return carry

        lax.fori_loop(0, 4, project, 0)

    def attend_rows(pair, core, j):
        cols = columns(pair, 128)
        rows = slice(j * BLOCK, j * BLOCK + BLOCK)
        blocks = block_of(core, j) + 1
        q_pair = q_own[pair, rows, :]
        q_half = (q_pair * half0, q_pair * half1)
        t_pre = dot_nt(q_pair, kp[pair]) * scale + pre_mask
        tops = [jnp.where(first, t_pre, NEG_LARGE), jnp.where(first, NEG_LARGE, t_pre)]
        for kb in range(blocks):
            keys = kv[core_of(kb), pair, 0, (kb // 2) * BLOCK : (kb // 2 + 1) * BLOCK, :]
            for h in range(2):
                t = dot_nt(q_half[h], keys) * scale + bias[j, kb]
                ts[h, kb] = t
                tops[h] = jnp.maximum(tops[h], jnp.maximum(t[:, :128], t[:, 128:]))
        highest = [jnp.max(tops[h], axis=1, keepdims=True) for h in range(2)]
        e_pre = jnp.exp2(t_pre - jnp.where(first, highest[0], highest[1]))
        sums = [jnp.where(first, e_pre, 0.0), jnp.where(first, 0.0, e_pre)]
        mixed = [jnp.zeros((BLOCK, 128), jnp.float32) for _ in range(2)]
        for kb in range(blocks):
            values = kv[core_of(kb), pair, 1, (kb // 2) * BLOCK : (kb // 2 + 1) * BLOCK, :]
            for h in range(2):
                e = jnp.exp2(ts[h, kb] - highest[h])
                sums[h] += e[:, :128] + e[:, 128:]
                mixed[h] += dot_nn(e.astype(jnp.bfloat16), values)
        total = [jnp.sum(sums[h], axis=1, keepdims=True) for h in range(2)]
        share = [1.0 / total[h] for h in range(2)]
        p_pre = (e_pre * jnp.where(first, share[0], share[1])).astype(jnp.bfloat16)
        result = jnp.where(first, mixed[0] * share[0], mixed[1] * share[1]) + dot_nn(p_pre, vp[pair])
        o_own[rows, cols] = result.astype(jnp.bfloat16)
        logs = [highest[h] + jnp.log(total[h]) * LOG2E for h in range(2)]
        lse[pair, rows, :] = jnp.where(first, logs[0], logs[1])

    def attend(j, relay_at):
        def kv_wait(q, carry):
            to_core(kv.at[s, pl.ds(2 * q, 2), :, block_rows(j)], kv_ssem.at[j, q], kv_rsem.at[j, q]).wait_send()
            arrived(kv.at[other, pl.ds(2 * q, 2), :, block_rows(j)], kv_rsem.at[j, q])
            return carry

        lax.fori_loop(0, 4, kv_wait, 0)
        for core in range(2):
            for block in range(2):

                @pl.when(jnp.logical_and(s == core, j == block))
                def _():
                    def attend_pair(pair, carry):
                        relay_steps(relay_at, jnp.where(jnp.logical_and(pair == 4, role == 0), relay_at + 1, relay_at))
                        attend_rows(pair, core, block)
                        return carry

                    lax.fori_loop(0, 8, attend_pair, 0)

        rows = block_rows(j)
        after[rows, :] = (
            x_in[rows, :].astype(jnp.float32) + dot_nn(o_own[rows, :], wo[...].reshape(1024, 1024)) + vector(2)
        )

        def norm_two(rows):
            centred, inverse = standardize(after[rows, :])
            normed[rows, :] = (centred * inverse * vector(3) + vector(4)).astype(jnp.bfloat16)
            acc[rows, :] = after[rows, :] + vector(5)

        over_rows(j, norm_two)

    def feed(j, i):
        rows = block_rows(j)
        q = quarter(i)
        u = dot_nn(normed[rows, :], wud[q, 0:1024, :]) + vec[q, 6:7, :]
        u2 = u * u
        t = jnp.tanh(u * (GELU_A + (GELU_A * GELU_B) * u2))
        half_t = 0.5 + 0.5 * t
        wide[rows, :] = (u * half_t).astype(jnp.bfloat16)
        inner = u * (GELU_A + (3.0 * GELU_A * GELU_B) * u2)
        slope[q, rows, :] = (half_t + 0.5 * inner * (1.0 - t * t)).astype(jnp.bfloat16)
        acc[rows, :] += dot_nn(wide[rows, :], wud[q, 1024:2048, :])

    def hand_copies(j, k):
        rows = block_rows(j)
        landing, sem = ((x_in, x_sem), (act_out, act_sem), (g_in, g_sem), (ig_out, ig_sem))[k]
        if k % 2:
            dst, sem, target = landing.at[micro], sem.at[micro], (role, d, block_of(s, j))
        else:
            dst, sem, target = landing.at[rows], sem.at[j], (s, d, partner)
        return pltpu.make_async_remote_copy(
            src_ref=y_out.at[rows], dst_ref=dst, send_sem=hand_sem.at[k, j], recv_sem=sem,
            device_id=target, device_id_type=MESH,
        )

    def hand_on(j):
        rows = block_rows(j)
        y_out[rows, :] = acc[rows, :].astype(jnp.bfloat16)

        @pl.when(role == 0)
        def _():
            hand_copies(j, 0).start()

        hand_copies(j, 1).start()

    def upto(n, table):
        total = jnp.int32(0)
        for k, entry in enumerate(table):
            total += jnp.where(n >= k, entry - (table[k - 1] if k else 0), 0)
        return total

    early_table = (0, 1, 2, 4, 6, 7, 8, 9, 11, 13, 15, 15, 15, 15)
    late_table = (AHEAD, 9, 10, 11, 13, 15, 15, 15, 15, 15, 15, 15, 15, 15)

    def forward(n, carry):
        stage = jnp.where(role == 0, n // 2, n % 7)
        j = jnp.where(role == 0, n % 2, n // 7)
        before = jnp.where(
            role == 0,
            jnp.where(n == 0, 0, upto(n - 1, early_table)) + jnp.where(jnp.logical_or(n == 3, n == 4), 1, 0),
            jnp.where(n == 0, AHEAD, upto(n - 1, late_table)),
        )
        until = jnp.where(role == 0, upto(n, early_table), upto(n, late_table))
        relay_steps(before, until)

        @pl.when(jnp.logical_and(role == 0, n == 6))
        def _():
            cot_copies(lambda copy: copy.start())

        @pl.when(stage == 0)
        def _():
            enter(j)

        @pl.when(stage == 1)
        def _():
            attend(j, until)

        @pl.when(jnp.logical_and(stage >= 2, stage < 6))
        def _():
            feed(j, stage - 2)

        @pl.when(stage == 6)
        def _():
            hand_on(j)

        return carry

    lax.fori_loop(0, 14, forward, 0)

    def back_rows(pair, core, j):
        cols = columns(pair, 128)
        rows = slice(j * BLOCK, j * BLOCK + BLOCK)
        q_pair = q_own[pair, rows, :]
        q_half = (q_pair * half0, q_pair * half1)
        g_pair = wide[rows, cols]
        g_half = (g_pair * half0, g_pair * half1)
        product = g_pair.astype(jnp.float32) * o_own[rows, cols].astype(jnp.float32)
        row_term = [
            jnp.sum(jnp.where(first, product, 0.0), axis=1, keepdims=True),
            jnp.sum(jnp.where(first, 0.0, product), axis=1, keepdims=True),
        ]
        logs = lse[pair, rows, :]
        log_half = (logs[:, 0:1], logs[:, 64:65])
        p_pre = jnp.exp2(dot_nt(q_pair, kp[pair]) * scale + pre_mask - logs)
        dp_pre = dot_nt(g_pair, vp[pair])
        ds_pre = (p_pre * (dp_pre - jnp.where(first, row_term[0], row_term[1]))).astype(jnp.bfloat16)
        pv = dot_tn(p_pre.astype(jnp.bfloat16), g_pair)
        pk = dot_tn(ds_pre, q_pair)
        pk = jnp.where(first16, pk[0:16, :], pk[64:80, :]) * HEAD_DIM ** (-0.5)
        pv = jnp.where(first16, pv[0:16, :], pv[64:80, :])
        pg[pair, 0] = pk if j else pg[pair, 0] + pk
        pg[pair, 1] = pv if j else pg[pair, 1] + pv
        dq_pre = dot_nn(ds_pre, kp[pair])
        dqs = [jnp.zeros((BLOCK, 128), jnp.float32) for _ in range(2)]
        for kb in range(4):
            held = dkv_own if core_of(kb) == core else dkv_send
            at = slice((kb // 2) * BLOCK, (kb // 2 + 1) * BLOCK)
            if kb > block_of(core, j):
                if j:
                    held[pair, 0, at, :] = jnp.zeros((BLOCK, 128), jnp.bfloat16)
                    held[pair, 1, at, :] = jnp.zeros((BLOCK, 128), jnp.bfloat16)
                continue
            keys = kv[core_of(kb), pair, 0, at, :]
            values = kv[core_of(kb), pair, 1, at, :]
            dv, dk = 0.0, 0.0
            if j == 0:
                dk = held[pair, 0, at, :].astype(jnp.float32)
                dv = held[pair, 1, at, :].astype(jnp.float32)
            for h in range(2):
                probs = jnp.exp2(dot_nt(q_half[h], keys) * scale + bias[j, kb] - log_half[h])
                grad_probs = dot_nt(g_half[h], values)
                grad_scores = (probs * (grad_probs - row_term[h])).astype(jnp.bfloat16)
                dv += dot_tn(probs.astype(jnp.bfloat16), g_half[h])
                dk += dot_tn(grad_scores, q_half[h])
                dqs[h] += dot_nn(grad_scores, keys)
            held[pair, 0, at, :] = dk.astype(jnp.bfloat16)
            held[pair, 1, at, :] = dv.astype(jnp.bfloat16)
        dq = (jnp.where(first, dqs[0], dqs[1]) + dq_pre) * HEAD_DIM ** (-0.5)
        q_own[pair, rows, :] = dq.astype(jnp.bfloat16)

    def dkv_copy(j, pair):
        rows = block_rows(j)
        return pltpu.make_async_remote_copy(
            src_ref=dkv_send.at[pair, :, rows], dst_ref=dkv_recv.at[pair, :, rows],
            send_sem=dkv_ssem.at[j, pair], recv_sem=dkv_rsem.at[j, pair],
            device_id=(other, d, z), device_id_type=MESH,
        )

    contribution = micro * 2 + s

    def backward(n, carry):
        j = 1 - n
        rows = block_rows(j)
        arrived(g_in.at[rows], g_sem.at[j])
        acc[rows, :] = jnp.zeros((BLOCK, 1024), jnp.float32)

        def feed_back(q, carry):
            grad_act = dot_nt(g_in[rows, :], wud[q, 1024:2048, :])
            wide[rows, :] = (grad_act * slope[q, rows, :].astype(jnp.float32)).astype(jnp.bfloat16)
            acc[rows, :] += dot_nt(wide[rows, :], wud[q, 0:1024, :])
            return carry

        lax.fori_loop(0, 4, feed_back, 0)

        def middle(rows):
            dv = norm_back(after[rows, :], vector(3), acc[rows, :])
            normed[rows, :] = (g_in[rows, :].astype(jnp.float32) + dv).astype(jnp.bfloat16)

        over_rows(j, middle)
        wide[rows, :] = dot_nt(normed[rows, :], wo[...].reshape(1024, 1024)).astype(jnp.bfloat16)
        for core in range(2):
            for block in range(2):

                @pl.when(jnp.logical_and(s == core, j == block))
                def _():
                    def back_pair(pair, carry):
                        back_rows(pair, core, block)
                        dkv_copy(block, pair).start()
                        return carry

                    lax.fori_loop(0, 8, back_pair, 0)

        acc[rows, :] = jnp.zeros((BLOCK, 1024), jnp.float32)

        def project_back(q, carry):
            for p in range(2):
                pair = 2 * q + p
                dkv_copy(j, pair).wait()
                dq = q_own[pair, rows, :].astype(jnp.float32)
                dk = dkv_own[pair, 0, rows, :].astype(jnp.float32) + dkv_recv[pair, 0, rows, :].astype(jnp.float32)
                dv = dkv_own[pair, 1, rows, :].astype(jnp.float32) + dkv_recv[pair, 1, rows, :].astype(jnp.float32)
                dk = pltpu.roll(dk * HEAD_DIM ** (-0.5), 64, 1)
                gt[:, p * 384 : p * 384 + 128] = jnp.where(first, dq, dk).astype(jnp.bfloat16)
                gt[:, p * 384 + 128 : p * 384 + 256] = jnp.where(first, dv, dq).astype(jnp.bfloat16)
                gt[:, p * 384 + 256 : p * 384 + 384] = jnp.where(first, dk, dv).astype(jnp.bfloat16)
            acc[rows, :] += dot_nt(gt[...], wq[q])
            return carry

        lax.fori_loop(0, 4, project_back, 0)

        @pl.when(role == 0)
        def _():
            hand_copies(j, 0).wait_send()

        hand_copies(j, 1).wait_send()

        def give_back(rows):
            dv = norm_back(x_in[rows, :].astype(jnp.float32), vector(0), acc[rows, :])
            y_out[rows, :] = (normed[rows, :].astype(jnp.float32) + dv).astype(jnp.bfloat16)

        over_rows(j, give_back)

        @pl.when(role == 1)
        def _():
            hand_copies(j, 2).start()

        hand_copies(j, 3).start()
        return carry

    lax.fori_loop(0, 2, backward, 0)
    for q in range(4):
        sends.start_or_keep(
            pg.at[2 * q : 2 * q + 2], pg_near.at[contribution], pg_sem.at[contribution], (role, d, q),
            jnp.logical_and(role == s, z == q),
        )

    for k in range(4):
        arrived(pg_near.at[k], pg_sem.at[k])
    pg_far[d] = (pg_near[0] + pg_near[1]) + (pg_near[2] + pg_near[3])
    for k in range(1, 4):
        sends.start(pg_far.at[d], pg_far.at[d], far_sem.at[d], (s, (d + k) % 4, z))
    for k in range(1, 4):
        arrived(pg_far.at[(d + k) % 4], far_sem.at[(d + k) % 4])
    total_pg = (pg_far[0] + pg_far[1]) + (pg_far[2] + pg_far[3])
    for p in range(2):
        keys, values = total_pg[p, 0], total_pg[p, 1]
        sum_out[:, p * 256 : p * 256 + 128] = jnp.where(first16, keys, pltpu.roll(values, 64, 1))
        sum_out[:, p * 256 + 128 : p * 256 + 256] = jnp.where(first16, pltpu.roll(keys, 64, 1), values)
    here = s * 4 + z
    hidden_all[here] = dot_nt(sum_out[...].astype(jnp.bfloat16), pw[...])
    for ds in range(2):
        for dz in range(4):
            if ds or dz:
                sends.start(hidden_all.at[here], hidden_all.at[here], hidden_sem.at[here],
                            ((s + ds) % 2, d, (z + dz) % 4))
    for ds in range(2):
        for dz in range(4):
            if ds or dz:
                there = ((s + ds) % 2) * 4 + (z + dz) % 4
                arrived(hidden_all.at[there], hidden_sem.at[there])
    hidden_sum = hidden_all[0]
    for k in range(1, 8):
        hidden_sum += hidden_all[k]
    hidden_out[...] = hidden_sum

    @pl.when(jnp.logical_not(feeds_zero))
    def _():
        lax.fori_loop(0, 3, supply_done, 0)

        def firsts_done(i, carry):
            for w in range(2):
                supply_first(w, i, lambda copy: copy.wait_send())
            return carry

        lax.fori_loop(0, 3, firsts_done, 0)

    def relays_done(m, carry):
        for stage in range(3):
            relay_copy(m, stage).wait_send()
        return carry

    lax.fori_loop(0, UNITS, relays_done, 0)
    cot_copies(lambda copy: copy.wait_send())
    for j in range(2):

        @pl.when(role == 1)
        def _():
            hand_copies(j, 2).wait_send()

        hand_copies(j, 3).wait_send()

    for k in range(2):
        arrived(act_out.at[k], act_sem.at[k])
        arrived(ig_out.at[k], ig_sem.at[k])
    sends.finish()


def run_layers(x, cot, wq, wo, wu, wd, vec, pre, pw, ends):
    bf, f32 = jnp.bfloat16, jnp.float32
    vm, dma = pltpu.VMEM, pltpu.SemaphoreType.DMA
    rows = 2 * BLOCK
    width = x.shape[-1]
    pairs = width // 128
    scratch = [
        vm((4,) + wq.shape, bf), vm((4,) + wo.shape, bf), vm((4, 2 * wu.shape[0], width), bf),
        vm((4,) + vec.shape, f32), vm((4,) + pre.shape, bf),
        vm((rows, width), bf), vm((rows, width), bf), vm((rows, width), bf), vm((rows, width), bf),
        vm((2, pairs, 2, rows, 128), bf), vm((pairs, rows, 128), bf), vm((rows, width), bf),
        vm((pairs, rows, 128), f32), vm((2, 4, BLOCK, BLOCK), f32), vm((rows, width), f32), vm((rows, width), f32),
        vm((4, rows, wu.shape[1]), bf), vm((rows, wu.shape[1]), bf),
        vm((pairs, 2, 16, 128), f32), vm((4, 2, 2, 16, 128), f32), vm((4, 2, 2, 16, 128), f32), vm((8, 16, pw.shape[0]), f32),
        vm((2, 4, BLOCK, BLOCK), f32),
        vm((pairs, 2, rows, 128), bf), vm((pairs, 2, rows, 128), bf), vm((pairs, 2, rows, 128), bf),
        vm((pairs, 128, 128), bf), vm((pairs, 128, 128), bf),
        vm((BLOCK, wq.shape[1]), bf),
        dma((96,)), dma((4,)), dma((4,)), dma((2,)), dma((2,)), dma((2,)), dma((2,)), dma((4,)),
        dma((2, 4)), dma((2, 4)), dma((2, 4)), dma((2, 4)),
        dma((UNITS,)), dma((UNITS,)), dma((UNITS,)), dma((UNITS,)), dma((6, 2)), dma((UNITS, 2)), dma((UNITS,)), dma((UNITS,)), dma((UNITS,)),
        pltpu.SemaphoreType.REGULAR,
        dma((2, 4)), dma((2, 4)), dma((2, pairs)), dma((2, pairs)), dma((4,)), dma((4,)), dma((8,)),
        dma((4, 2)), dma((2,)),
    ]
    anywhere = pl.BlockSpec(memory_space=pl.ANY)
    return pl.pallas_call(
        layer_kernel,
        out_shape=(
            jax.ShapeDtypeStruct(x.shape, bf), jax.ShapeDtypeStruct(x.shape, bf),
            jax.ShapeDtypeStruct((16, pw.shape[1]), f32), jax.ShapeDtypeStruct((16, pw.shape[0]), f32),
        ),
        in_specs=[anywhere] * 8 + [pl.BlockSpec(memory_space=pltpu.VMEM), pl.BlockSpec(memory_space=pltpu.SMEM)],
        out_specs=(anywhere, anywhere, pl.BlockSpec(memory_space=pltpu.VMEM), pl.BlockSpec(memory_space=pltpu.VMEM)),
        scratch_shapes=scratch,
        name="two_layers",
        compiler_params=pltpu.CompilerParams(
            collective_id=0, has_side_effects=True, vmem_limit_bytes=63 * 2**20
        ),
    )(x, cot, wq, wo, wu, wd, vec, pre, pw, ends)


def pair_body(
    layer_input, cotangent, example_lengths, attn_gain, attn_shift, query_key_value_weight, qkv_bias,
    attention_output_weight, out_bias, ffn_gain, ffn_shift, up_projection_weight, up_projection_bias,
    down_projection_weight, down_bias, prefix_table, mid_weight, mid_bias, prefix_weight, prefix_bias,
):
    hidden_pre = jnp.dot(
        prefix_table, mid_weight, preferred_element_type=jnp.float32
    ) + mid_bias.astype(jnp.float32)
    hidden_act = jnp.tanh(hidden_pre)
    hidden_low = hidden_act.astype(jnp.bfloat16)
    prefix_kv = (
        jnp.dot(hidden_low, prefix_weight, preferred_element_type=jnp.float32)
        + prefix_bias.astype(jnp.float32)
    ).astype(jnp.bfloat16)
    pre = jnp.pad(prefix_kv, ((0, 6), (0, 0)))
    pieces = [attn_gain, attn_shift, out_bias, ffn_gain, ffn_shift, down_bias, up_projection_bias, qkv_bias]
    width = layer_input.shape[-1]
    vec = jnp.concatenate(
        [jnp.pad(p.astype(jnp.float32), ((0, 0), (0, width - p.shape[1]))) for p in pieces], axis=0
    )
    ends = jnp.cumsum(example_lengths[:, 0], axis=-1).astype(jnp.int32)
    activations, input_grads, prefix_sum, hidden_grad = run_layers(
        layer_input[:, 0], cotangent[:, 0], query_key_value_weight[0], attention_output_weight[0],
        up_projection_weight[0], down_projection_weight[0], vec, pre, prefix_weight, ends,
    )
    return (activations[None, :, None], input_grads[None, :, None]) + prefix_back(
        prefix_sum[:PREFIX], hidden_grad[:PREFIX], hidden_act, hidden_low, prefix_table, mid_weight
    )


def solution(mesh):
    placed = (
        P(None, "dp", "mp", None),
        P(None, "dp", "mp", None),
        P(None, "dp", None),
        P("section", None),
        P("section", None),
        P("section", None, "mp"),
        P("section", "mp"),
        P("section", "mp", None),
        P("section", None),
        P("section", None),
        P("section", None),
        P("section", None, "mp"),
        P("section", "mp"),
        P("section", "mp", None),
        P("section", None),
        P(),
        P(),
        P(),
        P(None, ("section", "mp")),
        P(("section", "mp")),
    )
    paired = mesh.shape["mp"] == 4 and mesh.shape["dp"] == 4
    return jax.shard_map(
        pair_body if paired else body,
        mesh=mesh,
        in_specs=placed,
        out_specs=(
            P("section", None, "dp", "mp", None),
            P("section", None, "dp", "mp", None),
            P(),
            P(),
            P(),
            P(None, ("section", "mp")),
            P(("section", "mp")),
        ),
        check_vma=False,
    )
```

```python
import jax
import jax.numpy as jnp
from jax import lax
from jax.experimental import pallas as pl
from jax.experimental.pallas import tpu as pltpu
from jax.sharding import PartitionSpec as P

HEAD_DIM = 64
PREFIX = 10
SEQ_LEN = 1024


EPSILON = 1e-05
NEG_LARGE = -1e30
GELU_A = 0.7978845608028654
GELU_B = 0.044715


def norm_rows(values, gain, shift):
    average = jnp.mean(values, axis=-1, keepdims=True)
    centred = values - average
    spread = jnp.mean(centred * centred, axis=-1, keepdims=True)
    return centred * lax.rsqrt(spread + EPSILON) * gain + shift


def norm_input_grad(values, gain, shift, incoming):

    def apply_norm(inputs):
        return norm_rows(inputs, gain, shift)

    norm_value, norm_back = jax.vjp(apply_norm, values)
    return norm_back(incoming)[0]


def gelu_tanh(values):
    return jax.nn.gelu(values, approximate=True)


def visible_of(lengths, first_row, count):
    run_ends = jnp.cumsum(lengths, axis=-1)
    keys_at = jnp.arange(SEQ_LEN, dtype=jnp.int32)
    query_at = first_row + jnp.arange(count, dtype=jnp.int32)
    key_seg = jnp.sum((keys_at[None, :, None] >= run_ends[:, None, :]).astype(jnp.int32), axis=-1)
    query_seg = jnp.sum(
        (query_at[None, :, None] >= run_ends[:, None, :]).astype(jnp.int32), axis=-1
    )
    causal = (query_at[:, None] >= keys_at[None, :])[None]
    inside = (query_seg[:, :, None] == key_seg[:, None, :]) & causal
    leading = jnp.ones((lengths.shape[0], count, PREFIX), dtype=bool)
    return jnp.concatenate([leading, inside], axis=2)


def gather_rows(piece):
    return lax.all_gather(piece, "mp", axis=1, tiled=True)


def reduce_rows(partial_sum):
    return lax.psum_scatter(
        partial_sum.astype(jnp.bfloat16), "mp", scatter_dimension=1, tiled=True
    ).astype(jnp.float32)


def with_prefix(prefix_kv, pair_keys, pair_values, heads_count):
    prefix_pair = prefix_kv.reshape(PREFIX, heads_count, 2, HEAD_DIM)
    key_rows = jnp.concatenate([prefix_pair[None, :, :, 0], pair_keys], axis=1)
    value_rows = jnp.concatenate([prefix_pair[None, :, :, 1], pair_values], axis=1)
    return (key_rows, value_rows)


def attend(query_rows, key_rows, value_rows, visible):
    score_scale = HEAD_DIM ** (-0.5)
    scores = (
        jnp.einsum("sqhd,skhd->shqk", query_rows, key_rows, preferred_element_type=jnp.float32)
        * score_scale
    )
    scores = jnp.where(visible[:, None], scores, NEG_LARGE)
    highest = jnp.max(scores, axis=-1, keepdims=True)
    raised = jnp.exp(scores - highest)
    softmax_probs = raised / jnp.sum(raised, axis=-1, keepdims=True)
    probs_low = softmax_probs.astype(jnp.bfloat16)
    head_mixed_rows = jnp.einsum(
        "shqk,skhd->sqhd", probs_low, value_rows, preferred_element_type=jnp.float32
    )
    batch_size, query_count, heads_count, head_size = head_mixed_rows.shape
    head_mixed_rows = head_mixed_rows.astype(jnp.bfloat16).reshape(
        batch_size, query_count, heads_count * head_size
    )
    return (softmax_probs, probs_low, head_mixed_rows)


def attend_back(grad_mix, query_rows, key_rows, value_rows, softmax_probs, probs_low):
    grad_heads = grad_mix.reshape(query_rows.shape)
    grad_probs = jnp.einsum(
        "sqhd,skhd->shqk", grad_heads, value_rows, preferred_element_type=jnp.float32
    )
    value_grad = jnp.einsum(
        "shqk,sqhd->skhd", probs_low, grad_heads, preferred_element_type=jnp.float32
    )
    row_term = jnp.sum(grad_probs * softmax_probs, axis=-1, keepdims=True)
    grad_scores = (softmax_probs * (grad_probs - row_term)).astype(jnp.bfloat16)
    score_scale = HEAD_DIM ** (-0.5)
    query_grad = (
        jnp.einsum("shqk,skhd->sqhd", grad_scores, key_rows, preferred_element_type=jnp.float32)
        * score_scale
    )
    key_grad = (
        jnp.einsum("shqk,sqhd->skhd", grad_scores, query_rows, preferred_element_type=jnp.float32)
        * score_scale
    )
    return (query_grad, key_grad, value_grad)


def prefix_part(key_grad, value_grad):
    pair_sum = jnp.stack(
        [jnp.sum(key_grad[:, :PREFIX], axis=0), jnp.sum(value_grad[:, :PREFIX], axis=0)], axis=2
    )
    return pair_sum.reshape(PREFIX, -1)


def tensor_forward(own_rows, weights, prefix_kv, visible):
    (
        attn_gain,
        attn_shift,
        query_key_value_weight,
        qkv_bias,
        attention_output_weight,
        out_bias,
        ffn_gain,
        ffn_shift,
        up_projection_weight,
        up_projection_bias,
        down_projection_weight,
        down_bias,
        out_full,
    ) = weights
    normed = norm_rows(own_rows, attn_gain, attn_shift).astype(jnp.bfloat16)
    normalized_input_rows = gather_rows(normed)
    batch_size, seq_len, model_width = normalized_input_rows.shape
    heads_here = query_key_value_weight.shape[1] // (3 * HEAD_DIM)
    projected = (
        jnp.einsum(
            "naj,jk->nak",
            normalized_input_rows,
            query_key_value_weight,
            preferred_element_type=jnp.float32,
        )
        + qkv_bias
    )
    triple = projected.astype(jnp.bfloat16).reshape(batch_size, seq_len, heads_here, 3, HEAD_DIM)
    query_rows = triple[:, :, :, 0]
    key_rows, value_rows = with_prefix(
        prefix_kv, triple[:, :, :, 1], triple[:, :, :, 2], heads_here
    )
    softmax_probs, probs_low, head_mixed_rows = attend(query_rows, key_rows, value_rows, visible)
    attn_part = reduce_rows(
        jnp.einsum(
            "hgm,mt->hgt",
            head_mixed_rows,
            attention_output_weight,
            preferred_element_type=jnp.float32,
        )
    )
    after_attn = own_rows + attn_part + out_bias
    normed_two = norm_rows(after_attn, ffn_gain, ffn_shift).astype(jnp.bfloat16)
    second_norm_rows = gather_rows(normed_two)
    up_pre = (
        jnp.einsum(
            "rmy,yq->rmq",
            second_norm_rows,
            up_projection_weight,
            preferred_element_type=jnp.float32,
        )
        + up_projection_bias
    )
    gelu_output_rows = gelu_tanh(up_pre).astype(jnp.bfloat16)
    mlp_part = reduce_rows(
        jnp.einsum(
            "epj,jq->epq",
            gelu_output_rows,
            down_projection_weight,
            preferred_element_type=jnp.float32,
        )
    )
    result = after_attn + mlp_part + down_bias
    kept_values = (query_rows, key_rows, value_rows, softmax_probs, probs_low, after_attn, up_pre)
    return (result, kept_values)


def tensor_backward(own_rows, arriving, weights, kept_values):
    (
        attn_gain,
        attn_shift,
        query_key_value_weight,
        qkv_bias,
        attention_output_weight,
        out_bias,
        ffn_gain,
        ffn_shift,
        up_projection_weight,
        up_projection_bias,
        down_projection_weight,
        down_bias,
        out_full,
    ) = weights
    query_rows, key_rows, value_rows, softmax_probs, probs_low, after_attn, up_pre = kept_values
    gradient_gathered = gather_rows(arriving)
    gradient_activation = jnp.einsum(
        "bhi,vi->bhv", gradient_gathered, down_projection_weight, preferred_element_type=jnp.float32
    )
    gelu_value, gelu_back = jax.vjp(gelu_tanh, up_pre)
    gradient_up_projection = gelu_back(gradient_activation)[0].astype(jnp.bfloat16)
    grad_two = reduce_rows(
        jnp.einsum(
            "yca,ja->ycj",
            gradient_up_projection,
            up_projection_weight,
            preferred_element_type=jnp.float32,
        )
    )
    grad_after = norm_input_grad(after_attn, ffn_gain, ffn_shift, grad_two)
    grad_mid = (grad_after + arriving.astype(jnp.float32)).astype(jnp.bfloat16)
    middle_gathered = gather_rows(grad_mid)
    grad_mix = jnp.einsum(
        "taq,kq->tak", middle_gathered, attention_output_weight, preferred_element_type=jnp.float32
    ).astype(jnp.bfloat16)
    query_grad, key_grad, value_grad = attend_back(
        grad_mix, query_rows, key_rows, value_rows, softmax_probs, probs_low
    )
    prefix_g = prefix_part(key_grad, value_grad)
    batch_size, seq_len = (query_grad.shape[0], query_grad.shape[1])
    gradient_query_key_value = jnp.stack(
        [query_grad, key_grad[:, PREFIX:], value_grad[:, PREFIX:]], axis=3
    )
    gradient_query_key_value = gradient_query_key_value.astype(jnp.bfloat16).reshape(
        batch_size, seq_len, -1
    )
    grad_one = reduce_rows(
        jnp.einsum(
            "tvq,xq->tvx",
            gradient_query_key_value,
            query_key_value_weight,
            preferred_element_type=jnp.float32,
        )
    )
    grad_input = norm_input_grad(own_rows, attn_gain, attn_shift, grad_one)
    grad_input = (grad_input + grad_mid.astype(jnp.float32)).astype(jnp.bfloat16)
    return (grad_input, prefix_g)


def prefix_back(prefix_sum, hidden_grad, hidden_act, hidden_low, prefix_table, mid_weight):
    prefix_low = prefix_sum.astype(jnp.bfloat16)
    prefix_bias_grad = jnp.sum(prefix_low.astype(jnp.float32), axis=0)
    prefix_weight_grad = jnp.dot(hidden_low.T, prefix_low, preferred_element_type=jnp.float32)
    pre_grad = (hidden_grad * (1.0 - hidden_act * hidden_act)).astype(jnp.bfloat16)
    mid_bias_grad = jnp.sum(pre_grad.astype(jnp.float32), axis=0)
    mid_weight_grad = jnp.dot(prefix_table.T, pre_grad, preferred_element_type=jnp.float32)
    table_grad = jnp.dot(pre_grad, mid_weight.T, preferred_element_type=jnp.float32)
    return (table_grad, mid_weight_grad, mid_bias_grad, prefix_weight_grad, prefix_bias_grad)


def both_layers(piece):
    return lax.all_gather(piece[0], "section", axis=0, tiled=False)


def body(
    layer_input,
    cotangent,
    example_lengths,
    attn_gain,
    attn_shift,
    query_key_value_weight,
    qkv_bias,
    attention_output_weight,
    out_bias,
    ffn_gain,
    ffn_shift,
    up_projection_weight,
    up_projection_bias,
    down_projection_weight,
    down_bias,
    prefix_table,
    mid_weight,
    mid_bias,
    prefix_weight,
    prefix_bias,
):
    layers = lax.axis_size("section")
    section_index = lax.axis_index("section")
    hidden_pre = jnp.dot(
        prefix_table, mid_weight, preferred_element_type=jnp.float32
    ) + mid_bias.astype(jnp.float32)
    hidden_act = jnp.tanh(hidden_pre)
    hidden_low = hidden_act.astype(jnp.bfloat16)
    prefix_kv = (
        jnp.dot(hidden_low, prefix_weight, preferred_element_type=jnp.float32)
        + prefix_bias.astype(jnp.float32)
    ).astype(jnp.bfloat16)
    prefix_all = lax.all_gather(prefix_kv, "section", axis=0, tiled=False)
    floats = [
        both_layers(piece).astype(jnp.float32)
        for piece in (attn_gain, attn_shift, qkv_bias, out_bias, ffn_gain, ffn_shift,
                      up_projection_bias, down_bias)
    ]
    matrices = [
        both_layers(piece)
        for piece in (query_key_value_weight, attention_output_weight,
                      up_projection_weight, down_projection_weight)
    ]

    def weights_of(layer):
        g1, s1, bq, bo, g2, s2, bu, bd = [piece[layer] for piece in floats]
        wq, wo, wu, wd = [piece[layer] for piece in matrices]
        return (g1, s1, wq, bq, wo, bo, g2, s2, wu, bu, wd, bd, wo)

    batch_count = layer_input.shape[0]
    own_input = lax.dynamic_index_in_dim(layer_input, section_index, 0, keepdims=False)
    own_cotangent = lax.dynamic_index_in_dim(cotangent, section_index, 0, keepdims=False)
    lengths = lax.dynamic_index_in_dim(example_lengths, section_index, 0, keepdims=False)
    visible = visible_of(lengths, 0, SEQ_LEN)
    entering = own_input
    entered, produced, kept = [], [], []
    for layer in range(layers):
        entered.append(entering.astype(jnp.float32))
        result, kept_values = tensor_forward(
            entered[layer], weights_of(layer), prefix_all[layer], visible
        )
        entering = result.astype(jnp.bfloat16)
        produced.append(entering)
        kept.append(kept_values)
    gradient = own_cotangent
    sent_grads = [None] * layers
    prefix_parts = [None] * layers
    for layer in reversed(range(layers)):
        gradient, prefix_parts[layer] = tensor_backward(
            entered[layer], gradient, weights_of(layer), kept[layer]
        )
        sent_grads[layer] = gradient
    activations = lax.all_to_all(jnp.stack(produced), "section", 0, 0, tiled=False)
    input_grads = lax.all_to_all(jnp.stack(sent_grads), "section", 0, 0, tiled=False)
    prefix_sum = lax.psum(jnp.stack(prefix_parts), ("dp", "section"))
    prefix_sum = lax.dynamic_index_in_dim(prefix_sum, section_index, 0, keepdims=False)
    hidden_part = jnp.dot(
        prefix_sum.astype(jnp.bfloat16), prefix_weight.T, preferred_element_type=jnp.float32
    )
    hidden_grad = lax.psum(hidden_part, ("section", "mp"))
    return (activations[None], input_grads[None]) + prefix_back(
        prefix_sum, hidden_grad, hidden_act, hidden_low, prefix_table, mid_weight
    )


MESH = pl.DeviceIdType.MESH
BLOCK = 256
LOG2E = 1.4426950408889634
CHUNK = 128
UNITS = 12
AHEAD = 8
UNIT_ROWS = 512
PART_ROWS = UNIT_ROWS // 8


def role_of(z):
    return (((z + 1) // 2) + 1) % 2


def block_of(s, j):
    return j * 3 + s * (1 - 2 * j)


def core_of(block):
    return ((block + 1) // 2) % 2


def guarded(when, action):
    if when is None:
        action()
    else:
        pl.when(when)(action)


def dot_nn(a, b):
    return lax.dot_general(a, b, (((1,), (0,)), ((), ())), preferred_element_type=jnp.float32)


def dot_nt(a, b):
    return lax.dot_general(a, b, (((1,), (1,)), ((), ())), preferred_element_type=jnp.float32)


def dot_tn(a, b):
    return lax.dot_general(a, b, (((0,), (0,)), ((), ())), preferred_element_type=jnp.float32)


class Sends:
    def __init__(self, sems):
        self.sems, self.used, self.pending = sems, 0, []

    def start(self, src, dst, recv_sem, target, when=None):
        copy = pltpu.make_async_remote_copy(
            src_ref=src, dst_ref=dst, send_sem=self.sems.at[self.used], recv_sem=recv_sem,
            device_id=target, device_id_type=MESH,
        )
        self.used += 1
        guarded(when, copy.start)
        self.pending.append((when, copy))

    def start_or_keep(self, src, dst, recv_sem, target, is_here, when=True):
        @pl.when(jnp.logical_and(when, is_here))
        def _():
            pltpu.make_async_copy(src, dst, recv_sem).start()

        self.start(src, dst, recv_sem, target, when=jnp.logical_and(when, jnp.logical_not(is_here)))

    def finish(self):
        for when, copy in self.pending:
            guarded(when, copy.wait_send)
        self.pending = []


def layer_kernel(
    x_hbm, cot_hbm, wq_hbm, wo_hbm, wu_hbm, wd_hbm,
    g1, s1, bo, g2, s2, bd, bu, bq, table, mid_w, mid_b, pw, pb, lengths,
    act_out, ig_out, sum_out, hidden_out, tanh_out,
    vec_own, pre_full, pre_own, wq, wo, wud, vec, pre,
    x_in, g_in, y_out, normed, kv, q_own, o_own, lse, bias, after, acc, slope, wide,
    pg, pg_near, pg_far, hidden_core, hidden_all, ts, dkv_own, dkv_send, dkv_recv, kp, vp, gt,
    ssem, vec_sem, pre_sem, x_sem, g_sem, act_sem, ig_sem, own_sem, z_sem, a_sem, b_sem, c_sem,
    zr_sem, ar_sem, br_sem, cr_sem, fs_sem, zs_sem, as_sem, bs_sem, cs_sem, go_sem,
    kv_ssem, kv_rsem, dkv_ssem, dkv_rsem, pg_sem, far_sem, core_sem, hidden_sem,
    hand_sem, cot_sem, pg_ssem, far_ssem, mid_sem,
):
    s, d, z = lax.axis_index("section"), lax.axis_index("dp"), lax.axis_index("mp")
    role, micro = role_of(z), z // 2
    other = 1 - s
    partner = z + 1 - 2 * (z % 2)
    x_near, y_near = d + 1 - 2 * (d % 2), (d + 2) % 4
    near1 = jnp.where(s == 0, x_near, y_near)
    near2 = jnp.where(s == 0, y_near, x_near)
    sends = Sends(ssem)

    barrier = pltpu.get_barrier_semaphore()
    for ds in range(2):
        for dz in range(4):
            if ds or dz:
                pl.semaphore_signal(barrier, inc=1, device_id=((s + ds) % 2, d, (z + dz) % 4), device_id_type=MESH)
    for near in (x_near, y_near, 3 - d):
        pl.semaphore_signal(barrier, inc=1, device_id=(s, near, z), device_id_type=MESH)
    pl.semaphore_wait(barrier, 10)

    def arrived(dst, sem):
        pltpu.make_async_remote_copy(
            src_ref=dst, dst_ref=dst, send_sem=ssem.at[0], recv_sem=sem,
            device_id=(other, d, z), device_id_type=MESH,
        ).wait_recv()

    low_plane, high_plane = jnp.where(s == 0, 1, 0), jnp.where(s == 0, 2, 3)
    planes = (low_plane, high_plane)
    mine = s == core_of(z)
    row_slot = pl.ds(pl.multiple_of((z // 2) * BLOCK, BLOCK), BLOCK)

    def send_block(source, landing, sem, k, chip, when):
        when = jnp.logical_and(mine, when)

        @pl.when(jnp.logical_and(when, z == chip))
        def _():
            pltpu.make_async_copy(source.at[k], landing.at[row_slot], sem.at[z // 2]).start()

        sends.start(source.at[k], landing.at[row_slot], sem.at[z // 2], (s, d, chip),
                    when=jnp.logical_and(when, z != chip))

    def send_small(when):
        for t in planes:
            for h in range(2):
                is_here = jnp.logical_and(z == t, s == h)
                sends.start_or_keep(pre_own, pre.at[z], pre_sem.at[z], (h, d, t), is_here, when)

    def send_x(when):
        for k, chip in ((0, 1), (1, 2)):
            send_block(x_hbm, x_in, x_sem, k, chip, when)

    toward = jnp.where(z < 2, 1, -1)

    def quarter(i):
        return (z + 4 + toward * i) % 4

    def taker(i):
        low, high = (z + 3 - i) % 4, (z + 1 + i) % 4
        return jnp.where(low == low_plane, low, high), jnp.logical_or(low == low_plane, high == high_plane)

    swapped = (d % 2) * 2 + d // 2
    place = jnp.where(s == 0, d, swapped)
    pair_start = (place // 2) * 2
    far_start = 2 - pair_start
    firsts = ((wq_hbm, wq), (wo_hbm, wo))

    def eighths(rows, start, count, h):
        return pl.ds(pl.multiple_of((start + 4 * h) * rows, rows), rows * count)

    def supply_first(w, i, then):
        t, taken = taker(i)
        held, full = firsts[w]

        @pl.when(taken)
        def _():
            for h in range(2):
                at = eighths(held.shape[0] // 8, swapped if h else d, 1, h)
                then(pltpu.make_async_remote_copy(
                    src_ref=held.at[at], dst_ref=full.at[z, at], send_sem=fs_sem.at[3 * w + i, h],
                    recv_sem=z_sem.at[w, z], device_id=(h, d, t), device_id_type=MESH,
                ))

    def supply_firsts(when, w):
        @pl.when(when)
        def _():
            def one(i, carry):
                supply_first(w, i, lambda copy: copy.start())
                return carry

            lax.fori_loop(0, 3, one, 0)

    def firsts_done(when, w):
        @pl.when(when)
        def _():
            def one(i, carry):
                supply_first(w, i, lambda copy: copy.wait_send())
                return carry

            lax.fori_loop(0, 3, one, 0)

    def supply_copies(i, c, then):
        t, taken = taker(i)
        held, base = ((wu_hbm, 0), (wd_hbm, 1024))[c // 2]

        @pl.when(taken)
        def _():
            for h in range(2):
                at = eighths(PART_ROWS, swapped if h else d, 1, h)
                start = (c % 2) * UNIT_ROWS + at.start
                then(pltpu.make_async_remote_copy(
                    src_ref=held.at[pl.ds(pl.multiple_of(start, PART_ROWS), PART_ROWS)],
                    dst_ref=wud.at[z, pl.ds(pl.multiple_of(base + start, PART_ROWS), PART_ROWS)],
                    send_sem=zs_sem.at[4 * i + c, h], recv_sem=zr_sem.at[4 * i + c],
                    device_id=(h, d, t), device_id_type=MESH,
                ))

    def supply_all(i, carry):
        for c in range(4):
            supply_copies(i, c, lambda copy: copy.start())
        return carry

    def supply_done(i, carry):
        for c in range(4):
            supply_copies(i, c, lambda copy: copy.wait_send())
        return carry

    def supply_paced(i, carry):
        for c in range(4):
            supply_copies(i, c, lambda copy: copy.start())
            if c:
                supply_copies(i, c - 1, lambda copy: copy.wait_send())
        supply_copies(i, 3, lambda copy: copy.wait_send())
        return carry

    feeds_zero = jnp.logical_and(role == 1, s == 0)
    feeds_zero_late = jnp.logical_and(role == 0, s == 0)
    feeds_one = jnp.logical_and(role == 0, s == 1)
    feeds_one_late = jnp.logical_and(role == 1, s == 1)
    supply_firsts(s == 0, 0)
    mid_copies = mid_w.shape[1] // 128

    def mid_copy(n, half):
        return pltpu.make_async_copy(
            mid_w.at[half * 512 : half * 512 + 512, n * 128 : n * 128 + 128], q_own.at[2 * n + half],
            mid_sem.at[2 * n + half],
        )

    for n in range(mid_copies):
        for half in range(2):
            mid_copy(n, half).start()
    for k, row in enumerate((g1, s1, bo, g2, s2, bd)):
        vec_own[k : k + 1, :] = row[...].astype(jnp.float32)

    @pl.when(role == s)
    def _():
        pltpu.make_async_copy(vec_own, vec.at[0], vec_sem.at[0]).start()

    sends.start(vec_own, vec.at[0], vec_sem.at[0], (other, d, z), when=role == s)
    tanh_out[...] = jnp.zeros(tanh_out.shape, jnp.float32)
    for n in range(mid_copies):
        for half in range(2):
            mid_copy(n, half).wait()
        cols = slice(n * 128, n * 128 + 128)
        part_sum = dot_nn(table[:, 0:512], q_own[2 * n]) + dot_nn(table[:, 512:1024], q_own[2 * n + 1])
        tanh_out[0:PREFIX, cols] = jnp.tanh(part_sum + mid_b[...].astype(jnp.float32).reshape(1, -1)[:, cols])
    pre_full[...] = dot_nn(tanh_out[...].astype(jnp.bfloat16), pw[...]) + pb[...].astype(jnp.float32).reshape(1, -1)
    half_width = pre_full.shape[1]
    for k, row in enumerate((bu, bq)):
        for n in range(2):
            piece = row[:, n * half_width : min((n + 1) * half_width, row.shape[1])]
            pre_full[PREFIX + 2 * k + n : PREFIX + 2 * k + n + 1, 0 : piece.shape[1]] = piece.astype(jnp.float32)
    pre_own[...] = pre_full[...].astype(jnp.bfloat16)
    send_small(feeds_zero)
    firsts_done(feeds_zero, 0)
    supply_firsts(feeds_zero, 1)
    send_x(feeds_zero)
    owned = ((wq_hbm, wq.at[z]), (wo_hbm, wo.at[z]), (wu_hbm, wud.at[z, 0:1024]), (wd_hbm, wud.at[z, 1024:2048]))
    for w, (held, full) in enumerate(owned):
        @pl.when(role == s)
        def _():
            pltpu.make_async_copy(held, full, own_sem.at[w]).start()

        sends.start(held, full, own_sem.at[w], (other, d, z), when=role == s)

    @pl.when(feeds_zero)
    def _():
        lax.fori_loop(0, 3, supply_paced, 0)

    @pl.when(feeds_one_late)
    def _():
        pl.semaphore_wait(go_sem, 1)

    send_small(feeds_one_late)
    supply_firsts(feeds_one_late, 0)
    supply_firsts(feeds_one_late, 1)

    first_units = [(w, i) for w in (0, 1) for i in range(1, 4)]

    def first_piece(w, i, start, count):
        full = firsts[w][1]
        return full.at[quarter(i), eighths(full.shape[1] // 8, start, count, s)]

    def relay_first(step):
        stages = [first_units[step - k] if 0 <= step - k < len(first_units) else None for k in range(4)]
        if stages[0]:
            w, i = stages[0]
            q = quarter(i)
            arrived(first_piece(w, i, place, 1), z_sem.at[w, q])
            sends.start(first_piece(w, i, place, 1), first_piece(w, i, place, 1), a_sem.at[w, q], (s, near1, z))
        if stages[1]:
            w, i = stages[1]
            q = quarter(i)
            arrived(first_piece(w, i, pair_start + 1 - place % 2, 1), a_sem.at[w, q])
            sends.start(first_piece(w, i, pair_start, 2), first_piece(w, i, pair_start, 2), b_sem.at[w, q], (s, near2, z))
        if stages[2]:
            w, i = stages[2]
            q = quarter(i)
            arrived(first_piece(w, i, far_start, 2), b_sem.at[w, q])
            sends.start(first_piece(w, i, 0, 4), first_piece(w, i, 0, 4), c_sem.at[w, q], (other, d, z))
        if stages[3]:
            w, i = stages[3]
            full = firsts[w][1]
            arrived(full.at[quarter(i), eighths(full.shape[1] // 8, 0, 4, other)], c_sem.at[w, quarter(i)])

    for step in range(len(first_units) + 3):
        relay_first(step)
        if step == 0:
            send_x(role == 0)
            send_small(feeds_zero_late)
            supply_firsts(feeds_zero_late, 1)
        if step == 3:
            @pl.when(feeds_one)
            def _():
                pl.semaphore_signal(go_sem, inc=1, device_id=(1, d, partner), device_id_type=MESH)

            supply_firsts(feeds_one, 0)
        if step == 6:
            send_small(feeds_one)
            supply_firsts(feeds_one, 1)

        @pl.when(feeds_zero_late)
        def _():
            if 1 <= step < 5:
                supply_copies(0, step - 1, lambda copy: copy.start())

    @pl.when(feeds_one_late)
    def _():
        lax.fori_loop(0, 3, supply_all, 0)

    def unit_piece(m, start, count, h):
        q = quarter(1 + m // 4)
        first_row = (m % 4) * UNIT_ROWS + (start + 4 * h) * PART_ROWS
        return wud.at[q, pl.ds(pl.multiple_of(first_row, PART_ROWS), PART_ROWS * count)]

    def relay_copy(m, stage):
        start, count = ((place, 1), (pair_start, 2), (0, 4))[stage]
        at = unit_piece(m, start, count, s)
        return pltpu.make_async_remote_copy(
            src_ref=at, dst_ref=at, send_sem=(as_sem, bs_sem, cs_sem)[stage].at[m],
            recv_sem=(ar_sem, br_sem, cr_sem)[stage].at[m],
            device_id=((s, near1, z), (s, near2, z), (other, d, z))[stage], device_id_type=MESH,
        )

    def relay(n):
        for c in range(4):

            @pl.when(jnp.logical_and(feeds_one, jnp.logical_and(n < UNITS // 2, n % 2 == c // 2)))
            def _():
                supply_copies(n // 2, c, lambda copy: copy.start())

        for k in range(4):
            m = n - k

            @pl.when(jnp.logical_and(m >= 0, m < UNITS))
            def _():
                if k == 0:
                    arrived(unit_piece(m, place, 1, s), zr_sem.at[m])
                if k == 1:
                    arrived(unit_piece(m, pair_start + 1 - place % 2, 1, s), ar_sem.at[m])
                if k == 2:
                    arrived(unit_piece(m, far_start, 2, s), br_sem.at[m])
                if k == 3:
                    arrived(unit_piece(m, 0, 4, other), cr_sem.at[m])
                if k < 3:
                    relay_copy(m, k).start()

    def cot_copies(then):
        for k, chip in ((0, 0), (1, 3)):

            @pl.when(jnp.logical_and(mine, z != chip))
            def _():
                then(pltpu.make_async_remote_copy(
                    src_ref=cot_hbm.at[k], dst_ref=g_in.at[row_slot], send_sem=cot_sem.at[k],
                    recv_sem=g_sem.at[z // 2], device_id=(s, d, chip), device_id_type=MESH,
                ))

    for k, chip in ((0, 0), (1, 3)):

        @pl.when(jnp.logical_and(mine, z == chip))
        def _():
            pltpu.make_async_copy(cot_hbm.at[k], g_in.at[row_slot], g_sem.at[z // 2]).start()

    @pl.when(role == 1)
    def _():
        cot_copies(lambda copy: copy.start())
    def relay_steps(start, stop):
        def one(n, carry):
            relay(n)
            return carry

        lax.fori_loop(start, stop, one, 0)

    relay_steps(0, jnp.where(role == 1, AHEAD, 0))
    arrived(wq.at[z], own_sem.at[0])
    arrived(wo.at[z], own_sem.at[1])
    arrived(wud.at[z, 0:1024], own_sem.at[2])
    arrived(wud.at[z, 1024:2048], own_sem.at[3])
    arrived(vec.at[0], vec_sem.at[0])
    for q in range(4):
        arrived(pre.at[q], pre_sem.at[q])
        carried = pre[q].astype(jnp.float32)
        for k in range(2):
            for n in range(2):
                row = PREFIX + 2 * k + n
                vec[q, 6 + k : 7 + k, n * half_width : (n + 1) * half_width] = carried[row : row + 1, :]

    first16 = lax.broadcasted_iota(jnp.int32, (16, 128), 1) < HEAD_DIM
    first = lax.broadcasted_iota(jnp.int32, (BLOCK, 128), 1) < HEAD_DIM
    lane = lax.broadcasted_iota(jnp.int32, (1, 128), 1)
    half0 = jnp.where(lane < HEAD_DIM, 1.0, 0.0).astype(jnp.bfloat16)
    half1 = jnp.where(lane < HEAD_DIM, 0.0, 1.0).astype(jnp.bfloat16)
    pre_mask = jnp.where(lane % HEAD_DIM < PREFIX, 0.0, NEG_LARGE)
    kp[...] = jnp.zeros(kp.shape, kp.dtype)
    vp[...] = jnp.zeros(vp.shape, vp.dtype)
    for q in range(4):
        for p in range(2):
            t0 = pre[q, :, p * 256 : p * 256 + 128].astype(jnp.float32)
            t1 = pre[q, :, p * 256 + 128 : p * 256 + 256].astype(jnp.float32)
            kp[2 * q + p, 0:16, :] = jnp.where(first16, t0, 0.0).astype(jnp.bfloat16)
            kp[2 * q + p, 64:80, :] = jnp.where(first16, 0.0, pltpu.roll(t1, 64, 1)).astype(jnp.bfloat16)
            vp[2 * q + p, 0:16, :] = jnp.where(first16, pltpu.roll(t0, 64, 1), 0.0).astype(jnp.bfloat16)
            vp[2 * q + p, 64:80, :] = jnp.where(first16, 0.0, t1).astype(jnp.bfloat16)

    for j in range(2):
        row0 = block_of(s, j) * BLOCK
        row_at = row0 + lax.broadcasted_iota(jnp.int32, (BLOCK, 1), 0)
        begin = jnp.zeros((BLOCK, 1), jnp.int32)
        end = 0
        for e in range(lengths.shape[1]):
            end = end + lengths[micro, e]
            begin = jnp.where(row_at >= end, end, begin)

        def mask_block(kb, carry):
            key_at = kb * BLOCK + lax.broadcasted_iota(jnp.int32, (BLOCK, BLOCK), 1)
            keep = jnp.logical_and(key_at <= row_at, key_at >= begin)
            bias[2 * j + kb] = jnp.where(keep, 0.0, NEG_LARGE)
            return carry

        lax.fori_loop(0, 2 + 2 * j, mask_block, 0)

    def vector(k, q=0, width=1024):
        return vec[q, k : k + 1, 0:width]

    def columns(n, width):
        return pl.ds(pl.multiple_of(n * width, width), width)

    def block_rows(j):
        return pl.ds(pl.multiple_of(j * BLOCK, BLOCK), BLOCK)

    def over_rows(j, action):
        def one(c, carry):
            action(pl.ds(pl.multiple_of(j * BLOCK + c * CHUNK, CHUNK), CHUNK))
            return carry

        lax.fori_loop(0, BLOCK // CHUNK, one, 0)

    def standardize(v):
        average = jnp.mean(v, axis=-1, keepdims=True)
        centred = v - average
        spread = jnp.mean(centred * centred, axis=-1, keepdims=True)
        return centred, lax.rsqrt(spread + EPSILON)

    def norm_back(v, gain, incoming):
        centred, inverse = standardize(v)
        xhat = centred * inverse
        e = incoming * gain
        return (e - jnp.mean(e, axis=-1, keepdims=True) - xhat * jnp.mean(e * xhat, axis=-1, keepdims=True)) * inverse

    def to_core(ref, send_sem, recv_sem):
        return pltpu.make_async_remote_copy(
            src_ref=ref, dst_ref=ref, send_sem=send_sem, recv_sem=recv_sem,
            device_id=(other, d, z), device_id_type=MESH,
        )

    scale = LOG2E * HEAD_DIM ** (-0.5)

    def enter(j):
        rows = block_rows(j)
        arrived(x_in.at[rows], x_sem.at[j])

        def norm_one(rows):
            centred, inverse = standardize(x_in[rows, :].astype(jnp.float32))
            normed[rows, :] = (centred * inverse * vector(0) + vector(1)).astype(jnp.bfloat16)

        over_rows(j, norm_one)

        def project(q, carry):
            triple = dot_nn(normed[rows, :], wq[q]) + vec[q, 7:8, 0:768]
            for p in range(2):
                t0, t1, t2 = (triple[:, p * 384 + n * 128 : p * 384 + n * 128 + 128] for n in range(3))
                q_own[2 * q + p, rows, :] = jnp.where(first, t0, t1).astype(jnp.bfloat16)
                kv[s, 2 * q + p, 0, rows, :] = pltpu.roll(jnp.where(first, t2, t0), 64, 1).astype(jnp.bfloat16)
                kv[s, 2 * q + p, 1, rows, :] = jnp.where(first, t1, t2).astype(jnp.bfloat16)
            to_core(kv.at[s, pl.ds(2 * q, 2), :, rows], kv_ssem.at[j, q], kv_rsem.at[j, q]).start()
            return carry

        lax.fori_loop(0, 4, project, 0)

    def attend_rows(pair, core, j):
        cols = columns(pair, 128)
        rows = slice(j * BLOCK, j * BLOCK + BLOCK)
        blocks = block_of(core, j) + 1
        q_pair = q_own[pair, rows, :]
        q_half = (q_pair * half0, q_pair * half1)
        t_pre = dot_nt(q_pair, kp[pair]) * scale + pre_mask
        tops = [jnp.where(first, t_pre, NEG_LARGE), jnp.where(first, NEG_LARGE, t_pre)]
        for kb in range(blocks):
            keys = kv[core_of(kb), pair, 0, (kb // 2) * BLOCK : (kb // 2 + 1) * BLOCK, :]
            for h in range(2):
                t = dot_nt(q_half[h], keys) * scale + bias[2 * j + kb]
                ts[h, kb] = t
                tops[h] = jnp.maximum(tops[h], jnp.maximum(t[:, :128], t[:, 128:]))
        highest = [jnp.max(tops[h], axis=1, keepdims=True) for h in range(2)]
        e_pre = jnp.exp2(t_pre - jnp.where(first, highest[0], highest[1]))
        sums = [jnp.where(first, e_pre, 0.0), jnp.where(first, 0.0, e_pre)]
        mixed = [jnp.zeros((BLOCK, 128), jnp.float32) for _ in range(2)]
        for kb in range(blocks):
            values = kv[core_of(kb), pair, 1, (kb // 2) * BLOCK : (kb // 2 + 1) * BLOCK, :]
            for h in range(2):
                e = jnp.exp2(ts[h, kb] - highest[h])
                sums[h] += e[:, :128] + e[:, 128:]
                mixed[h] += dot_nn(e.astype(jnp.bfloat16), values)
        total = [jnp.sum(sums[h], axis=1, keepdims=True) for h in range(2)]
        share = [1.0 / total[h] for h in range(2)]
        p_pre = (e_pre * jnp.where(first, share[0], share[1])).astype(jnp.bfloat16)
        result = jnp.where(first, mixed[0] * share[0], mixed[1] * share[1]) + dot_nn(p_pre, vp[pair])
        o_own[rows, cols] = result.astype(jnp.bfloat16)
        logs = [highest[h] + jnp.log(total[h]) * LOG2E for h in range(2)]
        lse[pair, rows, :] = jnp.where(first, logs[0], logs[1])

    def attend(j, relay_at):
        def kv_wait(q, carry):
            to_core(kv.at[s, pl.ds(2 * q, 2), :, block_rows(j)], kv_ssem.at[j, q], kv_rsem.at[j, q]).wait_send()
            arrived(kv.at[other, pl.ds(2 * q, 2), :, block_rows(j)], kv_rsem.at[j, q])
            return carry

        lax.fori_loop(0, 4, kv_wait, 0)
        for core in range(2):
            for block in range(2):

                @pl.when(jnp.logical_and(s == core, j == block))
                def _():
                    def attend_pair(pair, carry):
                        relay_steps(relay_at, jnp.where(jnp.logical_and(pair == 4, role == 0), relay_at + 1, relay_at))
                        attend_rows(pair, core, block)
                        return carry

                    lax.fori_loop(0, 8, attend_pair, 0)

        rows = block_rows(j)
        after[rows, :] = (
            x_in[rows, :].astype(jnp.float32) + dot_nn(o_own[rows, :], wo[...].reshape(1024, 1024)) + vector(2)
        )

        def norm_two(rows):
            centred, inverse = standardize(after[rows, :])
            normed[rows, :] = (centred * inverse * vector(3) + vector(4)).astype(jnp.bfloat16)
            acc[rows, :] = after[rows, :] + vector(5)

        over_rows(j, norm_two)

    def feed(j, i):
        rows = block_rows(j)
        q = quarter(i)
        u = dot_nn(normed[rows, :], wud[q, 0:1024, :]) + vec[q, 6:7, :]
        u2 = u * u
        t = jnp.tanh(u * (GELU_A + (GELU_A * GELU_B) * u2))
        half_t = 0.5 + 0.5 * t
        wide[rows, :] = (u * half_t).astype(jnp.bfloat16)
        inner = u * (GELU_A + (3.0 * GELU_A * GELU_B) * u2)
        slope[q, rows, :] = (half_t + 0.5 * inner * (1.0 - t * t)).astype(jnp.bfloat16)
        acc[rows, :] += dot_nn(wide[rows, :], wud[q, 1024:2048, :])

    def hand_copies(j, k):
        rows = block_rows(j)
        landing, sem = ((x_in, x_sem), (act_out, act_sem), (g_in, g_sem), (ig_out, ig_sem))[k]
        if k % 2:
            dst, sem, target = landing.at[micro], sem.at[micro], (role, d, block_of(s, j))
        else:
            dst, sem, target = landing.at[rows], sem.at[j], (s, d, partner)
        return pltpu.make_async_remote_copy(
            src_ref=y_out.at[rows], dst_ref=dst, send_sem=hand_sem.at[k, j], recv_sem=sem,
            device_id=target, device_id_type=MESH,
        )

    def hand_on(j):
        rows = block_rows(j)
        y_out[rows, :] = acc[rows, :].astype(jnp.bfloat16)

        @pl.when(role == 1)
        def _():
            hand_copies(j, 1).start()

        @pl.when(jnp.logical_and(role == 0, j == 0))
        def _():
            hand_copies(0, 0).start()

        @pl.when(jnp.logical_and(role == 0, j == 1))
        def _():
            hand_copies(0, 0).wait_send()
            hand_copies(1, 0).start()
            hand_copies(1, 0).wait_send()
            for block in range(2):
                hand_copies(block, 1).start()

    def upto(n, table):
        total = jnp.int32(0)
        for k, entry in enumerate(table):
            total += jnp.where(n >= k, entry - (table[k - 1] if k else 0), 0)
        return total

    early_table = (0, 1, 2, 4, 6, 7, 8, 9, 11, 13, 15, 15, 15, 15)
    late_table = (AHEAD, 9, 10, 11, 13, 15, 15, 15, 15, 15, 15, 15, 15, 15)

    def forward(n, carry):
        turn = jnp.where(n == 11, 12, jnp.where(n == 12, 11, n))
        stage = jnp.where(role == 0, turn // 2, n % 7)
        j = jnp.where(role == 0, turn % 2, n // 7)
        before = jnp.where(
            role == 0,
            jnp.where(n == 0, 0, upto(n - 1, early_table)) + jnp.where(jnp.logical_or(n == 3, n == 4), 1, 0),
            jnp.where(n == 0, AHEAD, upto(n - 1, late_table)),
        )
        until = jnp.where(role == 0, upto(n, early_table), upto(n, late_table))
        relay_steps(before, until)

        @pl.when(jnp.logical_and(role == 0, n == 6))
        def _():
            cot_copies(lambda copy: copy.start())

        @pl.when(stage == 0)
        def _():
            enter(j)

        @pl.when(stage == 1)
        def _():
            attend(j, until)

        @pl.when(jnp.logical_and(stage >= 2, stage < 6))
        def _():
            feed(j, stage - 2)

        @pl.when(stage == 6)
        def _():
            hand_on(j)

        return carry

    lax.fori_loop(0, 14, forward, 0)

    def back_rows(pair, core, j):
        cols = columns(pair, 128)
        rows = slice(j * BLOCK, j * BLOCK + BLOCK)
        q_pair = q_own[pair, rows, :]
        q_half = (q_pair * half0, q_pair * half1)
        g_pair = wide[rows, cols]
        g_half = (g_pair * half0, g_pair * half1)
        product = g_pair.astype(jnp.float32) * o_own[rows, cols].astype(jnp.float32)
        row_term = [
            jnp.sum(jnp.where(first, product, 0.0), axis=1, keepdims=True),
            jnp.sum(jnp.where(first, 0.0, product), axis=1, keepdims=True),
        ]
        logs = lse[pair, rows, :]
        log_half = (logs[:, 0:1], logs[:, 64:65])
        p_pre = jnp.exp2(dot_nt(q_pair, kp[pair]) * scale + pre_mask - logs)
        dp_pre = dot_nt(g_pair, vp[pair])
        ds_pre = (p_pre * (dp_pre - jnp.where(first, row_term[0], row_term[1]))).astype(jnp.bfloat16)
        pv = dot_tn(p_pre.astype(jnp.bfloat16), g_pair)
        pk = dot_tn(ds_pre, q_pair)
        pk = jnp.where(first16, pk[0:16, :], pk[64:80, :]) * HEAD_DIM ** (-0.5)
        pv = jnp.where(first16, pv[0:16, :], pv[64:80, :])
        pg[pair, 0] = pk if j else pg[pair, 0] + pk
        pg[pair, 1] = pv if j else pg[pair, 1] + pv
        dq_pre = dot_nn(ds_pre, kp[pair])
        dqs = [jnp.zeros((BLOCK, 128), jnp.float32) for _ in range(2)]
        for kb in range(4):
            held = dkv_own if core_of(kb) == core else dkv_send
            at = slice((kb // 2) * BLOCK, (kb // 2 + 1) * BLOCK)
            if kb > block_of(core, j):
                if j:
                    held[pair, 0, at, :] = jnp.zeros((BLOCK, 128), jnp.bfloat16)
                    held[pair, 1, at, :] = jnp.zeros((BLOCK, 128), jnp.bfloat16)
                continue
            keys = kv[core_of(kb), pair, 0, at, :]
            values = kv[core_of(kb), pair, 1, at, :]
            dv, dk = 0.0, 0.0
            if j == 0:
                dk = held[pair, 0, at, :].astype(jnp.float32)
                dv = held[pair, 1, at, :].astype(jnp.float32)
            for h in range(2):
                probs = jnp.exp2(dot_nt(q_half[h], keys) * scale + bias[2 * j + kb] - log_half[h])
                grad_probs = dot_nt(g_half[h], values)
                grad_scores = (probs * (grad_probs - row_term[h])).astype(jnp.bfloat16)
                dv += dot_tn(probs.astype(jnp.bfloat16), g_half[h])
                dk += dot_tn(grad_scores, q_half[h])
                dqs[h] += dot_nn(grad_scores, keys)
            held[pair, 0, at, :] = dk.astype(jnp.bfloat16)
            held[pair, 1, at, :] = dv.astype(jnp.bfloat16)
        dq = (jnp.where(first, dqs[0], dqs[1]) + dq_pre) * HEAD_DIM ** (-0.5)
        q_own[pair, rows, :] = dq.astype(jnp.bfloat16)

    def dkv_copy(j, pair):
        rows = block_rows(j)
        return pltpu.make_async_remote_copy(
            src_ref=dkv_send.at[pair, :, rows], dst_ref=dkv_recv.at[pair, :, rows],
            send_sem=dkv_ssem.at[j, pair], recv_sem=dkv_rsem.at[j, pair],
            device_id=(other, d, z), device_id_type=MESH,
        )

    contribution = micro * 2 + s

    def pg_copy(q):
        return pltpu.make_async_remote_copy(
            src_ref=pg.at[2 * q : 2 * q + 2], dst_ref=pg_near.at[contribution], send_sem=pg_ssem.at[q],
            recv_sem=pg_sem.at[contribution], device_id=(role, d, q), device_id_type=MESH,
        )

    def far_copy(k):
        return pltpu.make_async_remote_copy(
            src_ref=pg_far.at[d], dst_ref=pg_far.at[d], send_sem=far_ssem.at[k - 1], recv_sem=far_sem.at[d],
            device_id=(s, (d + k) % 4, z), device_id_type=MESH,
        )

    def sum_near():
        for k in range(4):
            arrived(pg_near.at[k], pg_sem.at[k])
        pg_far[d] = (pg_near[0] + pg_near[1]) + (pg_near[2] + pg_near[3])
        for k in range(1, 4):
            far_copy(k).start()

    def backward(n, carry):
        j = 1 - n
        rows = block_rows(j)
        arrived(g_in.at[rows], g_sem.at[j])
        acc[rows, :] = jnp.zeros((BLOCK, 1024), jnp.float32)

        def feed_back(q, carry):
            grad_act = dot_nt(g_in[rows, :], wud[q, 1024:2048, :])
            wide[rows, :] = (grad_act * slope[q, rows, :].astype(jnp.float32)).astype(jnp.bfloat16)
            acc[rows, :] += dot_nt(wide[rows, :], wud[q, 0:1024, :])
            return carry

        lax.fori_loop(0, 4, feed_back, 0)

        def middle(rows):
            dv = norm_back(after[rows, :], vector(3), acc[rows, :])
            normed[rows, :] = (g_in[rows, :].astype(jnp.float32) + dv).astype(jnp.bfloat16)

        over_rows(j, middle)
        wide[rows, :] = dot_nt(normed[rows, :], wo[...].reshape(1024, 1024)).astype(jnp.bfloat16)
        for core in range(2):
            for block in range(2):

                @pl.when(jnp.logical_and(s == core, j == block))
                def _():
                    def back_pair(pair, carry):
                        back_rows(pair, core, block)
                        dkv_copy(block, pair).start()
                        return carry

                    lax.fori_loop(0, 8, back_pair, 0)

        @pl.when(j == 0)
        def _():
            for q in range(4):
                is_here = jnp.logical_and(role == s, z == q)

                @pl.when(is_here)
                def _():
                    pltpu.make_async_copy(
                        pg.at[2 * q : 2 * q + 2], pg_near.at[contribution], pg_sem.at[contribution]
                    ).start()

                @pl.when(jnp.logical_not(is_here))
                def _():
                    pg_copy(q).start()

        acc[rows, :] = jnp.zeros((BLOCK, 1024), jnp.float32)

        def project_back(q, carry):
            for p in range(2):
                pair = 2 * q + p
                dkv_copy(j, pair).wait()
                dq = q_own[pair, rows, :].astype(jnp.float32)
                dk = dkv_own[pair, 0, rows, :].astype(jnp.float32) + dkv_recv[pair, 0, rows, :].astype(jnp.float32)
                dv = dkv_own[pair, 1, rows, :].astype(jnp.float32) + dkv_recv[pair, 1, rows, :].astype(jnp.float32)
                dk = pltpu.roll(dk * HEAD_DIM ** (-0.5), 64, 1)
                gt[:, p * 384 : p * 384 + 128] = jnp.where(first, dq, dk).astype(jnp.bfloat16)
                gt[:, p * 384 + 128 : p * 384 + 256] = jnp.where(first, dv, dq).astype(jnp.bfloat16)
                gt[:, p * 384 + 256 : p * 384 + 384] = jnp.where(first, dk, dv).astype(jnp.bfloat16)
            acc[rows, :] += dot_nt(gt[...], wq[q])
            return carry

        lax.fori_loop(0, 4, project_back, 0)

        @pl.when(jnp.logical_and(j == 0, role == 0))
        def _():
            sum_near()

        hand_copies(j, 1).wait_send()

        def give_back(rows):
            dv = norm_back(x_in[rows, :].astype(jnp.float32), vector(0), acc[rows, :])
            y_out[rows, :] = (normed[rows, :].astype(jnp.float32) + dv).astype(jnp.bfloat16)

        over_rows(j, give_back)

        @pl.when(role == 0)
        def _():
            hand_copies(j, 3).start()

        @pl.when(jnp.logical_and(role == 1, j == 1))
        def _():
            hand_copies(1, 2).start()

        @pl.when(jnp.logical_and(role == 1, j == 0))
        def _():
            hand_copies(0, 2).start()
            hand_copies(1, 2).wait_send()
            hand_copies(0, 2).wait_send()
            for block in range(2):
                hand_copies(block, 3).start()

        return carry

    lax.fori_loop(0, 2, backward, 0)
    @pl.when(role == 1)
    def _():
        sum_near()

    for k in range(1, 4):
        arrived(pg_far.at[(d + k) % 4], far_sem.at[(d + k) % 4])
    total_pg = (pg_far[0] + pg_far[1]) + (pg_far[2] + pg_far[3])
    for p in range(2):
        keys, values = total_pg[p, 0], total_pg[p, 1]
        sum_out[:, p * 256 : p * 256 + 128] = jnp.where(first16, keys, pltpu.roll(values, 64, 1))
        sum_out[:, p * 256 + 128 : p * 256 + 256] = jnp.where(first16, pltpu.roll(keys, 64, 1), values)
    hidden_core[s] = dot_nt(sum_out[...].astype(jnp.bfloat16), pw[...])
    sends.start(hidden_core.at[s], hidden_core.at[s], core_sem.at[s], (other, d, z))
    arrived(hidden_core.at[other], core_sem.at[other])
    hidden_all[z] = hidden_core[0] + hidden_core[1]
    for k in range(1, 4):
        sends.start(hidden_all.at[z], hidden_all.at[z], hidden_sem.at[z], (s, d, (z + k) % 4))
    for k in range(1, 4):
        arrived(hidden_all.at[(z + k) % 4], hidden_sem.at[(z + k) % 4])
    hidden_out[...] = (hidden_all[0] + hidden_all[1]) + (hidden_all[2] + hidden_all[3])

    @pl.when(jnp.logical_not(feeds_zero))
    def _():
        lax.fori_loop(0, 3, supply_done, 0)

    firsts_done(jnp.logical_not(feeds_zero), 0)
    firsts_done(True, 1)

    def relays_done(m, carry):
        for stage in range(3):
            relay_copy(m, stage).wait_send()
        return carry

    lax.fori_loop(0, UNITS, relays_done, 0)
    cot_copies(lambda copy: copy.wait_send())
    for k in range(1, 4):
        far_copy(k).wait_send()
    for q in range(4):

        @pl.when(jnp.logical_not(jnp.logical_and(role == s, z == q)))
        def _():
            pg_copy(q).wait_send()

    for j in range(2):

        hand_copies(j, 3).wait_send()

    for k in range(2):
        arrived(act_out.at[k], act_sem.at[k])
        arrived(ig_out.at[k], ig_sem.at[k])
    sends.finish()


def run_layers(x, cot, wq, wo, wu, wd, *small):
    bf, f32 = jnp.bfloat16, jnp.float32
    vm, dma = pltpu.VMEM, pltpu.SemaphoreType.DMA
    rows = 2 * BLOCK
    width = x.shape[-1]
    pairs = width // 128
    pw = small[-3]
    scratch = [
        vm((8, width), f32), vm((16, pw.shape[1]), f32), vm((16, pw.shape[1]), bf), vm((4,) + wq.shape, bf), vm((4,) + wo.shape, bf), vm((4, 2 * wu.shape[0], width), bf),
        vm((4, 8, width), f32), vm((4, 16, pw.shape[1]), bf),
        vm((rows, width), bf), vm((rows, width), bf), vm((rows, width), bf), vm((rows, width), bf),
        vm((2, pairs, 2, rows, 128), bf), vm((pairs, rows, 128), bf), vm((rows, width), bf),
        vm((pairs, rows, 128), f32), vm((6, BLOCK, BLOCK), f32), vm((rows, width), f32), vm((rows, width), f32),
        vm((4, rows, wu.shape[1]), bf), vm((rows, wu.shape[1]), bf),
        vm((pairs, 2, 16, 128), f32), vm((4, 2, 2, 16, 128), f32), vm((4, 2, 2, 16, 128), f32), vm((2, 16, pw.shape[0]), f32), vm((4, 16, pw.shape[0]), f32),
        vm((2, 4, BLOCK, BLOCK), f32),
        vm((pairs, 2, rows, 128), bf), vm((pairs, 2, rows, 128), bf), vm((pairs, 2, rows, 128), bf),
        vm((pairs, 128, 128), bf), vm((pairs, 128, 128), bf),
        vm((BLOCK, wq.shape[1]), bf),
        dma((96,)), dma((4,)), dma((4,)), dma((2,)), dma((2,)), dma((2,)), dma((2,)), dma((4,)),
        dma((2, 4)), dma((2, 4)), dma((2, 4)), dma((2, 4)),
        dma((UNITS,)), dma((UNITS,)), dma((UNITS,)), dma((UNITS,)), dma((6, 2)), dma((UNITS, 2)), dma((UNITS,)), dma((UNITS,)), dma((UNITS,)),
        pltpu.SemaphoreType.REGULAR,
        dma((2, 4)), dma((2, 4)), dma((2, pairs)), dma((2, pairs)), dma((4,)), dma((4,)), dma((2,)), dma((4,)),
        dma((4, 2)), dma((2,)), dma((4,)), dma((3,)), dma((8,)),
    ]
    anywhere = pl.BlockSpec(memory_space=pl.ANY)
    local = pl.BlockSpec(memory_space=pltpu.VMEM)
    return pl.pallas_call(
        layer_kernel,
        out_shape=(
            jax.ShapeDtypeStruct(x.shape, bf), jax.ShapeDtypeStruct(x.shape, bf),
            jax.ShapeDtypeStruct((16, pw.shape[1]), f32), jax.ShapeDtypeStruct((16, pw.shape[0]), f32),
            jax.ShapeDtypeStruct((16, pw.shape[0]), f32),
        ),
        in_specs=[anywhere] * 6 + [local] * 9 + [anywhere] + [local] * 3 + [pl.BlockSpec(memory_space=pltpu.SMEM)],
        out_specs=(anywhere, anywhere, local, local, local),
        scratch_shapes=scratch,
        name="two_layers",
        compiler_params=pltpu.CompilerParams(
            collective_id=0, has_side_effects=True, vmem_limit_bytes=63 * 2**20
        ),
    )(x, cot, wq, wo, wu, wd, *small)


def prefix_kernel(
    prefix_sum, hidden_grad, hidden_act, table, mid_w,
    table_grad, mid_w_grad, mid_b_grad, prefix_w_grad, prefix_b_grad, table_full,
):
    prefix_low = prefix_sum[...].astype(jnp.bfloat16)
    act = hidden_act[...]
    prefix_b_grad[...] = jnp.sum(prefix_low.astype(jnp.float32), axis=0, keepdims=True)
    prefix_w_grad[...] = dot_tn(act.astype(jnp.bfloat16), prefix_low)
    pre_grad = (hidden_grad[...] * (1.0 - act * act)).astype(jnp.bfloat16)
    mid_b_grad[...] = jnp.sum(pre_grad.astype(jnp.float32), axis=0, keepdims=True)
    table_full[...] = jnp.zeros(table_full.shape, jnp.float32)
    table_full[0:PREFIX, :] = table[...].astype(jnp.float32)
    mid_w_grad[...] = dot_tn(table_full[...].astype(jnp.bfloat16), pre_grad)
    table_grad[...] = dot_nt(pre_grad, mid_w[...])[0:PREFIX, :]


def run_prefix_back(prefix_sum, hidden_grad, hidden_act, table, mid_w):
    f32 = jnp.float32
    hidden, own = mid_w.shape[1], prefix_sum.shape[1]
    return pl.pallas_call(
        prefix_kernel,
        out_shape=tuple(
            jax.ShapeDtypeStruct(shape, f32)
            for shape in (table.shape, mid_w.shape, (1, hidden), (hidden, own), (1, own))
        ),
        scratch_shapes=[pltpu.VMEM((16, table.shape[1]), f32)],
        name="prefix_network",
        compiler_params=pltpu.CompilerParams(vmem_limit_bytes=48 * 2**20),
    )(prefix_sum, hidden_grad, hidden_act, table, mid_w)


def pair_body(
    layer_input, cotangent, example_lengths, attn_gain, attn_shift, query_key_value_weight, qkv_bias,
    attention_output_weight, out_bias, ffn_gain, ffn_shift, up_projection_weight, up_projection_bias,
    down_projection_weight, down_bias, prefix_table, mid_weight, mid_bias, prefix_weight, prefix_bias,
):
    activations, input_grads, prefix_sum, hidden_grad, hidden_act = run_layers(
        layer_input[:, 0], cotangent[:, 0], query_key_value_weight[0], attention_output_weight[0],
        up_projection_weight[0], down_projection_weight[0],
        attn_gain, attn_shift, out_bias, ffn_gain, ffn_shift, down_bias, up_projection_bias, qkv_bias,
        prefix_table, mid_weight, mid_bias, prefix_weight, prefix_bias, example_lengths[:, 0],
    )
    table_grad, mid_weight_grad, mid_bias_grad, prefix_weight_grad, prefix_bias_grad = run_prefix_back(
        prefix_sum, hidden_grad, hidden_act, prefix_table, mid_weight
    )
    return (
        activations[None, :, None], input_grads[None, :, None],
        table_grad, mid_weight_grad, mid_bias_grad[0], prefix_weight_grad, prefix_bias_grad[0],
    )


def solution(mesh):
    placed = (
        P(None, "dp", "mp", None),
        P(None, "dp", "mp", None),
        P(None, "dp", None),
        P("section", None),
        P("section", None),
        P("section", None, "mp"),
        P("section", "mp"),
        P("section", "mp", None),
        P("section", None),
        P("section", None),
        P("section", None),
        P("section", None, "mp"),
        P("section", "mp"),
        P("section", "mp", None),
        P("section", None),
        P(),
        P(),
        P(),
        P(None, ("section", "mp")),
        P(("section", "mp")),
    )
    paired = mesh.shape["mp"] == 4 and mesh.shape["dp"] == 4
    return jax.shard_map(
        pair_body if paired else body,
        mesh=mesh,
        in_specs=placed,
        out_specs=(
            P("section", None, "dp", "mp", None),
            P("section", None, "dp", "mp", None),
            P(),
            P(),
            P(),
            P(None, ("section", "mp")),
            P(("section", "mp")),
        ),
        check_vma=False,
    )
```

```python
import jax
import jax.numpy as jnp
from jax import lax
from jax.experimental import pallas as pl
from jax.experimental.pallas import tpu as pltpu
from jax.sharding import PartitionSpec as P

HEAD_DIM = 64
PREFIX = 10
SEQ_LEN = 1024


EPSILON = 1e-05
NEG_LARGE = -1e30
GELU_A = 0.7978845608028654
GELU_B = 0.044715


def norm_rows(values, gain, shift):
    average = jnp.mean(values, axis=-1, keepdims=True)
    centred = values - average
    spread = jnp.mean(centred * centred, axis=-1, keepdims=True)
    return centred * lax.rsqrt(spread + EPSILON) * gain + shift


def norm_input_grad(values, gain, shift, incoming):

    def apply_norm(inputs):
        return norm_rows(inputs, gain, shift)

    norm_value, norm_back = jax.vjp(apply_norm, values)
    return norm_back(incoming)[0]


def gelu_tanh(values):
    return jax.nn.gelu(values, approximate=True)


def visible_of(lengths, first_row, count):
    run_ends = jnp.cumsum(lengths, axis=-1)
    keys_at = jnp.arange(SEQ_LEN, dtype=jnp.int32)
    query_at = first_row + jnp.arange(count, dtype=jnp.int32)
    key_seg = jnp.sum((keys_at[None, :, None] >= run_ends[:, None, :]).astype(jnp.int32), axis=-1)
    query_seg = jnp.sum(
        (query_at[None, :, None] >= run_ends[:, None, :]).astype(jnp.int32), axis=-1
    )
    causal = (query_at[:, None] >= keys_at[None, :])[None]
    inside = (query_seg[:, :, None] == key_seg[:, None, :]) & causal
    leading = jnp.ones((lengths.shape[0], count, PREFIX), dtype=bool)
    return jnp.concatenate([leading, inside], axis=2)


def gather_rows(piece):
    return lax.all_gather(piece, "mp", axis=1, tiled=True)


def reduce_rows(partial_sum):
    return lax.psum_scatter(
        partial_sum.astype(jnp.bfloat16), "mp", scatter_dimension=1, tiled=True
    ).astype(jnp.float32)


def with_prefix(prefix_kv, pair_keys, pair_values, heads_count):
    prefix_pair = prefix_kv.reshape(PREFIX, heads_count, 2, HEAD_DIM)
    key_rows = jnp.concatenate([prefix_pair[None, :, :, 0], pair_keys], axis=1)
    value_rows = jnp.concatenate([prefix_pair[None, :, :, 1], pair_values], axis=1)
    return (key_rows, value_rows)


def attend(query_rows, key_rows, value_rows, visible):
    score_scale = HEAD_DIM ** (-0.5)
    scores = (
        jnp.einsum("sqhd,skhd->shqk", query_rows, key_rows, preferred_element_type=jnp.float32)
        * score_scale
    )
    scores = jnp.where(visible[:, None], scores, NEG_LARGE)
    highest = jnp.max(scores, axis=-1, keepdims=True)
    raised = jnp.exp(scores - highest)
    softmax_probs = raised / jnp.sum(raised, axis=-1, keepdims=True)
    probs_low = softmax_probs.astype(jnp.bfloat16)
    head_mixed_rows = jnp.einsum(
        "shqk,skhd->sqhd", probs_low, value_rows, preferred_element_type=jnp.float32
    )
    batch_size, query_count, heads_count, head_size = head_mixed_rows.shape
    head_mixed_rows = head_mixed_rows.astype(jnp.bfloat16).reshape(
        batch_size, query_count, heads_count * head_size
    )
    return (softmax_probs, probs_low, head_mixed_rows)


def attend_back(grad_mix, query_rows, key_rows, value_rows, softmax_probs, probs_low):
    grad_heads = grad_mix.reshape(query_rows.shape)
    grad_probs = jnp.einsum(
        "sqhd,skhd->shqk", grad_heads, value_rows, preferred_element_type=jnp.float32
    )
    value_grad = jnp.einsum(
        "shqk,sqhd->skhd", probs_low, grad_heads, preferred_element_type=jnp.float32
    )
    row_term = jnp.sum(grad_probs * softmax_probs, axis=-1, keepdims=True)
    grad_scores = (softmax_probs * (grad_probs - row_term)).astype(jnp.bfloat16)
    score_scale = HEAD_DIM ** (-0.5)
    query_grad = (
        jnp.einsum("shqk,skhd->sqhd", grad_scores, key_rows, preferred_element_type=jnp.float32)
        * score_scale
    )
    key_grad = (
        jnp.einsum("shqk,sqhd->skhd", grad_scores, query_rows, preferred_element_type=jnp.float32)
        * score_scale
    )
    return (query_grad, key_grad, value_grad)


def prefix_part(key_grad, value_grad):
    pair_sum = jnp.stack(
        [jnp.sum(key_grad[:, :PREFIX], axis=0), jnp.sum(value_grad[:, :PREFIX], axis=0)], axis=2
    )
    return pair_sum.reshape(PREFIX, -1)


def tensor_forward(own_rows, weights, prefix_kv, visible):
    (
        attn_gain,
        attn_shift,
        query_key_value_weight,
        qkv_bias,
        attention_output_weight,
        out_bias,
        ffn_gain,
        ffn_shift,
        up_projection_weight,
        up_projection_bias,
        down_projection_weight,
        down_bias,
        out_full,
    ) = weights
    normed = norm_rows(own_rows, attn_gain, attn_shift).astype(jnp.bfloat16)
    normalized_input_rows = gather_rows(normed)
    batch_size, seq_len, model_width = normalized_input_rows.shape
    heads_here = query_key_value_weight.shape[1] // (3 * HEAD_DIM)
    projected = (
        jnp.einsum(
            "naj,jk->nak",
            normalized_input_rows,
            query_key_value_weight,
            preferred_element_type=jnp.float32,
        )
        + qkv_bias
    )
    triple = projected.astype(jnp.bfloat16).reshape(batch_size, seq_len, heads_here, 3, HEAD_DIM)
    query_rows = triple[:, :, :, 0]
    key_rows, value_rows = with_prefix(
        prefix_kv, triple[:, :, :, 1], triple[:, :, :, 2], heads_here
    )
    softmax_probs, probs_low, head_mixed_rows = attend(query_rows, key_rows, value_rows, visible)
    attn_part = reduce_rows(
        jnp.einsum(
            "hgm,mt->hgt",
            head_mixed_rows,
            attention_output_weight,
            preferred_element_type=jnp.float32,
        )
    )
    after_attn = own_rows + attn_part + out_bias
    normed_two = norm_rows(after_attn, ffn_gain, ffn_shift).astype(jnp.bfloat16)
    second_norm_rows = gather_rows(normed_two)
    up_pre = (
        jnp.einsum(
            "rmy,yq->rmq",
            second_norm_rows,
            up_projection_weight,
            preferred_element_type=jnp.float32,
        )
        + up_projection_bias
    )
    gelu_output_rows = gelu_tanh(up_pre).astype(jnp.bfloat16)
    mlp_part = reduce_rows(
        jnp.einsum(
            "epj,jq->epq",
            gelu_output_rows,
            down_projection_weight,
            preferred_element_type=jnp.float32,
        )
    )
    result = after_attn + mlp_part + down_bias
    kept_values = (query_rows, key_rows, value_rows, softmax_probs, probs_low, after_attn, up_pre)
    return (result, kept_values)


def tensor_backward(own_rows, arriving, weights, kept_values):
    (
        attn_gain,
        attn_shift,
        query_key_value_weight,
        qkv_bias,
        attention_output_weight,
        out_bias,
        ffn_gain,
        ffn_shift,
        up_projection_weight,
        up_projection_bias,
        down_projection_weight,
        down_bias,
        out_full,
    ) = weights
    query_rows, key_rows, value_rows, softmax_probs, probs_low, after_attn, up_pre = kept_values
    gradient_gathered = gather_rows(arriving)
    gradient_activation = jnp.einsum(
        "bhi,vi->bhv", gradient_gathered, down_projection_weight, preferred_element_type=jnp.float32
    )
    gelu_value, gelu_back = jax.vjp(gelu_tanh, up_pre)
    gradient_up_projection = gelu_back(gradient_activation)[0].astype(jnp.bfloat16)
    grad_two = reduce_rows(
        jnp.einsum(
            "yca,ja->ycj",
            gradient_up_projection,
            up_projection_weight,
            preferred_element_type=jnp.float32,
        )
    )
    grad_after = norm_input_grad(after_attn, ffn_gain, ffn_shift, grad_two)
    grad_mid = (grad_after + arriving.astype(jnp.float32)).astype(jnp.bfloat16)
    middle_gathered = gather_rows(grad_mid)
    grad_mix = jnp.einsum(
        "taq,kq->tak", middle_gathered, attention_output_weight, preferred_element_type=jnp.float32
    ).astype(jnp.bfloat16)
    query_grad, key_grad, value_grad = attend_back(
        grad_mix, query_rows, key_rows, value_rows, softmax_probs, probs_low
    )
    prefix_g = prefix_part(key_grad, value_grad)
    batch_size, seq_len = (query_grad.shape[0], query_grad.shape[1])
    gradient_query_key_value = jnp.stack(
        [query_grad, key_grad[:, PREFIX:], value_grad[:, PREFIX:]], axis=3
    )
    gradient_query_key_value = gradient_query_key_value.astype(jnp.bfloat16).reshape(
        batch_size, seq_len, -1
    )
    grad_one = reduce_rows(
        jnp.einsum(
            "tvq,xq->tvx",
            gradient_query_key_value,
            query_key_value_weight,
            preferred_element_type=jnp.float32,
        )
    )
    grad_input = norm_input_grad(own_rows, attn_gain, attn_shift, grad_one)
    grad_input = (grad_input + grad_mid.astype(jnp.float32)).astype(jnp.bfloat16)
    return (grad_input, prefix_g)


def prefix_back(prefix_sum, hidden_grad, hidden_act, hidden_low, prefix_table, mid_weight):
    prefix_low = prefix_sum.astype(jnp.bfloat16)
    prefix_bias_grad = jnp.sum(prefix_low.astype(jnp.float32), axis=0)
    prefix_weight_grad = jnp.dot(hidden_low.T, prefix_low, preferred_element_type=jnp.float32)
    pre_grad = (hidden_grad * (1.0 - hidden_act * hidden_act)).astype(jnp.bfloat16)
    mid_bias_grad = jnp.sum(pre_grad.astype(jnp.float32), axis=0)
    mid_weight_grad = jnp.dot(prefix_table.T, pre_grad, preferred_element_type=jnp.float32)
    table_grad = jnp.dot(pre_grad, mid_weight.T, preferred_element_type=jnp.float32)
    return (table_grad, mid_weight_grad, mid_bias_grad, prefix_weight_grad, prefix_bias_grad)


def both_layers(piece):
    return lax.all_gather(piece[0], "section", axis=0, tiled=False)


def body(
    layer_input,
    cotangent,
    example_lengths,
    attn_gain,
    attn_shift,
    query_key_value_weight,
    qkv_bias,
    attention_output_weight,
    out_bias,
    ffn_gain,
    ffn_shift,
    up_projection_weight,
    up_projection_bias,
    down_projection_weight,
    down_bias,
    prefix_table,
    mid_weight,
    mid_bias,
    prefix_weight,
    prefix_bias,
):
    layers = lax.axis_size("section")
    section_index = lax.axis_index("section")
    hidden_pre = jnp.dot(
        prefix_table, mid_weight, preferred_element_type=jnp.float32
    ) + mid_bias.astype(jnp.float32)
    hidden_act = jnp.tanh(hidden_pre)
    hidden_low = hidden_act.astype(jnp.bfloat16)
    prefix_kv = (
        jnp.dot(hidden_low, prefix_weight, preferred_element_type=jnp.float32)
        + prefix_bias.astype(jnp.float32)
    ).astype(jnp.bfloat16)
    prefix_all = lax.all_gather(prefix_kv, "section", axis=0, tiled=False)
    floats = [
        both_layers(piece).astype(jnp.float32)
        for piece in (attn_gain, attn_shift, qkv_bias, out_bias, ffn_gain, ffn_shift,
                      up_projection_bias, down_bias)
    ]
    matrices = [
        both_layers(piece)
        for piece in (query_key_value_weight, attention_output_weight,
                      up_projection_weight, down_projection_weight)
    ]

    def weights_of(layer):
        g1, s1, bq, bo, g2, s2, bu, bd = [piece[layer] for piece in floats]
        wq, wo, wu, wd = [piece[layer] for piece in matrices]
        return (g1, s1, wq, bq, wo, bo, g2, s2, wu, bu, wd, bd, wo)

    batch_count = layer_input.shape[0]
    own_input = lax.dynamic_index_in_dim(layer_input, section_index, 0, keepdims=False)
    own_cotangent = lax.dynamic_index_in_dim(cotangent, section_index, 0, keepdims=False)
    lengths = lax.dynamic_index_in_dim(example_lengths, section_index, 0, keepdims=False)
    visible = visible_of(lengths, 0, SEQ_LEN)
    entering = own_input
    entered, produced, kept = [], [], []
    for layer in range(layers):
        entered.append(entering.astype(jnp.float32))
        result, kept_values = tensor_forward(
            entered[layer], weights_of(layer), prefix_all[layer], visible
        )
        entering = result.astype(jnp.bfloat16)
        produced.append(entering)
        kept.append(kept_values)
    gradient = own_cotangent
    sent_grads = [None] * layers
    prefix_parts = [None] * layers
    for layer in reversed(range(layers)):
        gradient, prefix_parts[layer] = tensor_backward(
            entered[layer], gradient, weights_of(layer), kept[layer]
        )
        sent_grads[layer] = gradient
    activations = lax.all_to_all(jnp.stack(produced), "section", 0, 0, tiled=False)
    input_grads = lax.all_to_all(jnp.stack(sent_grads), "section", 0, 0, tiled=False)
    prefix_sum = lax.psum(jnp.stack(prefix_parts), ("dp", "section"))
    prefix_sum = lax.dynamic_index_in_dim(prefix_sum, section_index, 0, keepdims=False)
    hidden_part = jnp.dot(
        prefix_sum.astype(jnp.bfloat16), prefix_weight.T, preferred_element_type=jnp.float32
    )
    hidden_grad = lax.psum(hidden_part, ("section", "mp"))
    return (activations[None], input_grads[None]) + prefix_back(
        prefix_sum, hidden_grad, hidden_act, hidden_low, prefix_table, mid_weight
    )


MESH = pl.DeviceIdType.MESH
BLOCK = 256
LOG2E = 1.4426950408889634
CHUNK = 128
UNITS = 12
AHEAD = 10
UNIT_ROWS = 512
PART_ROWS = UNIT_ROWS // 8


def role_of(z):
    return (((z + 1) // 2) + 1) % 2


def block_of(s, j):
    return j * 3 + s * (1 - 2 * j)


def core_of(block):
    return ((block + 1) // 2) % 2


def guarded(when, action):
    if when is None:
        action()
    else:
        pl.when(when)(action)


def dot_nn(a, b):
    return lax.dot_general(a, b, (((1,), (0,)), ((), ())), preferred_element_type=jnp.float32)


def dot_nt(a, b):
    return lax.dot_general(a, b, (((1,), (1,)), ((), ())), preferred_element_type=jnp.float32)


def dot_tn(a, b):
    return lax.dot_general(a, b, (((0,), (0,)), ((), ())), preferred_element_type=jnp.float32)


class Sends:
    def __init__(self, sems):
        self.sems, self.used, self.pending = sems, 0, []

    def start(self, src, dst, recv_sem, target, when=None):
        copy = pltpu.make_async_remote_copy(
            src_ref=src, dst_ref=dst, send_sem=self.sems.at[self.used], recv_sem=recv_sem,
            device_id=target, device_id_type=MESH,
        )
        self.used += 1
        guarded(when, copy.start)
        self.pending.append((when, copy))

    def start_or_keep(self, src, dst, recv_sem, target, is_here, when=True):
        @pl.when(jnp.logical_and(when, is_here))
        def _():
            pltpu.make_async_copy(src, dst, recv_sem).start()

        self.start(src, dst, recv_sem, target, when=jnp.logical_and(when, jnp.logical_not(is_here)))

    def finish(self):
        for when, copy in self.pending:
            guarded(when, copy.wait_send)
        self.pending = []


def layer_kernel(
    x_hbm, cot_hbm, wq_hbm, wo_hbm, wu_hbm, wd_hbm,
    g1, s1, bo, g2, s2, bd, bu, bq, table, mid_w, mid_b, pw, pb, lengths,
    act_out, ig_out, sum_out, hidden_out, tanh_out,
    vec_own, pre_full, pre_own, wq, wo, wud, vec, pre,
    x_in, g_in, y_out, normed, kv, q_own, o_own, lse, bias, after, acc, slope, wide,
    pg, pg_near, pg_far, hidden_core, hidden_all, ts, dkv_own, dkv_send, dkv_recv, kp, vp, gt,
    ssem, vec_sem, pre_sem, x_sem, g_sem, act_sem, ig_sem, own_sem, z_sem, a_sem, b_sem, c_sem,
    zr_sem, ar_sem, br_sem, cr_sem, fs_sem, zs_sem, as_sem, bs_sem, cs_sem, go_sem,
    kv_ssem, kv_rsem, dkv_ssem, dkv_rsem, pg_sem, far_sem, core_sem, hidden_sem,
    hand_sem, cot_sem, x_ssem, pg_ssem, far_ssem, mid_sem,
):
    s, d, z = lax.axis_index("section"), lax.axis_index("dp"), lax.axis_index("mp")
    role, micro = role_of(z), z // 2
    other = 1 - s
    partner = z + 1 - 2 * (z % 2)
    x_near, y_near = d + 1 - 2 * (d % 2), (d + 2) % 4
    near1 = jnp.where(s == 0, x_near, y_near)
    near2 = jnp.where(s == 0, y_near, x_near)
    sends = Sends(ssem)

    barrier = pltpu.get_barrier_semaphore()
    for ds in range(2):
        for dz in range(4):
            if ds or dz:
                pl.semaphore_signal(barrier, inc=1, device_id=((s + ds) % 2, d, (z + dz) % 4), device_id_type=MESH)
    for near in (x_near, y_near, 3 - d):
        pl.semaphore_signal(barrier, inc=1, device_id=(s, near, z), device_id_type=MESH)
    pl.semaphore_wait(barrier, 10)

    def arrived(dst, sem):
        pltpu.make_async_remote_copy(
            src_ref=dst, dst_ref=dst, send_sem=ssem.at[0], recv_sem=sem,
            device_id=(other, d, z), device_id_type=MESH,
        ).wait_recv()

    low_plane, high_plane = jnp.where(s == 0, 1, 0), jnp.where(s == 0, 2, 3)
    planes = (low_plane, high_plane)
    mine = s == core_of(z)
    row_slot = pl.ds(pl.multiple_of((z // 2) * BLOCK, BLOCK), BLOCK)

    def send_small(when):
        for t in planes:
            for h in range(2):
                is_here = jnp.logical_and(z == t, s == h)
                sends.start_or_keep(pre_own, pre.at[z], pre_sem.at[z], (h, d, t), is_here, when)

    def row_copies(source, landing, send_sem, sem, chips, then):
        for k, chip in enumerate(chips):

            @pl.when(jnp.logical_and(mine, z != chip))
            def _():
                then(pltpu.make_async_remote_copy(
                    src_ref=source.at[k], dst_ref=landing.at[row_slot], send_sem=send_sem.at[k],
                    recv_sem=sem.at[z // 2], device_id=(s, d, chip), device_id_type=MESH,
                ))

    def keep_rows(source, landing, sem, chips):
        for k, chip in enumerate(chips):

            @pl.when(jnp.logical_and(mine, z == chip))
            def _():
                pltpu.make_async_copy(source.at[k], landing.at[row_slot], sem.at[z // 2]).start()

    def x_copies(then):
        row_copies(x_hbm, x_in, x_ssem, x_sem, (1, 2), then)

    def cot_copies(then):
        row_copies(cot_hbm, g_in, cot_sem, g_sem, (0, 3), then)

    keep_rows(x_hbm, x_in, x_sem, (1, 2))
    keep_rows(cot_hbm, g_in, g_sem, (0, 3))

    toward = jnp.where(z < 2, 1, -1)

    def quarter(i):
        return (z + 4 + toward * i) % 4

    def taker(i):
        low, high = (z + 3 - i) % 4, (z + 1 + i) % 4
        return jnp.where(low == low_plane, low, high), jnp.logical_or(low == low_plane, high == high_plane)

    swapped = (d % 2) * 2 + d // 2
    place = jnp.where(s == 0, d, swapped)
    pair_start = (place // 2) * 2
    far_start = 2 - pair_start
    firsts = ((wq_hbm, wq), (wo_hbm, wo))

    def eighths(rows, start, count, h):
        return pl.ds(pl.multiple_of((start + 4 * h) * rows, rows), rows * count)

    def supply_first(w, i, then):
        t, taken = taker(i)
        held, full = firsts[w]

        @pl.when(taken)
        def _():
            for h in range(2):
                at = eighths(held.shape[0] // 8, swapped if h else d, 1, h)
                then(pltpu.make_async_remote_copy(
                    src_ref=held.at[at], dst_ref=full.at[z, at], send_sem=fs_sem.at[3 * w + i, h],
                    recv_sem=z_sem.at[w, z], device_id=(h, d, t), device_id_type=MESH,
                ))

    def supply_firsts(when, w):
        @pl.when(when)
        def _():
            def one(i, carry):
                supply_first(w, i, lambda copy: copy.start())
                return carry

            lax.fori_loop(0, 3, one, 0)

    def firsts_done(when, w):
        @pl.when(when)
        def _():
            def one(i, carry):
                supply_first(w, i, lambda copy: copy.wait_send())
                return carry

            lax.fori_loop(0, 3, one, 0)

    def supply_copies(i, c, then):
        t, taken = taker(i)
        held, base = ((wu_hbm, 0), (wd_hbm, 1024))[c // 2]

        @pl.when(taken)
        def _():
            for h in range(2):
                at = eighths(PART_ROWS, swapped if h else d, 1, h)
                start = (c % 2) * UNIT_ROWS + at.start
                then(pltpu.make_async_remote_copy(
                    src_ref=held.at[pl.ds(pl.multiple_of(start, PART_ROWS), PART_ROWS)],
                    dst_ref=wud.at[z, pl.ds(pl.multiple_of(base + start, PART_ROWS), PART_ROWS)],
                    send_sem=zs_sem.at[4 * i + c, h], recv_sem=zr_sem.at[4 * i + c],
                    device_id=(h, d, t), device_id_type=MESH,
                ))

    def supply_all(i, carry):
        for c in range(4):
            supply_copies(i, c, lambda copy: copy.start())
        return carry

    def supply_done(i, carry):
        for c in range(4):
            supply_copies(i, c, lambda copy: copy.wait_send())
        return carry

    feeds_zero = jnp.logical_and(role == 1, s == 0)
    feeds_zero_late = jnp.logical_and(role == 0, s == 0)
    feeds_one = jnp.logical_and(role == 0, s == 1)
    feeds_one_late = jnp.logical_and(role == 1, s == 1)
    supply_firsts(s == 0, 0)

    @pl.when(feeds_one)
    def _():
        for w in range(2):
            supply_first(w, 0, lambda copy: copy.start())
        supply_all(0, 0)

    mid_copies = mid_w.shape[1] // 128

    def mid_copy(n, half):
        return pltpu.make_async_copy(
            mid_w.at[half * 512 : half * 512 + 512, n * 128 : n * 128 + 128], q_own.at[2 * n + half],
            mid_sem.at[2 * n + half],
        )

    for n in range(mid_copies):
        for half in range(2):
            mid_copy(n, half).start()
    for k, row in enumerate((g1, s1, bo, g2, s2, bd)):
        vec_own[k : k + 1, :] = row[...].astype(jnp.float32)

    @pl.when(role == s)
    def _():
        pltpu.make_async_copy(vec_own, vec.at[0], vec_sem.at[0]).start()

    sends.start(vec_own, vec.at[0], vec_sem.at[0], (other, d, z), when=role == s)
    tanh_out[...] = jnp.zeros(tanh_out.shape, jnp.float32)
    for n in range(mid_copies):
        for half in range(2):
            mid_copy(n, half).wait()
        cols = slice(n * 128, n * 128 + 128)
        part_sum = dot_nn(table[:, 0:512], q_own[2 * n]) + dot_nn(table[:, 512:1024], q_own[2 * n + 1])
        tanh_out[0:PREFIX, cols] = jnp.tanh(part_sum + mid_b[...].astype(jnp.float32).reshape(1, -1)[:, cols])
    pre_full[...] = dot_nn(tanh_out[...].astype(jnp.bfloat16), pw[...]) + pb[...].astype(jnp.float32).reshape(1, -1)
    half_width = pre_full.shape[1]
    for k, row in enumerate((bu, bq)):
        for n in range(2):
            piece = row[:, n * half_width : min((n + 1) * half_width, row.shape[1])]
            pre_full[PREFIX + 2 * k + n : PREFIX + 2 * k + n + 1, 0 : piece.shape[1]] = piece.astype(jnp.float32)
    pre_own[...] = pre_full[...].astype(jnp.bfloat16)
    send_small(feeds_zero)
    firsts_done(feeds_zero, 0)
    supply_firsts(feeds_zero, 1)

    @pl.when(feeds_zero)
    def _():
        x_copies(lambda copy: copy.start())
    owned = ((wq_hbm, wq.at[z]), (wo_hbm, wo.at[z]), (wu_hbm, wud.at[z, 0:1024]), (wd_hbm, wud.at[z, 1024:2048]))
    for w, (held, full) in enumerate(owned):
        @pl.when(role == s)
        def _():
            pltpu.make_async_copy(held, full, own_sem.at[w]).start()

        sends.start(held, full, own_sem.at[w], (other, d, z), when=role == s)

    @pl.when(feeds_zero)
    def _():
        x_copies(lambda copy: copy.wait_send())
        lax.fori_loop(0, 3, supply_all, 0)

    @pl.when(feeds_one_late)
    def _():
        pl.semaphore_wait(go_sem, 1)

    send_small(feeds_one_late)
    supply_firsts(feeds_one_late, 0)
    supply_firsts(feeds_one_late, 1)

    first_units = [(w, i) for w in (0, 1) for i in range(1, 4)]

    def first_piece(w, i, start, count):
        full = firsts[w][1]
        return full.at[quarter(i), eighths(full.shape[1] // 8, start, count, s)]

    def relay_first(step):
        stages = [first_units[step - k] if 0 <= step - k < len(first_units) else None for k in range(4)]
        if stages[0]:
            w, i = stages[0]
            q = quarter(i)
            arrived(first_piece(w, i, place, 1), z_sem.at[w, q])
            sends.start(first_piece(w, i, place, 1), first_piece(w, i, place, 1), a_sem.at[w, q], (s, near1, z))
        if stages[1]:
            w, i = stages[1]
            q = quarter(i)
            arrived(first_piece(w, i, pair_start + 1 - place % 2, 1), a_sem.at[w, q])
            sends.start(first_piece(w, i, pair_start, 2), first_piece(w, i, pair_start, 2), b_sem.at[w, q], (s, near2, z))
        if stages[2]:
            w, i = stages[2]
            q = quarter(i)
            arrived(first_piece(w, i, far_start, 2), b_sem.at[w, q])
            sends.start(first_piece(w, i, 0, 4), first_piece(w, i, 0, 4), c_sem.at[w, q], (other, d, z))
        if stages[3]:
            w, i = stages[3]
            full = firsts[w][1]
            arrived(full.at[quarter(i), eighths(full.shape[1] // 8, 0, 4, other)], c_sem.at[w, quarter(i)])

    for step in range(len(first_units) + 3):
        relay_first(step)
        if step == 0:
            @pl.when(role == 0)
            def _():
                x_copies(lambda copy: copy.start())

            send_small(feeds_zero_late)
            supply_firsts(feeds_zero_late, 1)
        if step == 3:
            @pl.when(feeds_one)
            def _():
                pl.semaphore_signal(go_sem, inc=1, device_id=(1, d, partner), device_id_type=MESH)

                supply_first(0, 1, lambda copy: copy.start())

            send_small(feeds_one)
        if step == 6:
            @pl.when(feeds_one)
            def _():
                supply_first(1, 1, lambda copy: copy.start())


        @pl.when(feeds_zero_late)
        def _():
            if 1 <= step < 5:
                supply_copies(0, step - 1, lambda copy: copy.start())

    @pl.when(feeds_one_late)
    def _():
        lax.fori_loop(0, 3, supply_all, 0)

    def unit_piece(m, start, count, h):
        q = quarter(1 + m // 4)
        first_row = (m % 4) * UNIT_ROWS + (start + 4 * h) * PART_ROWS
        return wud.at[q, pl.ds(pl.multiple_of(first_row, PART_ROWS), PART_ROWS * count)]

    def relay_copy(m, stage):
        start, count = ((place, 1), (pair_start, 2), (0, 4))[stage]
        at = unit_piece(m, start, count, s)
        return pltpu.make_async_remote_copy(
            src_ref=at, dst_ref=at, send_sem=(as_sem, bs_sem, cs_sem)[stage].at[m],
            recv_sem=(ar_sem, br_sem, cr_sem)[stage].at[m],
            device_id=((s, near1, z), (s, near2, z), (other, d, z))[stage], device_id_type=MESH,
        )

    def relay(n):
        for c in range(4):

            @pl.when(jnp.logical_and(feeds_one, n == c))
            def _():
                supply_copies(1, c, lambda copy: copy.start())

        for k, lag in enumerate((0, 1, 3, 4)):
            m = n - lag

            @pl.when(jnp.logical_and(m >= 0, m < UNITS))
            def _():
                if k == 0:
                    arrived(unit_piece(m, place, 1, s), zr_sem.at[m])
                if k == 1:
                    arrived(unit_piece(m, pair_start + 1 - place % 2, 1, s), ar_sem.at[m])
                if k == 2:
                    arrived(unit_piece(m, far_start, 2, s), br_sem.at[m])
                if k == 3:
                    arrived(unit_piece(m, 0, 4, other), cr_sem.at[m])
                if k < 3:
                    relay_copy(m, k).start()

    @pl.when(role == 1)
    def _():
        cot_copies(lambda copy: copy.start())
    def relay_steps(start, stop):
        def one(n, carry):
            relay(n)
            return carry

        lax.fori_loop(start, stop, one, 0)

    relay_steps(0, jnp.where(role == 1, AHEAD, 0))
    arrived(wq.at[z], own_sem.at[0])
    arrived(wo.at[z], own_sem.at[1])
    arrived(wud.at[z, 0:1024], own_sem.at[2])
    arrived(wud.at[z, 1024:2048], own_sem.at[3])
    arrived(vec.at[0], vec_sem.at[0])
    for q in range(4):
        arrived(pre.at[q], pre_sem.at[q])
        carried = pre[q].astype(jnp.float32)
        for k in range(2):
            for n in range(2):
                row = PREFIX + 2 * k + n
                vec[q, 6 + k : 7 + k, n * half_width : (n + 1) * half_width] = carried[row : row + 1, :]

    first16 = lax.broadcasted_iota(jnp.int32, (16, 128), 1) < HEAD_DIM
    first = lax.broadcasted_iota(jnp.int32, (BLOCK, 128), 1) < HEAD_DIM
    lane = lax.broadcasted_iota(jnp.int32, (1, 128), 1)
    half0 = jnp.where(lane < HEAD_DIM, 1.0, 0.0).astype(jnp.bfloat16)
    half1 = jnp.where(lane < HEAD_DIM, 0.0, 1.0).astype(jnp.bfloat16)
    upper = lax.broadcasted_iota(jnp.int32, (128, BLOCK), 0) < HEAD_DIM
    slot = lax.broadcasted_iota(jnp.int32, (128, 1), 0)
    pre_mask_down = jnp.where(slot % HEAD_DIM < PREFIX, 0.0, NEG_LARGE)
    pre_mask = jnp.where(lane % HEAD_DIM < PREFIX, 0.0, NEG_LARGE)
    kp[...] = jnp.zeros(kp.shape, kp.dtype)
    vp[...] = jnp.zeros(vp.shape, vp.dtype)
    for q in range(4):
        for p in range(2):
            t0 = pre[q, :, p * 256 : p * 256 + 128].astype(jnp.float32)
            t1 = pre[q, :, p * 256 + 128 : p * 256 + 256].astype(jnp.float32)
            kp[2 * q + p, 0:16, :] = jnp.where(first16, t0, 0.0).astype(jnp.bfloat16)
            kp[2 * q + p, 64:80, :] = jnp.where(first16, 0.0, pltpu.roll(t1, 64, 1)).astype(jnp.bfloat16)
            vp[2 * q + p, 0:16, :] = jnp.where(first16, pltpu.roll(t0, 64, 1), 0.0).astype(jnp.bfloat16)
            vp[2 * q + p, 64:80, :] = jnp.where(first16, 0.0, t1).astype(jnp.bfloat16)

    def mask_blocks(keys_down):
        for j in range(2):
            row0 = block_of(s, j) * BLOCK
            row_at = row0 + lax.broadcasted_iota(jnp.int32, (1, BLOCK) if keys_down else (BLOCK, 1), int(keys_down))
            begin = jnp.zeros(row_at.shape, jnp.int32)
            end = 0
            for e in range(lengths.shape[1]):
                end = end + lengths[micro, e]
                begin = jnp.where(row_at >= end, end, begin)

            def mask_block(kb, carry):
                key_at = kb * BLOCK + lax.broadcasted_iota(jnp.int32, (BLOCK, BLOCK), 1 - int(keys_down))
                keep = jnp.logical_and(key_at <= row_at, key_at >= begin)
                bias[2 * j + kb] = jnp.where(keep, 0.0, NEG_LARGE)
                return carry

            lax.fori_loop(0, 2 + 2 * j, mask_block, 0)

    mask_blocks(False)

    def vector(k, q=0, width=1024):
        return vec[q, k : k + 1, 0:width]

    def columns(n, width):
        return pl.ds(pl.multiple_of(n * width, width), width)

    def block_rows(j):
        return pl.ds(pl.multiple_of(j * BLOCK, BLOCK), BLOCK)

    def over_rows(j, action):
        def one(c, carry):
            action(pl.ds(pl.multiple_of(j * BLOCK + c * CHUNK, CHUNK), CHUNK))
            return carry

        lax.fori_loop(0, BLOCK // CHUNK, one, 0)

    def standardize(v):
        average = jnp.mean(v, axis=-1, keepdims=True)
        centred = v - average
        spread = jnp.mean(centred * centred, axis=-1, keepdims=True)
        return centred, lax.rsqrt(spread + EPSILON)

    def norm_back(v, gain, incoming):
        centred, inverse = standardize(v)
        xhat = centred * inverse
        e = incoming * gain
        return (e - jnp.mean(e, axis=-1, keepdims=True) - xhat * jnp.mean(e * xhat, axis=-1, keepdims=True)) * inverse

    def to_core(ref, send_sem, recv_sem):
        return pltpu.make_async_remote_copy(
            src_ref=ref, dst_ref=ref, send_sem=send_sem, recv_sem=recv_sem,
            device_id=(other, d, z), device_id_type=MESH,
        )

    scale = LOG2E * HEAD_DIM ** (-0.5)

    def enter(j):
        rows = block_rows(j)
        arrived(x_in.at[rows], x_sem.at[j])

        def norm_one(rows):
            centred, inverse = standardize(x_in[rows, :].astype(jnp.float32))
            normed[rows, :] = (centred * inverse * vector(0) + vector(1)).astype(jnp.bfloat16)

        over_rows(j, norm_one)

        def project(q, carry):
            triple = dot_nn(normed[rows, :], wq[q]) + vec[q, 7:8, 0:768]
            for p in range(2):
                t0, t1, t2 = (triple[:, p * 384 + n * 128 : p * 384 + n * 128 + 128] for n in range(3))
                q_own[2 * q + p, rows, :] = jnp.where(first, t0, t1).astype(jnp.bfloat16)
                kv[s, 2 * q + p, 0, rows, :] = pltpu.roll(jnp.where(first, t2, t0), 64, 1).astype(jnp.bfloat16)
                kv[s, 2 * q + p, 1, rows, :] = jnp.where(first, t1, t2).astype(jnp.bfloat16)
            to_core(kv.at[s, pl.ds(2 * q, 2), :, rows], kv_ssem.at[j, q], kv_rsem.at[j, q]).start()
            return carry

        lax.fori_loop(0, 4, project, 0)

    def attend_rows(pair, core, j):
        cols = columns(pair, 128)
        rows = slice(j * BLOCK, j * BLOCK + BLOCK)
        blocks = block_of(core, j) + 1
        q_pair = q_own[pair, rows, :]
        q_half = (q_pair * half0, q_pair * half1)
        t_pre = dot_nt(q_pair, kp[pair]) * scale + pre_mask
        tops = [jnp.where(first, t_pre, NEG_LARGE), jnp.where(first, NEG_LARGE, t_pre)]
        for kb in range(blocks):
            keys = kv[core_of(kb), pair, 0, (kb // 2) * BLOCK : (kb // 2 + 1) * BLOCK, :]
            for h in range(2):
                t = dot_nt(q_half[h], keys) * scale + bias[2 * j + kb]
                ts[h, kb] = t
                tops[h] = jnp.maximum(tops[h], jnp.maximum(t[:, :128], t[:, 128:]))
        highest = [jnp.max(tops[h], axis=1, keepdims=True) for h in range(2)]
        e_pre = jnp.exp2(t_pre - jnp.where(first, highest[0], highest[1]))
        sums = [jnp.where(first, e_pre, 0.0), jnp.where(first, 0.0, e_pre)]
        mixed = [jnp.zeros((BLOCK, 128), jnp.float32) for _ in range(2)]
        for kb in range(blocks):
            values = kv[core_of(kb), pair, 1, (kb // 2) * BLOCK : (kb // 2 + 1) * BLOCK, :]
            for h in range(2):
                e = jnp.exp2(ts[h, kb] - highest[h])
                sums[h] += e[:, :128] + e[:, 128:]
                mixed[h] += dot_nn(e.astype(jnp.bfloat16), values)
        total = [jnp.sum(sums[h], axis=1, keepdims=True) for h in range(2)]
        share = [1.0 / total[h] for h in range(2)]
        p_pre = (e_pre * jnp.where(first, share[0], share[1])).astype(jnp.bfloat16)
        result = jnp.where(first, mixed[0] * share[0], mixed[1] * share[1]) + dot_nn(p_pre, vp[pair])
        o_own[rows, cols] = result.astype(jnp.bfloat16)
        logs = [highest[h] + jnp.log(total[h]) * LOG2E for h in range(2)]
        lse[pair, rows, :] = jnp.where(first, logs[0], logs[1])

    def attend(j, relay_at):
        def kv_wait(q, carry):
            to_core(kv.at[s, pl.ds(2 * q, 2), :, block_rows(j)], kv_ssem.at[j, q], kv_rsem.at[j, q]).wait_send()
            arrived(kv.at[other, pl.ds(2 * q, 2), :, block_rows(j)], kv_rsem.at[j, q])
            return carry

        lax.fori_loop(0, 4, kv_wait, 0)
        for core in range(2):
            for block in range(2):

                @pl.when(jnp.logical_and(s == core, j == block))
                def _():
                    def attend_pair(pair, carry):
                        relay_steps(relay_at, jnp.where(jnp.logical_and(pair == 4, relay_at < UNITS + 4), relay_at + 1, relay_at))
                        attend_rows(pair, core, block)
                        return carry

                    lax.fori_loop(0, 8, attend_pair, 0)

        rows = block_rows(j)
        after[rows, :] = (
            x_in[rows, :].astype(jnp.float32) + dot_nn(o_own[rows, :], wo[...].reshape(1024, 1024)) + vector(2)
        )

        def norm_two(rows):
            centred, inverse = standardize(after[rows, :])
            normed[rows, :] = (centred * inverse * vector(3) + vector(4)).astype(jnp.bfloat16)
            acc[rows, :] = after[rows, :] + vector(5)

        over_rows(j, norm_two)

    def feed(j, i):
        rows = block_rows(j)
        q = quarter(i)
        u = dot_nn(normed[rows, :], wud[q, 0:1024, :]) + vec[q, 6:7, :]
        u2 = u * u
        t = jnp.tanh(u * (GELU_A + (GELU_A * GELU_B) * u2))
        half_t = 0.5 + 0.5 * t
        wide[rows, :] = (u * half_t).astype(jnp.bfloat16)
        inner = u * (GELU_A + (3.0 * GELU_A * GELU_B) * u2)
        slope[q, rows, :] = (half_t + 0.5 * inner * (1.0 - t * t)).astype(jnp.bfloat16)
        acc[rows, :] += dot_nn(wide[rows, :], wud[q, 1024:2048, :])

    def hand_copies(j, k):
        rows = block_rows(j)
        landing, sem = ((x_in, x_sem), (act_out, act_sem), (g_in, g_sem), (ig_out, ig_sem))[k]
        if k % 2:
            dst, sem, target = landing.at[micro], sem.at[micro], (role, d, block_of(s, j))
        else:
            dst, sem, target = landing.at[rows], sem.at[j], (s, d, partner)
        return pltpu.make_async_remote_copy(
            src_ref=y_out.at[rows], dst_ref=dst, send_sem=hand_sem.at[k, j], recv_sem=sem,
            device_id=target, device_id_type=MESH,
        )

    def hand_on(j):
        rows = block_rows(j)
        y_out[rows, :] = acc[rows, :].astype(jnp.bfloat16)

        @pl.when(role == 1)
        def _():
            hand_copies(j, 1).start()

        @pl.when(jnp.logical_and(role == 0, j == 0))
        def _():
            hand_copies(0, 0).start()

        @pl.when(jnp.logical_and(role == 0, j == 1))
        def _():
            hand_copies(0, 0).wait_send()
            hand_copies(1, 0).start()
            hand_copies(1, 0).wait_send()
            for block in range(2):
                hand_copies(block, 1).start()

    def upto(n, table):
        total = jnp.int32(0)
        for k, entry in enumerate(table):
            total += jnp.where(n >= k, entry - (table[k - 1] if k else 0), 0)
        return total

    early_table = (0, 1, 2, 4, 6, 7, 8, 10, 12, 14, 16, 16, 16, 16)
    late_table = (AHEAD, 11, 13, 14, 15, 16, 16, 16, 16, 16, 16, 16, 16, 16)

    def forward(n, carry):
        turn = jnp.where(n == 11, 12, jnp.where(n == 12, 11, n))
        stage = jnp.where(role == 0, turn // 2, n % 7)
        j = jnp.where(role == 0, turn % 2, n // 7)
        before = jnp.where(
            role == 0,
            jnp.where(n == 0, 0, upto(n - 1, early_table)) + jnp.where(jnp.logical_or(n == 3, n == 4), 1, 0),
            jnp.where(n == 0, AHEAD, upto(n - 1, late_table)) + jnp.where(n == 2, 1, 0),
        )
        until = jnp.where(role == 0, upto(n, early_table), upto(n, late_table))
        relay_steps(before, until)

        @pl.when(jnp.logical_and(role == 0, n == 6))
        def _():
            cot_copies(lambda copy: copy.start())

        @pl.when(stage == 0)
        def _():
            enter(j)

        @pl.when(stage == 1)
        def _():
            attend(j, until)

        @pl.when(jnp.logical_and(stage >= 2, stage < 6))
        def _():
            feed(j, stage - 2)

        @pl.when(stage == 6)
        def _():
            hand_on(j)

        return carry

    lax.fori_loop(0, 14, forward, 0)

    def back_rows(pair, core, j):
        cols = columns(pair, 128)
        rows = slice(j * BLOCK, j * BLOCK + BLOCK)
        q_pair = q_own[pair, rows, :]
        q_half = (q_pair * half0, q_pair * half1)
        g_pair = wide[rows, cols]
        g_half = (g_pair * half0, g_pair * half1)
        product = g_pair.astype(jnp.float32) * o_own[rows, cols].astype(jnp.float32)
        row_term = [
            jnp.sum(jnp.where(first, product, 0.0), axis=1, keepdims=True),
            jnp.sum(jnp.where(first, 0.0, product), axis=1, keepdims=True),
        ]
        logs = jnp.transpose(lse[pair, rows, :])
        terms = jnp.transpose(jnp.where(first, row_term[0], row_term[1]))
        log_half = (logs[0:1, :], logs[64:65, :])
        term_half = (terms[0:1, :], terms[64:65, :])
        p_pre = jnp.exp2(dot_nt(kp[pair], q_pair) * scale + pre_mask_down - logs)
        dp_pre = dot_nt(vp[pair], g_pair)
        ds_pre = (p_pre * (dp_pre - terms)).astype(jnp.bfloat16)
        pv = dot_nn(p_pre.astype(jnp.bfloat16), g_pair)
        pk = dot_nn(ds_pre, q_pair)
        pk = jnp.where(first16, pk[0:16, :], pk[64:80, :]) * HEAD_DIM ** (-0.5)
        pv = jnp.where(first16, pv[0:16, :], pv[64:80, :])
        pg[pair, 0] = pk if j else pg[pair, 0] + pk
        pg[pair, 1] = pv if j else pg[pair, 1] + pv
        dq_pre = dot_tn(kp[pair], ds_pre)
        dqs = [jnp.zeros((128, BLOCK), jnp.float32) for _ in range(2)]
        for kb in range(4):
            held = dkv_own if core_of(kb) == core else dkv_send
            at = slice((kb // 2) * BLOCK, (kb // 2 + 1) * BLOCK)
            if kb > block_of(core, j):
                if j:
                    held[pair, 0, at, :] = jnp.zeros((BLOCK, 128), jnp.bfloat16)
                    held[pair, 1, at, :] = jnp.zeros((BLOCK, 128), jnp.bfloat16)
                continue
            keys = kv[core_of(kb), pair, 0, at, :]
            values = kv[core_of(kb), pair, 1, at, :]
            dv, dk = 0.0, 0.0
            if j == 0:
                dk = held[pair, 0, at, :].astype(jnp.float32)
                dv = held[pair, 1, at, :].astype(jnp.float32)
            for h in range(2):
                probs = jnp.exp2(dot_nt(keys, q_half[h]) * scale + bias[2 * j + kb] - log_half[h])
                grad_probs = dot_nt(values, g_half[h])
                grad_scores = (probs * (grad_probs - term_half[h])).astype(jnp.bfloat16)
                dv += dot_nn(probs.astype(jnp.bfloat16), g_half[h])
                dk += dot_nn(grad_scores, q_half[h])
                dqs[h] += dot_tn(keys, grad_scores)
            held[pair, 0, at, :] = dk.astype(jnp.bfloat16)
            held[pair, 1, at, :] = dv.astype(jnp.bfloat16)
        dq = (jnp.where(upper, dqs[0], dqs[1]) + dq_pre) * HEAD_DIM ** (-0.5)
        q_own[pair, rows, :] = jnp.transpose(dq).astype(jnp.bfloat16)

    def dkv_copy(j, pair):
        rows = block_rows(j)
        return pltpu.make_async_remote_copy(
            src_ref=dkv_send.at[pair, :, rows], dst_ref=dkv_recv.at[pair, :, rows],
            send_sem=dkv_ssem.at[j, pair], recv_sem=dkv_rsem.at[j, pair],
            device_id=(other, d, z), device_id_type=MESH,
        )

    contribution = micro * 2 + s

    def pg_copy(q):
        return pltpu.make_async_remote_copy(
            src_ref=pg.at[2 * q : 2 * q + 2], dst_ref=pg_near.at[contribution], send_sem=pg_ssem.at[q],
            recv_sem=pg_sem.at[contribution], device_id=(role, d, q), device_id_type=MESH,
        )

    def far_copy(k):
        return pltpu.make_async_remote_copy(
            src_ref=pg_far.at[d], dst_ref=pg_far.at[d], send_sem=far_ssem.at[k - 1], recv_sem=far_sem.at[d],
            device_id=(s, (d + k) % 4, z), device_id_type=MESH,
        )

    def sum_near():
        for k in range(4):
            arrived(pg_near.at[k], pg_sem.at[k])
        pg_far[d] = (pg_near[0] + pg_near[1]) + (pg_near[2] + pg_near[3])
        for k in range(1, 4):
            far_copy(k).start()

    def backward(n, carry):
        j = 1 - n
        rows = block_rows(j)
        arrived(g_in.at[rows], g_sem.at[j])
        acc[rows, :] = jnp.zeros((BLOCK, 1024), jnp.float32)

        def feed_back(q, carry):
            grad_act = dot_nt(g_in[rows, :], wud[q, 1024:2048, :])
            wide[rows, :] = (grad_act * slope[q, rows, :].astype(jnp.float32)).astype(jnp.bfloat16)
            acc[rows, :] += dot_nt(wide[rows, :], wud[q, 0:1024, :])
            return carry

        lax.fori_loop(0, 4, feed_back, 0)

        def middle(rows):
            dv = norm_back(after[rows, :], vector(3), acc[rows, :])
            normed[rows, :] = (g_in[rows, :].astype(jnp.float32) + dv).astype(jnp.bfloat16)

        over_rows(j, middle)
        wide[rows, :] = dot_nt(normed[rows, :], wo[...].reshape(1024, 1024)).astype(jnp.bfloat16)
        for core in range(2):
            for block in range(2):

                @pl.when(jnp.logical_and(s == core, j == block))
                def _():
                    def back_pair(pair, carry):
                        back_rows(pair, core, block)
                        dkv_copy(block, pair).start()
                        return carry

                    lax.fori_loop(0, 8, back_pair, 0)

        @pl.when(j == 0)
        def _():
            for q in range(4):
                is_here = jnp.logical_and(role == s, z == q)

                @pl.when(is_here)
                def _():
                    pltpu.make_async_copy(
                        pg.at[2 * q : 2 * q + 2], pg_near.at[contribution], pg_sem.at[contribution]
                    ).start()

                @pl.when(jnp.logical_not(is_here))
                def _():
                    pg_copy(q).start()

        acc[rows, :] = jnp.zeros((BLOCK, 1024), jnp.float32)

        def project_back(q, carry):
            for p in range(2):
                pair = 2 * q + p
                dkv_copy(j, pair).wait()
                dq = q_own[pair, rows, :].astype(jnp.float32)
                dk = dkv_own[pair, 0, rows, :].astype(jnp.float32) + dkv_recv[pair, 0, rows, :].astype(jnp.float32)
                dv = dkv_own[pair, 1, rows, :].astype(jnp.float32) + dkv_recv[pair, 1, rows, :].astype(jnp.float32)
                dk = pltpu.roll(dk * HEAD_DIM ** (-0.5), 64, 1)
                gt[:, p * 384 : p * 384 + 128] = jnp.where(first, dq, dk).astype(jnp.bfloat16)
                gt[:, p * 384 + 128 : p * 384 + 256] = jnp.where(first, dv, dq).astype(jnp.bfloat16)
                gt[:, p * 384 + 256 : p * 384 + 384] = jnp.where(first, dk, dv).astype(jnp.bfloat16)
            acc[rows, :] += dot_nt(gt[...], wq[q])
            return carry

        lax.fori_loop(0, 4, project_back, 0)

        @pl.when(jnp.logical_and(j == 0, role == 0))
        def _():
            sum_near()

        hand_copies(j, 1).wait_send()

        def give_back(rows):
            dv = norm_back(x_in[rows, :].astype(jnp.float32), vector(0), acc[rows, :])
            y_out[rows, :] = (normed[rows, :].astype(jnp.float32) + dv).astype(jnp.bfloat16)

        over_rows(j, give_back)

        @pl.when(role == 0)
        def _():
            hand_copies(j, 3).start()

        @pl.when(jnp.logical_and(role == 1, j == 1))
        def _():
            hand_copies(1, 2).start()

        @pl.when(jnp.logical_and(role == 1, j == 0))
        def _():
            hand_copies(0, 2).start()
            hand_copies(1, 2).wait_send()
            hand_copies(0, 2).wait_send()
            for block in range(2):
                hand_copies(block, 3).start()

        return carry

    mask_blocks(True)
    lax.fori_loop(0, 2, backward, 0)
    @pl.when(role == 1)
    def _():
        sum_near()

    for k in range(1, 4):
        arrived(pg_far.at[(d + k) % 4], far_sem.at[(d + k) % 4])
    total_pg = (pg_far[0] + pg_far[1]) + (pg_far[2] + pg_far[3])
    for p in range(2):
        keys, values = total_pg[p, 0], total_pg[p, 1]
        sum_out[:, p * 256 : p * 256 + 128] = jnp.where(first16, keys, pltpu.roll(values, 64, 1))
        sum_out[:, p * 256 + 128 : p * 256 + 256] = jnp.where(first16, pltpu.roll(keys, 64, 1), values)
    hidden_core[s] = dot_nt(sum_out[...].astype(jnp.bfloat16), pw[...])
    sends.start(hidden_core.at[s], hidden_core.at[s], core_sem.at[s], (other, d, z))
    arrived(hidden_core.at[other], core_sem.at[other])
    hidden_all[z] = hidden_core[0] + hidden_core[1]
    for k in range(1, 4):
        sends.start(hidden_all.at[z], hidden_all.at[z], hidden_sem.at[z], (s, d, (z + k) % 4))
    for k in range(1, 4):
        arrived(hidden_all.at[(z + k) % 4], hidden_sem.at[(z + k) % 4])
    hidden_out[...] = (hidden_all[0] + hidden_all[1]) + (hidden_all[2] + hidden_all[3])

    lax.fori_loop(0, 3, supply_done, 0)

    @pl.when(role == 0)
    def _():
        x_copies(lambda copy: copy.wait_send())

    @pl.when(feeds_one_late)
    def _():
        x_copies(lambda copy: copy.wait_send())

    firsts_done(jnp.logical_not(feeds_zero), 0)
    firsts_done(True, 1)

    def relays_done(m, carry):
        for stage in range(3):
            relay_copy(m, stage).wait_send()
        return carry

    lax.fori_loop(0, UNITS, relays_done, 0)
    cot_copies(lambda copy: copy.wait_send())
    for k in range(1, 4):
        far_copy(k).wait_send()
    for q in range(4):

        @pl.when(jnp.logical_not(jnp.logical_and(role == s, z == q)))
        def _():
            pg_copy(q).wait_send()

    for j in range(2):

        hand_copies(j, 3).wait_send()

    for k in range(2):
        arrived(act_out.at[k], act_sem.at[k])
        arrived(ig_out.at[k], ig_sem.at[k])
    sends.finish()


def run_layers(x, cot, wq, wo, wu, wd, *small):
    bf, f32 = jnp.bfloat16, jnp.float32
    vm, dma = pltpu.VMEM, pltpu.SemaphoreType.DMA
    rows = 2 * BLOCK
    width = x.shape[-1]
    pairs = width // 128
    pw = small[-3]
    scratch = [
        vm((8, width), f32), vm((16, pw.shape[1]), f32), vm((16, pw.shape[1]), bf), vm((4,) + wq.shape, bf), vm((4,) + wo.shape, bf), vm((4, 2 * wu.shape[0], width), bf),
        vm((4, 8, width), f32), vm((4, 16, pw.shape[1]), bf),
        vm((rows, width), bf), vm((rows, width), bf), vm((rows, width), bf), vm((rows, width), bf),
        vm((2, pairs, 2, rows, 128), bf), vm((pairs, rows, 128), bf), vm((rows, width), bf),
        vm((pairs, rows, 128), f32), vm((6, BLOCK, BLOCK), f32), vm((rows, width), f32), vm((rows, width), f32),
        vm((4, rows, wu.shape[1]), bf), vm((rows, wu.shape[1]), bf),
        vm((pairs, 2, 16, 128), f32), vm((4, 2, 2, 16, 128), f32), vm((4, 2, 2, 16, 128), f32), vm((2, 16, pw.shape[0]), f32), vm((4, 16, pw.shape[0]), f32),
        vm((2, 4, BLOCK, BLOCK), f32),
        vm((pairs, 2, rows, 128), bf), vm((pairs, 2, rows, 128), bf), vm((pairs, 2, rows, 128), bf),
        vm((pairs, 128, 128), bf), vm((pairs, 128, 128), bf),
        vm((BLOCK, wq.shape[1]), bf),
        dma((96,)), dma((4,)), dma((4,)), dma((2,)), dma((2,)), dma((2,)), dma((2,)), dma((4,)),
        dma((2, 4)), dma((2, 4)), dma((2, 4)), dma((2, 4)),
        dma((UNITS,)), dma((UNITS,)), dma((UNITS,)), dma((UNITS,)), dma((6, 2)), dma((UNITS, 2)), dma((UNITS,)), dma((UNITS,)), dma((UNITS,)),
        pltpu.SemaphoreType.REGULAR,
        dma((2, 4)), dma((2, 4)), dma((2, pairs)), dma((2, pairs)), dma((4,)), dma((4,)), dma((2,)), dma((4,)),
        dma((4, 2)), dma((2,)), dma((2,)), dma((4,)), dma((3,)), dma((8,)),
    ]
    anywhere = pl.BlockSpec(memory_space=pl.ANY)
    local = pl.BlockSpec(memory_space=pltpu.VMEM)
    return pl.pallas_call(
        layer_kernel,
        out_shape=(
            jax.ShapeDtypeStruct(x.shape, bf), jax.ShapeDtypeStruct(x.shape, bf),
            jax.ShapeDtypeStruct((16, pw.shape[1]), f32), jax.ShapeDtypeStruct((16, pw.shape[0]), f32),
            jax.ShapeDtypeStruct((16, pw.shape[0]), f32),
        ),
        in_specs=[anywhere] * 6 + [local] * 9 + [anywhere] + [local] * 3 + [pl.BlockSpec(memory_space=pltpu.SMEM)],
        out_specs=(anywhere, anywhere, local, local, local),
        scratch_shapes=scratch,
        name="two_layers",
        compiler_params=pltpu.CompilerParams(
            collective_id=0, has_side_effects=True, vmem_limit_bytes=63 * 2**20
        ),
    )(x, cot, wq, wo, wu, wd, *small)


def prefix_kernel(
    prefix_sum, hidden_grad, hidden_act, table, mid_w,
    table_grad, mid_w_grad, mid_b_grad, prefix_w_grad, prefix_b_grad, table_full,
):
    prefix_low = prefix_sum[...].astype(jnp.bfloat16)
    act = hidden_act[...]
    prefix_b_grad[...] = jnp.sum(prefix_low.astype(jnp.float32), axis=0, keepdims=True)
    prefix_w_grad[...] = dot_tn(act.astype(jnp.bfloat16), prefix_low)
    pre_grad = (hidden_grad[...] * (1.0 - act * act)).astype(jnp.bfloat16)
    mid_b_grad[...] = jnp.sum(pre_grad.astype(jnp.float32), axis=0, keepdims=True)
    table_full[...] = jnp.zeros(table_full.shape, jnp.float32)
    table_full[0:PREFIX, :] = table[...].astype(jnp.float32)
    mid_w_grad[...] = dot_tn(table_full[...].astype(jnp.bfloat16), pre_grad)
    table_grad[...] = dot_nt(pre_grad, mid_w[...])[0:PREFIX, :]


def run_prefix_back(prefix_sum, hidden_grad, hidden_act, table, mid_w):
    f32 = jnp.float32
    hidden, own = mid_w.shape[1], prefix_sum.shape[1]
    return pl.pallas_call(
        prefix_kernel,
        out_shape=tuple(
            jax.ShapeDtypeStruct(shape, f32)
            for shape in (table.shape, mid_w.shape, (1, hidden), (hidden, own), (1, own))
        ),
        scratch_shapes=[pltpu.VMEM((16, table.shape[1]), f32)],
        name="prefix_network",
        compiler_params=pltpu.CompilerParams(vmem_limit_bytes=48 * 2**20),
    )(prefix_sum, hidden_grad, hidden_act, table, mid_w)


def pair_body(
    layer_input, cotangent, example_lengths, attn_gain, attn_shift, query_key_value_weight, qkv_bias,
    attention_output_weight, out_bias, ffn_gain, ffn_shift, up_projection_weight, up_projection_bias,
    down_projection_weight, down_bias, prefix_table, mid_weight, mid_bias, prefix_weight, prefix_bias,
):
    activations, input_grads, prefix_sum, hidden_grad, hidden_act = run_layers(
        layer_input[:, 0], cotangent[:, 0], query_key_value_weight[0], attention_output_weight[0],
        up_projection_weight[0], down_projection_weight[0],
        attn_gain, attn_shift, out_bias, ffn_gain, ffn_shift, down_bias, up_projection_bias, qkv_bias,
        prefix_table, mid_weight, mid_bias, prefix_weight, prefix_bias, example_lengths[:, 0],
    )
    table_grad, mid_weight_grad, mid_bias_grad, prefix_weight_grad, prefix_bias_grad = run_prefix_back(
        prefix_sum, hidden_grad, hidden_act, prefix_table, mid_weight
    )
    return (
        activations[None, :, None], input_grads[None, :, None],
        table_grad, mid_weight_grad, mid_bias_grad[0], prefix_weight_grad, prefix_bias_grad[0],
    )


def solution(mesh):
    placed = (
        P(None, "dp", "mp", None),
        P(None, "dp", "mp", None),
        P(None, "dp", None),
        P("section", None),
        P("section", None),
        P("section", None, "mp"),
        P("section", "mp"),
        P("section", "mp", None),
        P("section", None),
        P("section", None),
        P("section", None),
        P("section", None, "mp"),
        P("section", "mp"),
        P("section", "mp", None),
        P("section", None),
        P(),
        P(),
        P(),
        P(None, ("section", "mp")),
        P(("section", "mp")),
    )
    paired = mesh.shape["mp"] == 4 and mesh.shape["dp"] == 4
    return jax.shard_map(
        pair_body if paired else body,
        mesh=mesh,
        in_specs=placed,
        out_specs=(
            P("section", None, "dp", "mp", None),
            P("section", None, "dp", "mp", None),
            P(),
            P(),
            P(),
            P(None, ("section", "mp")),
            P(("section", "mp")),
        ),
        check_vma=False,
    )
```

```python
import jax
import jax.numpy as jnp
from jax import lax
from jax.experimental import pallas as pl
from jax.experimental.pallas import tpu as pltpu
from jax.sharding import PartitionSpec as P

HEAD_DIM = 64
PREFIX = 10
SEQ_LEN = 1024


EPSILON = 1e-05
NEG_LARGE = -1e30
GELU_A = 0.7978845608028654
GELU_B = 0.044715


def norm_rows(values, gain, shift):
    average = jnp.mean(values, axis=-1, keepdims=True)
    centred = values - average
    spread = jnp.mean(centred * centred, axis=-1, keepdims=True)
    return centred * lax.rsqrt(spread + EPSILON) * gain + shift


def norm_input_grad(values, gain, shift, incoming):

    def apply_norm(inputs):
        return norm_rows(inputs, gain, shift)

    norm_value, norm_back = jax.vjp(apply_norm, values)
    return norm_back(incoming)[0]


def gelu_tanh(values):
    return jax.nn.gelu(values, approximate=True)


def visible_of(lengths, first_row, count):
    run_ends = jnp.cumsum(lengths, axis=-1)
    keys_at = jnp.arange(SEQ_LEN, dtype=jnp.int32)
    query_at = first_row + jnp.arange(count, dtype=jnp.int32)
    key_seg = jnp.sum((keys_at[None, :, None] >= run_ends[:, None, :]).astype(jnp.int32), axis=-1)
    query_seg = jnp.sum(
        (query_at[None, :, None] >= run_ends[:, None, :]).astype(jnp.int32), axis=-1
    )
    causal = (query_at[:, None] >= keys_at[None, :])[None]
    inside = (query_seg[:, :, None] == key_seg[:, None, :]) & causal
    leading = jnp.ones((lengths.shape[0], count, PREFIX), dtype=bool)
    return jnp.concatenate([leading, inside], axis=2)


def gather_rows(piece):
    return lax.all_gather(piece, "mp", axis=1, tiled=True)


def reduce_rows(partial_sum):
    return lax.psum_scatter(
        partial_sum.astype(jnp.bfloat16), "mp", scatter_dimension=1, tiled=True
    ).astype(jnp.float32)


def with_prefix(prefix_kv, pair_keys, pair_values, heads_count):
    prefix_pair = prefix_kv.reshape(PREFIX, heads_count, 2, HEAD_DIM)
    key_rows = jnp.concatenate([prefix_pair[None, :, :, 0], pair_keys], axis=1)
    value_rows = jnp.concatenate([prefix_pair[None, :, :, 1], pair_values], axis=1)
    return (key_rows, value_rows)


def attend(query_rows, key_rows, value_rows, visible):
    score_scale = HEAD_DIM ** (-0.5)
    scores = (
        jnp.einsum("sqhd,skhd->shqk", query_rows, key_rows, preferred_element_type=jnp.float32)
        * score_scale
    )
    scores = jnp.where(visible[:, None], scores, NEG_LARGE)
    highest = jnp.max(scores, axis=-1, keepdims=True)
    raised = jnp.exp(scores - highest)
    softmax_probs = raised / jnp.sum(raised, axis=-1, keepdims=True)
    probs_low = softmax_probs.astype(jnp.bfloat16)
    head_mixed_rows = jnp.einsum(
        "shqk,skhd->sqhd", probs_low, value_rows, preferred_element_type=jnp.float32
    )
    batch_size, query_count, heads_count, head_size = head_mixed_rows.shape
    head_mixed_rows = head_mixed_rows.astype(jnp.bfloat16).reshape(
        batch_size, query_count, heads_count * head_size
    )
    return (softmax_probs, probs_low, head_mixed_rows)


def attend_back(grad_mix, query_rows, key_rows, value_rows, softmax_probs, probs_low):
    grad_heads = grad_mix.reshape(query_rows.shape)
    grad_probs = jnp.einsum(
        "sqhd,skhd->shqk", grad_heads, value_rows, preferred_element_type=jnp.float32
    )
    value_grad = jnp.einsum(
        "shqk,sqhd->skhd", probs_low, grad_heads, preferred_element_type=jnp.float32
    )
    row_term = jnp.sum(grad_probs * softmax_probs, axis=-1, keepdims=True)
    grad_scores = (softmax_probs * (grad_probs - row_term)).astype(jnp.bfloat16)
    score_scale = HEAD_DIM ** (-0.5)
    query_grad = (
        jnp.einsum("shqk,skhd->sqhd", grad_scores, key_rows, preferred_element_type=jnp.float32)
        * score_scale
    )
    key_grad = (
        jnp.einsum("shqk,sqhd->skhd", grad_scores, query_rows, preferred_element_type=jnp.float32)
        * score_scale
    )
    return (query_grad, key_grad, value_grad)


def prefix_part(key_grad, value_grad):
    pair_sum = jnp.stack(
        [jnp.sum(key_grad[:, :PREFIX], axis=0), jnp.sum(value_grad[:, :PREFIX], axis=0)], axis=2
    )
    return pair_sum.reshape(PREFIX, -1)


def tensor_forward(own_rows, weights, prefix_kv, visible):
    (
        attn_gain,
        attn_shift,
        query_key_value_weight,
        qkv_bias,
        attention_output_weight,
        out_bias,
        ffn_gain,
        ffn_shift,
        up_projection_weight,
        up_projection_bias,
        down_projection_weight,
        down_bias,
        out_full,
    ) = weights
    normed = norm_rows(own_rows, attn_gain, attn_shift).astype(jnp.bfloat16)
    normalized_input_rows = gather_rows(normed)
    batch_size, seq_len, model_width = normalized_input_rows.shape
    heads_here = query_key_value_weight.shape[1] // (3 * HEAD_DIM)
    projected = (
        jnp.einsum(
            "naj,jk->nak",
            normalized_input_rows,
            query_key_value_weight,
            preferred_element_type=jnp.float32,
        )
        + qkv_bias
    )
    triple = projected.astype(jnp.bfloat16).reshape(batch_size, seq_len, heads_here, 3, HEAD_DIM)
    query_rows = triple[:, :, :, 0]
    key_rows, value_rows = with_prefix(
        prefix_kv, triple[:, :, :, 1], triple[:, :, :, 2], heads_here
    )
    softmax_probs, probs_low, head_mixed_rows = attend(query_rows, key_rows, value_rows, visible)
    attn_part = reduce_rows(
        jnp.einsum(
            "hgm,mt->hgt",
            head_mixed_rows,
            attention_output_weight,
            preferred_element_type=jnp.float32,
        )
    )
    after_attn = own_rows + attn_part + out_bias
    normed_two = norm_rows(after_attn, ffn_gain, ffn_shift).astype(jnp.bfloat16)
    second_norm_rows = gather_rows(normed_two)
    up_pre = (
        jnp.einsum(
            "rmy,yq->rmq",
            second_norm_rows,
            up_projection_weight,
            preferred_element_type=jnp.float32,
        )
        + up_projection_bias
    )
    gelu_output_rows = gelu_tanh(up_pre).astype(jnp.bfloat16)
    mlp_part = reduce_rows(
        jnp.einsum(
            "epj,jq->epq",
            gelu_output_rows,
            down_projection_weight,
            preferred_element_type=jnp.float32,
        )
    )
    result = after_attn + mlp_part + down_bias
    kept_values = (query_rows, key_rows, value_rows, softmax_probs, probs_low, after_attn, up_pre)
    return (result, kept_values)


def tensor_backward(own_rows, arriving, weights, kept_values):
    (
        attn_gain,
        attn_shift,
        query_key_value_weight,
        qkv_bias,
        attention_output_weight,
        out_bias,
        ffn_gain,
        ffn_shift,
        up_projection_weight,
        up_projection_bias,
        down_projection_weight,
        down_bias,
        out_full,
    ) = weights
    query_rows, key_rows, value_rows, softmax_probs, probs_low, after_attn, up_pre = kept_values
    gradient_gathered = gather_rows(arriving)
    gradient_activation = jnp.einsum(
        "bhi,vi->bhv", gradient_gathered, down_projection_weight, preferred_element_type=jnp.float32
    )
    gelu_value, gelu_back = jax.vjp(gelu_tanh, up_pre)
    gradient_up_projection = gelu_back(gradient_activation)[0].astype(jnp.bfloat16)
    grad_two = reduce_rows(
        jnp.einsum(
            "yca,ja->ycj",
            gradient_up_projection,
            up_projection_weight,
            preferred_element_type=jnp.float32,
        )
    )
    grad_after = norm_input_grad(after_attn, ffn_gain, ffn_shift, grad_two)
    grad_mid = (grad_after + arriving.astype(jnp.float32)).astype(jnp.bfloat16)
    middle_gathered = gather_rows(grad_mid)
    grad_mix = jnp.einsum(
        "taq,kq->tak", middle_gathered, attention_output_weight, preferred_element_type=jnp.float32
    ).astype(jnp.bfloat16)
    query_grad, key_grad, value_grad = attend_back(
        grad_mix, query_rows, key_rows, value_rows, softmax_probs, probs_low
    )
    prefix_g = prefix_part(key_grad, value_grad)
    batch_size, seq_len = (query_grad.shape[0], query_grad.shape[1])
    gradient_query_key_value = jnp.stack(
        [query_grad, key_grad[:, PREFIX:], value_grad[:, PREFIX:]], axis=3
    )
    gradient_query_key_value = gradient_query_key_value.astype(jnp.bfloat16).reshape(
        batch_size, seq_len, -1
    )
    grad_one = reduce_rows(
        jnp.einsum(
            "tvq,xq->tvx",
            gradient_query_key_value,
            query_key_value_weight,
            preferred_element_type=jnp.float32,
        )
    )
    grad_input = norm_input_grad(own_rows, attn_gain, attn_shift, grad_one)
    grad_input = (grad_input + grad_mid.astype(jnp.float32)).astype(jnp.bfloat16)
    return (grad_input, prefix_g)


def prefix_back(prefix_sum, hidden_grad, hidden_act, hidden_low, prefix_table, mid_weight):
    prefix_low = prefix_sum.astype(jnp.bfloat16)
    prefix_bias_grad = jnp.sum(prefix_low.astype(jnp.float32), axis=0)
    prefix_weight_grad = jnp.dot(hidden_low.T, prefix_low, preferred_element_type=jnp.float32)
    pre_grad = (hidden_grad * (1.0 - hidden_act * hidden_act)).astype(jnp.bfloat16)
    mid_bias_grad = jnp.sum(pre_grad.astype(jnp.float32), axis=0)
    mid_weight_grad = jnp.dot(prefix_table.T, pre_grad, preferred_element_type=jnp.float32)
    table_grad = jnp.dot(pre_grad, mid_weight.T, preferred_element_type=jnp.float32)
    return (table_grad, mid_weight_grad, mid_bias_grad, prefix_weight_grad, prefix_bias_grad)


def both_layers(piece):
    return lax.all_gather(piece[0], "section", axis=0, tiled=False)


def body(
    layer_input,
    cotangent,
    example_lengths,
    attn_gain,
    attn_shift,
    query_key_value_weight,
    qkv_bias,
    attention_output_weight,
    out_bias,
    ffn_gain,
    ffn_shift,
    up_projection_weight,
    up_projection_bias,
    down_projection_weight,
    down_bias,
    prefix_table,
    mid_weight,
    mid_bias,
    prefix_weight,
    prefix_bias,
):
    layers = lax.axis_size("section")
    section_index = lax.axis_index("section")
    hidden_pre = jnp.dot(
        prefix_table, mid_weight, preferred_element_type=jnp.float32
    ) + mid_bias.astype(jnp.float32)
    hidden_act = jnp.tanh(hidden_pre)
    hidden_low = hidden_act.astype(jnp.bfloat16)
    prefix_kv = (
        jnp.dot(hidden_low, prefix_weight, preferred_element_type=jnp.float32)
        + prefix_bias.astype(jnp.float32)
    ).astype(jnp.bfloat16)
    prefix_all = lax.all_gather(prefix_kv, "section", axis=0, tiled=False)
    floats = [
        both_layers(piece).astype(jnp.float32)
        for piece in (attn_gain, attn_shift, qkv_bias, out_bias, ffn_gain, ffn_shift,
                      up_projection_bias, down_bias)
    ]
    matrices = [
        both_layers(piece)
        for piece in (query_key_value_weight, attention_output_weight,
                      up_projection_weight, down_projection_weight)
    ]

    def weights_of(layer):
        g1, s1, bq, bo, g2, s2, bu, bd = [piece[layer] for piece in floats]
        wq, wo, wu, wd = [piece[layer] for piece in matrices]
        return (g1, s1, wq, bq, wo, bo, g2, s2, wu, bu, wd, bd, wo)

    batch_count = layer_input.shape[0]
    own_input = lax.dynamic_index_in_dim(layer_input, section_index, 0, keepdims=False)
    own_cotangent = lax.dynamic_index_in_dim(cotangent, section_index, 0, keepdims=False)
    lengths = lax.dynamic_index_in_dim(example_lengths, section_index, 0, keepdims=False)
    visible = visible_of(lengths, 0, SEQ_LEN)
    entering = own_input
    entered, produced, kept = [], [], []
    for layer in range(layers):
        entered.append(entering.astype(jnp.float32))
        result, kept_values = tensor_forward(
            entered[layer], weights_of(layer), prefix_all[layer], visible
        )
        entering = result.astype(jnp.bfloat16)
        produced.append(entering)
        kept.append(kept_values)
    gradient = own_cotangent
    sent_grads = [None] * layers
    prefix_parts = [None] * layers
    for layer in reversed(range(layers)):
        gradient, prefix_parts[layer] = tensor_backward(
            entered[layer], gradient, weights_of(layer), kept[layer]
        )
        sent_grads[layer] = gradient
    activations = lax.all_to_all(jnp.stack(produced), "section", 0, 0, tiled=False)
    input_grads = lax.all_to_all(jnp.stack(sent_grads), "section", 0, 0, tiled=False)
    prefix_sum = lax.psum(jnp.stack(prefix_parts), ("dp", "section"))
    prefix_sum = lax.dynamic_index_in_dim(prefix_sum, section_index, 0, keepdims=False)
    hidden_part = jnp.dot(
        prefix_sum.astype(jnp.bfloat16), prefix_weight.T, preferred_element_type=jnp.float32
    )
    hidden_grad = lax.psum(hidden_part, ("section", "mp"))
    return (activations[None], input_grads[None]) + prefix_back(
        prefix_sum, hidden_grad, hidden_act, hidden_low, prefix_table, mid_weight
    )


MESH = pl.DeviceIdType.MESH
BLOCK = 256
LOG2E = 1.4426950408889634
CHUNK = 128
UNITS = 12
AHEAD = 10
UNIT_ROWS = 512
PART_ROWS = UNIT_ROWS // 8


def role_of(z):
    return (((z + 1) // 2) + 1) % 2


def block_of(s, j):
    return j * 3 + s * (1 - 2 * j)


def core_of(block):
    return ((block + 1) // 2) % 2


def guarded(when, action):
    if when is None:
        action()
    else:
        pl.when(when)(action)


def dot_nn(a, b):
    return lax.dot_general(a, b, (((1,), (0,)), ((), ())), preferred_element_type=jnp.float32)


def dot_nt(a, b):
    return lax.dot_general(a, b, (((1,), (1,)), ((), ())), preferred_element_type=jnp.float32)


def dot_tn(a, b):
    return lax.dot_general(a, b, (((0,), (0,)), ((), ())), preferred_element_type=jnp.float32)


class Sends:
    def __init__(self, sems):
        self.sems, self.used, self.pending = sems, 0, []

    def start(self, src, dst, recv_sem, target, when=None):
        copy = pltpu.make_async_remote_copy(
            src_ref=src, dst_ref=dst, send_sem=self.sems.at[self.used], recv_sem=recv_sem,
            device_id=target, device_id_type=MESH,
        )
        self.used += 1
        guarded(when, copy.start)
        self.pending.append((when, copy))

    def start_or_keep(self, src, dst, recv_sem, target, is_here, when=True):
        @pl.when(jnp.logical_and(when, is_here))
        def _():
            pltpu.make_async_copy(src, dst, recv_sem).start()

        self.start(src, dst, recv_sem, target, when=jnp.logical_and(when, jnp.logical_not(is_here)))

    def finish(self):
        for when, copy in self.pending:
            guarded(when, copy.wait_send)
        self.pending = []


def layer_kernel(
    x_hbm, cot_hbm, wq_hbm, wo_hbm, wu_hbm, wd_hbm,
    g1, s1, bo, g2, s2, bd, bu, bq, table, mid_w, mid_b, pw, pb, lengths,
    act_out, ig_out, sum_out, hidden_out, tanh_out,
    vec_own, pre_full, pre_own, wq, wo, wud, vec, pre,
    x_in, g_in, y_out, normed, kv, q_own, o_own, lse, bias, after, acc, slope, wide,
    pg, pg_near, pg_far, hidden_core, hidden_all, ts, dkv_own, dkv_send, dkv_recv, kp, vp, gt,
    ssem, vec_sem, pre_sem, x_sem, g_sem, act_sem, ig_sem, own_sem, z_sem, a_sem, b_sem, c_sem,
    zr_sem, ar_sem, br_sem, cr_sem, fs_sem, zs_sem, as_sem, bs_sem, cs_sem, go_sem,
    kv_ssem, kv_rsem, dkv_ssem, dkv_rsem, pg_sem, far_sem, core_sem, hidden_sem,
    hand_sem, cot_sem, x_ssem, pg_ssem, far_ssem, mid_sem,
):
    s, d, z = lax.axis_index("section"), lax.axis_index("dp"), lax.axis_index("mp")
    role, micro = role_of(z), z // 2
    other = 1 - s
    partner = z + 1 - 2 * (z % 2)
    x_near, y_near = d + 1 - 2 * (d % 2), (d + 2) % 4
    near1 = jnp.where(s == 0, x_near, y_near)
    near2 = jnp.where(s == 0, y_near, x_near)
    sends = Sends(ssem)

    barrier = pltpu.get_barrier_semaphore()
    for ds in range(2):
        for dz in range(4):
            if ds or dz:
                pl.semaphore_signal(barrier, inc=1, device_id=((s + ds) % 2, d, (z + dz) % 4), device_id_type=MESH)
    for near in (x_near, y_near, 3 - d):
        pl.semaphore_signal(barrier, inc=1, device_id=(s, near, z), device_id_type=MESH)
    pl.semaphore_wait(barrier, 10)

    def arrived(dst, sem):
        pltpu.make_async_remote_copy(
            src_ref=dst, dst_ref=dst, send_sem=ssem.at[0], recv_sem=sem,
            device_id=(other, d, z), device_id_type=MESH,
        ).wait_recv()

    low_plane, high_plane = jnp.where(s == 0, 1, 0), jnp.where(s == 0, 2, 3)
    planes = (low_plane, high_plane)
    mine = s == core_of(z)
    row_slot = pl.ds(pl.multiple_of((z // 2) * BLOCK, BLOCK), BLOCK)

    def send_small(when):
        for t in planes:
            for h in range(2):
                is_here = jnp.logical_and(z == t, s == h)
                sends.start_or_keep(pre_own, pre.at[z], pre_sem.at[z], (h, d, t), is_here, when)

    def row_copies(source, landing, send_sem, sem, chips, then):
        for k, chip in enumerate(chips):

            @pl.when(jnp.logical_and(mine, z != chip))
            def _():
                then(pltpu.make_async_remote_copy(
                    src_ref=source.at[k], dst_ref=landing.at[row_slot], send_sem=send_sem.at[k],
                    recv_sem=sem.at[z // 2], device_id=(s, d, chip), device_id_type=MESH,
                ))

    def keep_rows(source, landing, sem, chips):
        for k, chip in enumerate(chips):

            @pl.when(jnp.logical_and(mine, z == chip))
            def _():
                pltpu.make_async_copy(source.at[k], landing.at[row_slot], sem.at[z // 2]).start()

    def x_copies(then):
        row_copies(x_hbm, x_in, x_ssem, x_sem, (1, 2), then)

    def cot_copies(then):
        row_copies(cot_hbm, g_in, cot_sem, g_sem, (0, 3), then)

    keep_rows(x_hbm, x_in, x_sem, (1, 2))
    keep_rows(cot_hbm, g_in, g_sem, (0, 3))

    toward = jnp.where(z < 2, 1, -1)

    def quarter(i):
        return (z + 4 + toward * i) % 4

    def taker(i):
        low, high = (z + 3 - i) % 4, (z + 1 + i) % 4
        return jnp.where(low == low_plane, low, high), jnp.logical_or(low == low_plane, high == high_plane)

    swapped = (d % 2) * 2 + d // 2
    place = jnp.where(s == 0, d, swapped)
    pair_start = (place // 2) * 2
    far_start = 2 - pair_start
    firsts = ((wq_hbm, wq), (wo_hbm, wo))

    def eighths(rows, start, count, h):
        return pl.ds(pl.multiple_of((start + 4 * h) * rows, rows), rows * count)

    def supply_first(w, i, then):
        t, taken = taker(i)
        held, full = firsts[w]

        @pl.when(taken)
        def _():
            for h in range(2):
                at = eighths(held.shape[0] // 8, swapped if h else d, 1, h)
                then(pltpu.make_async_remote_copy(
                    src_ref=held.at[at], dst_ref=full.at[z, at], send_sem=fs_sem.at[3 * w + i, h],
                    recv_sem=z_sem.at[w, z], device_id=(h, d, t), device_id_type=MESH,
                ))

    def supply_firsts(when, w):
        @pl.when(when)
        def _():
            def one(i, carry):
                supply_first(w, i, lambda copy: copy.start())
                return carry

            lax.fori_loop(0, 3, one, 0)

    def firsts_done(when, w):
        @pl.when(when)
        def _():
            def one(i, carry):
                supply_first(w, i, lambda copy: copy.wait_send())
                return carry

            lax.fori_loop(0, 3, one, 0)

    def supply_copies(i, c, then):
        t, taken = taker(i)
        held, base = ((wu_hbm, 0), (wd_hbm, 1024))[c // 2]

        @pl.when(taken)
        def _():
            for h in range(2):
                at = eighths(PART_ROWS, swapped if h else d, 1, h)
                start = (c % 2) * UNIT_ROWS + at.start
                then(pltpu.make_async_remote_copy(
                    src_ref=held.at[pl.ds(pl.multiple_of(start, PART_ROWS), PART_ROWS)],
                    dst_ref=wud.at[z, pl.ds(pl.multiple_of(base + start, PART_ROWS), PART_ROWS)],
                    send_sem=zs_sem.at[4 * i + c, h], recv_sem=zr_sem.at[4 * i + c],
                    device_id=(h, d, t), device_id_type=MESH,
                ))

    def supply_all(i, carry):
        for c in range(4):
            supply_copies(i, c, lambda copy: copy.start())
        return carry

    def supply_done(i, carry):
        for c in range(4):
            supply_copies(i, c, lambda copy: copy.wait_send())
        return carry

    feeds_zero = jnp.logical_and(role == 1, s == 0)
    feeds_zero_late = jnp.logical_and(role == 0, s == 0)
    feeds_one = jnp.logical_and(role == 0, s == 1)
    feeds_one_late = jnp.logical_and(role == 1, s == 1)
    supply_firsts(s == 0, 0)

    @pl.when(feeds_one)
    def _():
        for w in range(2):
            supply_first(w, 0, lambda copy: copy.start())
        supply_all(0, 0)

    mid_copies = mid_w.shape[1] // 128

    def mid_copy(n, half):
        return pltpu.make_async_copy(
            mid_w.at[half * 512 : half * 512 + 512, n * 128 : n * 128 + 128], q_own.at[2 * n + half],
            mid_sem.at[2 * n + half],
        )

    for n in range(mid_copies):
        for half in range(2):
            mid_copy(n, half).start()
    for k, row in enumerate((g1, s1, bo, g2, s2, bd)):
        vec_own[k : k + 1, :] = row[...].astype(jnp.float32)

    @pl.when(role == s)
    def _():
        pltpu.make_async_copy(vec_own, vec.at[0], vec_sem.at[0]).start()

    sends.start(vec_own, vec.at[0], vec_sem.at[0], (other, d, z), when=role == s)
    tanh_out[...] = jnp.zeros(tanh_out.shape, jnp.float32)
    for n in range(mid_copies):
        for half in range(2):
            mid_copy(n, half).wait()
        cols = slice(n * 128, n * 128 + 128)
        part_sum = dot_nn(table[:, 0:512], q_own[2 * n]) + dot_nn(table[:, 512:1024], q_own[2 * n + 1])
        tanh_out[0:PREFIX, cols] = jnp.tanh(part_sum + mid_b[...].astype(jnp.float32).reshape(1, -1)[:, cols])
    pre_full[...] = dot_nn(tanh_out[...].astype(jnp.bfloat16), pw[...]) + pb[...].astype(jnp.float32).reshape(1, -1)
    half_width = pre_full.shape[1]
    for k, row in enumerate((bu, bq)):
        for n in range(2):
            piece = row[:, n * half_width : min((n + 1) * half_width, row.shape[1])]
            pre_full[PREFIX + 2 * k + n : PREFIX + 2 * k + n + 1, 0 : piece.shape[1]] = piece.astype(jnp.float32)
    pre_own[...] = pre_full[...].astype(jnp.bfloat16)
    send_small(feeds_zero)
    firsts_done(feeds_zero, 0)
    supply_firsts(feeds_zero, 1)

    @pl.when(feeds_zero)
    def _():
        x_copies(lambda copy: copy.start())
    owned = ((wq_hbm, wq.at[z]), (wo_hbm, wo.at[z]), (wu_hbm, wud.at[z, 0:1024]), (wd_hbm, wud.at[z, 1024:2048]))
    for w, (held, full) in enumerate(owned):
        @pl.when(role == s)
        def _():
            pltpu.make_async_copy(held, full, own_sem.at[w]).start()

        sends.start(held, full, own_sem.at[w], (other, d, z), when=role == s)

    @pl.when(feeds_zero)
    def _():
        x_copies(lambda copy: copy.wait_send())
        lax.fori_loop(0, 3, supply_all, 0)

    @pl.when(feeds_one_late)
    def _():
        pl.semaphore_wait(go_sem, 1)

    send_small(feeds_one_late)
    supply_firsts(feeds_one_late, 0)
    supply_firsts(feeds_one_late, 1)

    first_units = [(w, i) for w in (0, 1) for i in range(1, 4)]

    def first_piece(w, i, start, count):
        full = firsts[w][1]
        return full.at[quarter(i), eighths(full.shape[1] // 8, start, count, s)]

    def relay_first(step):
        stages = [first_units[step - k] if 0 <= step - k < len(first_units) else None for k in range(4)]
        if stages[0]:
            w, i = stages[0]
            q = quarter(i)
            arrived(first_piece(w, i, place, 1), z_sem.at[w, q])
            sends.start(first_piece(w, i, place, 1), first_piece(w, i, place, 1), a_sem.at[w, q], (s, near1, z))
        if stages[1]:
            w, i = stages[1]
            q = quarter(i)
            arrived(first_piece(w, i, pair_start + 1 - place % 2, 1), a_sem.at[w, q])
            sends.start(first_piece(w, i, pair_start, 2), first_piece(w, i, pair_start, 2), b_sem.at[w, q], (s, near2, z))
        if stages[2]:
            w, i = stages[2]
            q = quarter(i)
            arrived(first_piece(w, i, far_start, 2), b_sem.at[w, q])
            sends.start(first_piece(w, i, 0, 4), first_piece(w, i, 0, 4), c_sem.at[w, q], (other, d, z))
        if stages[3]:
            w, i = stages[3]
            full = firsts[w][1]
            arrived(full.at[quarter(i), eighths(full.shape[1] // 8, 0, 4, other)], c_sem.at[w, quarter(i)])

    for step in range(len(first_units) + 3):
        relay_first(step)
        if step == 0:
            @pl.when(role == 0)
            def _():
                x_copies(lambda copy: copy.start())

            send_small(feeds_zero_late)
            supply_firsts(feeds_zero_late, 1)
        if step == 3:
            @pl.when(feeds_one)
            def _():
                pl.semaphore_signal(go_sem, inc=1, device_id=(1, d, partner), device_id_type=MESH)

                supply_first(0, 1, lambda copy: copy.start())

            send_small(feeds_one)
        if step == 6:
            @pl.when(feeds_one)
            def _():
                supply_first(1, 1, lambda copy: copy.start())


        @pl.when(feeds_zero_late)
        def _():
            if 1 <= step < 5:
                supply_copies(0, step - 1, lambda copy: copy.start())

    @pl.when(feeds_one_late)
    def _():
        lax.fori_loop(0, 3, supply_all, 0)

    def unit_piece(m, start, count, h):
        q = quarter(1 + m // 4)
        first_row = (m % 4) * UNIT_ROWS + (start + 4 * h) * PART_ROWS
        return wud.at[q, pl.ds(pl.multiple_of(first_row, PART_ROWS), PART_ROWS * count)]

    def relay_copy(m, stage):
        start, count = ((place, 1), (pair_start, 2), (0, 4))[stage]
        at = unit_piece(m, start, count, s)
        return pltpu.make_async_remote_copy(
            src_ref=at, dst_ref=at, send_sem=(as_sem, bs_sem, cs_sem)[stage].at[m],
            recv_sem=(ar_sem, br_sem, cr_sem)[stage].at[m],
            device_id=((s, near1, z), (s, near2, z), (other, d, z))[stage], device_id_type=MESH,
        )

    def relay(n):
        for c in range(4):

            @pl.when(jnp.logical_and(feeds_one, n == c))
            def _():
                supply_copies(1, c, lambda copy: copy.start())

        for k, lag in enumerate((0, 1, 3, 4)):
            m = n - lag

            @pl.when(jnp.logical_and(m >= 0, m < UNITS))
            def _():
                if k == 0:
                    arrived(unit_piece(m, place, 1, s), zr_sem.at[m])
                if k == 1:
                    arrived(unit_piece(m, pair_start + 1 - place % 2, 1, s), ar_sem.at[m])
                if k == 2:
                    arrived(unit_piece(m, far_start, 2, s), br_sem.at[m])
                if k == 3:
                    arrived(unit_piece(m, 0, 4, other), cr_sem.at[m])
                if k < 3:
                    relay_copy(m, k).start()

    @pl.when(role == 1)
    def _():
        cot_copies(lambda copy: copy.start())
    def relay_steps(start, stop):
        def one(n, carry):
            relay(n)
            return carry

        lax.fori_loop(start, stop, one, 0)

    relay_steps(0, jnp.where(role == 1, AHEAD, 0))
    arrived(wq.at[z], own_sem.at[0])
    arrived(wo.at[z], own_sem.at[1])
    arrived(wud.at[z, 0:1024], own_sem.at[2])
    arrived(wud.at[z, 1024:2048], own_sem.at[3])
    arrived(vec.at[0], vec_sem.at[0])
    for q in range(4):
        arrived(pre.at[q], pre_sem.at[q])
        carried = pre[q].astype(jnp.float32)
        for k in range(2):
            for n in range(2):
                row = PREFIX + 2 * k + n
                vec[q, 6 + k : 7 + k, n * half_width : (n + 1) * half_width] = carried[row : row + 1, :]

    first16 = lax.broadcasted_iota(jnp.int32, (16, 128), 1) < HEAD_DIM
    first = lax.broadcasted_iota(jnp.int32, (BLOCK, 128), 1) < HEAD_DIM
    lane = lax.broadcasted_iota(jnp.int32, (1, 128), 1)
    half0 = jnp.where(lane < HEAD_DIM, 1.0, 0.0).astype(jnp.bfloat16)
    half1 = jnp.where(lane < HEAD_DIM, 0.0, 1.0).astype(jnp.bfloat16)
    upper = lax.broadcasted_iota(jnp.int32, (128, BLOCK), 0) < HEAD_DIM
    slot = lax.broadcasted_iota(jnp.int32, (128, 1), 0)
    pre_mask_down = jnp.where(slot % HEAD_DIM < PREFIX, 0.0, NEG_LARGE)
    pre_mask = jnp.where(lane % HEAD_DIM < PREFIX, 0.0, NEG_LARGE)
    kp[...] = jnp.zeros(kp.shape, kp.dtype)
    vp[...] = jnp.zeros(vp.shape, vp.dtype)
    for q in range(4):
        for p in range(2):
            t0 = pre[q, :, p * 256 : p * 256 + 128].astype(jnp.float32)
            t1 = pre[q, :, p * 256 + 128 : p * 256 + 256].astype(jnp.float32)
            kp[2 * q + p, 0:16, :] = jnp.where(first16, t0, 0.0).astype(jnp.bfloat16)
            kp[2 * q + p, 64:80, :] = jnp.where(first16, 0.0, pltpu.roll(t1, 64, 1)).astype(jnp.bfloat16)
            vp[2 * q + p, 0:16, :] = jnp.where(first16, pltpu.roll(t0, 64, 1), 0.0).astype(jnp.bfloat16)
            vp[2 * q + p, 64:80, :] = jnp.where(first16, 0.0, t1).astype(jnp.bfloat16)

    def mask_blocks(keys_down):
        for j in range(2):
            row0 = block_of(s, j) * BLOCK
            row_at = row0 + lax.broadcasted_iota(jnp.int32, (1, BLOCK) if keys_down else (BLOCK, 1), int(keys_down))
            begin = jnp.zeros(row_at.shape, jnp.int32)
            end = 0
            for e in range(lengths.shape[1]):
                end = end + lengths[micro, e]
                begin = jnp.where(row_at >= end, end, begin)

            def mask_block(kb, carry):
                key_at = kb * BLOCK + lax.broadcasted_iota(jnp.int32, (BLOCK, BLOCK), 1 - int(keys_down))
                keep = jnp.logical_and(key_at <= row_at, key_at >= begin)
                bias[2 * j + kb] = jnp.where(keep, 0.0, NEG_LARGE)
                return carry

            lax.fori_loop(0, 2 + 2 * j, mask_block, 0)

    mask_blocks(False)

    def vector(k, q=0, width=1024):
        return vec[q, k : k + 1, 0:width]

    def columns(n, width):
        return pl.ds(pl.multiple_of(n * width, width), width)

    def block_rows(j):
        return pl.ds(pl.multiple_of(j * BLOCK, BLOCK), BLOCK)

    def over_rows(j, action):
        def one(c, carry):
            action(pl.ds(pl.multiple_of(j * BLOCK + c * CHUNK, CHUNK), CHUNK))
            return carry

        lax.fori_loop(0, BLOCK // CHUNK, one, 0)

    def standardize(v):
        average = jnp.mean(v, axis=-1, keepdims=True)
        centred = v - average
        spread = jnp.mean(centred * centred, axis=-1, keepdims=True)
        return centred, lax.rsqrt(spread + EPSILON)

    def norm_back(v, gain, incoming):
        centred, inverse = standardize(v)
        xhat = centred * inverse
        e = incoming * gain
        return (e - jnp.mean(e, axis=-1, keepdims=True) - xhat * jnp.mean(e * xhat, axis=-1, keepdims=True)) * inverse

    def to_core(ref, send_sem, recv_sem):
        return pltpu.make_async_remote_copy(
            src_ref=ref, dst_ref=ref, send_sem=send_sem, recv_sem=recv_sem,
            device_id=(other, d, z), device_id_type=MESH,
        )

    scale = LOG2E * HEAD_DIM ** (-0.5)

    def enter(j):
        rows = block_rows(j)
        arrived(x_in.at[rows], x_sem.at[j])

        def norm_one(rows):
            centred, inverse = standardize(x_in[rows, :].astype(jnp.float32))
            normed[rows, :] = (centred * inverse * vector(0) + vector(1)).astype(jnp.bfloat16)

        over_rows(j, norm_one)

        def project(q, carry):
            triple = dot_nn(normed[rows, :], wq[q]) + vec[q, 7:8, 0:768]
            for p in range(2):
                t0, t1, t2 = (triple[:, p * 384 + n * 128 : p * 384 + n * 128 + 128] for n in range(3))
                q_own[2 * q + p, rows, :] = jnp.where(first, t0, t1).astype(jnp.bfloat16)
                kv[s, 2 * q + p, 0, rows, :] = pltpu.roll(jnp.where(first, t2, t0), 64, 1).astype(jnp.bfloat16)
                kv[s, 2 * q + p, 1, rows, :] = jnp.where(first, t1, t2).astype(jnp.bfloat16)
            to_core(kv.at[s, pl.ds(2 * q, 2), :, rows], kv_ssem.at[j, q], kv_rsem.at[j, q]).start()
            return carry

        lax.fori_loop(0, 4, project, 0)

    def attend_rows(pair, core, j):
        cols = columns(pair, 128)
        rows = slice(j * BLOCK, j * BLOCK + BLOCK)
        blocks = block_of(core, j) + 1
        q_pair = q_own[pair, rows, :]
        q_half = (q_pair * half0, q_pair * half1)
        t_pre = dot_nt(q_pair, kp[pair]) * scale + pre_mask
        tops = [jnp.where(first, t_pre, NEG_LARGE), jnp.where(first, NEG_LARGE, t_pre)]
        for kb in range(blocks):
            keys = kv[core_of(kb), pair, 0, (kb // 2) * BLOCK : (kb // 2 + 1) * BLOCK, :]
            for h in range(2):
                t = dot_nt(q_half[h], keys) * scale + bias[2 * j + kb]
                ts[h, kb] = t
                tops[h] = jnp.maximum(tops[h], jnp.maximum(t[:, :128], t[:, 128:]))
        highest = [jnp.max(tops[h], axis=1, keepdims=True) for h in range(2)]
        e_pre = jnp.exp2(t_pre - jnp.where(first, highest[0], highest[1]))
        sums = [jnp.where(first, e_pre, 0.0), jnp.where(first, 0.0, e_pre)]
        mixed = [jnp.zeros((BLOCK, 128), jnp.float32) for _ in range(2)]
        for kb in range(blocks):
            values = kv[core_of(kb), pair, 1, (kb // 2) * BLOCK : (kb // 2 + 1) * BLOCK, :]
            for h in range(2):
                e = jnp.exp2(ts[h, kb] - highest[h])
                sums[h] += e[:, :128] + e[:, 128:]
                mixed[h] += dot_nn(e.astype(jnp.bfloat16), values)
        total = [jnp.sum(sums[h], axis=1, keepdims=True) for h in range(2)]
        share = [1.0 / total[h] for h in range(2)]
        p_pre = (e_pre * jnp.where(first, share[0], share[1])).astype(jnp.bfloat16)
        result = jnp.where(first, mixed[0] * share[0], mixed[1] * share[1]) + dot_nn(p_pre, vp[pair])
        o_own[rows, cols] = result.astype(jnp.bfloat16)
        logs = [highest[h] + jnp.log(total[h]) * LOG2E for h in range(2)]
        lse[pair, rows, :] = jnp.where(first, logs[0], logs[1])

    def attend(j, relay_at):
        def kv_wait(q, carry):
            to_core(kv.at[s, pl.ds(2 * q, 2), :, block_rows(j)], kv_ssem.at[j, q], kv_rsem.at[j, q]).wait_send()
            arrived(kv.at[other, pl.ds(2 * q, 2), :, block_rows(j)], kv_rsem.at[j, q])
            return carry

        lax.fori_loop(0, 4, kv_wait, 0)
        for core in range(2):
            for block in range(2):

                @pl.when(jnp.logical_and(s == core, j == block))
                def _():
                    def attend_pair(pair, carry):
                        relay_steps(relay_at, jnp.where(jnp.logical_and(pair == 4, relay_at < UNITS + 4), relay_at + 1, relay_at))
                        attend_rows(pair, core, block)
                        return carry

                    lax.fori_loop(0, 8, attend_pair, 0)

        rows = block_rows(j)
        after[rows, :] = (
            x_in[rows, :].astype(jnp.float32) + dot_nn(o_own[rows, :], wo[...].reshape(1024, 1024)) + vector(2)
        )

        def norm_two(rows):
            centred, inverse = standardize(after[rows, :])
            normed[rows, :] = (centred * inverse * vector(3) + vector(4)).astype(jnp.bfloat16)
            acc[rows, :] = after[rows, :] + vector(5)

        over_rows(j, norm_two)

    def feed(j, i):
        rows = block_rows(j)
        q = quarter(i)
        u = dot_nn(normed[rows, :], wud[q, 0:1024, :]) + vec[q, 6:7, :]
        u2 = u * u
        t = jnp.tanh(u * (GELU_A + (GELU_A * GELU_B) * u2))
        half_t = 0.5 + 0.5 * t
        wide[rows, :] = (u * half_t).astype(jnp.bfloat16)
        inner = u * (GELU_A + (3.0 * GELU_A * GELU_B) * u2)
        slope[q, rows, :] = (half_t + 0.5 * inner * (1.0 - t * t)).astype(jnp.bfloat16)
        acc[rows, :] += dot_nn(wide[rows, :], wud[q, 1024:2048, :])

    def hand_copies(j, k):
        rows = block_rows(j)
        landing, sem = ((x_in, x_sem), (act_out, act_sem), (g_in, g_sem), (ig_out, ig_sem))[k]
        if k % 2:
            dst, sem, target = landing.at[micro], sem.at[micro], (role, d, block_of(s, j))
        else:
            dst, sem, target = landing.at[rows], sem.at[j], (s, d, partner)
        return pltpu.make_async_remote_copy(
            src_ref=y_out.at[rows], dst_ref=dst, send_sem=hand_sem.at[k, j], recv_sem=sem,
            device_id=target, device_id_type=MESH,
        )

    def hand_on(j):
        rows = block_rows(j)
        y_out[rows, :] = acc[rows, :].astype(jnp.bfloat16)

        @pl.when(role == 1)
        def _():
            hand_copies(j, 1).start()

        @pl.when(jnp.logical_and(role == 0, j == 0))
        def _():
            hand_copies(0, 0).start()

        @pl.when(jnp.logical_and(role == 0, j == 1))
        def _():
            hand_copies(0, 0).wait_send()
            hand_copies(1, 0).start()
            hand_copies(1, 0).wait_send()
            for block in range(2):
                hand_copies(block, 1).start()

    def upto(n, table):
        total = jnp.int32(0)
        for k, entry in enumerate(table):
            total += jnp.where(n >= k, entry - (table[k - 1] if k else 0), 0)
        return total

    early_table = (0, 1, 2, 4, 6, 7, 8, 10, 12, 14, 16, 16, 16, 16)
    late_table = (AHEAD, 11, 13, 14, 15, 16, 16, 16, 16, 16, 16, 16, 16, 16)

    def forward(n, carry):
        turn = jnp.where(n == 11, 12, jnp.where(n == 12, 11, n))
        stage = jnp.where(role == 0, turn // 2, n % 7)
        j = jnp.where(role == 0, turn % 2, n // 7)
        before = jnp.where(
            role == 0,
            jnp.where(n == 0, 0, upto(n - 1, early_table)) + jnp.where(jnp.logical_or(n == 3, n == 4), 1, 0),
            jnp.where(n == 0, AHEAD, upto(n - 1, late_table)) + jnp.where(n == 2, 1, 0),
        )
        until = jnp.where(role == 0, upto(n, early_table), upto(n, late_table))
        relay_steps(before, until)

        @pl.when(jnp.logical_and(role == 0, n == 6))
        def _():
            cot_copies(lambda copy: copy.start())

        @pl.when(stage == 0)
        def _():
            enter(j)

        @pl.when(stage == 1)
        def _():
            attend(j, until)

        @pl.when(jnp.logical_and(stage >= 2, stage < 6))
        def _():
            feed(j, stage - 2)

        @pl.when(stage == 6)
        def _():
            hand_on(j)

        return carry

    lax.fori_loop(0, 14, forward, 0)

    def back_rows(pair, core, j):
        cols = columns(pair, 128)
        rows = slice(j * BLOCK, j * BLOCK + BLOCK)
        q_pair = q_own[pair, rows, :]
        q_half = (q_pair * half0, q_pair * half1)
        g_pair = wide[rows, cols]
        g_half = (g_pair * half0, g_pair * half1)
        product = g_pair.astype(jnp.float32) * o_own[rows, cols].astype(jnp.float32)
        row_term = [
            jnp.sum(jnp.where(first, product, 0.0), axis=1, keepdims=True),
            jnp.sum(jnp.where(first, 0.0, product), axis=1, keepdims=True),
        ]
        logs = jnp.transpose(lse[pair, rows, :])
        terms = jnp.transpose(jnp.where(first, row_term[0], row_term[1]))
        log_half = (logs[0:1, :], logs[64:65, :])
        term_half = (terms[0:1, :], terms[64:65, :])
        p_pre = jnp.exp2(dot_nt(kp[pair], q_pair) * scale + pre_mask_down - logs)
        dp_pre = dot_nt(vp[pair], g_pair)
        ds_pre = (p_pre * (dp_pre - terms)).astype(jnp.bfloat16)
        pv = dot_nn(p_pre.astype(jnp.bfloat16), g_pair)
        pk = dot_nn(ds_pre, q_pair)
        pk = jnp.where(first16, pk[0:16, :], pk[64:80, :]) * HEAD_DIM ** (-0.5)
        pv = jnp.where(first16, pv[0:16, :], pv[64:80, :])
        pg[pair, 0] = pk if j else pg[pair, 0] + pk
        pg[pair, 1] = pv if j else pg[pair, 1] + pv
        dq_pre = dot_tn(kp[pair], ds_pre)
        dqs = [jnp.zeros((128, BLOCK), jnp.float32) for _ in range(2)]
        for kb in range(4):
            held = dkv_own if core_of(kb) == core else dkv_send
            at = slice((kb // 2) * BLOCK, (kb // 2 + 1) * BLOCK)
            if kb > block_of(core, j):
                if j:
                    held[pair, 0, at, :] = jnp.zeros((BLOCK, 128), jnp.bfloat16)
                    held[pair, 1, at, :] = jnp.zeros((BLOCK, 128), jnp.bfloat16)
                continue
            keys = kv[core_of(kb), pair, 0, at, :]
            values = kv[core_of(kb), pair, 1, at, :]
            dv, dk = 0.0, 0.0
            if j == 0:
                dk = held[pair, 0, at, :].astype(jnp.float32)
                dv = held[pair, 1, at, :].astype(jnp.float32)
            for h in range(2):
                probs = jnp.exp2(dot_nt(keys, q_half[h]) * scale + bias[2 * j + kb] - log_half[h])
                grad_probs = dot_nt(values, g_half[h])
                grad_scores = (probs * (grad_probs - term_half[h])).astype(jnp.bfloat16)
                dv += dot_nn(probs.astype(jnp.bfloat16), g_half[h])
                dk += dot_nn(grad_scores, q_half[h])
                dqs[h] += dot_tn(keys, grad_scores)
            held[pair, 0, at, :] = dk.astype(jnp.bfloat16)
            held[pair, 1, at, :] = dv.astype(jnp.bfloat16)
        dq = (jnp.where(upper, dqs[0], dqs[1]) + dq_pre) * HEAD_DIM ** (-0.5)
        q_own[pair, rows, :] = jnp.transpose(dq).astype(jnp.bfloat16)

    def dkv_copy(j, pair):
        rows = block_rows(j)
        return pltpu.make_async_remote_copy(
            src_ref=dkv_send.at[pair, :, rows], dst_ref=dkv_recv.at[pair, :, rows],
            send_sem=dkv_ssem.at[j, pair], recv_sem=dkv_rsem.at[j, pair],
            device_id=(other, d, z), device_id_type=MESH,
        )

    contribution = micro * 2 + s

    def pg_copy(q):
        return pltpu.make_async_remote_copy(
            src_ref=pg.at[2 * q : 2 * q + 2], dst_ref=pg_near.at[contribution], send_sem=pg_ssem.at[q],
            recv_sem=pg_sem.at[contribution], device_id=(role, d, q), device_id_type=MESH,
        )

    def far_copy(k):
        return pltpu.make_async_remote_copy(
            src_ref=pg_far.at[d], dst_ref=pg_far.at[d], send_sem=far_ssem.at[k - 1], recv_sem=far_sem.at[d],
            device_id=(s, (d + k) % 4, z), device_id_type=MESH,
        )

    def sum_near():
        for k in range(4):
            arrived(pg_near.at[k], pg_sem.at[k])
        pg_far[d] = (pg_near[0] + pg_near[1]) + (pg_near[2] + pg_near[3])
        for k in range(1, 4):
            far_copy(k).start()

    def backward(n, carry):
        j = 1 - n
        rows = block_rows(j)
        arrived(g_in.at[rows], g_sem.at[j])
        acc[rows, :] = jnp.zeros((BLOCK, 1024), jnp.float32)

        def feed_back(q, carry):
            grad_act = dot_nt(g_in[rows, :], wud[q, 1024:2048, :])
            wide[rows, :] = (grad_act * slope[q, rows, :].astype(jnp.float32)).astype(jnp.bfloat16)
            acc[rows, :] += dot_nt(wide[rows, :], wud[q, 0:1024, :])
            return carry

        lax.fori_loop(0, 4, feed_back, 0)

        def middle(rows):
            dv = norm_back(after[rows, :], vector(3), acc[rows, :])
            normed[rows, :] = (g_in[rows, :].astype(jnp.float32) + dv).astype(jnp.bfloat16)

        over_rows(j, middle)
        wide[rows, :] = dot_nt(normed[rows, :], wo[...].reshape(1024, 1024)).astype(jnp.bfloat16)
        for core in range(2):
            for block in range(2):

                @pl.when(jnp.logical_and(s == core, j == block))
                def _():
                    def back_pair(pair, carry):
                        back_rows(pair, core, block)
                        dkv_copy(block, pair).start()
                        return carry

                    lax.fori_loop(0, 8, back_pair, 0)

        @pl.when(j == 0)
        def _():
            for q in range(4):
                is_here = jnp.logical_and(role == s, z == q)

                @pl.when(is_here)
                def _():
                    pltpu.make_async_copy(
                        pg.at[2 * q : 2 * q + 2], pg_near.at[contribution], pg_sem.at[contribution]
                    ).start()

                @pl.when(jnp.logical_not(is_here))
                def _():
                    pg_copy(q).start()

        acc[rows, :] = jnp.zeros((BLOCK, 1024), jnp.float32)

        def project_back(q, carry):
            for p in range(2):
                pair = 2 * q + p
                dkv_copy(j, pair).wait()
                dq = q_own[pair, rows, :].astype(jnp.float32)
                dk = dkv_own[pair, 0, rows, :].astype(jnp.float32) + dkv_recv[pair, 0, rows, :].astype(jnp.float32)
                dv = dkv_own[pair, 1, rows, :].astype(jnp.float32) + dkv_recv[pair, 1, rows, :].astype(jnp.float32)
                dk = pltpu.roll(dk * HEAD_DIM ** (-0.5), 64, 1)
                gt[:, p * 384 : p * 384 + 128] = jnp.where(first, dq, dk).astype(jnp.bfloat16)
                gt[:, p * 384 + 128 : p * 384 + 256] = jnp.where(first, dv, dq).astype(jnp.bfloat16)
                gt[:, p * 384 + 256 : p * 384 + 384] = jnp.where(first, dk, dv).astype(jnp.bfloat16)
            acc[rows, :] += dot_nt(gt[...], wq[q])
            return carry

        lax.fori_loop(0, 4, project_back, 0)

        @pl.when(jnp.logical_and(j == 0, role == 0))
        def _():
            sum_near()

        hand_copies(j, 1).wait_send()

        def give_back(rows):
            dv = norm_back(x_in[rows, :].astype(jnp.float32), vector(0), acc[rows, :])
            y_out[rows, :] = (normed[rows, :].astype(jnp.float32) + dv).astype(jnp.bfloat16)

        over_rows(j, give_back)

        @pl.when(role == 0)
        def _():
            hand_copies(j, 3).start()

        @pl.when(jnp.logical_and(role == 1, j == 1))
        def _():
            hand_copies(1, 2).start()

        @pl.when(jnp.logical_and(role == 1, j == 0))
        def _():
            hand_copies(0, 2).start()
            hand_copies(1, 2).wait_send()
            hand_copies(0, 2).wait_send()
            for block in range(2):
                hand_copies(block, 3).start()

        return carry

    mask_blocks(True)
    lax.fori_loop(0, 2, backward, 0)
    @pl.when(role == 1)
    def _():
        sum_near()

    for k in range(1, 4):
        arrived(pg_far.at[(d + k) % 4], far_sem.at[(d + k) % 4])
    total_pg = (pg_far[0] + pg_far[1]) + (pg_far[2] + pg_far[3])
    for p in range(2):
        keys, values = total_pg[p, 0], total_pg[p, 1]
        sum_out[:, p * 256 : p * 256 + 128] = jnp.where(first16, keys, pltpu.roll(values, 64, 1))
        sum_out[:, p * 256 + 128 : p * 256 + 256] = jnp.where(first16, pltpu.roll(keys, 64, 1), values)
    hidden_core[s] = dot_nt(sum_out[...].astype(jnp.bfloat16), pw[...])
    sends.start(hidden_core.at[s], hidden_core.at[s], core_sem.at[s], (other, d, z))
    arrived(hidden_core.at[other], core_sem.at[other])
    hidden_all[z] = hidden_core[0] + hidden_core[1]
    for k in range(1, 4):
        sends.start(hidden_all.at[z], hidden_all.at[z], hidden_sem.at[z], (s, d, (z + k) % 4))
    for k in range(1, 4):
        arrived(hidden_all.at[(z + k) % 4], hidden_sem.at[(z + k) % 4])
    hidden_out[...] = (hidden_all[0] + hidden_all[1]) + (hidden_all[2] + hidden_all[3])

    lax.fori_loop(0, 3, supply_done, 0)

    @pl.when(role == 0)
    def _():
        x_copies(lambda copy: copy.wait_send())

    @pl.when(feeds_one_late)
    def _():
        x_copies(lambda copy: copy.wait_send())

    firsts_done(jnp.logical_not(feeds_zero), 0)
    firsts_done(True, 1)

    def relays_done(m, carry):
        for stage in range(3):
            relay_copy(m, stage).wait_send()
        return carry

    lax.fori_loop(0, UNITS, relays_done, 0)
    cot_copies(lambda copy: copy.wait_send())
    for k in range(1, 4):
        far_copy(k).wait_send()
    for q in range(4):

        @pl.when(jnp.logical_not(jnp.logical_and(role == s, z == q)))
        def _():
            pg_copy(q).wait_send()

    for j in range(2):

        hand_copies(j, 3).wait_send()

    for k in range(2):
        arrived(act_out.at[k], act_sem.at[k])
        arrived(ig_out.at[k], ig_sem.at[k])
    sends.finish()


def run_layers(x, cot, wq, wo, wu, wd, *small):
    bf, f32 = jnp.bfloat16, jnp.float32
    vm, dma = pltpu.VMEM, pltpu.SemaphoreType.DMA
    rows = 2 * BLOCK
    width = x.shape[-1]
    pairs = width // 128
    pw = small[-3]
    scratch = [
        vm((8, width), f32), vm((16, pw.shape[1]), f32), vm((16, pw.shape[1]), bf), vm((4,) + wq.shape, bf), vm((4,) + wo.shape, bf), vm((4, 2 * wu.shape[0], width), bf),
        vm((4, 8, width), f32), vm((4, 16, pw.shape[1]), bf),
        vm((rows, width), bf), vm((rows, width), bf), vm((rows, width), bf), vm((rows, width), bf),
        vm((2, pairs, 2, rows, 128), bf), vm((pairs, rows, 128), bf), vm((rows, width), bf),
        vm((pairs, rows, 128), f32), vm((6, BLOCK, BLOCK), f32), vm((rows, width), f32), vm((rows, width), f32),
        vm((4, rows, wu.shape[1]), bf), vm((rows, wu.shape[1]), bf),
        vm((pairs, 2, 16, 128), f32), vm((4, 2, 2, 16, 128), f32), vm((4, 2, 2, 16, 128), f32), vm((2, 16, pw.shape[0]), f32), vm((4, 16, pw.shape[0]), f32),
        vm((2, 4, BLOCK, BLOCK), f32),
        vm((pairs, 2, rows, 128), bf), vm((pairs, 2, rows, 128), bf), vm((pairs, 2, rows, 128), bf),
        vm((pairs, 128, 128), bf), vm((pairs, 128, 128), bf),
        vm((BLOCK, wq.shape[1]), bf),
        dma((96,)), dma((4,)), dma((4,)), dma((2,)), dma((2,)), dma((2,)), dma((2,)), dma((4,)),
        dma((2, 4)), dma((2, 4)), dma((2, 4)), dma((2, 4)),
        dma((UNITS,)), dma((UNITS,)), dma((UNITS,)), dma((UNITS,)), dma((6, 2)), dma((UNITS, 2)), dma((UNITS,)), dma((UNITS,)), dma((UNITS,)),
        pltpu.SemaphoreType.REGULAR,
        dma((2, 4)), dma((2, 4)), dma((2, pairs)), dma((2, pairs)), dma((4,)), dma((4,)), dma((2,)), dma((4,)),
        dma((4, 2)), dma((2,)), dma((2,)), dma((4,)), dma((3,)), dma((8,)),
    ]
    anywhere = pl.BlockSpec(memory_space=pl.ANY)
    local = pl.BlockSpec(memory_space=pltpu.VMEM)
    return pl.pallas_call(
        layer_kernel,
        out_shape=(
            jax.ShapeDtypeStruct(x.shape, bf), jax.ShapeDtypeStruct(x.shape, bf),
            jax.ShapeDtypeStruct((16, pw.shape[1]), f32), jax.ShapeDtypeStruct((16, pw.shape[0]), f32),
            jax.ShapeDtypeStruct((16, pw.shape[0]), f32),
        ),
        in_specs=[anywhere] * 6 + [local] * 9 + [anywhere] + [local] * 3 + [pl.BlockSpec(memory_space=pltpu.SMEM)],
        out_specs=(anywhere, anywhere, local, local, local),
        scratch_shapes=scratch,
        name="two_layers",
        compiler_params=pltpu.CompilerParams(
            collective_id=0, has_side_effects=True, vmem_limit_bytes=63 * 2**20
        ),
    )(x, cot, wq, wo, wu, wd, *small)


def prefix_kernel(
    prefix_sum, hidden_grad, hidden_act, table, mid_w, act_held, ig_held,
    table_grad, mid_w_grad, mid_b_grad, prefix_w_grad, prefix_b_grad, act_out, ig_out, table_full, stage, in_sem, out_sem,
):
    incoming, outgoing = [], []
    for n, (held, out) in enumerate(((act_held, act_out), (ig_held, ig_out))):
        for k in range(2):
            incoming.append(pltpu.make_async_copy(held.at[k], stage.at[n, k], in_sem.at[n, k]))
            outgoing.append(pltpu.make_async_copy(stage.at[n, k], out.at[k], out_sem.at[n, k]))
            incoming[-1].start()
    for arriving, leaving in zip(incoming, outgoing):
        arriving.wait()
        leaving.start()
    prefix_low = prefix_sum[...].astype(jnp.bfloat16)
    act = hidden_act[...]
    prefix_b_grad[...] = jnp.sum(prefix_low.astype(jnp.float32), axis=0, keepdims=True)
    prefix_w_grad[...] = dot_tn(act.astype(jnp.bfloat16), prefix_low)
    pre_grad = (hidden_grad[...] * (1.0 - act * act)).astype(jnp.bfloat16)
    mid_b_grad[...] = jnp.sum(pre_grad.astype(jnp.float32), axis=0, keepdims=True)
    table_full[...] = jnp.zeros(table_full.shape, jnp.float32)
    table_full[0:PREFIX, :] = table[...].astype(jnp.float32)
    mid_w_grad[...] = dot_tn(table_full[...].astype(jnp.bfloat16), pre_grad)
    table_grad[...] = dot_nt(pre_grad, mid_w[...])[0:PREFIX, :]
    for leaving in outgoing:
        leaving.wait()


def run_prefix_back(prefix_sum, hidden_grad, hidden_act, table, mid_w, activations, input_grads):
    f32 = jnp.float32
    hidden, own = mid_w.shape[1], prefix_sum.shape[1]
    local, anywhere = pl.BlockSpec(memory_space=pltpu.VMEM), pl.BlockSpec(memory_space=pl.ANY)
    rows = jax.ShapeDtypeStruct(activations.shape, activations.dtype)
    return pl.pallas_call(
        prefix_kernel,
        out_shape=tuple(
            jax.ShapeDtypeStruct(shape, f32)
            for shape in (table.shape, mid_w.shape, (1, hidden), (hidden, own), (1, own))
        ) + (rows, rows),
        in_specs=[local] * 5 + [anywhere] * 2,
        out_specs=(local,) * 5 + (anywhere,) * 2,
        scratch_shapes=[
            pltpu.VMEM((16, table.shape[1]), f32), pltpu.VMEM((2,) + activations.shape, activations.dtype),
            pltpu.SemaphoreType.DMA((2, 2)), pltpu.SemaphoreType.DMA((2, 2)),
        ],
        name="prefix_network",
        compiler_params=pltpu.CompilerParams(vmem_limit_bytes=60 * 2**20),
    )(prefix_sum, hidden_grad, hidden_act, table, mid_w, activations, input_grads)


def pair_body(
    layer_input, cotangent, example_lengths, attn_gain, attn_shift, query_key_value_weight, qkv_bias,
    attention_output_weight, out_bias, ffn_gain, ffn_shift, up_projection_weight, up_projection_bias,
    down_projection_weight, down_bias, prefix_table, mid_weight, mid_bias, prefix_weight, prefix_bias,
):
    activations, input_grads, prefix_sum, hidden_grad, hidden_act = run_layers(
        layer_input[:, 0], cotangent[:, 0], query_key_value_weight[0], attention_output_weight[0],
        up_projection_weight[0], down_projection_weight[0],
        attn_gain, attn_shift, out_bias, ffn_gain, ffn_shift, down_bias, up_projection_bias, qkv_bias,
        prefix_table, mid_weight, mid_bias, prefix_weight, prefix_bias, example_lengths[:, 0],
    )
    (
        table_grad, mid_weight_grad, mid_bias_grad, prefix_weight_grad, prefix_bias_grad, activations, input_grads,
    ) = run_prefix_back(prefix_sum, hidden_grad, hidden_act, prefix_table, mid_weight, activations, input_grads)
    return (
        activations[None, :, None], input_grads[None, :, None],
        table_grad, mid_weight_grad, mid_bias_grad[0], prefix_weight_grad, prefix_bias_grad[0],
    )


def solution(mesh):
    placed = (
        P(None, "dp", "mp", None),
        P(None, "dp", "mp", None),
        P(None, "dp", None),
        P("section", None),
        P("section", None),
        P("section", None, "mp"),
        P("section", "mp"),
        P("section", "mp", None),
        P("section", None),
        P("section", None),
        P("section", None),
        P("section", None, "mp"),
        P("section", "mp"),
        P("section", "mp", None),
        P("section", None),
        P(),
        P(),
        P(),
        P(None, ("section", "mp")),
        P(("section", "mp")),
    )
    paired = mesh.shape["mp"] == 4 and mesh.shape["dp"] == 4
    return jax.shard_map(
        pair_body if paired else body,
        mesh=mesh,
        in_specs=placed,
        out_specs=(
            P("section", None, "dp", "mp", None),
            P("section", None, "dp", "mp", None),
            P(),
            P(),
            P(),
            P(None, ("section", "mp")),
            P(("section", "mp")),
        ),
        check_vma=False,
    )
```

```python
import jax
import jax.numpy as jnp
from jax import lax
from jax.experimental import pallas as pl
from jax.experimental.pallas import tpu as pltpu
from jax.sharding import PartitionSpec as P

HEAD_DIM = 64
PREFIX = 10
SEQ_LEN = 1024


EPSILON = 1e-05
NEG_LARGE = -1e30
GELU_A = 0.7978845608028654
GELU_B = 0.044715


def norm_rows(values, gain, shift):
    average = jnp.mean(values, axis=-1, keepdims=True)
    centred = values - average
    spread = jnp.mean(centred * centred, axis=-1, keepdims=True)
    return centred * lax.rsqrt(spread + EPSILON) * gain + shift


def norm_input_grad(values, gain, shift, incoming):

    def apply_norm(inputs):
        return norm_rows(inputs, gain, shift)

    norm_value, norm_back = jax.vjp(apply_norm, values)
    return norm_back(incoming)[0]


def gelu_tanh(values):
    return jax.nn.gelu(values, approximate=True)


def visible_of(lengths, first_row, count):
    run_ends = jnp.cumsum(lengths, axis=-1)
    keys_at = jnp.arange(SEQ_LEN, dtype=jnp.int32)
    query_at = first_row + jnp.arange(count, dtype=jnp.int32)
    key_seg = jnp.sum((keys_at[None, :, None] >= run_ends[:, None, :]).astype(jnp.int32), axis=-1)
    query_seg = jnp.sum(
        (query_at[None, :, None] >= run_ends[:, None, :]).astype(jnp.int32), axis=-1
    )
    causal = (query_at[:, None] >= keys_at[None, :])[None]
    inside = (query_seg[:, :, None] == key_seg[:, None, :]) & causal
    leading = jnp.ones((lengths.shape[0], count, PREFIX), dtype=bool)
    return jnp.concatenate([leading, inside], axis=2)


def gather_rows(piece):
    return lax.all_gather(piece, "mp", axis=1, tiled=True)


def reduce_rows(partial_sum):
    return lax.psum_scatter(
        partial_sum.astype(jnp.bfloat16), "mp", scatter_dimension=1, tiled=True
    ).astype(jnp.float32)


def with_prefix(prefix_kv, pair_keys, pair_values, heads_count):
    prefix_pair = prefix_kv.reshape(PREFIX, heads_count, 2, HEAD_DIM)
    key_rows = jnp.concatenate([prefix_pair[None, :, :, 0], pair_keys], axis=1)
    value_rows = jnp.concatenate([prefix_pair[None, :, :, 1], pair_values], axis=1)
    return (key_rows, value_rows)


def attend(query_rows, key_rows, value_rows, visible):
    score_scale = HEAD_DIM ** (-0.5)
    scores = (
        jnp.einsum("sqhd,skhd->shqk", query_rows, key_rows, preferred_element_type=jnp.float32)
        * score_scale
    )
    scores = jnp.where(visible[:, None], scores, NEG_LARGE)
    highest = jnp.max(scores, axis=-1, keepdims=True)
    raised = jnp.exp(scores - highest)
    softmax_probs = raised / jnp.sum(raised, axis=-1, keepdims=True)
    probs_low = softmax_probs.astype(jnp.bfloat16)
    head_mixed_rows = jnp.einsum(
        "shqk,skhd->sqhd", probs_low, value_rows, preferred_element_type=jnp.float32
    )
    batch_size, query_count, heads_count, head_size = head_mixed_rows.shape
    head_mixed_rows = head_mixed_rows.astype(jnp.bfloat16).reshape(
        batch_size, query_count, heads_count * head_size
    )
    return (softmax_probs, probs_low, head_mixed_rows)


def attend_back(grad_mix, query_rows, key_rows, value_rows, softmax_probs, probs_low):
    grad_heads = grad_mix.reshape(query_rows.shape)
    grad_probs = jnp.einsum(
        "sqhd,skhd->shqk", grad_heads, value_rows, preferred_element_type=jnp.float32
    )
    value_grad = jnp.einsum(
        "shqk,sqhd->skhd", probs_low, grad_heads, preferred_element_type=jnp.float32
    )
    row_term = jnp.sum(grad_probs * softmax_probs, axis=-1, keepdims=True)
    grad_scores = (softmax_probs * (grad_probs - row_term)).astype(jnp.bfloat16)
    score_scale = HEAD_DIM ** (-0.5)
    query_grad = (
        jnp.einsum("shqk,skhd->sqhd", grad_scores, key_rows, preferred_element_type=jnp.float32)
        * score_scale
    )
    key_grad = (
        jnp.einsum("shqk,sqhd->skhd", grad_scores, query_rows, preferred_element_type=jnp.float32)
        * score_scale
    )
    return (query_grad, key_grad, value_grad)


def prefix_part(key_grad, value_grad):
    pair_sum = jnp.stack(
        [jnp.sum(key_grad[:, :PREFIX], axis=0), jnp.sum(value_grad[:, :PREFIX], axis=0)], axis=2
    )
    return pair_sum.reshape(PREFIX, -1)


def tensor_forward(own_rows, weights, prefix_kv, visible):
    (
        attn_gain,
        attn_shift,
        query_key_value_weight,
        qkv_bias,
        attention_output_weight,
        out_bias,
        ffn_gain,
        ffn_shift,
        up_projection_weight,
        up_projection_bias,
        down_projection_weight,
        down_bias,
        out_full,
    ) = weights
    normed = norm_rows(own_rows, attn_gain, attn_shift).astype(jnp.bfloat16)
    normalized_input_rows = gather_rows(normed)
    batch_size, seq_len, model_width = normalized_input_rows.shape
    heads_here = query_key_value_weight.shape[1] // (3 * HEAD_DIM)
    projected = (
        jnp.einsum(
            "naj,jk->nak",
            normalized_input_rows,
            query_key_value_weight,
            preferred_element_type=jnp.float32,
        )
        + qkv_bias
    )
    triple = projected.astype(jnp.bfloat16).reshape(batch_size, seq_len, heads_here, 3, HEAD_DIM)
    query_rows = triple[:, :, :, 0]
    key_rows, value_rows = with_prefix(
        prefix_kv, triple[:, :, :, 1], triple[:, :, :, 2], heads_here
    )
    softmax_probs, probs_low, head_mixed_rows = attend(query_rows, key_rows, value_rows, visible)
    attn_part = reduce_rows(
        jnp.einsum(
            "hgm,mt->hgt",
            head_mixed_rows,
            attention_output_weight,
            preferred_element_type=jnp.float32,
        )
    )
    after_attn = own_rows + attn_part + out_bias
    normed_two = norm_rows(after_attn, ffn_gain, ffn_shift).astype(jnp.bfloat16)
    second_norm_rows = gather_rows(normed_two)
    up_pre = (
        jnp.einsum(
            "rmy,yq->rmq",
            second_norm_rows,
            up_projection_weight,
            preferred_element_type=jnp.float32,
        )
        + up_projection_bias
    )
    gelu_output_rows = gelu_tanh(up_pre).astype(jnp.bfloat16)
    mlp_part = reduce_rows(
        jnp.einsum(
            "epj,jq->epq",
            gelu_output_rows,
            down_projection_weight,
            preferred_element_type=jnp.float32,
        )
    )
    result = after_attn + mlp_part + down_bias
    kept_values = (query_rows, key_rows, value_rows, softmax_probs, probs_low, after_attn, up_pre)
    return (result, kept_values)


def tensor_backward(own_rows, arriving, weights, kept_values):
    (
        attn_gain,
        attn_shift,
        query_key_value_weight,
        qkv_bias,
        attention_output_weight,
        out_bias,
        ffn_gain,
        ffn_shift,
        up_projection_weight,
        up_projection_bias,
        down_projection_weight,
        down_bias,
        out_full,
    ) = weights
    query_rows, key_rows, value_rows, softmax_probs, probs_low, after_attn, up_pre = kept_values
    gradient_gathered = gather_rows(arriving)
    gradient_activation = jnp.einsum(
        "bhi,vi->bhv", gradient_gathered, down_projection_weight, preferred_element_type=jnp.float32
    )
    gelu_value, gelu_back = jax.vjp(gelu_tanh, up_pre)
    gradient_up_projection = gelu_back(gradient_activation)[0].astype(jnp.bfloat16)
    grad_two = reduce_rows(
        jnp.einsum(
            "yca,ja->ycj",
            gradient_up_projection,
            up_projection_weight,
            preferred_element_type=jnp.float32,
        )
    )
    grad_after = norm_input_grad(after_attn, ffn_gain, ffn_shift, grad_two)
    grad_mid = (grad_after + arriving.astype(jnp.float32)).astype(jnp.bfloat16)
    middle_gathered = gather_rows(grad_mid)
    grad_mix = jnp.einsum(
        "taq,kq->tak", middle_gathered, attention_output_weight, preferred_element_type=jnp.float32
    ).astype(jnp.bfloat16)
    query_grad, key_grad, value_grad = attend_back(
        grad_mix, query_rows, key_rows, value_rows, softmax_probs, probs_low
    )
    prefix_g = prefix_part(key_grad, value_grad)
    batch_size, seq_len = (query_grad.shape[0], query_grad.shape[1])
    gradient_query_key_value = jnp.stack(
        [query_grad, key_grad[:, PREFIX:], value_grad[:, PREFIX:]], axis=3
    )
    gradient_query_key_value = gradient_query_key_value.astype(jnp.bfloat16).reshape(
        batch_size, seq_len, -1
    )
    grad_one = reduce_rows(
        jnp.einsum(
            "tvq,xq->tvx",
            gradient_query_key_value,
            query_key_value_weight,
            preferred_element_type=jnp.float32,
        )
    )
    grad_input = norm_input_grad(own_rows, attn_gain, attn_shift, grad_one)
    grad_input = (grad_input + grad_mid.astype(jnp.float32)).astype(jnp.bfloat16)
    return (grad_input, prefix_g)


def prefix_back(prefix_sum, hidden_grad, hidden_act, hidden_low, prefix_table, mid_weight):
    prefix_low = prefix_sum.astype(jnp.bfloat16)
    prefix_bias_grad = jnp.sum(prefix_low.astype(jnp.float32), axis=0)
    prefix_weight_grad = jnp.dot(hidden_low.T, prefix_low, preferred_element_type=jnp.float32)
    pre_grad = (hidden_grad * (1.0 - hidden_act * hidden_act)).astype(jnp.bfloat16)
    mid_bias_grad = jnp.sum(pre_grad.astype(jnp.float32), axis=0)
    mid_weight_grad = jnp.dot(prefix_table.T, pre_grad, preferred_element_type=jnp.float32)
    table_grad = jnp.dot(pre_grad, mid_weight.T, preferred_element_type=jnp.float32)
    return (table_grad, mid_weight_grad, mid_bias_grad, prefix_weight_grad, prefix_bias_grad)


def both_layers(piece):
    return lax.all_gather(piece[0], "section", axis=0, tiled=False)


def body(
    layer_input,
    cotangent,
    example_lengths,
    attn_gain,
    attn_shift,
    query_key_value_weight,
    qkv_bias,
    attention_output_weight,
    out_bias,
    ffn_gain,
    ffn_shift,
    up_projection_weight,
    up_projection_bias,
    down_projection_weight,
    down_bias,
    prefix_table,
    mid_weight,
    mid_bias,
    prefix_weight,
    prefix_bias,
):
    layers = lax.axis_size("section")
    section_index = lax.axis_index("section")
    hidden_pre = jnp.dot(
        prefix_table, mid_weight, preferred_element_type=jnp.float32
    ) + mid_bias.astype(jnp.float32)
    hidden_act = jnp.tanh(hidden_pre)
    hidden_low = hidden_act.astype(jnp.bfloat16)
    prefix_kv = (
        jnp.dot(hidden_low, prefix_weight, preferred_element_type=jnp.float32)
        + prefix_bias.astype(jnp.float32)
    ).astype(jnp.bfloat16)
    prefix_all = lax.all_gather(prefix_kv, "section", axis=0, tiled=False)
    floats = [
        both_layers(piece).astype(jnp.float32)
        for piece in (attn_gain, attn_shift, qkv_bias, out_bias, ffn_gain, ffn_shift,
                      up_projection_bias, down_bias)
    ]
    matrices = [
        both_layers(piece)
        for piece in (query_key_value_weight, attention_output_weight,
                      up_projection_weight, down_projection_weight)
    ]

    def weights_of(layer):
        g1, s1, bq, bo, g2, s2, bu, bd = [piece[layer] for piece in floats]
        wq, wo, wu, wd = [piece[layer] for piece in matrices]
        return (g1, s1, wq, bq, wo, bo, g2, s2, wu, bu, wd, bd, wo)

    batch_count = layer_input.shape[0]
    own_input = lax.dynamic_index_in_dim(layer_input, section_index, 0, keepdims=False)
    own_cotangent = lax.dynamic_index_in_dim(cotangent, section_index, 0, keepdims=False)
    lengths = lax.dynamic_index_in_dim(example_lengths, section_index, 0, keepdims=False)
    visible = visible_of(lengths, 0, SEQ_LEN)
    entering = own_input
    entered, produced, kept = [], [], []
    for layer in range(layers):
        entered.append(entering.astype(jnp.float32))
        result, kept_values = tensor_forward(
            entered[layer], weights_of(layer), prefix_all[layer], visible
        )
        entering = result.astype(jnp.bfloat16)
        produced.append(entering)
        kept.append(kept_values)
    gradient = own_cotangent
    sent_grads = [None] * layers
    prefix_parts = [None] * layers
    for layer in reversed(range(layers)):
        gradient, prefix_parts[layer] = tensor_backward(
            entered[layer], gradient, weights_of(layer), kept[layer]
        )
        sent_grads[layer] = gradient
    activations = lax.all_to_all(jnp.stack(produced), "section", 0, 0, tiled=False)
    input_grads = lax.all_to_all(jnp.stack(sent_grads), "section", 0, 0, tiled=False)
    prefix_sum = lax.psum(jnp.stack(prefix_parts), ("dp", "section"))
    prefix_sum = lax.dynamic_index_in_dim(prefix_sum, section_index, 0, keepdims=False)
    hidden_part = jnp.dot(
        prefix_sum.astype(jnp.bfloat16), prefix_weight.T, preferred_element_type=jnp.float32
    )
    hidden_grad = lax.psum(hidden_part, ("section", "mp"))
    return (activations[None], input_grads[None]) + prefix_back(
        prefix_sum, hidden_grad, hidden_act, hidden_low, prefix_table, mid_weight
    )


MESH = pl.DeviceIdType.MESH
BLOCK = 256
LOG2E = 1.4426950408889634
CHUNK = 128
UNITS = 12
AHEAD = 10
UNIT_ROWS = 512
PART_ROWS = UNIT_ROWS // 8


def role_of(z):
    return (((z + 1) // 2) + 1) % 2


def block_of(s, j):
    return j * 3 + s * (1 - 2 * j)


def core_of(block):
    return ((block + 1) // 2) % 2


def guarded(when, action):
    if when is None:
        action()
    else:
        pl.when(when)(action)


def dot_nn(a, b):
    return lax.dot_general(a, b, (((1,), (0,)), ((), ())), preferred_element_type=jnp.float32)


def dot_nt(a, b):
    return lax.dot_general(a, b, (((1,), (1,)), ((), ())), preferred_element_type=jnp.float32)


def dot_tn(a, b):
    return lax.dot_general(a, b, (((0,), (0,)), ((), ())), preferred_element_type=jnp.float32)


class Sends:
    def __init__(self, sems):
        self.sems, self.used, self.pending = sems, 0, []

    def start(self, src, dst, recv_sem, target, when=None):
        copy = pltpu.make_async_remote_copy(
            src_ref=src, dst_ref=dst, send_sem=self.sems.at[self.used], recv_sem=recv_sem,
            device_id=target, device_id_type=MESH,
        )
        self.used += 1
        guarded(when, copy.start)
        self.pending.append((when, copy))

    def start_or_keep(self, src, dst, recv_sem, target, is_here, when=True):
        @pl.when(jnp.logical_and(when, is_here))
        def _():
            pltpu.make_async_copy(src, dst, recv_sem).start()

        self.start(src, dst, recv_sem, target, when=jnp.logical_and(when, jnp.logical_not(is_here)))

    def finish(self):
        for when, copy in self.pending:
            guarded(when, copy.wait_send)
        self.pending = []


def layer_kernel(
    x_hbm, cot_hbm, wq_hbm, wo_hbm, wu_hbm, wd_hbm,
    g1, s1, bo, g2, s2, bd, bu, bq, table, mid_w, mid_b, pw, pb, lengths,
    act_out, ig_out, sum_out, hidden_out, tanh_out,
    vec_own, pre_full, pre_own, wq, wo, wud, vec, pre,
    x_in, g_in, y_out, normed, kv, q_own, o_own, lse, bias, after, acc, slope, wide,
    pg, pg_near, pg_far, hidden_core, hidden_all, ts, dkv_own, dkv_send, dkv_recv, kp, vp, gt,
    ssem, vec_sem, pre_sem, x_sem, g_sem, act_sem, ig_sem, own_sem, z_sem, a_sem, b_sem, c_sem,
    zr_sem, ar_sem, br_sem, cr_sem, fs_sem, zs_sem, as_sem, bs_sem, cs_sem, go_sem,
    kv_ssem, kv_rsem, dkv_ssem, dkv_rsem, pg_sem, far_sem, core_sem, hidden_sem,
    hand_sem, cot_sem, x_ssem, pg_ssem, far_ssem, mid_sem,
):
    s, d, z = lax.axis_index("section"), lax.axis_index("dp"), lax.axis_index("mp")
    role, micro = role_of(z), z // 2
    other = 1 - s
    partner = z + 1 - 2 * (z % 2)
    x_near, y_near = d + 1 - 2 * (d % 2), (d + 2) % 4
    near1 = jnp.where(s == 0, x_near, y_near)
    near2 = jnp.where(s == 0, y_near, x_near)
    sends = Sends(ssem)

    barrier = pltpu.get_barrier_semaphore()
    for ds in range(2):
        for dz in range(4):
            if ds or dz:
                pl.semaphore_signal(barrier, inc=1, device_id=((s + ds) % 2, d, (z + dz) % 4), device_id_type=MESH)
    for near in (x_near, y_near, 3 - d):
        pl.semaphore_signal(barrier, inc=1, device_id=(s, near, z), device_id_type=MESH)
    pl.semaphore_wait(barrier, 10)

    def arrived(dst, sem):
        pltpu.make_async_remote_copy(
            src_ref=dst, dst_ref=dst, send_sem=ssem.at[0], recv_sem=sem,
            device_id=(other, d, z), device_id_type=MESH,
        ).wait_recv()

    low_plane, high_plane = jnp.where(s == 0, 1, 0), jnp.where(s == 0, 2, 3)
    planes = (low_plane, high_plane)
    mine = s == core_of(z)
    row_slot = pl.ds(pl.multiple_of((z // 2) * BLOCK, BLOCK), BLOCK)

    def send_small(when):
        for t in planes:
            for h in range(2):
                is_here = jnp.logical_and(z == t, s == h)
                sends.start_or_keep(pre_own, pre.at[z], pre_sem.at[z], (h, d, t), is_here, when)

    def row_copies(source, landing, send_sem, sem, chips, then):
        for k, chip in enumerate(chips):

            @pl.when(jnp.logical_and(mine, z != chip))
            def _():
                then(pltpu.make_async_remote_copy(
                    src_ref=source.at[k], dst_ref=landing.at[row_slot], send_sem=send_sem.at[k],
                    recv_sem=sem.at[z // 2], device_id=(s, d, chip), device_id_type=MESH,
                ))

    def keep_rows(source, landing, sem, chips):
        for k, chip in enumerate(chips):

            @pl.when(jnp.logical_and(mine, z == chip))
            def _():
                pltpu.make_async_copy(source.at[k], landing.at[row_slot], sem.at[z // 2]).start()

    def x_copies(then):
        row_copies(x_hbm, x_in, x_ssem, x_sem, (1, 2), then)

    def cot_copies(then):
        row_copies(cot_hbm, g_in, cot_sem, g_sem, (0, 3), then)

    keep_rows(x_hbm, x_in, x_sem, (1, 2))
    keep_rows(cot_hbm, g_in, g_sem, (0, 3))

    toward = jnp.where(z < 2, 1, -1)

    def quarter(i):
        return (z + 4 + toward * i) % 4

    def taker(i):
        low, high = (z + 3 - i) % 4, (z + 1 + i) % 4
        return jnp.where(low == low_plane, low, high), jnp.logical_or(low == low_plane, high == high_plane)

    swapped = (d % 2) * 2 + d // 2
    place = jnp.where(s == 0, d, swapped)
    pair_start = (place // 2) * 2
    far_start = 2 - pair_start
    firsts = ((wq_hbm, wq), (wo_hbm, wo))

    def eighths(rows, start, count, h):
        return pl.ds(pl.multiple_of((start + 4 * h) * rows, rows), rows * count)

    def supply_first(w, i, then):
        t, taken = taker(i)
        held, full = firsts[w]

        @pl.when(taken)
        def _():
            for h in range(2):
                at = eighths(held.shape[0] // 8, swapped if h else d, 1, h)
                then(pltpu.make_async_remote_copy(
                    src_ref=held.at[at], dst_ref=full.at[z, at], send_sem=fs_sem.at[3 * w + i, h],
                    recv_sem=z_sem.at[w, z], device_id=(h, d, t), device_id_type=MESH,
                ))

    def supply_firsts(when, w):
        @pl.when(when)
        def _():
            def one(i, carry):
                supply_first(w, i, lambda copy: copy.start())
                return carry

            lax.fori_loop(0, 3, one, 0)

    def firsts_done(when, w):
        @pl.when(when)
        def _():
            def one(i, carry):
                supply_first(w, i, lambda copy: copy.wait_send())
                return carry

            lax.fori_loop(0, 3, one, 0)

    def supply_copies(i, c, then):
        t, taken = taker(i)
        held, base = ((wu_hbm, 0), (wd_hbm, 1024))[c // 2]

        @pl.when(taken)
        def _():
            for h in range(2):
                at = eighths(PART_ROWS, swapped if h else d, 1, h)
                start = (c % 2) * UNIT_ROWS + at.start
                then(pltpu.make_async_remote_copy(
                    src_ref=held.at[pl.ds(pl.multiple_of(start, PART_ROWS), PART_ROWS)],
                    dst_ref=wud.at[z, pl.ds(pl.multiple_of(base + start, PART_ROWS), PART_ROWS)],
                    send_sem=zs_sem.at[4 * i + c, h], recv_sem=zr_sem.at[4 * i + c],
                    device_id=(h, d, t), device_id_type=MESH,
                ))

    def supply_all(i, carry):
        for c in range(4):
            supply_copies(i, c, lambda copy: copy.start())
        return carry

    def supply_done(i, carry):
        for c in range(4):
            supply_copies(i, c, lambda copy: copy.wait_send())
        return carry

    feeds_zero = jnp.logical_and(role == 1, s == 0)
    feeds_zero_late = jnp.logical_and(role == 0, s == 0)
    feeds_one = jnp.logical_and(role == 0, s == 1)
    feeds_one_late = jnp.logical_and(role == 1, s == 1)
    supply_firsts(s == 0, 0)

    @pl.when(feeds_one)
    def _():
        for w in range(2):
            supply_first(w, 0, lambda copy: copy.start())
        supply_all(0, 0)

    mid_copies = mid_w.shape[1] // 128

    def mid_copy(n, half):
        return pltpu.make_async_copy(
            mid_w.at[half * 512 : half * 512 + 512, n * 128 : n * 128 + 128], q_own.at[2 * n + half],
            mid_sem.at[2 * n + half],
        )

    for n in range(mid_copies):
        for half in range(2):
            mid_copy(n, half).start()
    for k, row in enumerate((g1, s1, bo, g2, s2, bd)):
        vec_own[k : k + 1, :] = row[...].astype(jnp.float32)

    @pl.when(role == s)
    def _():
        pltpu.make_async_copy(vec_own, vec.at[0], vec_sem.at[0]).start()

    sends.start(vec_own, vec.at[0], vec_sem.at[0], (other, d, z), when=role == s)
    tanh_out[...] = jnp.zeros(tanh_out.shape, jnp.float32)
    for n in range(mid_copies):
        for half in range(2):
            mid_copy(n, half).wait()
        cols = slice(n * 128, n * 128 + 128)
        part_sum = dot_nn(table[:, 0:512], q_own[2 * n]) + dot_nn(table[:, 512:1024], q_own[2 * n + 1])
        tanh_out[0:PREFIX, cols] = jnp.tanh(part_sum + mid_b[...].astype(jnp.float32).reshape(1, -1)[:, cols])
    pre_full[...] = dot_nn(tanh_out[...].astype(jnp.bfloat16), pw[...]) + pb[...].astype(jnp.float32).reshape(1, -1)
    half_width = pre_full.shape[1]
    for k, row in enumerate((bu, bq)):
        for n in range(2):
            piece = row[:, n * half_width : min((n + 1) * half_width, row.shape[1])]
            pre_full[PREFIX + 2 * k + n : PREFIX + 2 * k + n + 1, 0 : piece.shape[1]] = piece.astype(jnp.float32)
    pre_own[...] = pre_full[...].astype(jnp.bfloat16)
    send_small(feeds_zero)
    firsts_done(feeds_zero, 0)
    supply_firsts(feeds_zero, 1)

    @pl.when(feeds_zero)
    def _():
        x_copies(lambda copy: copy.start())
    owned = ((wq_hbm, wq.at[z]), (wo_hbm, wo.at[z]), (wu_hbm, wud.at[z, 0:1024]), (wd_hbm, wud.at[z, 1024:2048]))
    for w, (held, full) in enumerate(owned):
        @pl.when(role == s)
        def _():
            pltpu.make_async_copy(held, full, own_sem.at[w]).start()

        sends.start(held, full, own_sem.at[w], (other, d, z), when=role == s)

    @pl.when(feeds_zero)
    def _():
        x_copies(lambda copy: copy.wait_send())
        lax.fori_loop(0, 3, supply_all, 0)

    @pl.when(feeds_one_late)
    def _():
        pl.semaphore_wait(go_sem, 1)

    send_small(feeds_one_late)
    supply_firsts(feeds_one_late, 0)
    supply_firsts(feeds_one_late, 1)

    first_units = [(w, i) for w in (0, 1) for i in range(1, 4)]

    def first_piece(w, i, start, count):
        full = firsts[w][1]
        return full.at[quarter(i), eighths(full.shape[1] // 8, start, count, s)]

    def relay_first(step):
        stages = [first_units[step - k] if 0 <= step - k < len(first_units) else None for k in range(4)]
        if stages[0]:
            w, i = stages[0]
            q = quarter(i)
            arrived(first_piece(w, i, place, 1), z_sem.at[w, q])
            sends.start(first_piece(w, i, place, 1), first_piece(w, i, place, 1), a_sem.at[w, q], (s, near1, z))
        if stages[1]:
            w, i = stages[1]
            q = quarter(i)
            arrived(first_piece(w, i, pair_start + 1 - place % 2, 1), a_sem.at[w, q])
            sends.start(first_piece(w, i, pair_start, 2), first_piece(w, i, pair_start, 2), b_sem.at[w, q], (s, near2, z))
        if stages[2]:
            w, i = stages[2]
            q = quarter(i)
            arrived(first_piece(w, i, far_start, 2), b_sem.at[w, q])
            sends.start(first_piece(w, i, 0, 4), first_piece(w, i, 0, 4), c_sem.at[w, q], (other, d, z))
        if stages[3]:
            w, i = stages[3]
            full = firsts[w][1]
            arrived(full.at[quarter(i), eighths(full.shape[1] // 8, 0, 4, other)], c_sem.at[w, quarter(i)])

    for step in range(len(first_units) + 3):
        relay_first(step)
        if step == 0:
            @pl.when(role == 0)
            def _():
                x_copies(lambda copy: copy.start())

            send_small(feeds_zero_late)
            supply_firsts(feeds_zero_late, 1)
        if step == 3:
            @pl.when(feeds_one)
            def _():
                pl.semaphore_signal(go_sem, inc=1, device_id=(1, d, partner), device_id_type=MESH)

                supply_first(0, 1, lambda copy: copy.start())

            send_small(feeds_one)
        if step == 6:
            @pl.when(feeds_one)
            def _():
                supply_first(1, 1, lambda copy: copy.start())


        @pl.when(feeds_zero_late)
        def _():
            if 1 <= step < 5:
                supply_copies(0, step - 1, lambda copy: copy.start())

    @pl.when(feeds_one_late)
    def _():
        lax.fori_loop(0, 3, supply_all, 0)

    def unit_piece(m, start, count, h):
        q = quarter(1 + m // 4)
        first_row = (m % 4) * UNIT_ROWS + (start + 4 * h) * PART_ROWS
        return wud.at[q, pl.ds(pl.multiple_of(first_row, PART_ROWS), PART_ROWS * count)]

    def relay_copy(m, stage):
        start, count = ((place, 1), (pair_start, 2), (0, 4))[stage]
        at = unit_piece(m, start, count, s)
        return pltpu.make_async_remote_copy(
            src_ref=at, dst_ref=at, send_sem=(as_sem, bs_sem, cs_sem)[stage].at[m],
            recv_sem=(ar_sem, br_sem, cr_sem)[stage].at[m],
            device_id=((s, near1, z), (s, near2, z), (other, d, z))[stage], device_id_type=MESH,
        )

    def relay(n):
        for c in range(4):

            @pl.when(jnp.logical_and(feeds_one, n == c))
            def _():
                supply_copies(1, c, lambda copy: copy.start())

        for k, lag in enumerate((0, 1, 3, 4)):
            m = n - lag

            @pl.when(jnp.logical_and(m >= 0, m < UNITS))
            def _():
                if k == 0:
                    arrived(unit_piece(m, place, 1, s), zr_sem.at[m])
                if k == 1:
                    arrived(unit_piece(m, pair_start + 1 - place % 2, 1, s), ar_sem.at[m])
                if k == 2:
                    arrived(unit_piece(m, far_start, 2, s), br_sem.at[m])
                if k == 3:
                    arrived(unit_piece(m, 0, 4, other), cr_sem.at[m])
                if k < 3:
                    relay_copy(m, k).start()

    @pl.when(role == 1)
    def _():
        cot_copies(lambda copy: copy.start())
    def relay_steps(start, stop):
        def one(n, carry):
            relay(n)
            return carry

        lax.fori_loop(start, stop, one, 0)

    relay_steps(0, jnp.where(role == 1, AHEAD, 0))
    arrived(wq.at[z], own_sem.at[0])
    arrived(wo.at[z], own_sem.at[1])
    arrived(wud.at[z, 0:1024], own_sem.at[2])
    arrived(wud.at[z, 1024:2048], own_sem.at[3])
    arrived(vec.at[0], vec_sem.at[0])
    for q in range(4):
        arrived(pre.at[q], pre_sem.at[q])
        carried = pre[q].astype(jnp.float32)
        for k in range(2):
            for n in range(2):
                row = PREFIX + 2 * k + n
                vec[q, 6 + k : 7 + k, n * half_width : (n + 1) * half_width] = carried[row : row + 1, :]

    first16 = lax.broadcasted_iota(jnp.int32, (16, 128), 1) < HEAD_DIM
    first = lax.broadcasted_iota(jnp.int32, (BLOCK, 128), 1) < HEAD_DIM
    lane = lax.broadcasted_iota(jnp.int32, (1, 128), 1)
    half0 = jnp.where(lane < HEAD_DIM, 1.0, 0.0).astype(jnp.bfloat16)
    half1 = jnp.where(lane < HEAD_DIM, 0.0, 1.0).astype(jnp.bfloat16)
    upper = lax.broadcasted_iota(jnp.int32, (128, BLOCK), 0) < HEAD_DIM
    slot = lax.broadcasted_iota(jnp.int32, (128, 1), 0)
    pre_mask_down = jnp.where(slot % HEAD_DIM < PREFIX, 0.0, NEG_LARGE)
    pre_mask = jnp.where(lane % HEAD_DIM < PREFIX, 0.0, NEG_LARGE)
    kp[...] = jnp.zeros(kp.shape, kp.dtype)
    vp[...] = jnp.zeros(vp.shape, vp.dtype)
    for q in range(4):
        for p in range(2):
            t0 = pre[q, :, p * 256 : p * 256 + 128].astype(jnp.float32)
            t1 = pre[q, :, p * 256 + 128 : p * 256 + 256].astype(jnp.float32)
            kp[2 * q + p, 0:16, :] = jnp.where(first16, t0, 0.0).astype(jnp.bfloat16)
            kp[2 * q + p, 64:80, :] = jnp.where(first16, 0.0, pltpu.roll(t1, 64, 1)).astype(jnp.bfloat16)
            vp[2 * q + p, 0:16, :] = jnp.where(first16, pltpu.roll(t0, 64, 1), 0.0).astype(jnp.bfloat16)
            vp[2 * q + p, 64:80, :] = jnp.where(first16, 0.0, t1).astype(jnp.bfloat16)

    def mask_blocks(keys_down):
        for j in range(2):
            row0 = block_of(s, j) * BLOCK
            row_at = row0 + lax.broadcasted_iota(jnp.int32, (1, BLOCK) if keys_down else (BLOCK, 1), int(keys_down))
            begin = jnp.zeros(row_at.shape, jnp.int32)
            end = 0
            for e in range(lengths.shape[1]):
                end = end + lengths[micro, e]
                begin = jnp.where(row_at >= end, end, begin)

            def mask_block(kb, carry):
                key_at = kb * BLOCK + lax.broadcasted_iota(jnp.int32, (BLOCK, BLOCK), 1 - int(keys_down))
                keep = jnp.logical_and(key_at <= row_at, key_at >= begin)
                bias[2 * j + kb] = jnp.where(keep, 0.0, NEG_LARGE)
                return carry

            lax.fori_loop(0, 2 + 2 * j, mask_block, 0)

    mask_blocks(False)

    def vector(k, q=0, width=1024):
        return vec[q, k : k + 1, 0:width]

    def columns(n, width):
        return pl.ds(pl.multiple_of(n * width, width), width)

    def block_rows(j):
        return pl.ds(pl.multiple_of(j * BLOCK, BLOCK), BLOCK)

    def over_rows(j, action):
        def one(c, carry):
            action(pl.ds(pl.multiple_of(j * BLOCK + c * CHUNK, CHUNK), CHUNK))
            return carry

        lax.fori_loop(0, BLOCK // CHUNK, one, 0)

    def standardize(v):
        average = jnp.mean(v, axis=-1, keepdims=True)
        centred = v - average
        spread = jnp.mean(centred * centred, axis=-1, keepdims=True)
        return centred, lax.rsqrt(spread + EPSILON)

    def norm_back(v, gain, incoming):
        centred, inverse = standardize(v)
        xhat = centred * inverse
        e = incoming * gain
        return (e - jnp.mean(e, axis=-1, keepdims=True) - xhat * jnp.mean(e * xhat, axis=-1, keepdims=True)) * inverse

    def to_core(ref, send_sem, recv_sem):
        return pltpu.make_async_remote_copy(
            src_ref=ref, dst_ref=ref, send_sem=send_sem, recv_sem=recv_sem,
            device_id=(other, d, z), device_id_type=MESH,
        )

    scale = LOG2E * HEAD_DIM ** (-0.5)

    def enter(j):
        rows = block_rows(j)
        arrived(x_in.at[rows], x_sem.at[j])

        def norm_one(rows):
            centred, inverse = standardize(x_in[rows, :].astype(jnp.float32))
            normed[rows, :] = (centred * inverse * vector(0) + vector(1)).astype(jnp.bfloat16)

        over_rows(j, norm_one)

        def project(q, carry):
            triple = dot_nn(normed[rows, :], wq[q]) + vec[q, 7:8, 0:768]
            for p in range(2):
                t0, t1, t2 = (triple[:, p * 384 + n * 128 : p * 384 + n * 128 + 128] for n in range(3))
                q_own[2 * q + p, rows, :] = jnp.where(first, t0, t1).astype(jnp.bfloat16)
                kv[s, 2 * q + p, 0, rows, :] = pltpu.roll(jnp.where(first, t2, t0), 64, 1).astype(jnp.bfloat16)
                kv[s, 2 * q + p, 1, rows, :] = jnp.where(first, t1, t2).astype(jnp.bfloat16)
            to_core(kv.at[s, pl.ds(2 * q, 2), :, rows], kv_ssem.at[j, q], kv_rsem.at[j, q]).start()
            return carry

        lax.fori_loop(0, 4, project, 0)

    def attend_rows(pair, core, j):
        cols = columns(pair, 128)
        rows = slice(j * BLOCK, j * BLOCK + BLOCK)
        blocks = block_of(core, j) + 1
        q_pair = q_own[pair, rows, :]
        q_half = (q_pair * half0, q_pair * half1)
        t_pre = dot_nt(q_pair, kp[pair]) * scale + pre_mask
        tops = [jnp.where(first, t_pre, NEG_LARGE), jnp.where(first, NEG_LARGE, t_pre)]
        for kb in range(blocks):
            keys = kv[core_of(kb), pair, 0, (kb // 2) * BLOCK : (kb // 2 + 1) * BLOCK, :]
            for h in range(2):
                t = dot_nt(q_half[h], keys) * scale + bias[2 * j + kb]
                ts[h, kb] = t
                tops[h] = jnp.maximum(tops[h], jnp.maximum(t[:, :128], t[:, 128:]))
        highest = [jnp.max(tops[h], axis=1, keepdims=True) for h in range(2)]
        e_pre = jnp.exp2(t_pre - jnp.where(first, highest[0], highest[1]))
        sums = [jnp.where(first, e_pre, 0.0), jnp.where(first, 0.0, e_pre)]
        mixed = [jnp.zeros((BLOCK, 128), jnp.float32) for _ in range(2)]
        for kb in range(blocks):
            values = kv[core_of(kb), pair, 1, (kb // 2) * BLOCK : (kb // 2 + 1) * BLOCK, :]
            for h in range(2):
                e = jnp.exp2(ts[h, kb] - highest[h])
                sums[h] += e[:, :128] + e[:, 128:]
                mixed[h] += dot_nn(e.astype(jnp.bfloat16), values)
        total = [jnp.sum(sums[h], axis=1, keepdims=True) for h in range(2)]
        share = [1.0 / total[h] for h in range(2)]
        p_pre = (e_pre * jnp.where(first, share[0], share[1])).astype(jnp.bfloat16)
        result = jnp.where(first, mixed[0] * share[0], mixed[1] * share[1]) + dot_nn(p_pre, vp[pair])
        o_own[rows, cols] = result.astype(jnp.bfloat16)
        logs = [highest[h] + jnp.log(total[h]) * LOG2E for h in range(2)]
        lse[pair, rows, :] = jnp.where(first, logs[0], logs[1])

    def attend(j, relay_at):
        def kv_wait(q, carry):
            to_core(kv.at[s, pl.ds(2 * q, 2), :, block_rows(j)], kv_ssem.at[j, q], kv_rsem.at[j, q]).wait_send()
            arrived(kv.at[other, pl.ds(2 * q, 2), :, block_rows(j)], kv_rsem.at[j, q])
            return carry

        lax.fori_loop(0, 4, kv_wait, 0)
        for core in range(2):
            for block in range(2):

                @pl.when(jnp.logical_and(s == core, j == block))
                def _():
                    def attend_pair(pair, carry):
                        relay_steps(relay_at, jnp.where(jnp.logical_and(pair == 4, relay_at < UNITS + 4), relay_at + 1, relay_at))
                        attend_rows(pair, core, block)
                        return carry

                    lax.fori_loop(0, 8, attend_pair, 0)

        rows = block_rows(j)
        after[rows, :] = (
            x_in[rows, :].astype(jnp.float32) + dot_nn(o_own[rows, :], wo[...].reshape(1024, 1024)) + vector(2)
        )

        def norm_two(rows):
            centred, inverse = standardize(after[rows, :])
            normed[rows, :] = (centred * inverse * vector(3) + vector(4)).astype(jnp.bfloat16)
            acc[rows, :] = after[rows, :] + vector(5)

        over_rows(j, norm_two)

    def feed(j, i):
        rows = block_rows(j)
        q = quarter(i)
        u = dot_nn(normed[rows, :], wud[q, 0:1024, :]) + vec[q, 6:7, :]
        v = u * (GELU_A + (GELU_A * GELU_B) * (u * u))
        half_t = 0.5 + 0.5 * jnp.tanh(v)
        wide[rows, :] = (u * half_t).astype(jnp.bfloat16)
        slope[q, rows, :] = (half_t + half_t * (1.0 - half_t) * (6.0 * v - (4.0 * GELU_A) * u)).astype(jnp.bfloat16)
        acc[rows, :] += dot_nn(wide[rows, :], wud[q, 1024:2048, :])

    def hand_copies(j, k):
        rows = block_rows(j)
        landing, sem = ((x_in, x_sem), (act_out, act_sem), (g_in, g_sem), (ig_out, ig_sem))[k]
        if k % 2:
            dst, sem, target = landing.at[micro], sem.at[micro], (role, d, block_of(s, j))
        else:
            dst, sem, target = landing.at[rows], sem.at[j], (s, d, partner)
        return pltpu.make_async_remote_copy(
            src_ref=y_out.at[rows], dst_ref=dst, send_sem=hand_sem.at[k, j], recv_sem=sem,
            device_id=target, device_id_type=MESH,
        )

    def hand_on(j):
        rows = block_rows(j)
        y_out[rows, :] = acc[rows, :].astype(jnp.bfloat16)

        @pl.when(role == 1)
        def _():
            hand_copies(j, 1).start()

        @pl.when(jnp.logical_and(role == 0, j == 0))
        def _():
            hand_copies(0, 0).start()

        @pl.when(jnp.logical_and(role == 0, j == 1))
        def _():
            hand_copies(0, 0).wait_send()
            hand_copies(1, 0).start()
            hand_copies(1, 0).wait_send()
            for block in range(2):
                hand_copies(block, 1).start()

    def upto(n, table):
        total = jnp.int32(0)
        for k, entry in enumerate(table):
            total += jnp.where(n >= k, entry - (table[k - 1] if k else 0), 0)
        return total

    early_table = (0, 1, 2, 4, 6, 7, 8, 10, 12, 14, 16, 16, 16, 16)
    late_table = (AHEAD, 11, 13, 14, 15, 16, 16, 16, 16, 16, 16, 16, 16, 16)

    def forward(n, carry):
        turn = jnp.where(n == 11, 12, jnp.where(n == 12, 11, n))
        stage = jnp.where(role == 0, turn // 2, n % 7)
        j = jnp.where(role == 0, turn % 2, n // 7)
        before = jnp.where(
            role == 0,
            jnp.where(n == 0, 0, upto(n - 1, early_table)) + jnp.where(jnp.logical_or(n == 3, n == 4), 1, 0),
            jnp.where(n == 0, AHEAD, upto(n - 1, late_table)) + jnp.where(n == 2, 1, 0),
        )
        until = jnp.where(role == 0, upto(n, early_table), upto(n, late_table))
        relay_steps(before, until)

        @pl.when(jnp.logical_and(role == 0, n == 6))
        def _():
            cot_copies(lambda copy: copy.start())

        @pl.when(stage == 0)
        def _():
            enter(j)

        @pl.when(stage == 1)
        def _():
            attend(j, until)

        @pl.when(jnp.logical_and(stage >= 2, stage < 6))
        def _():
            feed(j, stage - 2)

        @pl.when(stage == 6)
        def _():
            hand_on(j)

        return carry

    lax.fori_loop(0, 14, forward, 0)

    def back_rows(pair, core, j):
        cols = columns(pair, 128)
        rows = slice(j * BLOCK, j * BLOCK + BLOCK)
        q_pair = q_own[pair, rows, :]
        q_half = (q_pair * half0, q_pair * half1)
        g_pair = wide[rows, cols]
        g_half = (g_pair * half0, g_pair * half1)
        product = g_pair.astype(jnp.float32) * o_own[rows, cols].astype(jnp.float32)
        row_term = [
            jnp.sum(jnp.where(first, product, 0.0), axis=1, keepdims=True),
            jnp.sum(jnp.where(first, 0.0, product), axis=1, keepdims=True),
        ]
        logs = jnp.transpose(lse[pair, rows, :])
        terms = jnp.transpose(jnp.where(first, row_term[0], row_term[1]))
        log_half = (logs[0:1, :], logs[64:65, :])
        term_half = (terms[0:1, :], terms[64:65, :])
        p_pre = jnp.exp2(dot_nt(kp[pair], q_pair) * scale + pre_mask_down - logs)
        dp_pre = dot_nt(vp[pair], g_pair)
        ds_pre = (p_pre * (dp_pre - terms)).astype(jnp.bfloat16)
        pv = dot_nn(p_pre.astype(jnp.bfloat16), g_pair)
        pk = dot_nn(ds_pre, q_pair)
        pk = jnp.where(first16, pk[0:16, :], pk[64:80, :]) * HEAD_DIM ** (-0.5)
        pv = jnp.where(first16, pv[0:16, :], pv[64:80, :])
        pg[pair, 0] = pk if j else pg[pair, 0] + pk
        pg[pair, 1] = pv if j else pg[pair, 1] + pv
        dq_pre = dot_tn(kp[pair], ds_pre)
        dqs = [jnp.zeros((128, BLOCK), jnp.float32) for _ in range(2)]
        for kb in range(4):
            held = dkv_own if core_of(kb) == core else dkv_send
            at = slice((kb // 2) * BLOCK, (kb // 2 + 1) * BLOCK)
            if kb > block_of(core, j):
                if j:
                    held[pair, 0, at, :] = jnp.zeros((BLOCK, 128), jnp.bfloat16)
                    held[pair, 1, at, :] = jnp.zeros((BLOCK, 128), jnp.bfloat16)
                continue
            keys = kv[core_of(kb), pair, 0, at, :]
            values = kv[core_of(kb), pair, 1, at, :]
            dv, dk = 0.0, 0.0
            if j == 0:
                dk = held[pair, 0, at, :].astype(jnp.float32)
                dv = held[pair, 1, at, :].astype(jnp.float32)
            for h in range(2):
                probs = jnp.exp2(dot_nt(keys, q_half[h]) * scale + bias[2 * j + kb] - log_half[h])
                grad_probs = dot_nt(values, g_half[h])
                grad_scores = (probs * (grad_probs - term_half[h])).astype(jnp.bfloat16)
                dv += dot_nn(probs.astype(jnp.bfloat16), g_half[h])
                dk += dot_nn(grad_scores, q_half[h])
                dqs[h] += dot_tn(keys, grad_scores)
            held[pair, 0, at, :] = dk.astype(jnp.bfloat16)
            held[pair, 1, at, :] = dv.astype(jnp.bfloat16)
        dq = (jnp.where(upper, dqs[0], dqs[1]) + dq_pre) * HEAD_DIM ** (-0.5)
        q_own[pair, rows, :] = jnp.transpose(dq).astype(jnp.bfloat16)

    def dkv_copy(j, pair):
        rows = block_rows(j)
        return pltpu.make_async_remote_copy(
            src_ref=dkv_send.at[pair, :, rows], dst_ref=dkv_recv.at[pair, :, rows],
            send_sem=dkv_ssem.at[j, pair], recv_sem=dkv_rsem.at[j, pair],
            device_id=(other, d, z), device_id_type=MESH,
        )

    contribution = micro * 2 + s

    def pg_copy(q):
        return pltpu.make_async_remote_copy(
            src_ref=pg.at[2 * q : 2 * q + 2], dst_ref=pg_near.at[contribution], send_sem=pg_ssem.at[q],
            recv_sem=pg_sem.at[contribution], device_id=(role, d, q), device_id_type=MESH,
        )

    def far_copy(k):
        return pltpu.make_async_remote_copy(
            src_ref=pg_far.at[d], dst_ref=pg_far.at[d], send_sem=far_ssem.at[k - 1], recv_sem=far_sem.at[d],
            device_id=(s, (d + k) % 4, z), device_id_type=MESH,
        )

    def sum_near():
        for k in range(4):
            arrived(pg_near.at[k], pg_sem.at[k])
        pg_far[d] = (pg_near[0] + pg_near[1]) + (pg_near[2] + pg_near[3])
        for k in range(1, 4):
            far_copy(k).start()

    def backward(n, carry):
        j = 1 - n
        rows = block_rows(j)
        arrived(g_in.at[rows], g_sem.at[j])
        acc[rows, :] = jnp.zeros((BLOCK, 1024), jnp.float32)

        def feed_back(q, carry):
            grad_act = dot_nt(g_in[rows, :], wud[q, 1024:2048, :])
            wide[rows, :] = (grad_act * slope[q, rows, :].astype(jnp.float32)).astype(jnp.bfloat16)
            acc[rows, :] += dot_nt(wide[rows, :], wud[q, 0:1024, :])
            return carry

        lax.fori_loop(0, 4, feed_back, 0)

        def middle(rows):
            dv = norm_back(after[rows, :], vector(3), acc[rows, :])
            normed[rows, :] = (g_in[rows, :].astype(jnp.float32) + dv).astype(jnp.bfloat16)

        over_rows(j, middle)
        wide[rows, :] = dot_nt(normed[rows, :], wo[...].reshape(1024, 1024)).astype(jnp.bfloat16)
        for core in range(2):
            for block in range(2):

                @pl.when(jnp.logical_and(s == core, j == block))
                def _():
                    def back_pair(pair, carry):
                        back_rows(pair, core, block)
                        dkv_copy(block, pair).start()
                        return carry

                    lax.fori_loop(0, 8, back_pair, 0)

        @pl.when(j == 0)
        def _():
            for q in range(4):
                is_here = jnp.logical_and(role == s, z == q)

                @pl.when(is_here)
                def _():
                    pltpu.make_async_copy(
                        pg.at[2 * q : 2 * q + 2], pg_near.at[contribution], pg_sem.at[contribution]
                    ).start()

                @pl.when(jnp.logical_not(is_here))
                def _():
                    pg_copy(q).start()

        acc[rows, :] = jnp.zeros((BLOCK, 1024), jnp.float32)

        def project_back(q, carry):
            for p in range(2):
                pair = 2 * q + p
                dkv_copy(j, pair).wait()
                dq = q_own[pair, rows, :].astype(jnp.float32)
                dk = dkv_own[pair, 0, rows, :].astype(jnp.float32) + dkv_recv[pair, 0, rows, :].astype(jnp.float32)
                dv = dkv_own[pair, 1, rows, :].astype(jnp.float32) + dkv_recv[pair, 1, rows, :].astype(jnp.float32)
                dk = pltpu.roll(dk * HEAD_DIM ** (-0.5), 64, 1)
                gt[:, p * 384 : p * 384 + 128] = jnp.where(first, dq, dk).astype(jnp.bfloat16)
                gt[:, p * 384 + 128 : p * 384 + 256] = jnp.where(first, dv, dq).astype(jnp.bfloat16)
                gt[:, p * 384 + 256 : p * 384 + 384] = jnp.where(first, dk, dv).astype(jnp.bfloat16)
            acc[rows, :] += dot_nt(gt[...], wq[q])
            return carry

        lax.fori_loop(0, 4, project_back, 0)

        @pl.when(jnp.logical_and(j == 0, role == 0))
        def _():
            sum_near()

        hand_copies(j, 1).wait_send()

        def give_back(rows):
            dv = norm_back(x_in[rows, :].astype(jnp.float32), vector(0), acc[rows, :])
            y_out[rows, :] = (normed[rows, :].astype(jnp.float32) + dv).astype(jnp.bfloat16)

        over_rows(j, give_back)

        @pl.when(role == 0)
        def _():
            hand_copies(j, 3).start()

        @pl.when(jnp.logical_and(role == 1, j == 1))
        def _():
            hand_copies(1, 2).start()

        @pl.when(jnp.logical_and(role == 1, j == 0))
        def _():
            hand_copies(0, 2).start()
            hand_copies(1, 2).wait_send()
            hand_copies(0, 2).wait_send()
            for block in range(2):
                hand_copies(block, 3).start()

        return carry

    mask_blocks(True)
    lax.fori_loop(0, 2, backward, 0)
    @pl.when(role == 1)
    def _():
        sum_near()

    for k in range(1, 4):
        arrived(pg_far.at[(d + k) % 4], far_sem.at[(d + k) % 4])
    total_pg = (pg_far[0] + pg_far[1]) + (pg_far[2] + pg_far[3])
    for p in range(2):
        keys, values = total_pg[p, 0], total_pg[p, 1]
        sum_out[:, p * 256 : p * 256 + 128] = jnp.where(first16, keys, pltpu.roll(values, 64, 1))
        sum_out[:, p * 256 + 128 : p * 256 + 256] = jnp.where(first16, pltpu.roll(keys, 64, 1), values)
    hidden_core[s] = dot_nt(sum_out[...].astype(jnp.bfloat16), pw[...])
    sends.start(hidden_core.at[s], hidden_core.at[s], core_sem.at[s], (other, d, z))
    arrived(hidden_core.at[other], core_sem.at[other])
    hidden_all[z] = hidden_core[0] + hidden_core[1]
    for k in range(1, 4):
        sends.start(hidden_all.at[z], hidden_all.at[z], hidden_sem.at[z], (s, d, (z + k) % 4))
    for k in range(1, 4):
        arrived(hidden_all.at[(z + k) % 4], hidden_sem.at[(z + k) % 4])
    hidden_out[...] = (hidden_all[0] + hidden_all[1]) + (hidden_all[2] + hidden_all[3])

    lax.fori_loop(0, 3, supply_done, 0)

    @pl.when(role == 0)
    def _():
        x_copies(lambda copy: copy.wait_send())

    @pl.when(feeds_one_late)
    def _():
        x_copies(lambda copy: copy.wait_send())

    firsts_done(jnp.logical_not(feeds_zero), 0)
    firsts_done(True, 1)

    def relays_done(m, carry):
        for stage in range(3):
            relay_copy(m, stage).wait_send()
        return carry

    lax.fori_loop(0, UNITS, relays_done, 0)
    cot_copies(lambda copy: copy.wait_send())
    for k in range(1, 4):
        far_copy(k).wait_send()
    for q in range(4):

        @pl.when(jnp.logical_not(jnp.logical_and(role == s, z == q)))
        def _():
            pg_copy(q).wait_send()

    for j in range(2):

        hand_copies(j, 3).wait_send()

    for k in range(2):
        arrived(act_out.at[k], act_sem.at[k])
        arrived(ig_out.at[k], ig_sem.at[k])
    sends.finish()


def run_layers(x, cot, wq, wo, wu, wd, *small):
    bf, f32 = jnp.bfloat16, jnp.float32
    vm, dma = pltpu.VMEM, pltpu.SemaphoreType.DMA
    rows = 2 * BLOCK
    width = x.shape[-1]
    pairs = width // 128
    pw = small[-3]
    scratch = [
        vm((8, width), f32), vm((16, pw.shape[1]), f32), vm((16, pw.shape[1]), bf), vm((4,) + wq.shape, bf), vm((4,) + wo.shape, bf), vm((4, 2 * wu.shape[0], width), bf),
        vm((4, 8, width), f32), vm((4, 16, pw.shape[1]), bf),
        vm((rows, width), bf), vm((rows, width), bf), vm((rows, width), bf), vm((rows, width), bf),
        vm((2, pairs, 2, rows, 128), bf), vm((pairs, rows, 128), bf), vm((rows, width), bf),
        vm((pairs, rows, 128), f32), vm((6, BLOCK, BLOCK), f32), vm((rows, width), f32), vm((rows, width), f32),
        vm((4, rows, wu.shape[1]), bf), vm((rows, wu.shape[1]), bf),
        vm((pairs, 2, 16, 128), f32), vm((4, 2, 2, 16, 128), f32), vm((4, 2, 2, 16, 128), f32), vm((2, 16, pw.shape[0]), f32), vm((4, 16, pw.shape[0]), f32),
        vm((2, 4, BLOCK, BLOCK), f32),
        vm((pairs, 2, rows, 128), bf), vm((pairs, 2, rows, 128), bf), vm((pairs, 2, rows, 128), bf),
        vm((pairs, 128, 128), bf), vm((pairs, 128, 128), bf),
        vm((BLOCK, wq.shape[1]), bf),
        dma((96,)), dma((4,)), dma((4,)), dma((2,)), dma((2,)), dma((2,)), dma((2,)), dma((4,)),
        dma((2, 4)), dma((2, 4)), dma((2, 4)), dma((2, 4)),
        dma((UNITS,)), dma((UNITS,)), dma((UNITS,)), dma((UNITS,)), dma((6, 2)), dma((UNITS, 2)), dma((UNITS,)), dma((UNITS,)), dma((UNITS,)),
        pltpu.SemaphoreType.REGULAR,
        dma((2, 4)), dma((2, 4)), dma((2, pairs)), dma((2, pairs)), dma((4,)), dma((4,)), dma((2,)), dma((4,)),
        dma((4, 2)), dma((2,)), dma((2,)), dma((4,)), dma((3,)), dma((8,)),
    ]
    anywhere = pl.BlockSpec(memory_space=pl.ANY)
    local = pl.BlockSpec(memory_space=pltpu.VMEM)
    return pl.pallas_call(
        layer_kernel,
        out_shape=(
            jax.ShapeDtypeStruct(x.shape, bf), jax.ShapeDtypeStruct(x.shape, bf),
            jax.ShapeDtypeStruct((16, pw.shape[1]), f32), jax.ShapeDtypeStruct((16, pw.shape[0]), f32),
            jax.ShapeDtypeStruct((16, pw.shape[0]), f32),
        ),
        in_specs=[anywhere] * 6 + [local] * 9 + [anywhere] + [local] * 3 + [pl.BlockSpec(memory_space=pltpu.SMEM)],
        out_specs=(anywhere, anywhere, local, local, local),
        scratch_shapes=scratch,
        name="two_layers",
        compiler_params=pltpu.CompilerParams(
            collective_id=0, has_side_effects=True, vmem_limit_bytes=63 * 2**20
        ),
    )(x, cot, wq, wo, wu, wd, *small)


def prefix_kernel(
    prefix_sum, hidden_grad, hidden_act, table, mid_w, act_held, ig_held,
    table_grad, mid_w_grad, mid_b_grad, prefix_w_grad, prefix_b_grad, act_out, ig_out, table_full, stage, in_sem, out_sem,
):
    incoming, outgoing = [], []
    for n, (held, out) in enumerate(((act_held, act_out), (ig_held, ig_out))):
        for k in range(2):
            incoming.append(pltpu.make_async_copy(held.at[k], stage.at[n, k], in_sem.at[n, k]))
            outgoing.append(pltpu.make_async_copy(stage.at[n, k], out.at[k], out_sem.at[n, k]))
            incoming[-1].start()
    for arriving, leaving in zip(incoming, outgoing):
        arriving.wait()
        leaving.start()
    prefix_low = prefix_sum[...].astype(jnp.bfloat16)
    act = hidden_act[...]
    prefix_b_grad[...] = jnp.sum(prefix_low.astype(jnp.float32), axis=0, keepdims=True)
    prefix_w_grad[...] = dot_tn(act.astype(jnp.bfloat16), prefix_low)
    pre_grad = (hidden_grad[...] * (1.0 - act * act)).astype(jnp.bfloat16)
    mid_b_grad[...] = jnp.sum(pre_grad.astype(jnp.float32), axis=0, keepdims=True)
    table_full[...] = jnp.zeros(table_full.shape, jnp.float32)
    table_full[0:PREFIX, :] = table[...].astype(jnp.float32)
    mid_w_grad[...] = dot_tn(table_full[...].astype(jnp.bfloat16), pre_grad)
    table_grad[...] = dot_nt(pre_grad, mid_w[...])[0:PREFIX, :]
    for leaving in outgoing:
        leaving.wait()


def run_prefix_back(prefix_sum, hidden_grad, hidden_act, table, mid_w, activations, input_grads):
    f32 = jnp.float32
    hidden, own = mid_w.shape[1], prefix_sum.shape[1]
    local, anywhere = pl.BlockSpec(memory_space=pltpu.VMEM), pl.BlockSpec(memory_space=pl.ANY)
    rows = jax.ShapeDtypeStruct(activations.shape, activations.dtype)
    return pl.pallas_call(
        prefix_kernel,
        out_shape=tuple(
            jax.ShapeDtypeStruct(shape, f32)
            for shape in (table.shape, mid_w.shape, (1, hidden), (hidden, own), (1, own))
        ) + (rows, rows),
        in_specs=[local] * 5 + [anywhere] * 2,
        out_specs=(local,) * 5 + (anywhere,) * 2,
        scratch_shapes=[
            pltpu.VMEM((16, table.shape[1]), f32), pltpu.VMEM((2,) + activations.shape, activations.dtype),
            pltpu.SemaphoreType.DMA((2, 2)), pltpu.SemaphoreType.DMA((2, 2)),
        ],
        name="prefix_network",
        compiler_params=pltpu.CompilerParams(vmem_limit_bytes=60 * 2**20),
    )(prefix_sum, hidden_grad, hidden_act, table, mid_w, activations, input_grads)


def pair_body(
    layer_input, cotangent, example_lengths, attn_gain, attn_shift, query_key_value_weight, qkv_bias,
    attention_output_weight, out_bias, ffn_gain, ffn_shift, up_projection_weight, up_projection_bias,
    down_projection_weight, down_bias, prefix_table, mid_weight, mid_bias, prefix_weight, prefix_bias,
):
    activations, input_grads, prefix_sum, hidden_grad, hidden_act = run_layers(
        layer_input[:, 0], cotangent[:, 0], query_key_value_weight[0], attention_output_weight[0],
        up_projection_weight[0], down_projection_weight[0],
        attn_gain, attn_shift, out_bias, ffn_gain, ffn_shift, down_bias, up_projection_bias, qkv_bias,
        prefix_table, mid_weight, mid_bias, prefix_weight, prefix_bias, example_lengths[:, 0],
    )
    (
        table_grad, mid_weight_grad, mid_bias_grad, prefix_weight_grad, prefix_bias_grad, activations, input_grads,
    ) = run_prefix_back(prefix_sum, hidden_grad, hidden_act, prefix_table, mid_weight, activations, input_grads)
    return (
        activations[None, :, None], input_grads[None, :, None],
        table_grad, mid_weight_grad, mid_bias_grad[0], prefix_weight_grad, prefix_bias_grad[0],
    )


def solution(mesh):
    placed = (
        P(None, "dp", "mp", None),
        P(None, "dp", "mp", None),
        P(None, "dp", None),
        P("section", None),
        P("section", None),
        P("section", None, "mp"),
        P("section", "mp"),
        P("section", "mp", None),
        P("section", None),
        P("section", None),
        P("section", None),
        P("section", None, "mp"),
        P("section", "mp"),
        P("section", "mp", None),
        P("section", None),
        P(),
        P(),
        P(),
        P(None, ("section", "mp")),
        P(("section", "mp")),
    )
    paired = mesh.shape["mp"] == 4 and mesh.shape["dp"] == 4
    return jax.shard_map(
        pair_body if paired else body,
        mesh=mesh,
        in_specs=placed,
        out_specs=(
            P("section", None, "dp", "mp", None),
            P("section", None, "dp", "mp", None),
            P(),
            P(),
            P(),
            P(None, ("section", "mp")),
            P(("section", "mp")),
        ),
        check_vma=False,
    )
```

```python
import jax
import jax.numpy as jnp
from jax import lax
from jax.experimental import pallas as pl
from jax.experimental.pallas import tpu as pltpu
from jax.sharding import PartitionSpec as P

HEAD_DIM = 64
PREFIX = 10
SEQ_LEN = 1024


EPSILON = 1e-05
NEG_LARGE = -1e30
GELU_A = 0.7978845608028654
GELU_B = 0.044715


def norm_rows(values, gain, shift):
    average = jnp.mean(values, axis=-1, keepdims=True)
    centred = values - average
    spread = jnp.mean(centred * centred, axis=-1, keepdims=True)
    return centred * lax.rsqrt(spread + EPSILON) * gain + shift


def norm_input_grad(values, gain, shift, incoming):

    def apply_norm(inputs):
        return norm_rows(inputs, gain, shift)

    norm_value, norm_back = jax.vjp(apply_norm, values)
    return norm_back(incoming)[0]


def gelu_tanh(values):
    return jax.nn.gelu(values, approximate=True)


def visible_of(lengths, first_row, count):
    run_ends = jnp.cumsum(lengths, axis=-1)
    keys_at = jnp.arange(SEQ_LEN, dtype=jnp.int32)
    query_at = first_row + jnp.arange(count, dtype=jnp.int32)
    key_seg = jnp.sum((keys_at[None, :, None] >= run_ends[:, None, :]).astype(jnp.int32), axis=-1)
    query_seg = jnp.sum(
        (query_at[None, :, None] >= run_ends[:, None, :]).astype(jnp.int32), axis=-1
    )
    causal = (query_at[:, None] >= keys_at[None, :])[None]
    inside = (query_seg[:, :, None] == key_seg[:, None, :]) & causal
    leading = jnp.ones((lengths.shape[0], count, PREFIX), dtype=bool)
    return jnp.concatenate([leading, inside], axis=2)


def gather_rows(piece):
    return lax.all_gather(piece, "mp", axis=1, tiled=True)


def reduce_rows(partial_sum):
    return lax.psum_scatter(
        partial_sum.astype(jnp.bfloat16), "mp", scatter_dimension=1, tiled=True
    ).astype(jnp.float32)


def with_prefix(prefix_kv, pair_keys, pair_values, heads_count):
    prefix_pair = prefix_kv.reshape(PREFIX, heads_count, 2, HEAD_DIM)
    key_rows = jnp.concatenate([prefix_pair[None, :, :, 0], pair_keys], axis=1)
    value_rows = jnp.concatenate([prefix_pair[None, :, :, 1], pair_values], axis=1)
    return (key_rows, value_rows)


def attend(query_rows, key_rows, value_rows, visible):
    score_scale = HEAD_DIM ** (-0.5)
    scores = (
        jnp.einsum("sqhd,skhd->shqk", query_rows, key_rows, preferred_element_type=jnp.float32)
        * score_scale
    )
    scores = jnp.where(visible[:, None], scores, NEG_LARGE)
    highest = jnp.max(scores, axis=-1, keepdims=True)
    raised = jnp.exp(scores - highest)
    softmax_probs = raised / jnp.sum(raised, axis=-1, keepdims=True)
    probs_low = softmax_probs.astype(jnp.bfloat16)
    head_mixed_rows = jnp.einsum(
        "shqk,skhd->sqhd", probs_low, value_rows, preferred_element_type=jnp.float32
    )
    batch_size, query_count, heads_count, head_size = head_mixed_rows.shape
    head_mixed_rows = head_mixed_rows.astype(jnp.bfloat16).reshape(
        batch_size, query_count, heads_count * head_size
    )
    return (softmax_probs, probs_low, head_mixed_rows)


def attend_back(grad_mix, query_rows, key_rows, value_rows, softmax_probs, probs_low):
    grad_heads = grad_mix.reshape(query_rows.shape)
    grad_probs = jnp.einsum(
        "sqhd,skhd->shqk", grad_heads, value_rows, preferred_element_type=jnp.float32
    )
    value_grad = jnp.einsum(
        "shqk,sqhd->skhd", probs_low, grad_heads, preferred_element_type=jnp.float32
    )
    row_term = jnp.sum(grad_probs * softmax_probs, axis=-1, keepdims=True)
    grad_scores = (softmax_probs * (grad_probs - row_term)).astype(jnp.bfloat16)
    score_scale = HEAD_DIM ** (-0.5)
    query_grad = (
        jnp.einsum("shqk,skhd->sqhd", grad_scores, key_rows, preferred_element_type=jnp.float32)
        * score_scale
    )
    key_grad = (
        jnp.einsum("shqk,sqhd->skhd", grad_scores, query_rows, preferred_element_type=jnp.float32)
        * score_scale
    )
    return (query_grad, key_grad, value_grad)


def prefix_part(key_grad, value_grad):
    pair_sum = jnp.stack(
        [jnp.sum(key_grad[:, :PREFIX], axis=0), jnp.sum(value_grad[:, :PREFIX], axis=0)], axis=2
    )
    return pair_sum.reshape(PREFIX, -1)


def tensor_forward(own_rows, weights, prefix_kv, visible):
    (
        attn_gain,
        attn_shift,
        query_key_value_weight,
        qkv_bias,
        attention_output_weight,
        out_bias,
        ffn_gain,
        ffn_shift,
        up_projection_weight,
        up_projection_bias,
        down_projection_weight,
        down_bias,
        out_full,
    ) = weights
    normed = norm_rows(own_rows, attn_gain, attn_shift).astype(jnp.bfloat16)
    normalized_input_rows = gather_rows(normed)
    batch_size, seq_len, model_width = normalized_input_rows.shape
    heads_here = query_key_value_weight.shape[1] // (3 * HEAD_DIM)
    projected = (
        jnp.einsum(
            "naj,jk->nak",
            normalized_input_rows,
            query_key_value_weight,
            preferred_element_type=jnp.float32,
        )
        + qkv_bias
    )
    triple = projected.astype(jnp.bfloat16).reshape(batch_size, seq_len, heads_here, 3, HEAD_DIM)
    query_rows = triple[:, :, :, 0]
    key_rows, value_rows = with_prefix(
        prefix_kv, triple[:, :, :, 1], triple[:, :, :, 2], heads_here
    )
    softmax_probs, probs_low, head_mixed_rows = attend(query_rows, key_rows, value_rows, visible)
    attn_part = reduce_rows(
        jnp.einsum(
            "hgm,mt->hgt",
            head_mixed_rows,
            attention_output_weight,
            preferred_element_type=jnp.float32,
        )
    )
    after_attn = own_rows + attn_part + out_bias
    normed_two = norm_rows(after_attn, ffn_gain, ffn_shift).astype(jnp.bfloat16)
    second_norm_rows = gather_rows(normed_two)
    up_pre = (
        jnp.einsum(
            "rmy,yq->rmq",
            second_norm_rows,
            up_projection_weight,
            preferred_element_type=jnp.float32,
        )
        + up_projection_bias
    )
    gelu_output_rows = gelu_tanh(up_pre).astype(jnp.bfloat16)
    mlp_part = reduce_rows(
        jnp.einsum(
            "epj,jq->epq",
            gelu_output_rows,
            down_projection_weight,
            preferred_element_type=jnp.float32,
        )
    )
    result = after_attn + mlp_part + down_bias
    kept_values = (query_rows, key_rows, value_rows, softmax_probs, probs_low, after_attn, up_pre)
    return (result, kept_values)


def tensor_backward(own_rows, arriving, weights, kept_values):
    (
        attn_gain,
        attn_shift,
        query_key_value_weight,
        qkv_bias,
        attention_output_weight,
        out_bias,
        ffn_gain,
        ffn_shift,
        up_projection_weight,
        up_projection_bias,
        down_projection_weight,
        down_bias,
        out_full,
    ) = weights
    query_rows, key_rows, value_rows, softmax_probs, probs_low, after_attn, up_pre = kept_values
    gradient_gathered = gather_rows(arriving)
    gradient_activation = jnp.einsum(
        "bhi,vi->bhv", gradient_gathered, down_projection_weight, preferred_element_type=jnp.float32
    )
    gelu_value, gelu_back = jax.vjp(gelu_tanh, up_pre)
    gradient_up_projection = gelu_back(gradient_activation)[0].astype(jnp.bfloat16)
    grad_two = reduce_rows(
        jnp.einsum(
            "yca,ja->ycj",
            gradient_up_projection,
            up_projection_weight,
            preferred_element_type=jnp.float32,
        )
    )
    grad_after = norm_input_grad(after_attn, ffn_gain, ffn_shift, grad_two)
    grad_mid = (grad_after + arriving.astype(jnp.float32)).astype(jnp.bfloat16)
    middle_gathered = gather_rows(grad_mid)
    grad_mix = jnp.einsum(
        "taq,kq->tak", middle_gathered, attention_output_weight, preferred_element_type=jnp.float32
    ).astype(jnp.bfloat16)
    query_grad, key_grad, value_grad = attend_back(
        grad_mix, query_rows, key_rows, value_rows, softmax_probs, probs_low
    )
    prefix_g = prefix_part(key_grad, value_grad)
    batch_size, seq_len = (query_grad.shape[0], query_grad.shape[1])
    gradient_query_key_value = jnp.stack(
        [query_grad, key_grad[:, PREFIX:], value_grad[:, PREFIX:]], axis=3
    )
    gradient_query_key_value = gradient_query_key_value.astype(jnp.bfloat16).reshape(
        batch_size, seq_len, -1
    )
    grad_one = reduce_rows(
        jnp.einsum(
            "tvq,xq->tvx",
            gradient_query_key_value,
            query_key_value_weight,
            preferred_element_type=jnp.float32,
        )
    )
    grad_input = norm_input_grad(own_rows, attn_gain, attn_shift, grad_one)
    grad_input = (grad_input + grad_mid.astype(jnp.float32)).astype(jnp.bfloat16)
    return (grad_input, prefix_g)


def prefix_back(prefix_sum, hidden_grad, hidden_act, hidden_low, prefix_table, mid_weight):
    prefix_low = prefix_sum.astype(jnp.bfloat16)
    prefix_bias_grad = jnp.sum(prefix_low.astype(jnp.float32), axis=0)
    prefix_weight_grad = jnp.dot(hidden_low.T, prefix_low, preferred_element_type=jnp.float32)
    pre_grad = (hidden_grad * (1.0 - hidden_act * hidden_act)).astype(jnp.bfloat16)
    mid_bias_grad = jnp.sum(pre_grad.astype(jnp.float32), axis=0)
    mid_weight_grad = jnp.dot(prefix_table.T, pre_grad, preferred_element_type=jnp.float32)
    table_grad = jnp.dot(pre_grad, mid_weight.T, preferred_element_type=jnp.float32)
    return (table_grad, mid_weight_grad, mid_bias_grad, prefix_weight_grad, prefix_bias_grad)


def both_layers(piece):
    return lax.all_gather(piece[0], "section", axis=0, tiled=False)


def body(
    layer_input,
    cotangent,
    example_lengths,
    attn_gain,
    attn_shift,
    query_key_value_weight,
    qkv_bias,
    attention_output_weight,
    out_bias,
    ffn_gain,
    ffn_shift,
    up_projection_weight,
    up_projection_bias,
    down_projection_weight,
    down_bias,
    prefix_table,
    mid_weight,
    mid_bias,
    prefix_weight,
    prefix_bias,
):
    layers = lax.axis_size("section")
    section_index = lax.axis_index("section")
    hidden_pre = jnp.dot(
        prefix_table, mid_weight, preferred_element_type=jnp.float32
    ) + mid_bias.astype(jnp.float32)
    hidden_act = jnp.tanh(hidden_pre)
    hidden_low = hidden_act.astype(jnp.bfloat16)
    prefix_kv = (
        jnp.dot(hidden_low, prefix_weight, preferred_element_type=jnp.float32)
        + prefix_bias.astype(jnp.float32)
    ).astype(jnp.bfloat16)
    prefix_all = lax.all_gather(prefix_kv, "section", axis=0, tiled=False)
    floats = [
        both_layers(piece).astype(jnp.float32)
        for piece in (attn_gain, attn_shift, qkv_bias, out_bias, ffn_gain, ffn_shift,
                      up_projection_bias, down_bias)
    ]
    matrices = [
        both_layers(piece)
        for piece in (query_key_value_weight, attention_output_weight,
                      up_projection_weight, down_projection_weight)
    ]

    def weights_of(layer):
        g1, s1, bq, bo, g2, s2, bu, bd = [piece[layer] for piece in floats]
        wq, wo, wu, wd = [piece[layer] for piece in matrices]
        return (g1, s1, wq, bq, wo, bo, g2, s2, wu, bu, wd, bd, wo)

    batch_count = layer_input.shape[0]
    own_input = lax.dynamic_index_in_dim(layer_input, section_index, 0, keepdims=False)
    own_cotangent = lax.dynamic_index_in_dim(cotangent, section_index, 0, keepdims=False)
    lengths = lax.dynamic_index_in_dim(example_lengths, section_index, 0, keepdims=False)
    visible = visible_of(lengths, 0, SEQ_LEN)
    entering = own_input
    entered, produced, kept = [], [], []
    for layer in range(layers):
        entered.append(entering.astype(jnp.float32))
        result, kept_values = tensor_forward(
            entered[layer], weights_of(layer), prefix_all[layer], visible
        )
        entering = result.astype(jnp.bfloat16)
        produced.append(entering)
        kept.append(kept_values)
    gradient = own_cotangent
    sent_grads = [None] * layers
    prefix_parts = [None] * layers
    for layer in reversed(range(layers)):
        gradient, prefix_parts[layer] = tensor_backward(
            entered[layer], gradient, weights_of(layer), kept[layer]
        )
        sent_grads[layer] = gradient
    activations = lax.all_to_all(jnp.stack(produced), "section", 0, 0, tiled=False)
    input_grads = lax.all_to_all(jnp.stack(sent_grads), "section", 0, 0, tiled=False)
    prefix_sum = lax.psum(jnp.stack(prefix_parts), ("dp", "section"))
    prefix_sum = lax.dynamic_index_in_dim(prefix_sum, section_index, 0, keepdims=False)
    hidden_part = jnp.dot(
        prefix_sum.astype(jnp.bfloat16), prefix_weight.T, preferred_element_type=jnp.float32
    )
    hidden_grad = lax.psum(hidden_part, ("section", "mp"))
    return (activations[None], input_grads[None]) + prefix_back(
        prefix_sum, hidden_grad, hidden_act, hidden_low, prefix_table, mid_weight
    )


MESH = pl.DeviceIdType.MESH
BLOCK = 256
LOG2E = 1.4426950408889634
CHUNK = 256
UNITS = 12
AHEAD = 10
UNIT_ROWS = 512
PART_ROWS = UNIT_ROWS // 8


def role_of(z):
    return (((z + 1) // 2) + 1) % 2


def block_of(s, j):
    return j * 3 + s * (1 - 2 * j)


def core_of(block):
    return ((block + 1) // 2) % 2


def guarded(when, action):
    if when is None:
        action()
    else:
        pl.when(when)(action)


def dot_nn(a, b):
    return lax.dot_general(a, b, (((1,), (0,)), ((), ())), preferred_element_type=jnp.float32)


def dot_nt(a, b):
    return lax.dot_general(a, b, (((1,), (1,)), ((), ())), preferred_element_type=jnp.float32)


def dot_tn(a, b):
    return lax.dot_general(a, b, (((0,), (0,)), ((), ())), preferred_element_type=jnp.float32)


class Sends:
    def __init__(self, sems):
        self.sems, self.used, self.pending = sems, 0, []

    def start(self, src, dst, recv_sem, target, when=None):
        copy = pltpu.make_async_remote_copy(
            src_ref=src, dst_ref=dst, send_sem=self.sems.at[self.used], recv_sem=recv_sem,
            device_id=target, device_id_type=MESH,
        )
        self.used += 1
        guarded(when, copy.start)
        self.pending.append((when, copy))

    def start_or_keep(self, src, dst, recv_sem, target, is_here, when=True):
        @pl.when(jnp.logical_and(when, is_here))
        def _():
            pltpu.make_async_copy(src, dst, recv_sem).start()

        self.start(src, dst, recv_sem, target, when=jnp.logical_and(when, jnp.logical_not(is_here)))

    def finish(self):
        for when, copy in self.pending:
            guarded(when, copy.wait_send)
        self.pending = []


def layer_kernel(
    x_hbm, cot_hbm, wq_hbm, wo_hbm, wu_hbm, wd_hbm,
    g1, s1, bo, g2, s2, bd, bu, bq, table, mid_w, mid_b, pw, pb, lengths,
    act_out, ig_out, sum_out, hidden_out, tanh_out,
    vec_own, pre_full, pre_own, wq, wo, wud, vec, pre,
    x_in, g_in, y_out, normed, kv, q_own, o_own, lse, bias, after, acc, slope, wide,
    pg, pg_near, pg_far, hidden_core, hidden_all, ts, dkv_own, dkv_send, dkv_recv, kp, vp, gt,
    ssem, vec_sem, pre_sem, x_sem, g_sem, act_sem, ig_sem, own_sem, z_sem, a_sem, b_sem, c_sem,
    zr_sem, ar_sem, br_sem, cr_sem, fs_sem, zs_sem, as_sem, bs_sem, cs_sem, go_sem,
    kv_ssem, kv_rsem, dkv_ssem, dkv_rsem, pg_sem, far_sem, core_sem, hidden_sem,
    hand_sem, cot_sem, x_ssem, pg_ssem, far_ssem, mid_sem,
):
    s, d, z = lax.axis_index("section"), lax.axis_index("dp"), lax.axis_index("mp")
    role, micro = role_of(z), z // 2
    other = 1 - s
    partner = z + 1 - 2 * (z % 2)
    x_near, y_near = d + 1 - 2 * (d % 2), (d + 2) % 4
    near1 = jnp.where(s == 0, x_near, y_near)
    near2 = jnp.where(s == 0, y_near, x_near)
    sends = Sends(ssem)

    barrier = pltpu.get_barrier_semaphore()
    for ds in range(2):
        for dz in range(4):
            if ds or dz:
                pl.semaphore_signal(barrier, inc=1, device_id=((s + ds) % 2, d, (z + dz) % 4), device_id_type=MESH)
    for near in (x_near, y_near, 3 - d):
        pl.semaphore_signal(barrier, inc=1, device_id=(s, near, z), device_id_type=MESH)
    pl.semaphore_wait(barrier, 10)

    def arrived(dst, sem):
        pltpu.make_async_remote_copy(
            src_ref=dst, dst_ref=dst, send_sem=ssem.at[0], recv_sem=sem,
            device_id=(other, d, z), device_id_type=MESH,
        ).wait_recv()

    low_plane, high_plane = jnp.where(s == 0, 1, 0), jnp.where(s == 0, 2, 3)
    planes = (low_plane, high_plane)
    mine = s == core_of(z)
    row_slot = pl.ds(pl.multiple_of((z // 2) * BLOCK, BLOCK), BLOCK)

    def send_small(when):
        for t in planes:
            for h in range(2):
                is_here = jnp.logical_and(z == t, s == h)
                sends.start_or_keep(pre_own, pre.at[z], pre_sem.at[z], (h, d, t), is_here, when)

    def row_copies(source, landing, send_sem, sem, chips, then):
        for k, chip in enumerate(chips):

            @pl.when(jnp.logical_and(mine, z != chip))
            def _():
                then(pltpu.make_async_remote_copy(
                    src_ref=source.at[k], dst_ref=landing.at[row_slot], send_sem=send_sem.at[k],
                    recv_sem=sem.at[z // 2], device_id=(s, d, chip), device_id_type=MESH,
                ))

    def keep_rows(source, landing, sem, chips):
        for k, chip in enumerate(chips):

            @pl.when(jnp.logical_and(mine, z == chip))
            def _():
                pltpu.make_async_copy(source.at[k], landing.at[row_slot], sem.at[z // 2]).start()

    def x_copies(then):
        row_copies(x_hbm, x_in, x_ssem, x_sem, (1, 2), then)

    def cot_copies(then):
        row_copies(cot_hbm, g_in, cot_sem, g_sem, (0, 3), then)

    keep_rows(x_hbm, x_in, x_sem, (1, 2))
    keep_rows(cot_hbm, g_in, g_sem, (0, 3))

    toward = jnp.where(z < 2, 1, -1)

    def quarter(i):
        return (z + 4 + toward * i) % 4

    def taker(i):
        low, high = (z + 3 - i) % 4, (z + 1 + i) % 4
        return jnp.where(low == low_plane, low, high), jnp.logical_or(low == low_plane, high == high_plane)

    swapped = (d % 2) * 2 + d // 2
    place = jnp.where(s == 0, d, swapped)
    pair_start = (place // 2) * 2
    far_start = 2 - pair_start
    firsts = ((wq_hbm, wq), (wo_hbm, wo))

    def eighths(rows, start, count, h):
        return pl.ds(pl.multiple_of((start + 4 * h) * rows, rows), rows * count)

    def supply_first(w, i, then):
        t, taken = taker(i)
        held, full = firsts[w]

        @pl.when(taken)
        def _():
            for h in range(2):
                at = eighths(held.shape[0] // 8, swapped if h else d, 1, h)
                then(pltpu.make_async_remote_copy(
                    src_ref=held.at[at], dst_ref=full.at[z, at], send_sem=fs_sem.at[3 * w + i, h],
                    recv_sem=z_sem.at[w, z], device_id=(h, d, t), device_id_type=MESH,
                ))

    def supply_firsts(when, w):
        @pl.when(when)
        def _():
            def one(i, carry):
                supply_first(w, i, lambda copy: copy.start())
                return carry

            lax.fori_loop(0, 3, one, 0)

    def firsts_done(when, w):
        @pl.when(when)
        def _():
            def one(i, carry):
                supply_first(w, i, lambda copy: copy.wait_send())
                return carry

            lax.fori_loop(0, 3, one, 0)

    def supply_copies(i, c, then):
        t, taken = taker(i)
        held, base = ((wu_hbm, 0), (wd_hbm, 1024))[c // 2]

        @pl.when(taken)
        def _():
            for h in range(2):
                at = eighths(PART_ROWS, swapped if h else d, 1, h)
                start = (c % 2) * UNIT_ROWS + at.start
                then(pltpu.make_async_remote_copy(
                    src_ref=held.at[pl.ds(pl.multiple_of(start, PART_ROWS), PART_ROWS)],
                    dst_ref=wud.at[z, pl.ds(pl.multiple_of(base + start, PART_ROWS), PART_ROWS)],
                    send_sem=zs_sem.at[4 * i + c, h], recv_sem=zr_sem.at[4 * i + c],
                    device_id=(h, d, t), device_id_type=MESH,
                ))

    def supply_all(i, carry):
        for c in range(4):
            supply_copies(i, c, lambda copy: copy.start())
        return carry

    def supply_done(i, carry):
        for c in range(4):
            supply_copies(i, c, lambda copy: copy.wait_send())
        return carry

    feeds_zero = jnp.logical_and(role == 1, s == 0)
    feeds_zero_late = jnp.logical_and(role == 0, s == 0)
    feeds_one = jnp.logical_and(role == 0, s == 1)
    feeds_one_late = jnp.logical_and(role == 1, s == 1)
    supply_firsts(s == 0, 0)

    @pl.when(feeds_one)
    def _():
        for w in range(2):
            supply_first(w, 0, lambda copy: copy.start())
        supply_all(0, 0)

    mid_copies = mid_w.shape[1] // 128

    def mid_copy(n, half):
        return pltpu.make_async_copy(
            mid_w.at[half * 512 : half * 512 + 512, n * 128 : n * 128 + 128], q_own.at[2 * n + half],
            mid_sem.at[2 * n + half],
        )

    for n in range(mid_copies):
        for half in range(2):
            mid_copy(n, half).start()
    for k, row in enumerate((g1, s1, bo, g2, s2, bd)):
        vec_own[k : k + 1, :] = row[...].astype(jnp.float32)

    @pl.when(role == s)
    def _():
        pltpu.make_async_copy(vec_own, vec.at[0], vec_sem.at[0]).start()

    sends.start(vec_own, vec.at[0], vec_sem.at[0], (other, d, z), when=role == s)
    tanh_out[...] = jnp.zeros(tanh_out.shape, jnp.float32)
    for n in range(mid_copies):
        for half in range(2):
            mid_copy(n, half).wait()
        cols = slice(n * 128, n * 128 + 128)
        part_sum = dot_nn(table[:, 0:512], q_own[2 * n]) + dot_nn(table[:, 512:1024], q_own[2 * n + 1])
        tanh_out[0:PREFIX, cols] = jnp.tanh(part_sum + mid_b[...].astype(jnp.float32).reshape(1, -1)[:, cols])
    pre_full[...] = dot_nn(tanh_out[...].astype(jnp.bfloat16), pw[...]) + pb[...].astype(jnp.float32).reshape(1, -1)
    half_width = pre_full.shape[1]
    for k, row in enumerate((bu, bq)):
        for n in range(2):
            piece = row[:, n * half_width : min((n + 1) * half_width, row.shape[1])]
            pre_full[PREFIX + 2 * k + n : PREFIX + 2 * k + n + 1, 0 : piece.shape[1]] = piece.astype(jnp.float32)
    pre_own[...] = pre_full[...].astype(jnp.bfloat16)
    send_small(feeds_zero)
    firsts_done(feeds_zero, 0)
    supply_firsts(feeds_zero, 1)

    @pl.when(feeds_zero)
    def _():
        x_copies(lambda copy: copy.start())
    owned = ((wq_hbm, wq.at[z]), (wo_hbm, wo.at[z]), (wu_hbm, wud.at[z, 0:1024]), (wd_hbm, wud.at[z, 1024:2048]))
    for w, (held, full) in enumerate(owned):
        @pl.when(role == s)
        def _():
            pltpu.make_async_copy(held, full, own_sem.at[w]).start()

        sends.start(held, full, own_sem.at[w], (other, d, z), when=role == s)

    @pl.when(feeds_zero)
    def _():
        x_copies(lambda copy: copy.wait_send())
        lax.fori_loop(0, 3, supply_all, 0)

    @pl.when(feeds_one_late)
    def _():
        pl.semaphore_wait(go_sem, 1)

    send_small(feeds_one_late)
    supply_firsts(feeds_one_late, 0)
    supply_firsts(feeds_one_late, 1)

    first_units = [(w, i) for w in (0, 1) for i in range(1, 4)]

    def first_piece(w, i, start, count):
        full = firsts[w][1]
        return full.at[quarter(i), eighths(full.shape[1] // 8, start, count, s)]

    def relay_first(step):
        stages = [first_units[step - k] if 0 <= step - k < len(first_units) else None for k in range(4)]
        if stages[0]:
            w, i = stages[0]
            q = quarter(i)
            arrived(first_piece(w, i, place, 1), z_sem.at[w, q])
            sends.start(first_piece(w, i, place, 1), first_piece(w, i, place, 1), a_sem.at[w, q], (s, near1, z))
        if stages[1]:
            w, i = stages[1]
            q = quarter(i)
            arrived(first_piece(w, i, pair_start + 1 - place % 2, 1), a_sem.at[w, q])
            sends.start(first_piece(w, i, pair_start, 2), first_piece(w, i, pair_start, 2), b_sem.at[w, q], (s, near2, z))
        if stages[2]:
            w, i = stages[2]
            q = quarter(i)
            arrived(first_piece(w, i, far_start, 2), b_sem.at[w, q])
            sends.start(first_piece(w, i, 0, 4), first_piece(w, i, 0, 4), c_sem.at[w, q], (other, d, z))
        if stages[3]:
            w, i = stages[3]
            full = firsts[w][1]
            arrived(full.at[quarter(i), eighths(full.shape[1] // 8, 0, 4, other)], c_sem.at[w, quarter(i)])

    for step in range(len(first_units) + 3):
        relay_first(step)
        if step == 0:
            @pl.when(role == 0)
            def _():
                x_copies(lambda copy: copy.start())

            send_small(feeds_zero_late)
            supply_firsts(feeds_zero_late, 1)
        if step == 3:
            @pl.when(feeds_one)
            def _():
                pl.semaphore_signal(go_sem, inc=1, device_id=(1, d, partner), device_id_type=MESH)

                supply_first(0, 1, lambda copy: copy.start())

            send_small(feeds_one)
        if step == 6:
            @pl.when(feeds_one)
            def _():
                supply_first(1, 1, lambda copy: copy.start())


        @pl.when(feeds_zero_late)
        def _():
            if 1 <= step < 5:
                supply_copies(0, step - 1, lambda copy: copy.start())

    @pl.when(feeds_one_late)
    def _():
        lax.fori_loop(0, 3, supply_all, 0)

    def unit_piece(m, start, count, h):
        q = quarter(1 + m // 4)
        first_row = (m % 4) * UNIT_ROWS + (start + 4 * h) * PART_ROWS
        return wud.at[q, pl.ds(pl.multiple_of(first_row, PART_ROWS), PART_ROWS * count)]

    def relay_copy(m, stage):
        start, count = ((place, 1), (pair_start, 2), (0, 4))[stage]
        at = unit_piece(m, start, count, s)
        return pltpu.make_async_remote_copy(
            src_ref=at, dst_ref=at, send_sem=(as_sem, bs_sem, cs_sem)[stage].at[m],
            recv_sem=(ar_sem, br_sem, cr_sem)[stage].at[m],
            device_id=((s, near1, z), (s, near2, z), (other, d, z))[stage], device_id_type=MESH,
        )

    def relay(n):
        for c in range(4):

            @pl.when(jnp.logical_and(feeds_one, n == c))
            def _():
                supply_copies(1, c, lambda copy: copy.start())

        for k, lag in enumerate((0, 1, 3, 4)):
            m = n - lag

            @pl.when(jnp.logical_and(m >= 0, m < UNITS))
            def _():
                if k == 0:
                    arrived(unit_piece(m, place, 1, s), zr_sem.at[m])
                if k == 1:
                    arrived(unit_piece(m, pair_start + 1 - place % 2, 1, s), ar_sem.at[m])
                if k == 2:
                    arrived(unit_piece(m, far_start, 2, s), br_sem.at[m])
                if k == 3:
                    arrived(unit_piece(m, 0, 4, other), cr_sem.at[m])
                if k < 3:
                    relay_copy(m, k).start()

    @pl.when(role == 1)
    def _():
        cot_copies(lambda copy: copy.start())
    def relay_steps(start, stop):
        def one(n, carry):
            relay(n)
            return carry

        lax.fori_loop(start, stop, one, 0)

    relay_steps(0, jnp.where(role == 1, AHEAD, 0))
    arrived(wq.at[z], own_sem.at[0])
    arrived(wo.at[z], own_sem.at[1])
    arrived(wud.at[z, 0:1024], own_sem.at[2])
    arrived(wud.at[z, 1024:2048], own_sem.at[3])
    arrived(vec.at[0], vec_sem.at[0])
    for q in range(4):
        arrived(pre.at[q], pre_sem.at[q])
        carried = pre[q].astype(jnp.float32)
        for k in range(2):
            for n in range(2):
                row = PREFIX + 2 * k + n
                vec[q, 6 + k : 7 + k, n * half_width : (n + 1) * half_width] = carried[row : row + 1, :]

    first16 = lax.broadcasted_iota(jnp.int32, (16, 128), 1) < HEAD_DIM
    first = lax.broadcasted_iota(jnp.int32, (BLOCK, 128), 1) < HEAD_DIM
    lane = lax.broadcasted_iota(jnp.int32, (1, 128), 1)
    half0 = jnp.where(lane < HEAD_DIM, 1.0, 0.0).astype(jnp.bfloat16)
    half1 = jnp.where(lane < HEAD_DIM, 0.0, 1.0).astype(jnp.bfloat16)
    upper = lax.broadcasted_iota(jnp.int32, (128, BLOCK), 0) < HEAD_DIM
    slot = lax.broadcasted_iota(jnp.int32, (128, 1), 0)
    pre_mask_down = jnp.where(slot % HEAD_DIM < PREFIX, 0.0, NEG_LARGE)
    pre_mask = jnp.where(lane % HEAD_DIM < PREFIX, 0.0, NEG_LARGE)
    kp[...] = jnp.zeros(kp.shape, kp.dtype)
    vp[...] = jnp.zeros(vp.shape, vp.dtype)
    for q in range(4):
        for p in range(2):
            t0 = pre[q, :, p * 256 : p * 256 + 128].astype(jnp.float32)
            t1 = pre[q, :, p * 256 + 128 : p * 256 + 256].astype(jnp.float32)
            kp[2 * q + p, 0:16, :] = jnp.where(first16, t0, 0.0).astype(jnp.bfloat16)
            kp[2 * q + p, 64:80, :] = jnp.where(first16, 0.0, pltpu.roll(t1, 64, 1)).astype(jnp.bfloat16)
            vp[2 * q + p, 0:16, :] = jnp.where(first16, pltpu.roll(t0, 64, 1), 0.0).astype(jnp.bfloat16)
            vp[2 * q + p, 64:80, :] = jnp.where(first16, 0.0, t1).astype(jnp.bfloat16)

    def mask_blocks(keys_down):
        for j in range(2):
            row0 = block_of(s, j) * BLOCK
            row_at = row0 + lax.broadcasted_iota(jnp.int32, (1, BLOCK) if keys_down else (BLOCK, 1), int(keys_down))
            begin = jnp.zeros(row_at.shape, jnp.int32)
            end = 0
            for e in range(lengths.shape[1]):
                end = end + lengths[micro, e]
                begin = jnp.where(row_at >= end, end, begin)

            def mask_block(kb, carry):
                key_at = kb * BLOCK + lax.broadcasted_iota(jnp.int32, (BLOCK, BLOCK), 1 - int(keys_down))
                keep = jnp.logical_and(key_at <= row_at, key_at >= begin)
                bias[2 * j + kb] = jnp.where(keep, 0.0, NEG_LARGE)
                return carry

            lax.fori_loop(0, 2 + 2 * j, mask_block, 0)

    mask_blocks(False)

    def vector(k, q=0, width=1024):
        return vec[q, k : k + 1, 0:width]

    def columns(n, width):
        return pl.ds(pl.multiple_of(n * width, width), width)

    def block_rows(j):
        return pl.ds(pl.multiple_of(j * BLOCK, BLOCK), BLOCK)

    def over_rows(j, action):
        def one(c, carry):
            action(pl.ds(pl.multiple_of(j * BLOCK + c * CHUNK, CHUNK), CHUNK))
            return carry

        lax.fori_loop(0, BLOCK // CHUNK, one, 0)

    def standardize(v):
        average = jnp.mean(v, axis=-1, keepdims=True)
        centred = v - average
        spread = jnp.mean(centred * centred, axis=-1, keepdims=True)
        return centred, lax.rsqrt(spread + EPSILON)

    def norm_back(v, gain, incoming):
        centred, inverse = standardize(v)
        xhat = centred * inverse
        e = incoming * gain
        return (e - jnp.mean(e, axis=-1, keepdims=True) - xhat * jnp.mean(e * xhat, axis=-1, keepdims=True)) * inverse

    def to_core(ref, send_sem, recv_sem):
        return pltpu.make_async_remote_copy(
            src_ref=ref, dst_ref=ref, send_sem=send_sem, recv_sem=recv_sem,
            device_id=(other, d, z), device_id_type=MESH,
        )

    scale = LOG2E * HEAD_DIM ** (-0.5)

    def enter(j):
        rows = block_rows(j)
        arrived(x_in.at[rows], x_sem.at[j])

        def norm_one(rows):
            centred, inverse = standardize(x_in[rows, :].astype(jnp.float32))
            normed[rows, :] = (centred * inverse * vector(0) + vector(1)).astype(jnp.bfloat16)

        over_rows(j, norm_one)

        def project(q, carry):
            triple = dot_nn(normed[rows, :], wq[q]) + vec[q, 7:8, 0:768]
            for p in range(2):
                t0, t1, t2 = (triple[:, p * 384 + n * 128 : p * 384 + n * 128 + 128] for n in range(3))
                q_own[2 * q + p, rows, :] = jnp.where(first, t0, t1).astype(jnp.bfloat16)
                kv[s, 2 * q + p, 0, rows, :] = pltpu.roll(jnp.where(first, t2, t0), 64, 1).astype(jnp.bfloat16)
                kv[s, 2 * q + p, 1, rows, :] = jnp.where(first, t1, t2).astype(jnp.bfloat16)
            to_core(kv.at[s, pl.ds(2 * q, 2), :, rows], kv_ssem.at[j, q], kv_rsem.at[j, q]).start()
            return carry

        lax.fori_loop(0, 4, project, 0)

    def attend_rows(pair, core, j):
        cols = columns(pair, 128)
        rows = slice(j * BLOCK, j * BLOCK + BLOCK)
        blocks = block_of(core, j) + 1
        q_pair = q_own[pair, rows, :]
        q_half = (q_pair * half0, q_pair * half1)
        t_pre = dot_nt(q_pair, kp[pair]) * scale + pre_mask
        tops = [jnp.where(first, t_pre, NEG_LARGE), jnp.where(first, NEG_LARGE, t_pre)]
        for kb in range(blocks):
            keys = kv[core_of(kb), pair, 0, (kb // 2) * BLOCK : (kb // 2 + 1) * BLOCK, :]
            for h in range(2):
                t = dot_nt(q_half[h], keys) * scale + bias[2 * j + kb]
                ts[h, kb] = t
                tops[h] = jnp.maximum(tops[h], jnp.maximum(t[:, :128], t[:, 128:]))
        highest = [jnp.max(tops[h], axis=1, keepdims=True) for h in range(2)]
        e_pre = jnp.exp2(t_pre - jnp.where(first, highest[0], highest[1]))
        sums = [jnp.where(first, e_pre, 0.0), jnp.where(first, 0.0, e_pre)]
        mixed = [jnp.zeros((BLOCK, 128), jnp.float32) for _ in range(2)]
        for kb in range(blocks):
            values = kv[core_of(kb), pair, 1, (kb // 2) * BLOCK : (kb // 2 + 1) * BLOCK, :]
            for h in range(2):
                e = jnp.exp2(ts[h, kb] - highest[h])
                sums[h] += e[:, :128] + e[:, 128:]
                mixed[h] += dot_nn(e.astype(jnp.bfloat16), values)
        total = [jnp.sum(sums[h], axis=1, keepdims=True) for h in range(2)]
        share = [1.0 / total[h] for h in range(2)]
        p_pre = (e_pre * jnp.where(first, share[0], share[1])).astype(jnp.bfloat16)
        result = jnp.where(first, mixed[0] * share[0], mixed[1] * share[1]) + dot_nn(p_pre, vp[pair])
        o_own[rows, cols] = result.astype(jnp.bfloat16)
        logs = [highest[h] + jnp.log(total[h]) * LOG2E for h in range(2)]
        lse[pair, rows, :] = jnp.where(first, logs[0], logs[1])

    def attend(j, relay_at):
        def kv_wait(q, carry):
            to_core(kv.at[s, pl.ds(2 * q, 2), :, block_rows(j)], kv_ssem.at[j, q], kv_rsem.at[j, q]).wait_send()
            arrived(kv.at[other, pl.ds(2 * q, 2), :, block_rows(j)], kv_rsem.at[j, q])
            return carry

        lax.fori_loop(0, 4, kv_wait, 0)
        for core in range(2):
            for block in range(2):

                @pl.when(jnp.logical_and(s == core, j == block))
                def _():
                    def attend_pair(pair, carry):
                        relay_steps(relay_at, jnp.where(jnp.logical_and(pair == 4, relay_at < UNITS + 4), relay_at + 1, relay_at))
                        attend_rows(pair, core, block)
                        return carry

                    lax.fori_loop(0, 8, attend_pair, 0)

        rows = block_rows(j)
        after[rows, :] = (
            x_in[rows, :].astype(jnp.float32) + dot_nn(o_own[rows, :], wo[...].reshape(1024, 1024)) + vector(2)
        )

        def norm_two(rows):
            centred, inverse = standardize(after[rows, :])
            normed[rows, :] = (centred * inverse * vector(3) + vector(4)).astype(jnp.bfloat16)
            acc[rows, :] = after[rows, :] + vector(5)

        over_rows(j, norm_two)

    def feed(j, i):
        rows = block_rows(j)
        q = quarter(i)
        u = dot_nn(normed[rows, :], wud[q, 0:1024, :]) + vec[q, 6:7, :]
        v = u * (GELU_A + (GELU_A * GELU_B) * (u * u))
        half_t = 0.5 + 0.5 * jnp.tanh(v)
        wide[rows, :] = (u * half_t).astype(jnp.bfloat16)
        slope[q, rows, :] = (half_t + half_t * (1.0 - half_t) * (6.0 * v - (4.0 * GELU_A) * u)).astype(jnp.bfloat16)
        acc[rows, :] += dot_nn(wide[rows, :], wud[q, 1024:2048, :])

    def hand_copies(j, k):
        rows = block_rows(j)
        landing, sem = ((x_in, x_sem), (act_out, act_sem), (g_in, g_sem), (ig_out, ig_sem))[k]
        if k % 2:
            dst, sem, target = landing.at[micro], sem.at[micro], (role, d, block_of(s, j))
        else:
            dst, sem, target = landing.at[rows], sem.at[j], (s, d, partner)
        return pltpu.make_async_remote_copy(
            src_ref=y_out.at[rows], dst_ref=dst, send_sem=hand_sem.at[k, j], recv_sem=sem,
            device_id=target, device_id_type=MESH,
        )

    def hand_on(j):
        rows = block_rows(j)
        y_out[rows, :] = acc[rows, :].astype(jnp.bfloat16)

        @pl.when(role == 1)
        def _():
            hand_copies(j, 1).start()

        @pl.when(jnp.logical_and(role == 0, j == 0))
        def _():
            hand_copies(0, 0).start()

        @pl.when(jnp.logical_and(role == 0, j == 1))
        def _():
            hand_copies(0, 0).wait_send()
            hand_copies(1, 0).start()
            hand_copies(1, 0).wait_send()
            for block in range(2):
                hand_copies(block, 1).start()

    def upto(n, table):
        total = jnp.int32(0)
        for k, entry in enumerate(table):
            total += jnp.where(n >= k, entry - (table[k - 1] if k else 0), 0)
        return total

    early_table = (0, 1, 2, 4, 6, 7, 8, 10, 12, 14, 16, 16, 16, 16)
    late_table = (AHEAD, 11, 13, 14, 15, 16, 16, 16, 16, 16, 16, 16, 16, 16)

    def forward(n, carry):
        turn = jnp.where(n == 11, 12, jnp.where(n == 12, 11, n))
        stage = jnp.where(role == 0, turn // 2, n % 7)
        j = jnp.where(role == 0, turn % 2, n // 7)
        before = jnp.where(
            role == 0,
            jnp.where(n == 0, 0, upto(n - 1, early_table)) + jnp.where(jnp.logical_or(n == 3, n == 4), 1, 0),
            jnp.where(n == 0, AHEAD, upto(n - 1, late_table)) + jnp.where(n == 2, 1, 0),
        )
        until = jnp.where(role == 0, upto(n, early_table), upto(n, late_table))
        relay_steps(before, until)

        @pl.when(jnp.logical_and(role == 0, n == 6))
        def _():
            cot_copies(lambda copy: copy.start())

        @pl.when(stage == 0)
        def _():
            enter(j)

        @pl.when(stage == 1)
        def _():
            attend(j, until)

        @pl.when(jnp.logical_and(stage >= 2, stage < 6))
        def _():
            feed(j, stage - 2)

        @pl.when(stage == 6)
        def _():
            hand_on(j)

        return carry

    lax.fori_loop(0, 14, forward, 0)

    def back_rows(pair, core, j):
        cols = columns(pair, 128)
        rows = slice(j * BLOCK, j * BLOCK + BLOCK)
        q_pair = q_own[pair, rows, :]
        q_half = (q_pair * half0, q_pair * half1)
        g_pair = wide[rows, cols]
        g_half = (g_pair * half0, g_pair * half1)
        product = g_pair.astype(jnp.float32) * o_own[rows, cols].astype(jnp.float32)
        row_term = [
            jnp.sum(jnp.where(first, product, 0.0), axis=1, keepdims=True),
            jnp.sum(jnp.where(first, 0.0, product), axis=1, keepdims=True),
        ]
        logs = jnp.transpose(lse[pair, rows, :])
        terms = jnp.transpose(jnp.where(first, row_term[0], row_term[1]))
        log_half = (logs[0:1, :], logs[64:65, :])
        term_half = (terms[0:1, :], terms[64:65, :])
        p_pre = jnp.exp2(dot_nt(kp[pair], q_pair) * scale + pre_mask_down - logs)
        dp_pre = dot_nt(vp[pair], g_pair)
        ds_pre = (p_pre * (dp_pre - terms)).astype(jnp.bfloat16)
        pv = dot_nn(p_pre.astype(jnp.bfloat16), g_pair)
        pk = dot_nn(ds_pre, q_pair)
        pk = jnp.where(first16, pk[0:16, :], pk[64:80, :]) * HEAD_DIM ** (-0.5)
        pv = jnp.where(first16, pv[0:16, :], pv[64:80, :])
        pg[pair, 0] = pk if j else pg[pair, 0] + pk
        pg[pair, 1] = pv if j else pg[pair, 1] + pv
        dq_pre = dot_tn(kp[pair], ds_pre)
        dqs = [jnp.zeros((128, BLOCK), jnp.float32) for _ in range(2)]
        for kb in range(4):
            held = dkv_own if core_of(kb) == core else dkv_send
            at = slice((kb // 2) * BLOCK, (kb // 2 + 1) * BLOCK)
            if kb > block_of(core, j):
                if j:
                    held[pair, 0, at, :] = jnp.zeros((BLOCK, 128), jnp.bfloat16)
                    held[pair, 1, at, :] = jnp.zeros((BLOCK, 128), jnp.bfloat16)
                continue
            keys = kv[core_of(kb), pair, 0, at, :]
            values = kv[core_of(kb), pair, 1, at, :]
            dv, dk = 0.0, 0.0
            if j == 0:
                dk = held[pair, 0, at, :].astype(jnp.float32)
                dv = held[pair, 1, at, :].astype(jnp.float32)
            for h in range(2):
                probs = jnp.exp2(dot_nt(keys, q_half[h]) * scale + bias[2 * j + kb] - log_half[h])
                grad_probs = dot_nt(values, g_half[h])
                grad_scores = (probs * (grad_probs - term_half[h])).astype(jnp.bfloat16)
                dv += dot_nn(probs.astype(jnp.bfloat16), g_half[h])
                dk += dot_nn(grad_scores, q_half[h])
                dqs[h] += dot_tn(keys, grad_scores)
            held[pair, 0, at, :] = dk.astype(jnp.bfloat16)
            held[pair, 1, at, :] = dv.astype(jnp.bfloat16)
        dq = (jnp.where(upper, dqs[0], dqs[1]) + dq_pre) * HEAD_DIM ** (-0.5)
        q_own[pair, rows, :] = jnp.transpose(dq).astype(jnp.bfloat16)

    def dkv_copy(j, pair):
        rows = block_rows(j)
        return pltpu.make_async_remote_copy(
            src_ref=dkv_send.at[pair, :, rows], dst_ref=dkv_recv.at[pair, :, rows],
            send_sem=dkv_ssem.at[j, pair], recv_sem=dkv_rsem.at[j, pair],
            device_id=(other, d, z), device_id_type=MESH,
        )

    contribution = micro * 2 + s

    def pg_copy(q):
        return pltpu.make_async_remote_copy(
            src_ref=pg.at[2 * q : 2 * q + 2], dst_ref=pg_near.at[contribution], send_sem=pg_ssem.at[q],
            recv_sem=pg_sem.at[contribution], device_id=(role, d, q), device_id_type=MESH,
        )

    def far_copy(k):
        return pltpu.make_async_remote_copy(
            src_ref=pg_far.at[d], dst_ref=pg_far.at[d], send_sem=far_ssem.at[k - 1], recv_sem=far_sem.at[d],
            device_id=(s, (d + k) % 4, z), device_id_type=MESH,
        )

    def sum_near():
        for k in range(4):
            arrived(pg_near.at[k], pg_sem.at[k])
        pg_far[d] = (pg_near[0] + pg_near[1]) + (pg_near[2] + pg_near[3])
        for k in range(1, 4):
            far_copy(k).start()

    def backward(n, carry):
        j = 1 - n
        rows = block_rows(j)
        arrived(g_in.at[rows], g_sem.at[j])
        acc[rows, :] = jnp.zeros((BLOCK, 1024), jnp.float32)

        def feed_back(q, carry):
            grad_act = dot_nt(g_in[rows, :], wud[q, 1024:2048, :])
            wide[rows, :] = (grad_act * slope[q, rows, :].astype(jnp.float32)).astype(jnp.bfloat16)
            acc[rows, :] += dot_nt(wide[rows, :], wud[q, 0:1024, :])
            return carry

        lax.fori_loop(0, 4, feed_back, 0)

        def middle(rows):
            dv = norm_back(after[rows, :], vector(3), acc[rows, :])
            normed[rows, :] = (g_in[rows, :].astype(jnp.float32) + dv).astype(jnp.bfloat16)

        over_rows(j, middle)
        wide[rows, :] = dot_nt(normed[rows, :], wo[...].reshape(1024, 1024)).astype(jnp.bfloat16)
        for core in range(2):
            for block in range(2):

                @pl.when(jnp.logical_and(s == core, j == block))
                def _():
                    def back_pair(pair, carry):
                        back_rows(pair, core, block)
                        dkv_copy(block, pair).start()
                        return carry

                    lax.fori_loop(0, 8, back_pair, 0)

        @pl.when(j == 0)
        def _():
            for q in range(4):
                is_here = jnp.logical_and(role == s, z == q)

                @pl.when(is_here)
                def _():
                    pltpu.make_async_copy(
                        pg.at[2 * q : 2 * q + 2], pg_near.at[contribution], pg_sem.at[contribution]
                    ).start()

                @pl.when(jnp.logical_not(is_here))
                def _():
                    pg_copy(q).start()

        acc[rows, :] = jnp.zeros((BLOCK, 1024), jnp.float32)

        def project_back(q, carry):
            for p in range(2):
                pair = 2 * q + p
                dkv_copy(j, pair).wait()
                dq = q_own[pair, rows, :].astype(jnp.float32)
                dk = dkv_own[pair, 0, rows, :].astype(jnp.float32) + dkv_recv[pair, 0, rows, :].astype(jnp.float32)
                dv = dkv_own[pair, 1, rows, :].astype(jnp.float32) + dkv_recv[pair, 1, rows, :].astype(jnp.float32)
                dk = pltpu.roll(dk * HEAD_DIM ** (-0.5), 64, 1)
                gt[:, p * 384 : p * 384 + 128] = jnp.where(first, dq, dk).astype(jnp.bfloat16)
                gt[:, p * 384 + 128 : p * 384 + 256] = jnp.where(first, dv, dq).astype(jnp.bfloat16)
                gt[:, p * 384 + 256 : p * 384 + 384] = jnp.where(first, dk, dv).astype(jnp.bfloat16)
            acc[rows, :] += dot_nt(gt[...], wq[q])
            return carry

        lax.fori_loop(0, 4, project_back, 0)

        @pl.when(jnp.logical_and(j == 0, role == 0))
        def _():
            sum_near()

        hand_copies(j, 1).wait_send()

        def give_back(rows):
            dv = norm_back(x_in[rows, :].astype(jnp.float32), vector(0), acc[rows, :])
            y_out[rows, :] = (normed[rows, :].astype(jnp.float32) + dv).astype(jnp.bfloat16)

        over_rows(j, give_back)

        @pl.when(role == 0)
        def _():
            hand_copies(j, 3).start()

        @pl.when(jnp.logical_and(role == 1, j == 1))
        def _():
            hand_copies(1, 2).start()

        @pl.when(jnp.logical_and(role == 1, j == 0))
        def _():
            hand_copies(0, 2).start()
            hand_copies(1, 2).wait_send()
            hand_copies(0, 2).wait_send()
            for block in range(2):
                hand_copies(block, 3).start()

        return carry

    mask_blocks(True)
    lax.fori_loop(0, 2, backward, 0)
    @pl.when(role == 1)
    def _():
        sum_near()

    for k in range(1, 4):
        arrived(pg_far.at[(d + k) % 4], far_sem.at[(d + k) % 4])
    total_pg = (pg_far[0] + pg_far[1]) + (pg_far[2] + pg_far[3])
    for p in range(2):
        keys, values = total_pg[p, 0], total_pg[p, 1]
        sum_out[:, p * 256 : p * 256 + 128] = jnp.where(first16, keys, pltpu.roll(values, 64, 1))
        sum_out[:, p * 256 + 128 : p * 256 + 256] = jnp.where(first16, pltpu.roll(keys, 64, 1), values)
    hidden_core[s] = dot_nt(sum_out[...].astype(jnp.bfloat16), pw[...])
    sends.start(hidden_core.at[s], hidden_core.at[s], core_sem.at[s], (other, d, z))
    arrived(hidden_core.at[other], core_sem.at[other])
    hidden_all[z] = hidden_core[0] + hidden_core[1]
    for k in range(1, 4):
        sends.start(hidden_all.at[z], hidden_all.at[z], hidden_sem.at[z], (s, d, (z + k) % 4))
    for k in range(1, 4):
        arrived(hidden_all.at[(z + k) % 4], hidden_sem.at[(z + k) % 4])
    hidden_out[...] = (hidden_all[0] + hidden_all[1]) + (hidden_all[2] + hidden_all[3])

    lax.fori_loop(0, 3, supply_done, 0)

    @pl.when(role == 0)
    def _():
        x_copies(lambda copy: copy.wait_send())

    @pl.when(feeds_one_late)
    def _():
        x_copies(lambda copy: copy.wait_send())

    firsts_done(jnp.logical_not(feeds_zero), 0)
    firsts_done(True, 1)

    def relays_done(m, carry):
        for stage in range(3):
            relay_copy(m, stage).wait_send()
        return carry

    lax.fori_loop(0, UNITS, relays_done, 0)
    cot_copies(lambda copy: copy.wait_send())
    for k in range(1, 4):
        far_copy(k).wait_send()
    for q in range(4):

        @pl.when(jnp.logical_not(jnp.logical_and(role == s, z == q)))
        def _():
            pg_copy(q).wait_send()

    for j in range(2):

        hand_copies(j, 3).wait_send()

    for k in range(2):
        arrived(act_out.at[k], act_sem.at[k])
        arrived(ig_out.at[k], ig_sem.at[k])
    sends.finish()


def run_layers(x, cot, wq, wo, wu, wd, *small):
    bf, f32 = jnp.bfloat16, jnp.float32
    vm, dma = pltpu.VMEM, pltpu.SemaphoreType.DMA
    rows = 2 * BLOCK
    width = x.shape[-1]
    pairs = width // 128
    pw = small[-3]
    scratch = [
        vm((8, width), f32), vm((16, pw.shape[1]), f32), vm((16, pw.shape[1]), bf), vm((4,) + wq.shape, bf), vm((4,) + wo.shape, bf), vm((4, 2 * wu.shape[0], width), bf),
        vm((4, 8, width), f32), vm((4, 16, pw.shape[1]), bf),
        vm((rows, width), bf), vm((rows, width), bf), vm((rows, width), bf), vm((rows, width), bf),
        vm((2, pairs, 2, rows, 128), bf), vm((pairs, rows, 128), bf), vm((rows, width), bf),
        vm((pairs, rows, 128), f32), vm((6, BLOCK, BLOCK), f32), vm((rows, width), f32), vm((rows, width), f32),
        vm((4, rows, wu.shape[1]), bf), vm((rows, wu.shape[1]), bf),
        vm((pairs, 2, 16, 128), f32), vm((4, 2, 2, 16, 128), f32), vm((4, 2, 2, 16, 128), f32), vm((2, 16, pw.shape[0]), f32), vm((4, 16, pw.shape[0]), f32),
        vm((2, 4, BLOCK, BLOCK), f32),
        vm((pairs, 2, rows, 128), bf), vm((pairs, 2, rows, 128), bf), vm((pairs, 2, rows, 128), bf),
        vm((pairs, 128, 128), bf), vm((pairs, 128, 128), bf),
        vm((BLOCK, wq.shape[1]), bf),
        dma((96,)), dma((4,)), dma((4,)), dma((2,)), dma((2,)), dma((2,)), dma((2,)), dma((4,)),
        dma((2, 4)), dma((2, 4)), dma((2, 4)), dma((2, 4)),
        dma((UNITS,)), dma((UNITS,)), dma((UNITS,)), dma((UNITS,)), dma((6, 2)), dma((UNITS, 2)), dma((UNITS,)), dma((UNITS,)), dma((UNITS,)),
        pltpu.SemaphoreType.REGULAR,
        dma((2, 4)), dma((2, 4)), dma((2, pairs)), dma((2, pairs)), dma((4,)), dma((4,)), dma((2,)), dma((4,)),
        dma((4, 2)), dma((2,)), dma((2,)), dma((4,)), dma((3,)), dma((8,)),
    ]
    anywhere = pl.BlockSpec(memory_space=pl.ANY)
    local = pl.BlockSpec(memory_space=pltpu.VMEM)
    return pl.pallas_call(
        layer_kernel,
        out_shape=(
            jax.ShapeDtypeStruct(x.shape, bf), jax.ShapeDtypeStruct(x.shape, bf),
            jax.ShapeDtypeStruct((16, pw.shape[1]), f32), jax.ShapeDtypeStruct((16, pw.shape[0]), f32),
            jax.ShapeDtypeStruct((16, pw.shape[0]), f32),
        ),
        in_specs=[anywhere] * 6 + [local] * 9 + [anywhere] + [local] * 3 + [pl.BlockSpec(memory_space=pltpu.SMEM)],
        out_specs=(anywhere, anywhere, local, local, local),
        scratch_shapes=scratch,
        name="two_layers",
        compiler_params=pltpu.CompilerParams(
            collective_id=0, has_side_effects=True, vmem_limit_bytes=63 * 2**20
        ),
    )(x, cot, wq, wo, wu, wd, *small)


def prefix_kernel(
    prefix_sum, hidden_grad, hidden_act, table, mid_w, act_held, ig_held,
    table_grad, mid_w_grad, mid_b_grad, prefix_w_grad, prefix_b_grad, act_out, ig_out, table_full, stage, in_sem, out_sem,
):
    incoming, outgoing = [], []
    for n, (held, out) in enumerate(((act_held, act_out), (ig_held, ig_out))):
        for k in range(2):
            incoming.append(pltpu.make_async_copy(held.at[k], stage.at[n, k], in_sem.at[n, k]))
            outgoing.append(pltpu.make_async_copy(stage.at[n, k], out.at[k], out_sem.at[n, k]))
            incoming[-1].start()
    for arriving, leaving in zip(incoming, outgoing):
        arriving.wait()
        leaving.start()
    prefix_low = prefix_sum[...].astype(jnp.bfloat16)
    act = hidden_act[...]
    prefix_b_grad[...] = jnp.sum(prefix_low.astype(jnp.float32), axis=0, keepdims=True)
    prefix_w_grad[...] = dot_tn(act.astype(jnp.bfloat16), prefix_low)
    pre_grad = (hidden_grad[...] * (1.0 - act * act)).astype(jnp.bfloat16)
    mid_b_grad[...] = jnp.sum(pre_grad.astype(jnp.float32), axis=0, keepdims=True)
    table_full[...] = jnp.zeros(table_full.shape, jnp.float32)
    table_full[0:PREFIX, :] = table[...].astype(jnp.float32)
    mid_w_grad[...] = dot_tn(table_full[...].astype(jnp.bfloat16), pre_grad)
    table_grad[...] = dot_nt(pre_grad, mid_w[...])[0:PREFIX, :]
    for leaving in outgoing:
        leaving.wait()


def run_prefix_back(prefix_sum, hidden_grad, hidden_act, table, mid_w, activations, input_grads):
    f32 = jnp.float32
    hidden, own = mid_w.shape[1], prefix_sum.shape[1]
    local, anywhere = pl.BlockSpec(memory_space=pltpu.VMEM), pl.BlockSpec(memory_space=pl.ANY)
    rows = jax.ShapeDtypeStruct(activations.shape, activations.dtype)
    return pl.pallas_call(
        prefix_kernel,
        out_shape=tuple(
            jax.ShapeDtypeStruct(shape, f32)
            for shape in (table.shape, mid_w.shape, (1, hidden), (hidden, own), (1, own))
        ) + (rows, rows),
        in_specs=[local] * 5 + [anywhere] * 2,
        out_specs=(local,) * 5 + (anywhere,) * 2,
        scratch_shapes=[
            pltpu.VMEM((16, table.shape[1]), f32), pltpu.VMEM((2,) + activations.shape, activations.dtype),
            pltpu.SemaphoreType.DMA((2, 2)), pltpu.SemaphoreType.DMA((2, 2)),
        ],
        name="prefix_network",
        compiler_params=pltpu.CompilerParams(vmem_limit_bytes=60 * 2**20),
    )(prefix_sum, hidden_grad, hidden_act, table, mid_w, activations, input_grads)


def pair_body(
    layer_input, cotangent, example_lengths, attn_gain, attn_shift, query_key_value_weight, qkv_bias,
    attention_output_weight, out_bias, ffn_gain, ffn_shift, up_projection_weight, up_projection_bias,
    down_projection_weight, down_bias, prefix_table, mid_weight, mid_bias, prefix_weight, prefix_bias,
):
    activations, input_grads, prefix_sum, hidden_grad, hidden_act = run_layers(
        layer_input[:, 0], cotangent[:, 0], query_key_value_weight[0], attention_output_weight[0],
        up_projection_weight[0], down_projection_weight[0],
        attn_gain, attn_shift, out_bias, ffn_gain, ffn_shift, down_bias, up_projection_bias, qkv_bias,
        prefix_table, mid_weight, mid_bias, prefix_weight, prefix_bias, example_lengths[:, 0],
    )
    (
        table_grad, mid_weight_grad, mid_bias_grad, prefix_weight_grad, prefix_bias_grad, activations, input_grads,
    ) = run_prefix_back(prefix_sum, hidden_grad, hidden_act, prefix_table, mid_weight, activations, input_grads)
    return (
        activations[None, :, None], input_grads[None, :, None],
        table_grad, mid_weight_grad, mid_bias_grad[0], prefix_weight_grad, prefix_bias_grad[0],
    )


def solution(mesh):
    placed = (
        P(None, "dp", "mp", None),
        P(None, "dp", "mp", None),
        P(None, "dp", None),
        P("section", None),
        P("section", None),
        P("section", None, "mp"),
        P("section", "mp"),
        P("section", "mp", None),
        P("section", None),
        P("section", None),
        P("section", None),
        P("section", None, "mp"),
        P("section", "mp"),
        P("section", "mp", None),
        P("section", None),
        P(),
        P(),
        P(),
        P(None, ("section", "mp")),
        P(("section", "mp")),
    )
    paired = mesh.shape["mp"] == 4 and mesh.shape["dp"] == 4
    return jax.shard_map(
        pair_body if paired else body,
        mesh=mesh,
        in_specs=placed,
        out_specs=(
            P("section", None, "dp", "mp", None),
            P("section", None, "dp", "mp", None),
            P(),
            P(),
            P(),
            P(None, ("section", "mp")),
            P(("section", "mp")),
        ),
        check_vma=False,
    )
```
